128 devices in a mesh: dp: 64 (over z, y, x), narrow: 2 (over core).
Axes of the slice: x: 4, y: 4, z: 4, core: 2. Of those that a mesh axis runs over, the one named last changes fastest.
Arguments:
- inputs: bfloat16 [2, 128, 128, 896], P(None, ('dp', 'narrow')), may hold values from -6 to 6
- cotangent: bfloat16 [2, 128, 128, 896], P(None, ('dp', 'narrow')), may hold values from -6 to 6
- lengths: int32 [2, 128], replicated, may hold values from 32 to 128, as said below
- query_weight: float32 [896, 896], P(('dp', 'narrow')), may hold values from -0.1875 to 0.1875
- key_weight: float32 [896, 128], P(('dp', 'narrow')), may hold values from -0.1875 to 0.1875
- value_weight: float32 [896, 128], P(('dp', 'narrow')), may hold values from -0.1875 to 0.1875
- out_weight: float32 [896, 896], P(('dp', 'narrow')), may hold values from -0.5 to 0.5
- gate_weight: float32 [896, 4864], P(None, ('dp', 'narrow')), may hold values from -0.1875 to 0.1875
- up_weight: float32 [896, 4864], P(None, ('dp', 'narrow')), may hold values from -0.1875 to 0.1875
- down_weight: float32 [4864, 896], P(('dp', 'narrow')), may hold values from -0.15625 to 0.15625
- vectors: float32 [2944], P(('dp', 'narrow')), may hold values from -1.2 to 3.15
- query_prior: float32 [896, 896], P(('dp', 'narrow')), may hold values from -378.585832 to 378.585832
- key_prior: float32 [896, 128], P(('dp', 'narrow')), may hold values from -378.585832 to 378.585832
- value_prior: float32 [896, 128], P(('dp', 'narrow')), may hold values from -2523.9055 to 2523.9055
- out_prior: float32 [896, 896], P(('dp', 'narrow')), may hold values from -441.68347 to 441.68347
- gate_prior: float32 [896, 4864], P(None, ('dp', 'narrow')), may hold values from -883.36694 to 883.36694
- up_prior: float32 [896, 4864], P(None, ('dp', 'narrow')), may hold values from -1009.5622 to 1009.5622
- down_prior: float32 [4864, 896], P(('dp', 'narrow')), may hold values from -1009.5622 to 1009.5622
- first_prior: float32 [2944], P(('dp', 'narrow')), may hold values from -123.39094 to 123.39094
- second_prior: float32 [2944], P(('dp', 'narrow')), may hold values from 0.786432 to 314.5728
Outputs:
- block_output: bfloat16 [2, 128, 128, 896], P(None, ('dp', 'narrow'))
- input_grad: bfloat16 [2, 128, 128, 896], P(None, ('dp', 'narrow'))
- query_momentum: float32 [896, 896], P(('dp', 'narrow'))
- key_momentum: float32 [896, 128], P(('dp', 'narrow'))
- value_momentum: float32 [896, 128], P(('dp', 'narrow'))
- out_momentum: float32 [896, 896], P(('dp', 'narrow'))
- gate_momentum: float32 [896, 4864], P(None, ('dp', 'narrow'))
- up_momentum: float32 [896, 4864], P(None, ('dp', 'narrow'))
- down_momentum: float32 [4864, 896], P(('dp', 'narrow'))
- query_new: float32 [896, 896], P(('dp', 'narrow'))
- key_new: float32 [896, 128], P(('dp', 'narrow'))
- value_new: float32 [896, 128], P(('dp', 'narrow'))
- out_new: float32 [896, 896], P(('dp', 'narrow'))
- gate_new: float32 [896, 4864], P(None, ('dp', 'narrow'))
- up_new: float32 [896, 4864], P(None, ('dp', 'narrow'))
- down_new: float32 [4864, 896], P(('dp', 'narrow'))
- vector_first: float32 [2944], P(('dp', 'narrow'))
- vector_second: float32 [2944], P(('dp', 'narrow'))
- vector_new: float32 [2944], P(('dp', 'narrow'))
The draws below stay inside these ranges and needn't reach their ends.
Inputs may be any that keep to these rules, and one draw needn't show every extreme that they name: `lengths`: in every micro-batch one sequence has 128 live tokens and another 128 // 4.
All inputs are finite; a program needn't handle non-finite values.
Results may differ from the reference program's by a relative error of at most 0.024.
Values may be sent and summed in bfloat16 or wider, within the bound.
A program may use at most 320 MiB of HBM per device.

```python
import math
import jax
import jax.numpy as jnp
from jax import lax

D = 896
FF = 4864
HEADS = 14
KV_HEADS = 2
HEAD = 64
SLOT = 128
MB = 2
NS_STEPS = 2
STEP = 10
KV_WIDTH = 128
SEQS = 128


def rising(count):
    ramp = jnp.arange(count, dtype=jnp.float32) / max(count - 1, 1)
    return 0.6 + 1.2 * ramp


def live_root():
    return math.sqrt(0.6 * MB * SEQS * SLOT)


def prior_matrix(key, rows, cols, along, factor):
    noise = jnp.clip(jax.random.normal(key, (rows, cols), jnp.float32), -4.0, 4.0)
    if along == 0:
        profile = rising(rows)[:, None]
    else:
        profile = rising(cols)[None, :]
    return noise * profile * (factor * live_root())


def draw_query_prior(key, part):
    return prior_matrix(key, D, D, 0, 0.3)


def draw_key_prior(key, part):
    return prior_matrix(key, D, KV_HEADS * HEAD, 0, 0.3)


def draw_value_prior(key, part):
    return prior_matrix(key, D, KV_HEADS * HEAD, 0, 2.0)


def draw_out_prior(key, part):
    return prior_matrix(key, D, D, 0, 0.35)


def draw_gate_prior(key, part):
    return prior_matrix(key, D, FF, 1, 0.7)


def draw_up_prior(key, part):
    return prior_matrix(key, D, FF, 1, 0.8)


def draw_down_prior(key, part):
    return prior_matrix(key, FF, D, 0, 0.8)


def segment_scale():
    kv_width = KV_HEADS * HEAD
    pieces = [jnp.full((D,), 1.0, jnp.float32), jnp.full((D,), 1.3, jnp.float32), jnp.full((D,), 0.2, jnp.float32), jnp.full((kv_width,), 0.5, jnp.float32), jnp.full((kv_width,), 2.0, jnp.float32)]
    return jnp.concatenate(pieces) * live_root()


def draw_vectors(key, part):
    kv_width = KV_HEADS * HEAD
    keys = jax.random.split(key, 3)
    first_gain = rising(D) * jax.random.uniform(keys[0], (D,), jnp.float32, 0.7, 1.4)
    second_gain = rising(D) * jax.random.uniform(keys[1], (D,), jnp.float32, 0.7, 1.4)
    count = D + 2 * kv_width
    biases = 0.3 * jnp.clip(jax.random.normal(keys[2], (count,), jnp.float32), -4.0, 4.0)
    return jnp.concatenate([first_gain, second_gain, biases])


def draw_first_prior(key, part):
    scale = segment_scale()
    noise = jnp.clip(jax.random.normal(key, scale.shape, jnp.float32), -4.0, 4.0)
    return 0.11 * scale * noise


def draw_second_prior(key, part):
    scale = segment_scale()
    factor = jnp.exp(jax.random.uniform(key, scale.shape, jnp.float32, 0.0, math.log(4.0)))
    return 0.001 * scale * scale * factor


def draw_lengths(key, part):
    keys = jax.random.split(key, 3)
    base = jax.random.randint(keys[0], (MB, SEQS), SLOT // 4, SLOT + 1)
    longest = jax.random.randint(keys[1], (MB, 1), 0, SEQS)
    offset = jax.random.randint(keys[2], (MB, 1), 1, SEQS)
    shortest = (longest + offset) % SEQS
    column = jnp.arange(SEQS, dtype=jnp.int32)[None, :]
    base = jnp.where(column == longest, SLOT, base)
    return jnp.where(column == shortest, SLOT // 4, base).astype(jnp.int32)


def block_levels(own_key, dims, cuts, low, high):
    gain = 1.0
    for position, blocks in cuts:
        draws = jax.random.uniform(jax.random.fold_in(jax.random.fold_in(own_key, 6), position), (blocks,), jnp.float32, low / len(cuts), high / len(cuts))
        gain = gain * jnp.repeat(jnp.exp(draws), dims[position] // blocks).reshape((-1,) + (1,) * (len(dims) - 1 - position))
    return gain


def centred(stream_key, dims, deviation, most, cuts=(), kind=jnp.bfloat16):
    drawn = jax.random.normal(stream_key, dims, jnp.float32) * deviation
    if len(cuts) > 0:
        drawn = block_levels(stream_key, dims, cuts, -0.22, 0.18) * drawn
    return jnp.clip(drawn, min=-most, max=most).astype(kind)


def setup_inputs(seed: int = 0) -> dict:
    streams_of = jax.random.split(jax.random.key(seed), 21)
    return {
        "inputs": centred(streams_of[0], (MB, SEQS, SLOT, D), 1.0, 6.0, ((1, 128),)),
        "cotangent": centred(streams_of[1], (MB, SEQS, SLOT, D), 1.0, 6.0, ((1, 128),)),
        "lengths": draw_lengths(jax.random.fold_in(streams_of[20], 71), 0),
        "query_weight": centred(streams_of[3], (D, D), D ** -0.5, 0.1875, ((0, 128),), jnp.float32),
        "key_weight": centred(streams_of[4], (D, KV_WIDTH), D ** -0.5, 0.1875, ((0, 128),), jnp.float32),
        "value_weight": centred(streams_of[5], (D, KV_WIDTH), D ** -0.5, 0.1875, ((0, 128),), jnp.float32),
        "out_weight": centred(streams_of[6], (D, D), (D // 8) ** -0.5, 0.5, ((0, 128),), jnp.float32),
        "gate_weight": centred(streams_of[7], (D, FF), D ** -0.5, 0.1875, ((1, 128),), jnp.float32),
        "up_weight": centred(streams_of[8], (D, FF), D ** -0.5, 0.1875, ((1, 128),), jnp.float32),
        "down_weight": centred(streams_of[9], (FF, D), (FF // 4) ** -0.5, 0.15625, ((0, 128),), jnp.float32),
        "vectors": draw_vectors(jax.random.fold_in(streams_of[20], 71), 0),
        "query_prior": draw_query_prior(jax.random.fold_in(streams_of[20], 71), 0),
        "key_prior": draw_key_prior(jax.random.fold_in(streams_of[20], 71), 0),
        "value_prior": draw_value_prior(jax.random.fold_in(streams_of[20], 71), 0),
        "out_prior": draw_out_prior(jax.random.fold_in(streams_of[20], 71), 0),
        "gate_prior": draw_gate_prior(jax.random.fold_in(streams_of[20], 71), 0),
        "up_prior": draw_up_prior(jax.random.fold_in(streams_of[20], 71), 0),
        "down_prior": draw_down_prior(jax.random.fold_in(streams_of[20], 71), 0),
        "first_prior": draw_first_prior(jax.random.fold_in(streams_of[20], 71), 0),
        "second_prior": draw_second_prior(jax.random.fold_in(streams_of[20], 71), 0),
    }


NORM_EPSILON = 1e-06
ROPE_BASE = 1000000.0
MOMENTUM = 0.95
NEWTON_A = 3.4445
NEWTON_B = -4.775
NEWTON_C = 2.0315
MUON_RATE = 0.4
MUON_DECAY = 0.1
ADAM_RATE = 0.5
ADAM_DECAY = 0.01
BETA_FIRST = 0.9
BETA_SECOND = 0.999
ADAM_EPSILON = 1e-08
MASKED = -1e+30

@jax.custom_vjp
def low(v):
    return lax.optimization_barrier(v.astype(jnp.bfloat16)).astype(jnp.float32)

@jax.custom_vjp
def low_back(v):
    return v

def low_keep(v):
    return (low(v), None)

def low_pass(kept, grad):
    return (grad,)

def back_keep(v):
    return (v, None)

def back_low(kept, grad):
    return (low(grad),)
low.defvjp(low_keep, low_pass)
low_back.defvjp(back_keep, back_low)

def product(left, right):
    return jnp.dot(left, right, precision=lax.Precision.HIGHEST, preferred_element_type=jnp.float32)

def rotate_half(values):
    half = values.shape[-1] // 2
    return jnp.concatenate([-values[..., half:], values[..., :half]], axis=-1)

def rotary_tables(length):
    half = HEAD // 2
    freqs = ROPE_BASE ** (-jnp.arange(half, dtype=jnp.float32) * 2.0 / HEAD)
    angles = jnp.arange(length, dtype=jnp.float32)[:, None] * freqs[None, :]
    angles = jnp.concatenate([angles, angles], axis=-1)
    return (jnp.cos(angles), jnp.sin(angles))

def rotary(values, cosine, sine):
    return values * cosine[None, :, None, :] + rotate_half(values) * sine[None, :, None, :]

def block_forward(params, inputs, live, allowed, cosine, sine):
    query_weight, key_weight, value_weight, out_weight, gate_weight, up_weight, down_weight, vectors = params
    first_gain = vectors[:D]
    second_gain = vectors[D:2 * D]
    query_bias = vectors[2 * D:3 * D]
    key_bias = vectors[3 * D:3 * D + KV_WIDTH]
    value_bias = vectors[3 * D + KV_WIDTH:]
    batch, length = (inputs.shape[0], inputs.shape[1])
    group = HEADS // KV_HEADS
    first_scale = lax.rsqrt(lax.optimization_barrier(jnp.mean(inputs * inputs, axis=-1, keepdims=True)) + NORM_EPSILON)
    normed = low(inputs * first_scale * first_gain)
    queries = low_back(product(normed, query_weight) + query_bias)
    keys = low_back(product(normed, key_weight) + key_bias)
    values = low_back(product(normed, value_weight) + value_bias)
    queries = low(rotary(queries.reshape(batch, length, HEADS, HEAD), cosine, sine))
    queries = queries.reshape(batch, length, KV_HEADS, group, HEAD)
    keys = low(rotary(keys.reshape(batch, length, KV_HEADS, HEAD), cosine, sine))
    values = low(values).reshape(batch, length, KV_HEADS, HEAD)
    scores = jnp.einsum('bigrd,bjgd->bgrij', queries, keys, precision=lax.Precision.HIGHEST) * HEAD ** (-0.5)
    scores = low_back(scores)
    scores = jnp.where(allowed[:, None, None, :, :], scores, MASKED)
    weights = low(jax.nn.softmax(scores, axis=-1))
    mixed = jnp.einsum('bgrij,bjgd->bigrd', weights, values, precision=lax.Precision.HIGHEST)
    mixed = low(low_back(mixed.reshape(batch, length, D)))
    middle = inputs + low_back(product(mixed, out_weight))
    second_scale = lax.rsqrt(lax.optimization_barrier(jnp.mean(middle * middle, axis=-1, keepdims=True)) + NORM_EPSILON)
    normed_two = low(middle * second_scale * second_gain)
    gate = low_back(product(normed_two, gate_weight))
    up = low_back(product(normed_two, up_weight))
    hidden = low(jax.nn.silu(gate) * up)
    return (middle + low_back(product(hidden, down_weight))) * live[:, :, None]

def orthogonal(moment, left):
    squares = jnp.sum(moment * moment)
    current = low(moment / (jnp.sqrt(squares) + 1e-07))
    for step in range(NS_STEPS):
        gram = product(current, current.T) if left else product(current.T, current)
        gram_low = low(gram)
        mixer = low(NEWTON_B * gram + NEWTON_C * product(gram_low, gram_low))
        moved = product(mixer, current) if left else product(current, mixer)
        current = low(NEWTON_A * current + moved)
    return current

def reference(inputs, cotangent, lengths, query_weight, key_weight, value_weight, out_weight, gate_weight, up_weight, down_weight, vectors, query_prior, key_prior, value_prior, out_prior, gate_prior, up_prior, down_prior, first_prior, second_prior):
    masters = (query_weight, key_weight, value_weight, out_weight, gate_weight, up_weight, down_weight, vectors)
    copies = tuple((low(weight) for weight in masters))
    total = MB * SEQS
    group_size = math.gcd(total, max(1, 4096 // SLOT))
    count = total // group_size
    flat_in = inputs.astype(jnp.float32).reshape(count, group_size, SLOT, D)
    flat_back = cotangent.astype(jnp.float32).reshape(count, group_size, SLOT, D)
    flat_len = lengths.reshape(count, group_size).astype(jnp.int32)
    cosine, sine = rotary_tables(SLOT)
    positions = jnp.arange(SLOT, dtype=jnp.int32)

    def one_group(sums, pieces):
        block_in, block_back, block_len = pieces
        live = (positions[None, :] < block_len[:, None]).astype(jnp.float32)
        allowed = (positions[None, None, :] <= positions[None, :, None]) & (positions[None, None, :] < block_len[:, None, None])

        def apply(params, values):
            return block_forward(params, values, live, allowed, cosine, sine)
        outputs, pullback = jax.vjp(apply, copies, block_in)
        grad_params, grad_in = pullback(block_back)
        sums = jax.tree.map(lambda first, second: first + second, sums, grad_params)
        return (sums, (outputs.astype(jnp.bfloat16), grad_in.astype(jnp.bfloat16)))
    zeros = tuple((jnp.zeros_like(weight) for weight in copies))
    grads, (outputs, grad_inputs) = lax.scan(one_group, zeros, (flat_in, flat_back, flat_len))
    block_output = outputs.reshape(MB, SEQS, SLOT, D)
    input_grad = grad_inputs.reshape(MB, SEQS, SLOT, D)
    priors = (query_prior, key_prior, value_prior, out_prior, gate_prior, up_prior, down_prior)
    lefts = (False, False, False, False, True, True, False)
    momenta = []
    updated = []
    for index in range(7):
        moment = MOMENTUM * priors[index] + grads[index]
        ortho = orthogonal(moment, lefts[index])
        rows, cols = masters[index].shape
        factor = MUON_RATE * 0.2 * math.sqrt(max(rows, cols))
        momenta.append(moment)
        updated.append(masters[index] * (1.0 - MUON_RATE * MUON_DECAY) - factor * ortho)
    grad_vector = grads[7]
    vector_first = BETA_FIRST * first_prior + (1.0 - BETA_FIRST) * grad_vector
    vector_second = BETA_SECOND * second_prior + (1.0 - BETA_SECOND) * grad_vector * grad_vector
    first_hat = vector_first / (1.0 - BETA_FIRST ** STEP)
    second_hat = vector_second / (1.0 - BETA_SECOND ** STEP)
    vector_new = vectors * (1.0 - ADAM_RATE * ADAM_DECAY) - ADAM_RATE * first_hat / (jnp.sqrt(second_hat) + ADAM_EPSILON)
    return (block_output, input_grad, momenta[0], momenta[1], momenta[2], momenta[3], momenta[4], momenta[5], momenta[6], updated[0], updated[1], updated[2], updated[3], updated[4], updated[5], updated[6], vector_first, vector_second, vector_new)
```

```python
import math

import jax
import jax.numpy as jnp
from jax import lax
from jax.sharding import PartitionSpec as P

D = 896
FF = 4864
HEADS = 14
KV_HEADS = 2
HEAD = 64
STEP = 10


NORM_EPSILON = 1e-06
ROPE_BASE = 1000000.0
MOMENTUM = 0.95
NEWTON_A = 3.4445
NEWTON_B = -4.775
NEWTON_C = 2.0315
MUON_RATE = 0.4
MUON_DECAY = 0.1
ADAM_RATE = 0.5
ADAM_DECAY = 0.01
BETA_FIRST = 0.9
BETA_SECOND = 0.999
ADAM_EPSILON = 1e-08
MASKED = -1e30


def product(left, right):
    return jnp.dot(left, right, preferred_element_type=jnp.float32)


def inner_rows(left, right):
    return lax.dot_general(
        left, right, (((0,), (0,)), ((), ())), preferred_element_type=jnp.float32
    )


def outer_cols(left, right):
    return lax.dot_general(
        left, right, (((1,), (1,)), ((), ())), preferred_element_type=jnp.float32
    )


def rotate_half(values):
    half = values.shape[-1] // 2
    return jnp.concatenate([-values[..., half:], values[..., :half]], axis=-1)


def rotate_back(values):
    half = values.shape[-1] // 2
    return jnp.concatenate([values[..., half:], -values[..., :half]], axis=-1)


def rotary_tables(length):
    half = HEAD // 2
    freqs = ROPE_BASE ** (-jnp.arange(half, dtype=jnp.float32) * 2.0 / HEAD)
    angles = jnp.arange(length, dtype=jnp.float32)[:, None] * freqs[None, :]
    angles = jnp.concatenate([angles, angles], axis=-1)
    return (jnp.cos(angles), jnp.sin(angles))


def rotary(values, cosine, sine):
    return values * cosine[None, :, None, :] + rotate_half(values) * sine[None, :, None, :]


def rotary_grad(grads, cosine, sine):
    return grads * cosine[None, :, None, :] + rotate_back(grads * sine[None, :, None, :])


def norm_back(grad, normed, scale):
    return scale * (grad - normed * jnp.mean(grad * normed, axis=-1, keepdims=True))


def slot_pass(full, tokens, cotangent, lengths):
    (
        query_weight,
        key_weight,
        value_weight,
        out_weight,
        gate_rows,
        up_rows,
        down_weight,
        vectors,
    ) = full
    batch, rows = tokens.shape[0], tokens.shape[1]
    count = batch * rows
    kv_width = key_weight.shape[1]
    group = HEADS // KV_HEADS
    gains = vectors.astype(jnp.float32)
    first_gain = gains[:D]
    second_gain = gains[D : 2 * D]
    query_bias = gains[2 * D : 3 * D]
    key_bias = gains[3 * D : 3 * D + kv_width]
    value_bias = gains[3 * D + kv_width :]
    positions = jnp.arange(rows, dtype=jnp.int32)
    live = (positions[None, :] < lengths[:, None]).astype(jnp.float32).reshape(count, 1)
    allowed = (positions[None, None, :] <= positions[None, :, None]) & (
        positions[None, None, :] < lengths[:, None, None]
    )
    allowed = allowed[:, None, None]
    cosine, sine = rotary_tables(rows)
    inputs = tokens.astype(jnp.float32).reshape(count, D)
    first_scale = lax.rsqrt(jnp.mean(inputs * inputs, axis=-1, keepdims=True) + NORM_EPSILON)
    first_normed = inputs * first_scale
    normed = (first_normed * first_gain).astype(jnp.bfloat16)
    queries = product(normed, query_weight) + query_bias
    keys = product(normed, key_weight) + key_bias
    values = (product(normed, value_weight) + value_bias).astype(jnp.bfloat16)
    query_heads = rotary(queries.reshape(batch, rows, HEADS, HEAD), cosine, sine).astype(jnp.bfloat16)
    query_heads = query_heads.reshape(batch, rows, KV_HEADS, group, HEAD)
    key_heads = rotary(keys.reshape(batch, rows, KV_HEADS, HEAD), cosine, sine).astype(jnp.bfloat16)
    value_heads = values.reshape(batch, rows, KV_HEADS, HEAD)
    scores = jnp.einsum(
        "bigrd,bjgd->bgrij", query_heads, key_heads, preferred_element_type=jnp.float32
    )
    scores = jnp.where(allowed, scores * HEAD ** (-0.5), MASKED)
    peak = jnp.max(scores, axis=-1, keepdims=True)
    shifted = jnp.exp(scores - peak)
    total = jnp.sum(shifted, axis=-1, keepdims=True)
    probs = shifted / total
    weights = probs.astype(jnp.bfloat16)
    mixed = jnp.einsum("bgrij,bjgd->bigrd", weights, value_heads, preferred_element_type=jnp.float32)
    mixed = mixed.reshape(count, D).astype(jnp.bfloat16)
    middle = inputs + product(mixed, out_weight)
    second_scale = lax.rsqrt(jnp.mean(middle * middle, axis=-1, keepdims=True) + NORM_EPSILON)
    second_normed = middle * second_scale
    normed_two = (second_normed * second_gain).astype(jnp.bfloat16)
    gate = outer_cols(normed_two, gate_rows)
    up = outer_cols(normed_two, up_rows)
    sigma = jax.nn.sigmoid(gate)
    hidden = (gate * sigma * up).astype(jnp.bfloat16)
    result = ((middle + product(hidden, down_weight)) * live).astype(jnp.bfloat16)
    back = cotangent.astype(jnp.float32).reshape(count, D) * live
    back_half = back.astype(jnp.bfloat16)
    grad_down_w = inner_rows(hidden, back_half)
    grad_hidden = outer_cols(back_half, down_weight)
    grad_gate = (grad_hidden * up * sigma * (1.0 + gate * (1.0 - sigma))).astype(jnp.bfloat16)
    grad_up = (grad_hidden * gate * sigma).astype(jnp.bfloat16)
    grad_gate_w = inner_rows(grad_gate, normed_two)
    grad_up_w = inner_rows(grad_up, normed_two)
    grad_normed_two = product(grad_gate, gate_rows) + product(grad_up, up_rows)
    second_gain_grad = jnp.sum(grad_normed_two * second_normed, axis=0)
    grad_middle = back + norm_back(grad_normed_two * second_gain, second_normed, second_scale)
    branch_grad = grad_middle.astype(jnp.bfloat16)
    grad_out_w = inner_rows(mixed, branch_grad)
    grad_mixed = outer_cols(branch_grad, out_weight).astype(jnp.bfloat16)
    grad_mixed = grad_mixed.reshape(batch, rows, KV_HEADS, group, HEAD)
    grad_probs = jnp.einsum(
        "bigrd,bjgd->bgrij", grad_mixed, value_heads, preferred_element_type=jnp.float32
    )
    grad_scores = probs * (grad_probs - jnp.sum(probs * grad_probs, axis=-1, keepdims=True))
    grad_scores = grad_scores.astype(jnp.bfloat16)
    grad_query = jnp.einsum(
        "bgrij,bjgd->bigrd", grad_scores, key_heads, preferred_element_type=jnp.float32
    ) * HEAD ** (-0.5)
    grad_key = jnp.einsum(
        "bgrij,bigrd->bjgd", grad_scores, query_heads, preferred_element_type=jnp.float32
    ) * HEAD ** (-0.5)
    grad_value = jnp.einsum(
        "bgrij,bigrd->bjgd", weights, grad_mixed, preferred_element_type=jnp.float32
    )
    grad_value = grad_value.astype(jnp.bfloat16).reshape(count, kv_width)
    grad_query = (
        rotary_grad(grad_query.reshape(batch, rows, HEADS, HEAD), cosine, sine)
        .astype(jnp.bfloat16)
        .reshape(count, D)
    )
    grad_key = rotary_grad(grad_key, cosine, sine).astype(jnp.bfloat16).reshape(count, kv_width)
    query_bias_grad = jnp.sum(grad_query.astype(jnp.float32), axis=0)
    key_bias_grad = jnp.sum(grad_key.astype(jnp.float32), axis=0)
    value_bias_grad = jnp.sum(grad_value.astype(jnp.float32), axis=0)
    grad_query_w = inner_rows(normed, grad_query)
    grad_key_w = inner_rows(normed, grad_key)
    grad_value_w = inner_rows(normed, grad_value)
    grad_normed = (
        outer_cols(grad_query, query_weight)
        + outer_cols(grad_key, key_weight)
        + outer_cols(grad_value, value_weight)
    )
    first_gain_grad = jnp.sum(grad_normed * first_normed, axis=0)
    grad_inputs = (
        grad_middle + norm_back(grad_normed * first_gain, first_normed, first_scale)
    ).astype(jnp.bfloat16)
    vector_grad = jnp.concatenate(
        [first_gain_grad, second_gain_grad, query_bias_grad, key_bias_grad, value_bias_grad]
    )
    grads = (
        grad_query_w,
        grad_key_w,
        grad_value_w,
        grad_out_w,
        grad_gate_w,
        grad_up_w,
        grad_down_w,
        vector_grad,
    )
    return (
        result.reshape(batch, 1, rows, D),
        grad_inputs.reshape(batch, 1, rows, D),
        grads,
    )


def half(value):
    return value.astype(jnp.bfloat16)


def mixing(gram):
    gram_half = half(gram)
    first = half(NEWTON_B * gram + NEWTON_C * product(gram_half, gram_half))
    cross = product(gram_half, first)
    after = (
        NEWTON_A * NEWTON_A * gram + 2.0 * NEWTON_A * cross + product(half(cross), first)
    )
    after_half = half(after)
    second = NEWTON_B * after + NEWTON_C * product(after_half, after_half)
    return half(
        NEWTON_A * (first.astype(jnp.float32) + second) + product(first, half(second))
    )


def body(
    inputs,
    cotangent,
    lengths,
    query_weight,
    key_weight,
    value_weight,
    out_weight,
    gate_weight,
    up_weight,
    down_weight,
    vectors,
    query_prior,
    key_prior,
    value_prior,
    out_prior,
    gate_prior,
    up_prior,
    down_prior,
    first_prior,
    second_prior,
):
    axes = ("dp", "narrow")
    count = lax.axis_size("dp") * lax.axis_size("narrow")
    index = lax.axis_index("dp") * lax.axis_size("narrow") + lax.axis_index("narrow")
    rows = query_weight.shape[0]
    units = down_weight.shape[0]
    kv_width = key_weight.shape[1]
    packed = half(
        jnp.concatenate([query_weight, out_weight, gate_weight.T, up_weight.T, down_weight])
    )
    narrow = half(jnp.concatenate([key_weight, value_weight], axis=1))
    gathered = lax.all_gather(packed, axes, axis=0)
    gathered_narrow = lax.all_gather(narrow, axes, axis=0)
    gathered_vectors = lax.all_gather(half(vectors), axes, axis=0)
    cuts = (0, rows, 2 * rows, 2 * rows + units, 2 * rows + 2 * units, 2 * rows + 3 * units)
    pieces = [
        gathered[:, cuts[k] : cuts[k + 1]].reshape(count * (cuts[k + 1] - cuts[k]), D)
        for k in range(5)
    ]
    full = (
        pieces[0],
        gathered_narrow[:, :, :kv_width].reshape(D, kv_width),
        gathered_narrow[:, :, kv_width:].reshape(D, kv_width),
        pieces[1],
        pieces[2],
        pieces[3],
        pieces[4],
        gathered_vectors.reshape(-1),
    )
    own_lengths = lax.dynamic_slice_in_dim(lengths, index, 1, axis=1)[:, 0]
    block_output, input_grad, grads = slot_pass(full, inputs[:, 0], cotangent[:, 0], own_lengths)
    wide = jnp.concatenate(
        [
            half(grads[k]).reshape(count, -1, D)
            for k in (0, 3, 4, 5, 6)
        ],
        axis=1,
    )
    thin = jnp.concatenate(
        [
            half(grads[1]).reshape(count, rows, kv_width),
            half(grads[2]).reshape(count, rows, kv_width),
        ],
        axis=2,
    )
    own_wide = lax.psum_scatter(wide, axes, scatter_dimension=0).astype(jnp.float32)
    own_thin = lax.psum_scatter(thin, axes, scatter_dimension=0).astype(jnp.float32)
    grad_vector = lax.psum_scatter(grads[7], axes, scatter_dimension=0, tiled=True)
    owned = (
        own_wide[cuts[0] : cuts[1]],
        own_thin[:, :kv_width],
        own_thin[:, kv_width:],
        own_wide[cuts[1] : cuts[2]],
        own_wide[cuts[2] : cuts[3]],
        own_wide[cuts[3] : cuts[4]],
        own_wide[cuts[4] : cuts[5]],
    )
    priors = (
        query_prior,
        key_prior,
        value_prior,
        out_prior,
        gate_prior.T,
        up_prior.T,
        down_prior,
    )
    masters = (
        query_weight,
        key_weight,
        value_weight,
        out_weight,
        gate_weight,
        up_weight,
        down_weight,
    )
    shapes = ((D, D), (D, kv_width), (D, kv_width), (D, D), (D, FF), (D, FF), (FF, D))
    lefts = (False, False, False, False, True, True, False)
    momenta = tuple((MOMENTUM * priors[k] + owned[k] for k in range(7)))
    partial = [half(inner_rows(half(moment), half(moment))) for moment in momenta]
    big = lax.psum(jnp.stack([partial[k] for k in (0, 3, 4, 5, 6)]), axes).astype(jnp.float32)
    small = lax.psum(jnp.stack([partial[k] for k in (1, 2)]), axes).astype(jnp.float32)
    grams = (big[0], small[0], small[1], big[1], big[2], big[3], big[4])
    updated = []
    kept = []
    for k in range(7):
        gram = grams[k]
        norm = jnp.sqrt(jnp.trace(gram)) + 1e-07
        inverse = 1.0 / norm
        mixer = mixing(gram * inverse * inverse)
        current = momenta[k] * inverse
        current = NEWTON_A * NEWTON_A * current + product(half(current), mixer)
        factor = MUON_RATE * 0.2 * math.sqrt(max(shapes[k][0], shapes[k][1]))
        if lefts[k]:
            current = current.T
        updated.append(masters[k] * (1.0 - MUON_RATE * MUON_DECAY) - factor * current)
        kept.append(momenta[k].T if lefts[k] else momenta[k])
    vector_first = BETA_FIRST * first_prior + (1.0 - BETA_FIRST) * grad_vector
    vector_second = BETA_SECOND * second_prior + (1.0 - BETA_SECOND) * grad_vector * grad_vector
    first_hat = vector_first / (1.0 - BETA_FIRST**STEP)
    second_hat = vector_second / (1.0 - BETA_SECOND**STEP)
    vector_new = vectors * (1.0 - ADAM_RATE * ADAM_DECAY) - ADAM_RATE * first_hat / (
        jnp.sqrt(second_hat) + ADAM_EPSILON
    )
    return (
        block_output,
        input_grad,
        *kept,
        *updated,
        vector_first,
        vector_second,
        vector_new,
    )


def solution(mesh):
    placed = (
        P(None, ("dp", "narrow"), None, None),
        P(None, ("dp", "narrow"), None, None),
        P(),
        P(("dp", "narrow"), None),
        P(("dp", "narrow"), None),
        P(("dp", "narrow"), None),
        P(("dp", "narrow"), None),
        P(None, ("dp", "narrow")),
        P(None, ("dp", "narrow")),
        P(("dp", "narrow"), None),
        P(("dp", "narrow")),
        P(("dp", "narrow"), None),
        P(("dp", "narrow"), None),
        P(("dp", "narrow"), None),
        P(("dp", "narrow"), None),
        P(None, ("dp", "narrow")),
        P(None, ("dp", "narrow")),
        P(("dp", "narrow"), None),
        P(("dp", "narrow")),
        P(("dp", "narrow")),
    )
    return jax.shard_map(
        body,
        mesh=mesh,
        in_specs=placed,
        out_specs=(
            P(None, ("dp", "narrow"), None, None),
            P(None, ("dp", "narrow"), None, None),
            P(("dp", "narrow"), None),
            P(("dp", "narrow"), None),
            P(("dp", "narrow"), None),
            P(("dp", "narrow"), None),
            P(None, ("dp", "narrow")),
            P(None, ("dp", "narrow")),
            P(("dp", "narrow"), None),
            P(("dp", "narrow"), None),
            P(("dp", "narrow"), None),
            P(("dp", "narrow"), None),
            P(("dp", "narrow"), None),
            P(None, ("dp", "narrow")),
            P(None, ("dp", "narrow")),
            P(("dp", "narrow"), None),
            P(("dp", "narrow")),
            P(("dp", "narrow")),
            P(("dp", "narrow")),
        ),
        check_vma=False,
    )
```

```python
import math

import jax
import jax.numpy as jnp
from jax import lax
from jax.experimental import pallas as pl
from jax.experimental.pallas import tpu as pltpu
from jax.sharding import PartitionSpec as P

D = 896
FF = 4864
HEADS = 14
KV_HEADS = 2
HEAD = 64
STEP = 10


NORM_EPSILON = 1e-06
ROPE_BASE = 1000000.0
MOMENTUM = 0.95
NEWTON_A = 3.4445
NEWTON_B = -4.775
NEWTON_C = 2.0315
MUON_RATE = 0.4
MUON_DECAY = 0.1
ADAM_RATE = 0.5
ADAM_DECAY = 0.01
BETA_FIRST = 0.9
BETA_SECOND = 0.999
ADAM_EPSILON = 1e-08
MASKED = -1e30


def product(left, right):
    return jnp.dot(left, right, preferred_element_type=jnp.float32)


def inner_rows(left, right):
    return lax.dot_general(
        left, right, (((0,), (0,)), ((), ())), preferred_element_type=jnp.float32
    )


def outer_cols(left, right):
    return lax.dot_general(
        left, right, (((1,), (1,)), ((), ())), preferred_element_type=jnp.float32
    )


def rotate_half(values):
    half = values.shape[-1] // 2
    return jnp.concatenate([-values[..., half:], values[..., :half]], axis=-1)


def rotate_back(values):
    half = values.shape[-1] // 2
    return jnp.concatenate([values[..., half:], -values[..., :half]], axis=-1)


def rotary_tables(length):
    half = HEAD // 2
    freqs = ROPE_BASE ** (-jnp.arange(half, dtype=jnp.float32) * 2.0 / HEAD)
    angles = jnp.arange(length, dtype=jnp.float32)[:, None] * freqs[None, :]
    angles = jnp.concatenate([angles, angles], axis=-1)
    return (jnp.cos(angles), jnp.sin(angles))


def rotary(values, cosine, sine):
    return values * cosine[None, :, None, :] + rotate_half(values) * sine[None, :, None, :]


def rotary_grad(grads, cosine, sine):
    return grads * cosine[None, :, None, :] + rotate_back(grads * sine[None, :, None, :])


def norm_back(grad, normed, scale):
    return scale * (grad - normed * jnp.mean(grad * normed, axis=-1, keepdims=True))


MESH = pl.DeviceIdType.MESH
ROWS = 144
PART = 48
GATHER_ORDERS = ((2, 1, 0), (1, 0, 2), (0, 2, 1))


def my_coords():
    dp = lax.axis_index("dp")
    return (dp // 16, (dp // 4) % 4, dp % 4), lax.axis_index("narrow")


def device_of(coords, core):
    return (coords[0] * 16 + coords[1] * 4 + coords[2], core)


def shifted(coords, axis, by):
    out = list(coords)
    out[axis] = (coords[axis] + by) % 4
    return tuple(out)


def ring_barrier(coords, core):
    barrier = pltpu.get_barrier_semaphore()
    for axis in range(3):
        for by in (1, 3):
            pl.semaphore_signal(
                barrier, inc=1, device_id=device_of(shifted(coords, axis, by), core), device_id_type=MESH
            )
    pl.semaphore_signal(barrier, inc=1, device_id=device_of(coords, 1 - core), device_id_type=MESH)
    pl.semaphore_wait(barrier, 7)


def region(spec, part, rows=None):
    index = []
    for axis in range(2):
        s = spec[axis]
        index.append(pl.ds(*s) if isinstance(s, tuple) else s)
    s = spec[2]
    if isinstance(s, tuple):
        index += [pl.ds(s[0] // 2, s[1] // 2), slice(None)]
    else:
        index += [s // 2, s % 2]
    rows = (0, PART) if rows is None else rows
    return (*index, pl.ds(part * PART + rows[0], rows[1]), slice(None))


FULL = (0, 4)


def halves(spec, split_axis):
    if split_axis is None:
        return [(spec, (0, 32)), (spec, (32, 16))]
    out = []
    for h in range(2):
        s = list(spec)
        s[split_axis] = (2 * h, 2)
        out.append((tuple(s), None))
    return out


def gather_kernel(block_ref, out_ref, rest_ref, local_sem, send_sems, recv_sems, rest_sems):
    coords, core = my_coords()
    own = (coords[0], coords[1], coords[2])
    local = pltpu.make_async_copy(
        block_ref, out_ref.at[coords[0], coords[1], coords[2] // 2, coords[2] % 2], local_sem
    )
    local.start()
    ring_barrier(coords, core)
    local.wait()
    sends = []

    def send(part, phase, slot, piece, axis, by):
        spec, rows = piece
        ref = out_ref.at[region(spec, part, rows)]
        copy = pltpu.make_async_remote_copy(
            src_ref=ref,
            dst_ref=ref,
            send_sem=send_sems.at[part, phase, slot],
            recv_sem=recv_sems.at[part, phase, slot],
            device_id=device_of(shifted(coords, axis, by), core),
            device_id_type=MESH,
        )
        copy.start()
        sends.append(copy)

    def wait(part, phase, slot, piece):
        spec, rows = piece
        ref = out_ref.at[region(spec, part, rows)]
        pltpu.make_async_remote_copy(
            src_ref=ref,
            dst_ref=ref,
            send_sem=send_sems.at[part, phase, slot],
            recv_sem=recv_sems.at[part, phase, slot],
            device_id=device_of(shifted(coords, 0, 1), core),
            device_id_type=MESH,
        ).wait_recv()

    for phase in range(3):
        specs = []
        for part, order in enumerate(GATHER_ORDERS):
            axis = order[phase]
            split = order[phase - 1] if phase else None

            def spec_at(by, order=order, axis=axis):
                spec = [FULL if order.index(k) < phase else coords[k] for k in range(3)]
                spec[axis] = (coords[axis] + by) % 4
                return tuple(spec)

            specs.append((axis, spec_at, split))
        for part, (axis, spec_at, split) in enumerate(specs):
            h0, h1 = halves(spec_at(0), split)
            send(part, phase, 0, h0, axis, 1)
            send(part, phase, 1, h1, axis, 3)
            send(part, phase, 2, h1, axis, 1)
            send(part, phase, 3, h0, axis, 3)
        for part, (axis, spec_at, split) in enumerate(specs):
            wait(part, phase, 0, halves(spec_at(3), split)[0])
            send(part, phase, 4, halves(spec_at(3), split)[0], axis, 1)
            wait(part, phase, 1, halves(spec_at(1), split)[1])
            send(part, phase, 5, halves(spec_at(1), split)[1], axis, 3)
        for part, (axis, spec_at, split) in enumerate(specs):
            wait(part, phase, 2, halves(spec_at(3), split)[1])
            wait(part, phase, 3, halves(spec_at(1), split)[0])
            wait(part, phase, 4, halves(spec_at(2), split)[0])
            wait(part, phase, 5, halves(spec_at(2), split)[1])
    last = out_ref.at[:, :, :, 1, pl.ds(96, 48)]
    keep = pltpu.make_async_copy(last, rest_ref.at[core], local_sem)
    give = sibling_copy(last, rest_ref.at[core], rest_sems, 0, core)
    keep.start()
    give.start()
    keep.wait()
    give.wait()
    for copy in sends:
        copy.wait_send()


def gather_blocks(block):
    return pl.pallas_call(
        gather_kernel,
        out_shape=(
            jax.ShapeDtypeStruct((4, 4, 2, 2, ROWS, D), jnp.bfloat16),
            jax.ShapeDtypeStruct((2, 4, 4, 2, 48, D), jnp.bfloat16),
        ),
        in_specs=[pl.BlockSpec(memory_space=pl.ANY)],
        out_specs=(pl.BlockSpec(memory_space=pl.ANY),) * 2,
        scratch_shapes=[
            pltpu.SemaphoreType.DMA,
            pltpu.SemaphoreType.DMA((3, 3, 6)),
            pltpu.SemaphoreType.DMA((3, 3, 6)),
            pltpu.SemaphoreType.DMA((2, 1)),
        ],
        compiler_params=pltpu.CompilerParams(collective_id=0, has_side_effects=True),
    )(block)


def region_shape(spec, rows):
    shape = []
    for axis in range(2):
        if isinstance(spec[axis], tuple):
            shape.append(spec[axis][1])
    if isinstance(spec[2], tuple):
        shape += [spec[2][1] // 2, 2]
    return (*shape, PART if rows is None else rows[1], D)


SCATTER_ORDERS = tuple(order[::-1] for order in GATHER_ORDERS)


def static_specs(order, phase):
    spec = [FULL if order.index(k) > phase else 0 for k in range(3)]
    split = order[phase + 1] if phase < 2 else None
    return [region_shape(*piece) for piece in halves(tuple(spec), split)]


def each_block(shape, body):
    lead = shape[:-2]
    count = 1
    for n in lead:
        count *= n
    if count == 1:
        body((0,) * len(lead))
        return

    def step(k, carry):
        index = []
        for n in reversed(lead):
            index.append(k % n)
            k = k // n
        body(tuple(reversed(index)))
        return carry

    lax.fori_loop(0, count, step, 0)


def scatter_kernel(mlp_ref, rest_ref, out_ref, *scratch):
    buffers = scratch[:54]
    total, sibling, load_sems, send_sems, recv_sems, rest_sems = scratch[54:]
    coords, core = my_coords()
    loads = [
        pltpu.make_async_copy(
            mlp_ref.at[:, :, :, pl.ds(0, ROWS)], total.at[:, :, :, 0], load_sems.at[0]
        ),
        pltpu.make_async_copy(
            mlp_ref.at[:, :, :, pl.ds(ROWS, 96)], total.at[:, :, :, 1, pl.ds(0, 96)], load_sems.at[1]
        ),
        pltpu.make_async_copy(rest_ref.at[core], total.at[:, :, :, 1, pl.ds(96, 48)], load_sems.at[2]),
    ]
    for copy in loads:
        copy.start()
    ring_barrier(coords, core)
    give = sibling_copy(rest_ref.at[1 - core], sibling, rest_sems, 0, core)
    give.start()
    for copy in loads:
        copy.wait()
    give.wait()

    def join(index):
        place = (*index, 1, pl.ds(96, 48), slice(None))
        total[place] = half(total[place].astype(jnp.float32) + sibling[index].astype(jnp.float32))

    each_block((4, 4, 2, 48, D), join)
    sends = []

    def copy_of(part, phase, slot, piece, dst, axis, by):
        spec, rows = piece
        return pltpu.make_async_remote_copy(
            src_ref=total.at[region(spec, part, rows)],
            dst_ref=dst,
            send_sem=send_sems.at[part, phase, slot],
            recv_sem=recv_sems.at[part, phase, slot],
            device_id=device_of(shifted(coords, axis, by), core),
            device_id_type=MESH,
        )

    def send(*args):
        copy = copy_of(*args)
        copy.start()
        sends.append(copy)

    def add_piece(part, piece, *sources):
        spec, rows = piece
        shape = region_shape(spec, rows)
        base = region(spec, part, rows)

        def one(index):
            place = []
            position = 0
            for entry in base[:4]:
                if isinstance(entry, slice):
                    place.append(index[position])
                    position += 1
                elif isinstance(entry, pl.Slice):
                    place.append(entry.start + index[position])
                    position += 1
                else:
                    place.append(entry)
            place = (*place, base[4], slice(None))
            value = total[place].astype(jnp.float32)
            for source in sources:
                value = value + source[(*index, slice(None), slice(None))].astype(jnp.float32)
            total[place] = value.astype(jnp.bfloat16)

        each_block(shape, one)

    for phase in range(3):
        plans = []
        for part, order in enumerate(SCATTER_ORDERS):
            axis = order[phase]
            split = order[phase + 1] if phase < 2 else None

            def pieces_at(by, order=order, axis=axis, split=split):
                spec = [FULL if order.index(k) > phase else coords[k] for k in range(3)]
                spec[axis] = (coords[axis] + by) % 4
                return halves(tuple(spec), split)

            base = (part * 3 + phase) * 6
            bufs = buffers[base : base + 6]
            plans.append((axis, pieces_at, (bufs[0], bufs[1], bufs[2:4], bufs[4:6])))
        for part, (axis, pieces_at, bufs) in enumerate(plans):
            far_left, far_right, near_left, near_right = bufs
            send(part, phase, 0, pieces_at(2)[0], far_left, axis, 1)
            send(part, phase, 1, pieces_at(2)[1], far_right, axis, 3)
            send(part, phase, 2, pieces_at(1)[1], near_left[1], axis, 1)
            send(part, phase, 3, pieces_at(3)[0], near_right[0], axis, 3)
        for part, (axis, pieces_at, bufs) in enumerate(plans):
            far_left, far_right, near_left, near_right = bufs
            copy_of(part, phase, 0, pieces_at(2)[0], far_left, axis, 1).wait_recv()
            add_piece(part, pieces_at(1)[0], far_left)
            send(part, phase, 4, pieces_at(1)[0], near_left[0], axis, 1)
            copy_of(part, phase, 1, pieces_at(2)[1], far_right, axis, 3).wait_recv()
            add_piece(part, pieces_at(3)[1], far_right)
            send(part, phase, 5, pieces_at(3)[1], near_right[1], axis, 3)
        for part, (axis, pieces_at, bufs) in enumerate(plans):
            far_left, far_right, near_left, near_right = bufs
            copy_of(part, phase, 3, pieces_at(3)[0], near_right[0], axis, 3).wait_recv()
            copy_of(part, phase, 4, pieces_at(1)[0], near_left[0], axis, 1).wait_recv()
            add_piece(part, pieces_at(0)[0], near_left[0], near_right[0])
            copy_of(part, phase, 2, pieces_at(1)[1], near_left[1], axis, 1).wait_recv()
            copy_of(part, phase, 5, pieces_at(3)[1], near_right[1], axis, 3).wait_recv()
            add_piece(part, pieces_at(0)[1], near_left[1], near_right[1])
    for copy in sends:
        copy.wait_send()
    out_ref[...] = total[coords[0], coords[1], coords[2] // 2, coords[2] % 2]


def scatter_blocks(mlp, rest):
    scratch = []
    for order in SCATTER_ORDERS:
        for phase in range(3):
            h0, h1 = static_specs(order, phase)
            scratch += [pltpu.VMEM(shape, jnp.bfloat16) for shape in (h0, h1, h0, h1, h0, h1)]
    scratch += [
        pltpu.VMEM((4, 4, 2, 2, ROWS, D), jnp.bfloat16),
        pltpu.VMEM((4, 4, 2, 48, D), jnp.bfloat16),
        pltpu.SemaphoreType.DMA((3,)),
        pltpu.SemaphoreType.DMA((3, 3, 6)),
        pltpu.SemaphoreType.DMA((3, 3, 6)),
        pltpu.SemaphoreType.DMA((2, 1)),
    ]
    return pl.pallas_call(
        scatter_kernel,
        out_shape=jax.ShapeDtypeStruct((ROWS, D), jnp.bfloat16),
        in_specs=[pl.BlockSpec(memory_space=pl.ANY)] * 2,
        out_specs=pl.BlockSpec(memory_space=pltpu.VMEM),
        scratch_shapes=scratch,
        compiler_params=pltpu.CompilerParams(
            collective_id=1, has_side_effects=True, vmem_limit_bytes=56 * 2**20
        ),
    )(mlp, rest)


UNITS = 80
TILE_PAIRS = 8
TILE = TILE_PAIRS * UNITS
TILES = 32 // TILE_PAIRS
TOKENS = 256


def sibling_copy(src, dst, sems, slot, core):
    return pltpu.make_async_remote_copy(
        src_ref=src,
        dst_ref=dst,
        send_sem=sems.at[0, slot],
        recv_sem=sems.at[1, slot],
        device_id=(lax.axis_index("dp"), 1 - core),
        device_id_type=MESH,
    )


def mlp_kernel(
    h_ref, e_ref, gate_ref, up_ref, down_ref, out_ref, back_ref, grad_ref,
    h_all, e_all, out_acc, back_acc, parcel, arrived, sems,
):
    core = lax.axis_index("narrow")
    step = pl.program_id(0)

    @pl.when(step == 0)
    def _():
        barrier = pltpu.get_barrier_semaphore()
        pl.semaphore_signal(
            barrier, inc=1, device_id=(lax.axis_index("dp"), 1 - core), device_id_type=MESH
        )
        pl.semaphore_wait(barrier, 1)
        h_copy = sibling_copy(h_ref, h_all.at[core], sems, 0, core)
        e_copy = sibling_copy(e_ref, e_all.at[core], sems, 1, core)
        h_copy.start()
        e_copy.start()
        h_all[core] = h_ref[...]
        e_all[core] = e_ref[...]
        out_acc[...] = jnp.zeros_like(out_acc)
        back_acc[...] = jnp.zeros_like(back_acc)
        h_copy.wait()
        e_copy.wait()

    h = h_all[...].reshape(2 * TOKENS, D)
    e = e_all[...].reshape(2 * TOKENS, D)
    gate_w = gate_ref[...].reshape(TILE, D)
    up_w = up_ref[...].reshape(TILE, D)
    down_w = down_ref[...].reshape(TILE, D)
    gate = outer_cols(h, gate_w)
    up = outer_cols(h, up_w)
    sigma = jax.nn.sigmoid(gate)
    silu = gate * sigma
    hidden = half(silu * up)
    grad_hidden = outer_cols(e, down_w)
    out_acc[...] += product(hidden, down_w).reshape(2, TOKENS, D)
    grad_gate = half(grad_hidden * up * sigma * (1.0 + gate * (1.0 - sigma)))
    grad_up = half(grad_hidden * silu)
    back_acc[...] += (product(grad_gate, gate_w) + product(grad_up, up_w)).reshape(2, TOKENS, D)
    grad_ref[:, 0:UNITS] = half(inner_rows(grad_gate, h)).reshape(TILE_PAIRS, UNITS, D)
    grad_ref[:, UNITS : 2 * UNITS] = half(inner_rows(grad_up, h)).reshape(TILE_PAIRS, UNITS, D)
    grad_ref[:, 2 * UNITS :] = half(inner_rows(hidden, e)).reshape(TILE_PAIRS, UNITS, D)

    @pl.when(step == TILES - 1)
    def _():
        parcel[0] = half(out_acc[1 - core])
        parcel[1] = half(back_acc[1 - core])
        copy = sibling_copy(parcel, arrived, sems, 2, core)
        copy.start()
        copy.wait()
        out_ref[...] = out_acc[core] + arrived[0].astype(jnp.float32)
        back_ref[...] = back_acc[core] + arrived[1].astype(jnp.float32)


def mlp(normed_two, back_half, weights):
    whole = pl.BlockSpec((TOKENS, D), lambda i: (0, 0))
    return pl.pallas_call(
        mlp_kernel,
        grid=(TILES,),
        out_shape=(
            jax.ShapeDtypeStruct((TOKENS, D), jnp.float32),
            jax.ShapeDtypeStruct((TOKENS, D), jnp.float32),
            jax.ShapeDtypeStruct((32, 3 * UNITS, D), jnp.bfloat16),
        ),
        in_specs=[
            whole,
            whole,
            pl.BlockSpec((TILE_PAIRS, UNITS, D), lambda i: (i, 0, 0)),
            pl.BlockSpec((TILE_PAIRS, UNITS, D), lambda i: (i, 1, 0)),
            pl.BlockSpec((TILE_PAIRS, UNITS, D), lambda i: (i, 2, 0)),
        ],
        out_specs=(whole, whole, pl.BlockSpec((TILE_PAIRS, 3 * UNITS, D), lambda i: (i, 0, 0))),
        scratch_shapes=[
            pltpu.VMEM((2, TOKENS, D), jnp.bfloat16),
            pltpu.VMEM((2, TOKENS, D), jnp.bfloat16),
            pltpu.VMEM((2, TOKENS, D), jnp.float32),
            pltpu.VMEM((2, TOKENS, D), jnp.float32),
            pltpu.VMEM((2, TOKENS, D), jnp.bfloat16),
            pltpu.VMEM((2, TOKENS, D), jnp.bfloat16),
            pltpu.SemaphoreType.DMA((2, 3)),
        ],
        compiler_params=pltpu.CompilerParams(
            collective_id=2, has_side_effects=True, vmem_limit_bytes=58 * 2**20
        ),
    )(normed_two, back_half, weights, weights, weights)


def placement():
    row = lax.broadcasted_iota(jnp.int32, (1024, D), 0)
    feature = lax.broadcasted_iota(jnp.int32, (1024, D), 1)
    core, pair, slot = row // 512, (row // 16) % 32, row % 16
    source = 7 * (2 * (2 * pair + slot // 7) + core) + slot % 7
    return half(((source == feature) & (slot < 14)).astype(jnp.float32))


def swap_pair(value):
    return lax.ppermute(value, "dp", [(i, i ^ 1) for i in range(64)])


def pack_pair(pieces, parity):
    wide, narrow, vector = pieces
    extra = jnp.concatenate([narrow.reshape(2, D), jnp.pad(vector, (0, D - 23))[None]])
    own = half(jnp.concatenate([wide, extra]))
    other = swap_pair(own)
    even = jnp.where(parity == 0, own, other).astype(jnp.float32)
    odd = jnp.where(parity == 0, other, own).astype(jnp.float32)

    def two(start, size, pad):
        return [even[start : start + size], odd[start : start + size], jnp.zeros((pad, D), jnp.float32)]

    rows = [
        *two(0, 38, 4),
        *two(38, 38, 4),
        *two(76, 38, 4),
        *two(114, 7, 2),
        *two(121, 7, 2),
        *two(128, 3, 10),
    ]
    block = half(jnp.concatenate(rows))
    return jnp.where(parity == 0, block[:ROWS], block[ROWS:])


def unpack_rest(rest):
    rest = rest.reshape(2, 32, 48, D)
    place = placement()
    query = half(inner_rows(place, rest[:, :, 0:16].reshape(1024, D)))
    out = half(inner_rows(place, rest[:, :, 16:32].reshape(1024, D)))
    misc = rest[:, :, 32:38].reshape(2, 32, 2, 3, D)
    narrow = misc[:, :, :, :2].reshape(2, 32, 14, 256)
    narrow = jnp.pad(narrow, ((0, 0), (0, 0), (0, 2), (0, 0))).reshape(1024, 256)
    narrow = half(inner_rows(place, narrow))
    vectors = misc[:, :, :, 2, :23].transpose(1, 2, 0, 3).reshape(-1)
    return query, out, narrow, vectors


def pack_rest(query, out, narrow, vectors):
    vectors = vectors.reshape(32, 2, 2, 1, 23).transpose(2, 0, 1, 3, 4)
    vectors = jnp.pad(vectors, ((0, 0),) * 4 + ((0, D - 23),))
    narrow = narrow.reshape(2, 32, 16, 256)[:, :, :14].reshape(2, 32, 2, 2, D)
    misc = jnp.concatenate([narrow, vectors], axis=3).reshape(2, 32, 6, D)
    misc = jnp.pad(misc, ((0, 0), (0, 0), (0, 10), (0, 0)))
    rest = jnp.concatenate(
        [half(query).reshape(2, 32, 16, D), half(out).reshape(2, 32, 16, D), half(misc)], axis=2
    )
    return rest.reshape(2, 4, 4, 2, 48, D)


def slot_pass(full, tokens, cotangent, lengths):
    (
        query_weight,
        out_weight,
        narrow_weight,
        mlp_weights,
        vectors,
    ) = full
    batch, rows = tokens.shape[0], tokens.shape[1]
    count = batch * rows
    kv_width = KV_HEADS * HEAD
    key_weight = narrow_weight[:, :kv_width]
    value_weight = narrow_weight[:, kv_width:]
    place = placement()
    group = HEADS // KV_HEADS
    gains = vectors.astype(jnp.float32)
    first_gain = gains[:D]
    second_gain = gains[D : 2 * D]
    query_bias = gains[2 * D : 3 * D]
    key_bias = gains[3 * D : 3 * D + kv_width]
    value_bias = gains[3 * D + kv_width :]
    positions = jnp.arange(rows, dtype=jnp.int32)
    live = (positions[None, :] < lengths[:, None]).astype(jnp.float32).reshape(count, 1)
    allowed = (positions[None, None, :] <= positions[None, :, None]) & (
        positions[None, None, :] < lengths[:, None, None]
    )
    allowed = allowed[:, None, None]
    cosine, sine = rotary_tables(rows)
    inputs = tokens.astype(jnp.float32).reshape(count, D)
    first_scale = lax.rsqrt(jnp.mean(inputs * inputs, axis=-1, keepdims=True) + NORM_EPSILON)
    first_normed = inputs * first_scale
    normed = (first_normed * first_gain).astype(jnp.bfloat16)
    queries = product(normed, query_weight) + query_bias
    keys = product(normed, key_weight) + key_bias
    values = (product(normed, value_weight) + value_bias).astype(jnp.bfloat16)
    query_heads = rotary(queries.reshape(batch, rows, HEADS, HEAD), cosine, sine).astype(jnp.bfloat16)
    query_heads = query_heads.reshape(batch, rows, KV_HEADS, group, HEAD)
    key_heads = rotary(keys.reshape(batch, rows, KV_HEADS, HEAD), cosine, sine).astype(jnp.bfloat16)
    value_heads = values.reshape(batch, rows, KV_HEADS, HEAD)
    scores = jnp.einsum(
        "bigrd,bjgd->bgrij", query_heads, key_heads, preferred_element_type=jnp.float32
    )
    scores = jnp.where(allowed, scores * HEAD ** (-0.5), MASKED)
    peak = jnp.max(scores, axis=-1, keepdims=True)
    shifted = jnp.exp(scores - peak)
    total = jnp.sum(shifted, axis=-1, keepdims=True)
    probs = shifted / total
    weights = probs.astype(jnp.bfloat16)
    mixed = jnp.einsum("bgrij,bjgd->bigrd", weights, value_heads, preferred_element_type=jnp.float32)
    mixed = mixed.reshape(count, D).astype(jnp.bfloat16)
    middle = inputs + product(mixed, out_weight)
    second_scale = lax.rsqrt(jnp.mean(middle * middle, axis=-1, keepdims=True) + NORM_EPSILON)
    second_normed = middle * second_scale
    normed_two = (second_normed * second_gain).astype(jnp.bfloat16)
    back = cotangent.astype(jnp.float32).reshape(count, D) * live
    back_half = back.astype(jnp.bfloat16)
    fed, grad_normed_two, grad_mlp = mlp(normed_two, back_half, mlp_weights)
    result = ((middle + fed) * live).astype(jnp.bfloat16)
    second_gain_grad = jnp.sum(grad_normed_two * second_normed, axis=0)
    grad_middle = back + norm_back(grad_normed_two * second_gain, second_normed, second_scale)
    branch_grad = grad_middle.astype(jnp.bfloat16)
    grad_out_w = inner_rows(half(outer_cols(mixed, place)), branch_grad)
    grad_mixed = outer_cols(branch_grad, out_weight).astype(jnp.bfloat16)
    grad_mixed = grad_mixed.reshape(batch, rows, KV_HEADS, group, HEAD)
    grad_probs = jnp.einsum(
        "bigrd,bjgd->bgrij", grad_mixed, value_heads, preferred_element_type=jnp.float32
    )
    grad_scores = probs * (grad_probs - jnp.sum(probs * grad_probs, axis=-1, keepdims=True))
    grad_scores = grad_scores.astype(jnp.bfloat16)
    grad_query = jnp.einsum(
        "bgrij,bjgd->bigrd", grad_scores, key_heads, preferred_element_type=jnp.float32
    ) * HEAD ** (-0.5)
    grad_key = jnp.einsum(
        "bgrij,bigrd->bjgd", grad_scores, query_heads, preferred_element_type=jnp.float32
    ) * HEAD ** (-0.5)
    grad_value = jnp.einsum(
        "bgrij,bigrd->bjgd", weights, grad_mixed, preferred_element_type=jnp.float32
    )
    grad_value = grad_value.astype(jnp.bfloat16).reshape(count, kv_width)
    grad_query = (
        rotary_grad(grad_query.reshape(batch, rows, HEADS, HEAD), cosine, sine)
        .astype(jnp.bfloat16)
        .reshape(count, D)
    )
    grad_key = rotary_grad(grad_key, cosine, sine).astype(jnp.bfloat16).reshape(count, kv_width)
    query_bias_grad = jnp.sum(grad_query.astype(jnp.float32), axis=0)
    key_bias_grad = jnp.sum(grad_key.astype(jnp.float32), axis=0)
    value_bias_grad = jnp.sum(grad_value.astype(jnp.float32), axis=0)
    placed = half(outer_cols(normed, place))
    grad_query_w = inner_rows(placed, grad_query)
    grad_narrow_w = inner_rows(placed, jnp.concatenate([grad_key, grad_value], axis=1))
    grad_normed = (
        outer_cols(grad_query, query_weight)
        + outer_cols(grad_key, key_weight)
        + outer_cols(grad_value, value_weight)
    )
    first_gain_grad = jnp.sum(grad_normed * first_normed, axis=0)
    grad_inputs = (
        grad_middle + norm_back(grad_normed * first_gain, first_normed, first_scale)
    ).astype(jnp.bfloat16)
    vector_grad = jnp.concatenate(
        [first_gain_grad, second_gain_grad, query_bias_grad, key_bias_grad, value_bias_grad]
    )
    grads = (grad_mlp, pack_rest(grad_query_w, grad_out_w, grad_narrow_w, vector_grad))
    return (
        result.reshape(batch, 1, rows, D),
        grad_inputs.reshape(batch, 1, rows, D),
        grads,
    )


def half(value):
    return value.astype(jnp.bfloat16)


def mixing(gram):
    gram_half = half(gram)
    first = half(NEWTON_B * gram + NEWTON_C * product(gram_half, gram_half))
    cross = product(gram_half, first)
    after = (
        NEWTON_A * NEWTON_A * gram + 2.0 * NEWTON_A * cross + product(half(cross), first)
    )
    after_half = half(after)
    second = NEWTON_B * after + NEWTON_C * product(after_half, after_half)
    return half(
        NEWTON_A * (first.astype(jnp.float32) + second) + product(first, half(second))
    )


def body(
    inputs,
    cotangent,
    lengths,
    query_weight,
    key_weight,
    value_weight,
    out_weight,
    gate_weight,
    up_weight,
    down_weight,
    vectors,
    query_prior,
    key_prior,
    value_prior,
    out_prior,
    gate_prior,
    up_prior,
    down_prior,
    first_prior,
    second_prior,
):
    axes = ("dp", "narrow")
    chip = lax.axis_index("dp")
    core = lax.axis_index("narrow")
    parity = chip % 2
    kv_width = key_weight.shape[1]
    own = pack_pair(
        (
            jnp.concatenate([gate_weight.T, up_weight.T, down_weight, query_weight, out_weight]),
            jnp.concatenate([key_weight, value_weight], axis=1),
            vectors,
        ),
        parity,
    )
    gathered, rest = gather_blocks(own)
    query, out, narrow, gathered_vectors = unpack_rest(rest)
    full = (query, out, narrow, gathered.reshape(32, 2 * ROWS, D), gathered_vectors)
    own_lengths = lax.dynamic_slice_in_dim(lengths, chip * 2 + core, 1, axis=1)[:, 0]
    block_output, input_grad, grads = slot_pass(full, inputs[:, 0], cotangent[:, 0], own_lengths)
    reduced = scatter_blocks(grads[0].reshape(4, 4, 2, 3 * UNITS, D), grads[1])
    partner = swap_pair(reduced)
    both = jnp.where(
        parity == 0, jnp.concatenate([reduced, partner]), jnp.concatenate([partner, reduced])
    ).astype(jnp.float32)

    def mine(start, size):
        return lax.dynamic_slice_in_dim(both, start + parity * size, size, axis=0)

    tail = mine(272, 3)
    own_narrow = tail[:2].reshape(7, 2 * kv_width)
    grad_vector = tail[2, :23]
    owned = (
        mine(240, 7),
        own_narrow[:, :kv_width],
        own_narrow[:, kv_width:],
        mine(256, 7),
        mine(0, 38),
        mine(80, 38),
        mine(160, 38),
    )
    priors = (
        query_prior,
        key_prior,
        value_prior,
        out_prior,
        gate_prior.T,
        up_prior.T,
        down_prior,
    )
    masters = (
        query_weight,
        key_weight,
        value_weight,
        out_weight,
        gate_weight,
        up_weight,
        down_weight,
    )
    shapes = ((D, D), (D, kv_width), (D, kv_width), (D, D), (D, FF), (D, FF), (FF, D))
    lefts = (False, False, False, False, True, True, False)
    momenta = tuple((MOMENTUM * priors[k] + owned[k] for k in range(7)))
    partial = [half(inner_rows(half(moment), half(moment))) for moment in momenta]
    big = lax.psum(jnp.stack([partial[k] for k in (0, 3, 4, 5, 6)]), axes).astype(jnp.float32)
    small = lax.psum(jnp.stack([partial[k] for k in (1, 2)]), axes).astype(jnp.float32)
    grams = (big[0], small[0], small[1], big[1], big[2], big[3], big[4])
    updated = []
    kept = []
    for k in range(7):
        gram = grams[k]
        norm = jnp.sqrt(jnp.trace(gram)) + 1e-07
        inverse = 1.0 / norm
        mixer = mixing(gram * inverse * inverse)
        current = momenta[k] * inverse
        current = NEWTON_A * NEWTON_A * current + product(half(current), mixer)
        factor = MUON_RATE * 0.2 * math.sqrt(max(shapes[k][0], shapes[k][1]))
        if lefts[k]:
            current = current.T
        updated.append(masters[k] * (1.0 - MUON_RATE * MUON_DECAY) - factor * current)
        kept.append(momenta[k].T if lefts[k] else momenta[k])
    vector_first = BETA_FIRST * first_prior + (1.0 - BETA_FIRST) * grad_vector
    vector_second = BETA_SECOND * second_prior + (1.0 - BETA_SECOND) * grad_vector * grad_vector
    first_hat = vector_first / (1.0 - BETA_FIRST**STEP)
    second_hat = vector_second / (1.0 - BETA_SECOND**STEP)
    vector_new = vectors * (1.0 - ADAM_RATE * ADAM_DECAY) - ADAM_RATE * first_hat / (
        jnp.sqrt(second_hat) + ADAM_EPSILON
    )
    return (
        block_output,
        input_grad,
        *kept,
        *updated,
        vector_first,
        vector_second,
        vector_new,
    )


def solution(mesh):
    placed = (
        P(None, ("dp", "narrow"), None, None),
        P(None, ("dp", "narrow"), None, None),
        P(),
        P(("dp", "narrow"), None),
        P(("dp", "narrow"), None),
        P(("dp", "narrow"), None),
        P(("dp", "narrow"), None),
        P(None, ("dp", "narrow")),
        P(None, ("dp", "narrow")),
        P(("dp", "narrow"), None),
        P(("dp", "narrow")),
        P(("dp", "narrow"), None),
        P(("dp", "narrow"), None),
        P(("dp", "narrow"), None),
        P(("dp", "narrow"), None),
        P(None, ("dp", "narrow")),
        P(None, ("dp", "narrow")),
        P(("dp", "narrow"), None),
        P(("dp", "narrow")),
        P(("dp", "narrow")),
    )
    return jax.shard_map(
        body,
        mesh=mesh,
        in_specs=placed,
        out_specs=(
            P(None, ("dp", "narrow"), None, None),
            P(None, ("dp", "narrow"), None, None),
            P(("dp", "narrow"), None),
            P(("dp", "narrow"), None),
            P(("dp", "narrow"), None),
            P(("dp", "narrow"), None),
            P(None, ("dp", "narrow")),
            P(None, ("dp", "narrow")),
            P(("dp", "narrow"), None),
            P(("dp", "narrow"), None),
            P(("dp", "narrow"), None),
            P(("dp", "narrow"), None),
            P(("dp", "narrow"), None),
            P(None, ("dp", "narrow")),
            P(None, ("dp", "narrow")),
            P(("dp", "narrow"), None),
            P(("dp", "narrow")),
            P(("dp", "narrow")),
            P(("dp", "narrow")),
        ),
        check_vma=False,
    )
```

```python
import math

import jax
import jax.numpy as jnp
from jax import lax
from jax.experimental import pallas as pl
from jax.experimental.pallas import tpu as pltpu
from jax.sharding import PartitionSpec as P

D = 896
FF = 4864
HEADS = 14
KV_HEADS = 2
HEAD = 64
STEP = 10


NORM_EPSILON = 1e-06
ROPE_BASE = 1000000.0
MOMENTUM = 0.95
NEWTON_A = 3.4445
NEWTON_B = -4.775
NEWTON_C = 2.0315
MUON_RATE = 0.4
MUON_DECAY = 0.1
ADAM_RATE = 0.5
ADAM_DECAY = 0.01
BETA_FIRST = 0.9
BETA_SECOND = 0.999
ADAM_EPSILON = 1e-08
MASKED = -1e30


def product(left, right):
    return jnp.dot(left, right, preferred_element_type=jnp.float32)


def inner_rows(left, right):
    return lax.dot_general(
        left, right, (((0,), (0,)), ((), ())), preferred_element_type=jnp.float32
    )


def outer_cols(left, right):
    return lax.dot_general(
        left, right, (((1,), (1,)), ((), ())), preferred_element_type=jnp.float32
    )


def rotate_half(values):
    half = values.shape[-1] // 2
    return jnp.concatenate([-values[..., half:], values[..., :half]], axis=-1)


def rotate_back(values):
    half = values.shape[-1] // 2
    return jnp.concatenate([values[..., half:], -values[..., :half]], axis=-1)


def rotary_tables(length):
    half = HEAD // 2
    freqs = ROPE_BASE ** (-jnp.arange(half, dtype=jnp.float32) * 2.0 / HEAD)
    angles = jnp.arange(length, dtype=jnp.float32)[:, None] * freqs[None, :]
    angles = jnp.concatenate([angles, angles], axis=-1)
    return (jnp.cos(angles), jnp.sin(angles))


def rotary(values, cosine, sine):
    return values * cosine[None, :, None, :] + rotate_half(values) * sine[None, :, None, :]


def rotary_grad(grads, cosine, sine):
    return grads * cosine[None, :, None, :] + rotate_back(grads * sine[None, :, None, :])


def norm_back(grad, normed, scale):
    return scale * (grad - normed * jnp.mean(grad * normed, axis=-1, keepdims=True))


MESH = pl.DeviceIdType.MESH
ROWS = 144
PART = 48
GATHER_ORDERS = ((2, 1, 0), (1, 0, 2), (0, 2, 1))


def my_coords():
    dp = lax.axis_index("dp")
    return (dp // 16, (dp // 4) % 4, dp % 4), lax.axis_index("narrow")


def device_of(coords, core):
    return (coords[0] * 16 + coords[1] * 4 + coords[2], core)


def shifted(coords, axis, by):
    out = list(coords)
    out[axis] = (coords[axis] + by) % 4
    return tuple(out)


def ring_barrier(coords, core):
    barrier = pltpu.get_barrier_semaphore()
    for axis in range(3):
        for by in (1, 3):
            pl.semaphore_signal(
                barrier, inc=1, device_id=device_of(shifted(coords, axis, by), core), device_id_type=MESH
            )
    pl.semaphore_signal(barrier, inc=1, device_id=device_of(coords, 1 - core), device_id_type=MESH)
    pl.semaphore_wait(barrier, 7)


def region(spec, part, rows=None):
    index = []
    for axis in range(2):
        s = spec[axis]
        index.append(pl.ds(*s) if isinstance(s, tuple) else s)
    s = spec[2]
    if isinstance(s, tuple):
        index += [pl.ds(s[0] // 2, s[1] // 2), slice(None)]
    else:
        index += [s // 2, s % 2]
    rows = (0, PART) if rows is None else rows
    return (*index, pl.ds(part * PART + rows[0], rows[1]), slice(None))


FULL = (0, 4)


def halves(spec, split_axis):
    if split_axis is None:
        return [(spec, (0, 32)), (spec, (32, 16))]
    out = []
    for h in range(2):
        s = list(spec)
        s[split_axis] = (2 * h, 2)
        out.append((tuple(s), None))
    return out


def gather_kernel(
    block_ref, out_ref, rest_ref, held, local_sem, send_sems, recv_sems, rest_sems, store_sems
):
    coords, core = my_coords()
    local = pltpu.make_async_copy(
        block_ref, held.at[coords[0], coords[1], coords[2] // 2, coords[2] % 2], local_sem
    )
    local.start()
    ring_barrier(coords, core)
    local.wait()
    sends = []
    stores = []

    def copy_of(part, phase, slot, piece, axis, by):
        ref = held.at[region(piece[0], part, piece[1])]
        return pltpu.make_async_remote_copy(
            src_ref=ref,
            dst_ref=ref,
            send_sem=send_sems.at[part, phase, slot],
            recv_sem=recv_sems.at[part, phase, slot],
            device_id=device_of(shifted(coords, axis, by), core),
            device_id_type=MESH,
        )

    def send(*args):
        copy = copy_of(*args)
        copy.start()
        sends.append(copy)

    def store(part, slot, piece):
        place = region(piece[0], part, piece[1])
        copy = pltpu.make_async_copy(held.at[place], out_ref.at[place], store_sems.at[part, slot])
        copy.start()
        stores.append(copy)

    for phase in range(3):
        plans = []
        for part, order in enumerate(GATHER_ORDERS):
            axis = order[phase]
            split = order[phase - 1] if phase else None

            def pieces_at(by, order=order, axis=axis, split=split):
                spec = [FULL if order.index(k) < phase else coords[k] for k in range(3)]
                spec[axis] = (coords[axis] + by) % 4
                return halves(tuple(spec), split)

            plans.append((axis, pieces_at))
        for part, (axis, pieces_at) in enumerate(plans):
            h0, h1 = pieces_at(0)
            send(part, phase, 0, h0, axis, 1)
            send(part, phase, 1, h1, axis, 3)
            send(part, phase, 2, h1, axis, 1)
            send(part, phase, 3, h0, axis, 3)
            if phase == 2:
                store(part, 0, h0)
                store(part, 1, h1)
        for part, (axis, pieces_at) in enumerate(plans):
            first, second = pieces_at(3)[0], pieces_at(1)[1]
            copy_of(part, phase, 0, first, axis, 1).wait_recv()
            send(part, phase, 4, first, axis, 1)
            copy_of(part, phase, 1, second, axis, 3).wait_recv()
            send(part, phase, 5, second, axis, 3)
            if phase == 2:
                store(part, 2, first)
                store(part, 3, second)
        for part, (axis, pieces_at) in enumerate(plans):
            last = (pieces_at(3)[1], pieces_at(1)[0], pieces_at(2)[0], pieces_at(2)[1])
            for slot, piece in enumerate(last):
                copy_of(part, phase, 2 + slot, piece, axis, 1 if slot % 2 == 0 else 3).wait_recv()
                if phase == 2:
                    store(part, 4 + slot, piece)
    last = held.at[:, :, :, 1, pl.ds(96, 48)]
    keep = pltpu.make_async_copy(last, rest_ref.at[core], local_sem)
    give = sibling_copy(last, rest_ref.at[core], rest_sems, 0, core)
    keep.start()
    give.start()
    keep.wait()
    give.wait()
    for copy in stores:
        copy.wait()
    for copy in sends:
        copy.wait_send()


def gather_blocks(block):
    return pl.pallas_call(
        gather_kernel,
        out_shape=(
            jax.ShapeDtypeStruct((4, 4, 2, 2, ROWS, D), jnp.bfloat16),
            jax.ShapeDtypeStruct((2, 4, 4, 2, 48, D), jnp.bfloat16),
        ),
        in_specs=[pl.BlockSpec(memory_space=pl.ANY)],
        out_specs=(pl.BlockSpec(memory_space=pl.ANY),) * 2,
        scratch_shapes=[
            pltpu.VMEM((4, 4, 2, 2, ROWS, D), jnp.bfloat16),
            pltpu.SemaphoreType.DMA,
            pltpu.SemaphoreType.DMA((3, 3, 6)),
            pltpu.SemaphoreType.DMA((3, 3, 6)),
            pltpu.SemaphoreType.DMA((2, 1)),
            pltpu.SemaphoreType.DMA((3, 8)),
        ],
        compiler_params=pltpu.CompilerParams(
            collective_id=0, has_side_effects=True, vmem_limit_bytes=40 * 2**20
        ),
    )(block)


def region_shape(spec, rows):
    shape = []
    for axis in range(2):
        if isinstance(spec[axis], tuple):
            shape.append(spec[axis][1])
    if isinstance(spec[2], tuple):
        shape += [spec[2][1] // 2, 2]
    return (*shape, PART if rows is None else rows[1], D)


SCATTER_ORDERS = tuple(order[::-1] for order in GATHER_ORDERS)


def static_specs(order, phase):
    spec = [FULL if order.index(k) > phase else 0 for k in range(3)]
    split = order[phase + 1] if phase < 2 else None
    return [region_shape(*piece) for piece in halves(tuple(spec), split)]


def each_block(shape, body):
    lead = shape[:-2]
    count = 1
    for n in lead:
        count *= n
    if count == 1:
        body((0,) * len(lead))
        return

    def step(k, carry):
        index = []
        for n in reversed(lead):
            index.append(k % n)
            k = k // n
        body(tuple(reversed(index)))
        return carry

    lax.fori_loop(0, count, step, 0)


def scatter_kernel(mlp_ref, rest_ref, out_ref, *scratch):
    buffers = scratch[:54]
    total, sibling, load_sems, send_sems, recv_sems, rest_sems = scratch[54:]
    coords, core = my_coords()
    loads = [
        pltpu.make_async_copy(
            mlp_ref.at[:, :, :, pl.ds(0, ROWS)], total.at[:, :, :, 0], load_sems.at[0]
        ),
        pltpu.make_async_copy(
            mlp_ref.at[:, :, :, pl.ds(ROWS, 96)], total.at[:, :, :, 1, pl.ds(0, 96)], load_sems.at[1]
        ),
        pltpu.make_async_copy(rest_ref.at[core], total.at[:, :, :, 1, pl.ds(96, 48)], load_sems.at[2]),
    ]
    for copy in loads:
        copy.start()
    ring_barrier(coords, core)
    give = sibling_copy(rest_ref.at[1 - core], sibling, rest_sems, 0, core)
    give.start()
    for copy in loads:
        copy.wait()
    give.wait()

    def join(index):
        place = (*index, 1, pl.ds(96, 48), slice(None))
        total[place] = half(total[place].astype(jnp.float32) + sibling[index].astype(jnp.float32))

    each_block((4, 4, 2, 48, D), join)
    sends = []

    def copy_of(part, phase, slot, piece, dst, axis, by):
        spec, rows = piece
        return pltpu.make_async_remote_copy(
            src_ref=total.at[region(spec, part, rows)],
            dst_ref=dst,
            send_sem=send_sems.at[part, phase, slot],
            recv_sem=recv_sems.at[part, phase, slot],
            device_id=device_of(shifted(coords, axis, by), core),
            device_id_type=MESH,
        )

    def send(*args):
        copy = copy_of(*args)
        copy.start()
        sends.append(copy)

    def add_piece(part, piece, *sources):
        spec, rows = piece
        shape = region_shape(spec, rows)
        base = region(spec, part, rows)

        def one(index):
            place = []
            position = 0
            for entry in base[:4]:
                if isinstance(entry, slice):
                    place.append(index[position])
                    position += 1
                elif isinstance(entry, pl.Slice):
                    place.append(entry.start + index[position])
                    position += 1
                else:
                    place.append(entry)
            place = (*place, base[4], slice(None))
            value = total[place].astype(jnp.float32)
            for source in sources:
                value = value + source[(*index, slice(None), slice(None))].astype(jnp.float32)
            total[place] = value.astype(jnp.bfloat16)

        each_block(shape, one)

    for phase in range(3):
        plans = []
        for part, order in enumerate(SCATTER_ORDERS):
            axis = order[phase]
            split = order[phase + 1] if phase < 2 else None

            def pieces_at(by, order=order, axis=axis, split=split):
                spec = [FULL if order.index(k) > phase else coords[k] for k in range(3)]
                spec[axis] = (coords[axis] + by) % 4
                return halves(tuple(spec), split)

            base = (part * 3 + phase) * 6
            bufs = buffers[base : base + 6]
            plans.append((axis, pieces_at, (bufs[0], bufs[1], bufs[2:4], bufs[4:6])))
        for part, (axis, pieces_at, bufs) in enumerate(plans):
            far_left, far_right, near_left, near_right = bufs
            send(part, phase, 0, pieces_at(2)[0], far_left, axis, 1)
            send(part, phase, 1, pieces_at(2)[1], far_right, axis, 3)
            send(part, phase, 2, pieces_at(1)[1], near_left[1], axis, 1)
            send(part, phase, 3, pieces_at(3)[0], near_right[0], axis, 3)
        for part, (axis, pieces_at, bufs) in enumerate(plans):
            far_left, far_right, near_left, near_right = bufs
            copy_of(part, phase, 0, pieces_at(2)[0], far_left, axis, 1).wait_recv()
            add_piece(part, pieces_at(1)[0], far_left)
            send(part, phase, 4, pieces_at(1)[0], near_left[0], axis, 1)
            copy_of(part, phase, 1, pieces_at(2)[1], far_right, axis, 3).wait_recv()
            add_piece(part, pieces_at(3)[1], far_right)
            send(part, phase, 5, pieces_at(3)[1], near_right[1], axis, 3)
        for part, (axis, pieces_at, bufs) in enumerate(plans):
            far_left, far_right, near_left, near_right = bufs
            copy_of(part, phase, 3, pieces_at(3)[0], near_right[0], axis, 3).wait_recv()
            copy_of(part, phase, 4, pieces_at(1)[0], near_left[0], axis, 1).wait_recv()
            add_piece(part, pieces_at(0)[0], near_left[0], near_right[0])
            copy_of(part, phase, 2, pieces_at(1)[1], near_left[1], axis, 1).wait_recv()
            copy_of(part, phase, 5, pieces_at(3)[1], near_right[1], axis, 3).wait_recv()
            add_piece(part, pieces_at(0)[1], near_left[1], near_right[1])
    for copy in sends:
        copy.wait_send()
    out_ref[...] = total[coords[0], coords[1], coords[2] // 2, coords[2] % 2]


def scatter_blocks(mlp, rest):
    scratch = []
    for order in SCATTER_ORDERS:
        for phase in range(3):
            h0, h1 = static_specs(order, phase)
            scratch += [pltpu.VMEM(shape, jnp.bfloat16) for shape in (h0, h1, h0, h1, h0, h1)]
    scratch += [
        pltpu.VMEM((4, 4, 2, 2, ROWS, D), jnp.bfloat16),
        pltpu.VMEM((4, 4, 2, 48, D), jnp.bfloat16),
        pltpu.SemaphoreType.DMA((3,)),
        pltpu.SemaphoreType.DMA((3, 3, 6)),
        pltpu.SemaphoreType.DMA((3, 3, 6)),
        pltpu.SemaphoreType.DMA((2, 1)),
    ]
    return pl.pallas_call(
        scatter_kernel,
        out_shape=jax.ShapeDtypeStruct((ROWS, D), jnp.bfloat16),
        in_specs=[pl.BlockSpec(memory_space=pl.ANY)] * 2,
        out_specs=pl.BlockSpec(memory_space=pltpu.VMEM),
        scratch_shapes=scratch,
        compiler_params=pltpu.CompilerParams(
            collective_id=1, has_side_effects=True, vmem_limit_bytes=56 * 2**20
        ),
    )(mlp, rest)


UNITS = 80
TILE_PAIRS = 8
TILE = TILE_PAIRS * UNITS
TILES = 32 // TILE_PAIRS
TOKENS = 256


def sibling_copy(src, dst, sems, slot, core):
    return pltpu.make_async_remote_copy(
        src_ref=src,
        dst_ref=dst,
        send_sem=sems.at[0, slot],
        recv_sem=sems.at[1, slot],
        device_id=(lax.axis_index("dp"), 1 - core),
        device_id_type=MESH,
    )


def mlp_kernel(
    h_ref, e_ref, gate_ref, up_ref, down_ref, out_ref, back_ref, grad_ref,
    h_all, e_all, out_acc, back_acc, parcel, arrived, sems,
):
    core = lax.axis_index("narrow")
    step = pl.program_id(0)

    @pl.when(step == 0)
    def _():
        barrier = pltpu.get_barrier_semaphore()
        pl.semaphore_signal(
            barrier, inc=1, device_id=(lax.axis_index("dp"), 1 - core), device_id_type=MESH
        )
        pl.semaphore_wait(barrier, 1)
        h_copy = sibling_copy(h_ref, h_all.at[core], sems, 0, core)
        e_copy = sibling_copy(e_ref, e_all.at[core], sems, 1, core)
        h_copy.start()
        e_copy.start()
        h_all[core] = h_ref[...]
        e_all[core] = e_ref[...]
        out_acc[...] = jnp.zeros_like(out_acc)
        back_acc[...] = jnp.zeros_like(back_acc)
        h_copy.wait()
        e_copy.wait()

    h = h_all[...].reshape(2 * TOKENS, D)
    e = e_all[...].reshape(2 * TOKENS, D)
    gate_w = gate_ref[...].reshape(TILE, D)
    up_w = up_ref[...].reshape(TILE, D)
    down_w = down_ref[...].reshape(TILE, D)
    gate = outer_cols(h, gate_w)
    up = outer_cols(h, up_w)
    sigma = jax.nn.sigmoid(gate)
    silu = gate * sigma
    hidden = half(silu * up)
    grad_hidden = outer_cols(e, down_w)
    out_acc[...] += product(hidden, down_w).reshape(2, TOKENS, D)
    grad_gate = half(grad_hidden * up * sigma * (1.0 + gate * (1.0 - sigma)))
    grad_up = half(grad_hidden * silu)
    back_acc[...] += (product(grad_gate, gate_w) + product(grad_up, up_w)).reshape(2, TOKENS, D)
    grad_ref[:, 0:UNITS] = half(inner_rows(grad_gate, h)).reshape(TILE_PAIRS, UNITS, D)
    grad_ref[:, UNITS : 2 * UNITS] = half(inner_rows(grad_up, h)).reshape(TILE_PAIRS, UNITS, D)
    grad_ref[:, 2 * UNITS :] = half(inner_rows(hidden, e)).reshape(TILE_PAIRS, UNITS, D)

    @pl.when(step == TILES - 1)
    def _():
        parcel[0] = half(out_acc[1 - core])
        parcel[1] = half(back_acc[1 - core])
        copy = sibling_copy(parcel, arrived, sems, 2, core)
        copy.start()
        copy.wait()
        out_ref[...] = out_acc[core] + arrived[0].astype(jnp.float32)
        back_ref[...] = back_acc[core] + arrived[1].astype(jnp.float32)


def mlp(normed_two, back_half, weights):
    whole = pl.BlockSpec((TOKENS, D), lambda i: (0, 0))
    return pl.pallas_call(
        mlp_kernel,
        grid=(TILES,),
        out_shape=(
            jax.ShapeDtypeStruct((TOKENS, D), jnp.float32),
            jax.ShapeDtypeStruct((TOKENS, D), jnp.float32),
            jax.ShapeDtypeStruct((32, 3 * UNITS, D), jnp.bfloat16),
        ),
        in_specs=[
            whole,
            whole,
            pl.BlockSpec((TILE_PAIRS, UNITS, D), lambda i: (i, 0, 0)),
            pl.BlockSpec((TILE_PAIRS, UNITS, D), lambda i: (i, 1, 0)),
            pl.BlockSpec((TILE_PAIRS, UNITS, D), lambda i: (i, 2, 0)),
        ],
        out_specs=(whole, whole, pl.BlockSpec((TILE_PAIRS, 3 * UNITS, D), lambda i: (i, 0, 0))),
        scratch_shapes=[
            pltpu.VMEM((2, TOKENS, D), jnp.bfloat16),
            pltpu.VMEM((2, TOKENS, D), jnp.bfloat16),
            pltpu.VMEM((2, TOKENS, D), jnp.float32),
            pltpu.VMEM((2, TOKENS, D), jnp.float32),
            pltpu.VMEM((2, TOKENS, D), jnp.bfloat16),
            pltpu.VMEM((2, TOKENS, D), jnp.bfloat16),
            pltpu.SemaphoreType.DMA((2, 3)),
        ],
        compiler_params=pltpu.CompilerParams(
            collective_id=2, has_side_effects=True, vmem_limit_bytes=58 * 2**20
        ),
    )(normed_two, back_half, weights, weights, weights)


def placement():
    row = lax.broadcasted_iota(jnp.int32, (1024, D), 0)
    feature = lax.broadcasted_iota(jnp.int32, (1024, D), 1)
    core, pair, slot = row // 512, (row // 16) % 32, row % 16
    source = 7 * (2 * (2 * pair + slot // 7) + core) + slot % 7
    return half(((source == feature) & (slot < 14)).astype(jnp.float32))


def swap_pair(value):
    return lax.ppermute(value, "dp", [(i, i ^ 1) for i in range(64)])


def pack_pair(pieces, parity):
    wide, narrow, vector = pieces
    extra = jnp.concatenate([narrow.reshape(2, D), jnp.pad(vector, (0, D - 23))[None]])
    own = half(jnp.concatenate([wide, extra]))
    other = swap_pair(own)
    even = jnp.where(parity == 0, own, other).astype(jnp.float32)
    odd = jnp.where(parity == 0, other, own).astype(jnp.float32)

    def two(start, size, pad):
        return [even[start : start + size], odd[start : start + size], jnp.zeros((pad, D), jnp.float32)]

    rows = [
        *two(0, 38, 4),
        *two(38, 38, 4),
        *two(76, 38, 4),
        *two(114, 7, 2),
        *two(121, 7, 2),
        *two(128, 3, 10),
    ]
    block = half(jnp.concatenate(rows))
    return jnp.where(parity == 0, block[:ROWS], block[ROWS:])


def unpack_rest(rest):
    rest = rest.reshape(2, 32, 48, D)
    place = placement()
    query = half(inner_rows(place, rest[:, :, 0:16].reshape(1024, D)))
    out = half(inner_rows(place, rest[:, :, 16:32].reshape(1024, D)))
    misc = rest[:, :, 32:38].reshape(2, 32, 2, 3, D)
    narrow = misc[:, :, :, :2].reshape(2, 32, 14, 256)
    narrow = jnp.pad(narrow, ((0, 0), (0, 0), (0, 2), (0, 0))).reshape(1024, 256)
    narrow = half(inner_rows(place, narrow))
    vectors = misc[:, :, :, 2, :23].transpose(1, 2, 0, 3).reshape(-1)
    return query, out, narrow, vectors


def pack_rest(query, out, narrow, vectors):
    vectors = vectors.reshape(32, 2, 2, 1, 23).transpose(2, 0, 1, 3, 4)
    vectors = jnp.pad(vectors, ((0, 0),) * 4 + ((0, D - 23),))
    narrow = narrow.reshape(2, 32, 16, 256)[:, :, :14].reshape(2, 32, 2, 2, D)
    misc = jnp.concatenate([narrow, vectors], axis=3).reshape(2, 32, 6, D)
    misc = jnp.pad(misc, ((0, 0), (0, 0), (0, 10), (0, 0)))
    rest = jnp.concatenate(
        [half(query).reshape(2, 32, 16, D), half(out).reshape(2, 32, 16, D), half(misc)], axis=2
    )
    return rest.reshape(2, 4, 4, 2, 48, D)


def slot_pass(full, tokens, cotangent, lengths):
    (
        query_weight,
        out_weight,
        narrow_weight,
        mlp_weights,
        vectors,
    ) = full
    batch, rows = tokens.shape[0], tokens.shape[1]
    count = batch * rows
    kv_width = KV_HEADS * HEAD
    key_weight = narrow_weight[:, :kv_width]
    value_weight = narrow_weight[:, kv_width:]
    place = placement()
    group = HEADS // KV_HEADS
    gains = vectors.astype(jnp.float32)
    first_gain = gains[:D]
    second_gain = gains[D : 2 * D]
    query_bias = gains[2 * D : 3 * D]
    key_bias = gains[3 * D : 3 * D + kv_width]
    value_bias = gains[3 * D + kv_width :]
    positions = jnp.arange(rows, dtype=jnp.int32)
    live = (positions[None, :] < lengths[:, None]).astype(jnp.float32).reshape(count, 1)
    allowed = (positions[None, None, :] <= positions[None, :, None]) & (
        positions[None, None, :] < lengths[:, None, None]
    )
    allowed = allowed[:, None, None]
    cosine, sine = rotary_tables(rows)
    inputs = tokens.astype(jnp.float32).reshape(count, D)
    first_scale = lax.rsqrt(jnp.mean(inputs * inputs, axis=-1, keepdims=True) + NORM_EPSILON)
    first_normed = inputs * first_scale
    normed = (first_normed * first_gain).astype(jnp.bfloat16)
    queries = product(normed, query_weight) + query_bias
    keys = product(normed, key_weight) + key_bias
    values = (product(normed, value_weight) + value_bias).astype(jnp.bfloat16)
    query_heads = rotary(queries.reshape(batch, rows, HEADS, HEAD), cosine, sine).astype(jnp.bfloat16)
    query_heads = query_heads.reshape(batch, rows, KV_HEADS, group, HEAD)
    key_heads = rotary(keys.reshape(batch, rows, KV_HEADS, HEAD), cosine, sine).astype(jnp.bfloat16)
    value_heads = values.reshape(batch, rows, KV_HEADS, HEAD)
    scores = jnp.einsum(
        "bigrd,bjgd->bgrij", query_heads, key_heads, preferred_element_type=jnp.float32
    )
    scores = jnp.where(allowed, scores * HEAD ** (-0.5), MASKED)
    peak = jnp.max(scores, axis=-1, keepdims=True)
    shifted = jnp.exp(scores - peak)
    total = jnp.sum(shifted, axis=-1, keepdims=True)
    probs = shifted / total
    weights = probs.astype(jnp.bfloat16)
    mixed = jnp.einsum("bgrij,bjgd->bigrd", weights, value_heads, preferred_element_type=jnp.float32)
    mixed = mixed.reshape(count, D).astype(jnp.bfloat16)
    middle = inputs + product(mixed, out_weight)
    second_scale = lax.rsqrt(jnp.mean(middle * middle, axis=-1, keepdims=True) + NORM_EPSILON)
    second_normed = middle * second_scale
    normed_two = (second_normed * second_gain).astype(jnp.bfloat16)
    back = cotangent.astype(jnp.float32).reshape(count, D) * live
    back_half = back.astype(jnp.bfloat16)
    fed, grad_normed_two, grad_mlp = mlp(normed_two, back_half, mlp_weights)
    result = ((middle + fed) * live).astype(jnp.bfloat16)
    second_gain_grad = jnp.sum(grad_normed_two * second_normed, axis=0)
    grad_middle = back + norm_back(grad_normed_two * second_gain, second_normed, second_scale)
    branch_grad = grad_middle.astype(jnp.bfloat16)
    grad_out_w = inner_rows(half(outer_cols(mixed, place)), branch_grad)
    grad_mixed = outer_cols(branch_grad, out_weight).astype(jnp.bfloat16)
    grad_mixed = grad_mixed.reshape(batch, rows, KV_HEADS, group, HEAD)
    grad_probs = jnp.einsum(
        "bigrd,bjgd->bgrij", grad_mixed, value_heads, preferred_element_type=jnp.float32
    )
    grad_scores = probs * (grad_probs - jnp.sum(probs * grad_probs, axis=-1, keepdims=True))
    grad_scores = grad_scores.astype(jnp.bfloat16)
    grad_query = jnp.einsum(
        "bgrij,bjgd->bigrd", grad_scores, key_heads, preferred_element_type=jnp.float32
    ) * HEAD ** (-0.5)
    grad_key = jnp.einsum(
        "bgrij,bigrd->bjgd", grad_scores, query_heads, preferred_element_type=jnp.float32
    ) * HEAD ** (-0.5)
    grad_value = jnp.einsum(
        "bgrij,bigrd->bjgd", weights, grad_mixed, preferred_element_type=jnp.float32
    )
    grad_value = grad_value.astype(jnp.bfloat16).reshape(count, kv_width)
    grad_query = (
        rotary_grad(grad_query.reshape(batch, rows, HEADS, HEAD), cosine, sine)
        .astype(jnp.bfloat16)
        .reshape(count, D)
    )
    grad_key = rotary_grad(grad_key, cosine, sine).astype(jnp.bfloat16).reshape(count, kv_width)
    query_bias_grad = jnp.sum(grad_query.astype(jnp.float32), axis=0)
    key_bias_grad = jnp.sum(grad_key.astype(jnp.float32), axis=0)
    value_bias_grad = jnp.sum(grad_value.astype(jnp.float32), axis=0)
    placed = half(outer_cols(normed, place))
    grad_query_w = inner_rows(placed, grad_query)
    grad_narrow_w = inner_rows(placed, jnp.concatenate([grad_key, grad_value], axis=1))
    grad_normed = (
        outer_cols(grad_query, query_weight)
        + outer_cols(grad_key, key_weight)
        + outer_cols(grad_value, value_weight)
    )
    first_gain_grad = jnp.sum(grad_normed * first_normed, axis=0)
    grad_inputs = (
        grad_middle + norm_back(grad_normed * first_gain, first_normed, first_scale)
    ).astype(jnp.bfloat16)
    vector_grad = jnp.concatenate(
        [first_gain_grad, second_gain_grad, query_bias_grad, key_bias_grad, value_bias_grad]
    )
    grads = (grad_mlp, pack_rest(grad_query_w, grad_out_w, grad_narrow_w, vector_grad))
    return (
        result.reshape(batch, 1, rows, D),
        grad_inputs.reshape(batch, 1, rows, D),
        grads,
    )


def half(value):
    return value.astype(jnp.bfloat16)


def mixing(gram):
    gram_half = half(gram)
    first = half(NEWTON_B * gram + NEWTON_C * product(gram_half, gram_half))
    cross = product(gram_half, first)
    after = (
        NEWTON_A * NEWTON_A * gram + 2.0 * NEWTON_A * cross + product(half(cross), first)
    )
    after_half = half(after)
    second = NEWTON_B * after + NEWTON_C * product(after_half, after_half)
    return half(
        NEWTON_A * (first.astype(jnp.float32) + second) + product(first, half(second))
    )


BLOCKS = [(i, j) for i in range(7) for j in range(i, 7)]


def muon_kernel(
    sent_ref, big_ref, square_ref, narrow_ref,
    rows, job, gram_out, gram_in, gram_all, gram, back, narrow_back, big_got, square_got, narrow_got,
    job_sems, sum_sems, all_sems, back_send, back_recv,
):
    coords, core = my_coords()
    z, y, x = coords
    me = y * 4 + x

    def plane(peer):
        return device_of((z, peer // 4, peer % 4), core)

    def line(other, other_core):
        return device_of((other, y, x), other_core)

    barrier = pltpu.get_barrier_semaphore()
    for k in range(1, 8):
        t = (z * 2 + core + k) % 8
        pl.semaphore_signal(barrier, inc=1, device_id=line(t // 2, t % 2), device_id_type=MESH)
    for k in range(1, 16):
        pl.semaphore_signal(barrier, inc=1, device_id=plane((me + k) % 16), device_id_type=MESH)
    pl.semaphore_wait(barrier, 22)

    def returned(src, dst, send_slot, slot, device):
        return pltpu.make_async_remote_copy(
            src_ref=src,
            dst_ref=dst,
            send_sem=back_send.at[send_slot],
            recv_sem=back_recv.at[slot],
            device_id=device,
            device_id_type=MESH,
        )

    def remote(src, dst, sems, slot, device):
        return pltpu.make_async_remote_copy(
            src_ref=src,
            dst_ref=dst,
            send_sem=sems.at[0, slot],
            recv_sem=sems.at[1, slot],
            device_id=device,
            device_id_type=MESH,
        )

    own = z * 2 + core

    def job_copy(k):
        t = (own + k) % 8
        return remote(sent_ref.at[t // 2], rows.at[own], job_sems, k, line(t // 2, t % 2))

    def job_arrival(k):
        t = (own + 8 - k) % 8
        return remote(sent_ref.at[0], rows.at[t], job_sems, k, line(t // 2, t % 2))

    for k in range(1, 8):
        job_copy(k).start()
    rows[own] = sent_ref[z]
    for k in range(1, 8):
        job_arrival(k).wait_recv()

    @pl.when(z < 3)
    def _():
        job[...] = rows[...]

    for job_core in range(2):

        @pl.when((z == 3) & (core == job_core))
        def _():
            job[:, 0:16] = rows[:, 16 * job_core : 16 * job_core + 16]
            job[:, 16:48] = jnp.zeros((8, 32, D), jnp.bfloat16)

    flat = job[...].reshape(384, D)
    narrow = rows[:, 32:48, 0:256].reshape(128, 256)
    gram[...] = inner_rows(flat, flat)
    for index, (i, j) in enumerate(BLOCKS):
        gram_out[index // 2, index % 2] = half(
            gram[128 * i : 128 * i + 128, 128 * j : 128 * j + 128]
        )
    for t in range(2):
        part = narrow[:, 128 * t : 128 * t + 128]
        gram_out[14, t] = half(inner_rows(part, part))
        gram_out[15, t] = jnp.zeros((128, 128), jnp.bfloat16)

    def sum_copy(k):
        peer = (me + k) % 16
        return remote(gram_out.at[peer], gram_in.at[me], sum_sems, k, plane(peer))

    def sum_arrival(k):
        peer = (me + 16 - k) % 16
        return remote(gram_out.at[0], gram_in.at[peer], sum_sems, k, plane(peer))

    for k in range(1, 16):
        sum_copy(k).start()
    gram_in[me] = gram_out[me]
    for k in range(1, 16):
        sum_arrival(k).wait_recv()
    for t in range(2):
        value = gram_in[0, t].astype(jnp.float32)
        for s in range(1, 16):
            value = value + gram_in[s, t].astype(jnp.float32)
        gram_all[me, t] = half(value)

    def all_copy(k, peer):
        return remote(gram_all.at[peer], gram_all.at[peer], all_sems, k, plane((me + k) % 16))

    for k in range(1, 16):
        all_copy(k, me).start()
    for k in range(1, 16):
        all_copy(k, (me + 16 - k) % 16).wait_recv()

    eye = lax.broadcasted_iota(jnp.int32, (128, 128), 0) == lax.broadcasted_iota(
        jnp.int32, (128, 128), 1
    )

    def diagonal(block):
        return jnp.sum(jnp.where(eye, block, 0.0))

    trace = 0.0
    for index, (i, j) in enumerate(BLOCKS):
        block = gram_all[index // 2, index % 2].astype(jnp.float32)
        gram[128 * i : 128 * i + 128, 128 * j : 128 * j + 128] = block
        if i == j:
            trace = trace + diagonal(block)
        else:
            gram[128 * j : 128 * j + 128, 128 * i : 128 * i + 128] = block.T

    def finish(total, matrix, values):
        inverse = 1.0 / (jnp.sqrt(jnp.full((1, 1), total)) + 1e-07)
        mixer = mixing(matrix * (inverse * inverse))
        scaled = values.astype(jnp.float32) * inverse
        return half(NEWTON_A * NEWTON_A * scaled + product(half(scaled), mixer))

    back[...] = finish(trace, gram[...], flat).reshape(8, 48, D)
    for t in range(2):
        matrix = gram_all[14, t].astype(jnp.float32)
        part = narrow[:, 128 * t : 128 * t + 128]
        narrow_back[t] = finish(diagonal(matrix), matrix, part).reshape(8, 16, 128)

    @pl.when(z < 3)
    def _():
        copies = []
        for k in range(1, 4):
            other = (z + k) % 4
            copies.append(
                returned(
                    back.at[other * 2 + core], big_got.at[z], k, z, line(other, core)
                )
            )
        for copy in copies:
            copy.start()
        big_got[z] = back[own]
        for copy in copies:
            copy.wait_send()

    @pl.when(z == 3)
    def _():
        copies = []
        for k in range(1, 8):
            t = (own + k) % 8
            device = line(t // 2, t % 2)
            copies.append(
                returned(back.at[t, pl.ds(0, 16)], square_got.at[core], k, 3 + core, device)
            )
            copies.append(
                returned(narrow_back.at[core, t], narrow_got.at[core], 8 + k, 5 + core, device)
            )
        for copy in copies:
            copy.start()
        square_got[core] = back[own, 0:16]
        narrow_got[core] = narrow_back[core, own]
        for copy in copies:
            copy.wait_send()

    for plane_z in range(3):

        @pl.when(z != plane_z)
        def _():
            returned(
                back.at[0], big_got.at[plane_z], 0, plane_z, line(plane_z, core)
            ).wait_recv()

    for job_core in range(2):

        @pl.when((z != 3) | (core != job_core))
        def _():
            device = line(3, job_core)
            returned(
                back.at[0, pl.ds(0, 16)], square_got.at[job_core], 0, 3 + job_core, device
            ).wait_recv()
            returned(
                narrow_back.at[0, 0], narrow_got.at[job_core], 0, 5 + job_core, device
            ).wait_recv()

    for k in range(1, 8):
        job_copy(k).wait_send()
    for k in range(1, 16):
        sum_copy(k).wait_send()
        all_copy(k, me).wait_send()
    big_ref[...] = big_got[...]
    square_ref[...] = square_got[...]
    narrow_ref[...] = narrow_got[...]


def muon(sent):
    vmem = pl.BlockSpec(memory_space=pltpu.VMEM)
    return pl.pallas_call(
        muon_kernel,
        out_shape=(
            jax.ShapeDtypeStruct((3, 48, D), jnp.bfloat16),
            jax.ShapeDtypeStruct((2, 16, D), jnp.bfloat16),
            jax.ShapeDtypeStruct((2, 16, 128), jnp.bfloat16),
        ),
        in_specs=[vmem],
        out_specs=(vmem,) * 3,
        scratch_shapes=[
            pltpu.VMEM((8, 48, D), jnp.bfloat16),
            pltpu.VMEM((8, 48, D), jnp.bfloat16),
            pltpu.VMEM((16, 2, 128, 128), jnp.bfloat16),
            pltpu.VMEM((16, 2, 128, 128), jnp.bfloat16),
            pltpu.VMEM((16, 2, 128, 128), jnp.bfloat16),
            pltpu.VMEM((D, D), jnp.float32),
            pltpu.VMEM((8, 48, D), jnp.bfloat16),
            pltpu.VMEM((2, 8, 16, 128), jnp.bfloat16),
            pltpu.VMEM((3, 48, D), jnp.bfloat16),
            pltpu.VMEM((2, 16, D), jnp.bfloat16),
            pltpu.VMEM((2, 16, 128), jnp.bfloat16),
            pltpu.SemaphoreType.DMA((2, 8)),
            pltpu.SemaphoreType.DMA((2, 16)),
            pltpu.SemaphoreType.DMA((2, 16)),
            pltpu.SemaphoreType.DMA((16,)),
            pltpu.SemaphoreType.DMA((7,)),
        ],
        compiler_params=pltpu.CompilerParams(
            collective_id=3, has_side_effects=True, vmem_limit_bytes=58 * 2**20
        ),
    )(sent)


def body(
    inputs,
    cotangent,
    lengths,
    query_weight,
    key_weight,
    value_weight,
    out_weight,
    gate_weight,
    up_weight,
    down_weight,
    vectors,
    query_prior,
    key_prior,
    value_prior,
    out_prior,
    gate_prior,
    up_prior,
    down_prior,
    first_prior,
    second_prior,
):
    axes = ("dp", "narrow")
    chip = lax.axis_index("dp")
    core = lax.axis_index("narrow")
    parity = chip % 2
    kv_width = key_weight.shape[1]
    own = pack_pair(
        (
            jnp.concatenate([gate_weight.T, up_weight.T, down_weight, query_weight, out_weight]),
            jnp.concatenate([key_weight, value_weight], axis=1),
            vectors,
        ),
        parity,
    )
    gathered, rest = gather_blocks(own)
    query, out, narrow, gathered_vectors = unpack_rest(rest)
    full = (query, out, narrow, gathered.reshape(32, 2 * ROWS, D), gathered_vectors)
    own_lengths = lax.dynamic_slice_in_dim(lengths, chip * 2 + core, 1, axis=1)[:, 0]
    block_output, input_grad, grads = slot_pass(full, inputs[:, 0], cotangent[:, 0], own_lengths)
    reduced = scatter_blocks(grads[0].reshape(4, 4, 2, 3 * UNITS, D), grads[1])
    partner = swap_pair(reduced)
    both = jnp.where(
        parity == 0, jnp.concatenate([reduced, partner]), jnp.concatenate([partner, reduced])
    ).astype(jnp.float32)

    def mine(start, size):
        return lax.dynamic_slice_in_dim(both, start + parity * size, size, axis=0)

    tail = mine(272, 3)
    own_narrow = tail[:2].reshape(7, 2 * kv_width)
    grad_vector = tail[2, :23]
    owned = (
        mine(240, 7),
        own_narrow[:, :kv_width],
        own_narrow[:, kv_width:],
        mine(256, 7),
        mine(0, 38),
        mine(80, 38),
        mine(160, 38),
    )
    priors = (
        query_prior,
        key_prior,
        value_prior,
        out_prior,
        gate_prior.T,
        up_prior.T,
        down_prior,
    )
    masters = (
        query_weight,
        key_weight,
        value_weight,
        out_weight,
        gate_weight,
        up_weight,
        down_weight,
    )
    shapes = ((D, D), (D, kv_width), (D, kv_width), (D, D), (D, FF), (D, FF), (FF, D))
    lefts = (False, False, False, False, True, True, False)
    momenta = tuple((MOMENTUM * priors[k] + owned[k] for k in range(7)))

    def padded(value, count):
        return jnp.pad(value, ((0, count - value.shape[0]), (0, D - value.shape[1])))

    narrow_rows = jnp.concatenate([momenta[1], momenta[2]], axis=1)
    last = jnp.concatenate(
        [padded(momenta[0], 16), padded(momenta[3], 16), padded(narrow_rows, 16)]
    )
    sent = jnp.stack([padded(momenta[4], 48), padded(momenta[5], 48), padded(momenta[6], 48), last])
    big, square, thin = muon(half(sent))
    finals = (
        square[0, :7], thin[0, :7], thin[1, :7], square[1, :7], big[0, :38], big[1, :38], big[2, :38],
    )
    updated = []
    kept = []
    for k in range(7):
        current = finals[k].astype(jnp.float32)
        factor = MUON_RATE * 0.2 * math.sqrt(max(shapes[k][0], shapes[k][1]))
        if lefts[k]:
            current = current.T
        updated.append(masters[k] * (1.0 - MUON_RATE * MUON_DECAY) - factor * current)
        kept.append(momenta[k].T if lefts[k] else momenta[k])
    vector_first = BETA_FIRST * first_prior + (1.0 - BETA_FIRST) * grad_vector
    vector_second = BETA_SECOND * second_prior + (1.0 - BETA_SECOND) * grad_vector * grad_vector
    first_hat = vector_first / (1.0 - BETA_FIRST**STEP)
    second_hat = vector_second / (1.0 - BETA_SECOND**STEP)
    vector_new = vectors * (1.0 - ADAM_RATE * ADAM_DECAY) - ADAM_RATE * first_hat / (
        jnp.sqrt(second_hat) + ADAM_EPSILON
    )
    return (
        block_output,
        input_grad,
        *kept,
        *updated,
        vector_first,
        vector_second,
        vector_new,
    )


def solution(mesh):
    placed = (
        P(None, ("dp", "narrow"), None, None),
        P(None, ("dp", "narrow"), None, None),
        P(),
        P(("dp", "narrow"), None),
        P(("dp", "narrow"), None),
        P(("dp", "narrow"), None),
        P(("dp", "narrow"), None),
        P(None, ("dp", "narrow")),
        P(None, ("dp", "narrow")),
        P(("dp", "narrow"), None),
        P(("dp", "narrow")),
        P(("dp", "narrow"), None),
        P(("dp", "narrow"), None),
        P(("dp", "narrow"), None),
        P(("dp", "narrow"), None),
        P(None, ("dp", "narrow")),
        P(None, ("dp", "narrow")),
        P(("dp", "narrow"), None),
        P(("dp", "narrow")),
        P(("dp", "narrow")),
    )
    return jax.shard_map(
        body,
        mesh=mesh,
        in_specs=placed,
        out_specs=(
            P(None, ("dp", "narrow"), None, None),
            P(None, ("dp", "narrow"), None, None),
            P(("dp", "narrow"), None),
            P(("dp", "narrow"), None),
            P(("dp", "narrow"), None),
            P(("dp", "narrow"), None),
            P(None, ("dp", "narrow")),
            P(None, ("dp", "narrow")),
            P(("dp", "narrow"), None),
            P(("dp", "narrow"), None),
            P(("dp", "narrow"), None),
            P(("dp", "narrow"), None),
            P(("dp", "narrow"), None),
            P(None, ("dp", "narrow")),
            P(None, ("dp", "narrow")),
            P(("dp", "narrow"), None),
            P(("dp", "narrow")),
            P(("dp", "narrow")),
            P(("dp", "narrow")),
        ),
        check_vma=False,
    )
```

```python
import math

import jax
import jax.numpy as jnp
from jax import lax
from jax.experimental import pallas as pl
from jax.experimental.pallas import tpu as pltpu
from jax.sharding import PartitionSpec as P

D = 896
FF = 4864
HEADS = 14
KV_HEADS = 2
HEAD = 64
STEP = 10


NORM_EPSILON = 1e-06
ROPE_BASE = 1000000.0
MOMENTUM = 0.95
NEWTON_A = 3.4445
NEWTON_B = -4.775
NEWTON_C = 2.0315
MUON_RATE = 0.4
MUON_DECAY = 0.1
ADAM_RATE = 0.5
ADAM_DECAY = 0.01
BETA_FIRST = 0.9
BETA_SECOND = 0.999
ADAM_EPSILON = 1e-08
MASKED = -1e30


def product(left, right):
    return jnp.dot(left, right, preferred_element_type=jnp.float32)


def inner_rows(left, right):
    return lax.dot_general(
        left, right, (((0,), (0,)), ((), ())), preferred_element_type=jnp.float32
    )


def outer_cols(left, right):
    return lax.dot_general(
        left, right, (((1,), (1,)), ((), ())), preferred_element_type=jnp.float32
    )


def rotary_tables(length):
    half = HEAD // 2
    freqs = ROPE_BASE ** (-jnp.arange(half, dtype=jnp.float32) * 2.0 / HEAD)
    angles = jnp.arange(length, dtype=jnp.float32)[:, None] * freqs[None, :]
    angles = jnp.concatenate([angles, angles], axis=-1)
    return (jnp.cos(angles), jnp.sin(angles))


def norm_back(grad, normed, scale):
    return scale * (grad - normed * jnp.mean(grad * normed, axis=-1, keepdims=True))


MESH = pl.DeviceIdType.MESH
ROWS = 144
PART = 48
GATHER_ORDERS = ((2, 1, 0), (1, 0, 2), (0, 2, 1))


def my_coords():
    dp = lax.axis_index("dp")
    return (dp // 16, (dp // 4) % 4, dp % 4), lax.axis_index("narrow")


def device_of(coords, core):
    return (coords[0] * 16 + coords[1] * 4 + coords[2], core)


def shifted(coords, axis, by):
    out = list(coords)
    out[axis] = (coords[axis] + by) % 4
    return tuple(out)


def ring_barrier(coords, core):
    barrier = pltpu.get_barrier_semaphore()
    for axis in range(3):
        for by in (1, 3):
            pl.semaphore_signal(
                barrier, inc=1, device_id=device_of(shifted(coords, axis, by), core), device_id_type=MESH
            )
    pl.semaphore_signal(barrier, inc=1, device_id=device_of(coords, 1 - core), device_id_type=MESH)
    pl.semaphore_wait(barrier, 7)


def region(spec, part, rows=None):
    index = []
    for axis in range(2):
        s = spec[axis]
        index.append(pl.ds(*s) if isinstance(s, tuple) else s)
    s = spec[2]
    if isinstance(s, tuple):
        index += [pl.ds(s[0] // 2, s[1] // 2), slice(None)]
    else:
        index += [s // 2, s % 2]
    rows = (0, PART) if rows is None else rows
    return (*index, pl.ds(part * PART + rows[0], rows[1]), slice(None))


FULL = (0, 4)


def halves(spec, split_axis):
    if split_axis is None:
        return [(spec, (0, 32)), (spec, (32, 16))]
    out = []
    for h in range(2):
        s = list(spec)
        s[split_axis] = (2 * h, 2)
        out.append((tuple(s), None))
    return out


def gather_kernel(
    block_ref, out_ref, rest_ref, held, local_sem, send_sems, recv_sems, rest_sems, store_sems
):
    coords, core = my_coords()
    local = pltpu.make_async_copy(
        block_ref, held.at[coords[0], coords[1], coords[2] // 2, coords[2] % 2], local_sem
    )
    local.start()
    ring_barrier(coords, core)
    local.wait()
    sends = []
    stores = []

    def copy_of(part, phase, slot, piece, axis, by):
        ref = held.at[region(piece[0], part, piece[1])]
        return pltpu.make_async_remote_copy(
            src_ref=ref,
            dst_ref=ref,
            send_sem=send_sems.at[part, phase, slot],
            recv_sem=recv_sems.at[part, phase, slot],
            device_id=device_of(shifted(coords, axis, by), core),
            device_id_type=MESH,
        )

    def send(*args):
        copy = copy_of(*args)
        copy.start()
        sends.append(copy)

    def store(part, slot, piece):
        place = region(piece[0], part, piece[1])
        copy = pltpu.make_async_copy(held.at[place], out_ref.at[place], store_sems.at[part, slot])
        copy.start()
        stores.append(copy)

    for phase in range(3):
        plans = []
        for part, order in enumerate(GATHER_ORDERS):
            axis = order[phase]
            split = order[phase - 1] if phase else None

            def pieces_at(by, order=order, axis=axis, split=split):
                spec = [FULL if order.index(k) < phase else coords[k] for k in range(3)]
                spec[axis] = (coords[axis] + by) % 4
                return halves(tuple(spec), split)

            plans.append((axis, pieces_at))
        for part, (axis, pieces_at) in enumerate(plans):
            h0, h1 = pieces_at(0)
            send(part, phase, 0, h0, axis, 1)
            send(part, phase, 1, h1, axis, 3)
            send(part, phase, 2, h1, axis, 1)
            send(part, phase, 3, h0, axis, 3)
            if phase == 2:
                store(part, 0, h0)
                store(part, 1, h1)
        for part, (axis, pieces_at) in enumerate(plans):
            first, second = pieces_at(3)[0], pieces_at(1)[1]
            copy_of(part, phase, 0, first, axis, 1).wait_recv()
            send(part, phase, 4, first, axis, 1)
            copy_of(part, phase, 1, second, axis, 3).wait_recv()
            send(part, phase, 5, second, axis, 3)
            if phase == 2:
                store(part, 2, first)
                store(part, 3, second)
        for part, (axis, pieces_at) in enumerate(plans):
            last = (pieces_at(3)[1], pieces_at(1)[0], pieces_at(2)[0], pieces_at(2)[1])
            for slot, piece in enumerate(last):
                copy_of(part, phase, 2 + slot, piece, axis, 1 if slot % 2 == 0 else 3).wait_recv()
                if phase == 2:
                    store(part, 4 + slot, piece)
    last = held.at[:, :, :, 1, pl.ds(96, 48)]
    keep = pltpu.make_async_copy(last, rest_ref.at[core], local_sem)
    give = sibling_copy(last, rest_ref.at[core], rest_sems, 0, core)
    keep.start()
    give.start()
    keep.wait()
    give.wait()
    for copy in stores:
        copy.wait()
    for copy in sends:
        copy.wait_send()


def gather_blocks(block):
    return pl.pallas_call(
        gather_kernel,
        out_shape=(
            jax.ShapeDtypeStruct((4, 4, 2, 2, ROWS, D), jnp.bfloat16),
            jax.ShapeDtypeStruct((2, 4, 4, 2, 48, D), jnp.bfloat16),
        ),
        in_specs=[pl.BlockSpec(memory_space=pl.ANY)],
        out_specs=(pl.BlockSpec(memory_space=pl.ANY),) * 2,
        scratch_shapes=[
            pltpu.VMEM((4, 4, 2, 2, ROWS, D), jnp.bfloat16),
            pltpu.SemaphoreType.DMA,
            pltpu.SemaphoreType.DMA((3, 3, 6)),
            pltpu.SemaphoreType.DMA((3, 3, 6)),
            pltpu.SemaphoreType.DMA((2, 1)),
            pltpu.SemaphoreType.DMA((3, 8)),
        ],
        compiler_params=pltpu.CompilerParams(
            collective_id=0, has_side_effects=True, vmem_limit_bytes=40 * 2**20
        ),
    )(block)


def region_shape(spec, rows):
    shape = []
    for axis in range(2):
        if isinstance(spec[axis], tuple):
            shape.append(spec[axis][1])
    if isinstance(spec[2], tuple):
        shape += [spec[2][1] // 2, 2]
    return (*shape, PART if rows is None else rows[1], D)


SCATTER_ORDERS = tuple(order[::-1] for order in GATHER_ORDERS)


def static_specs(order, phase):
    spec = [FULL if order.index(k) > phase else 0 for k in range(3)]
    split = order[phase + 1] if phase < 2 else None
    return [region_shape(*piece) for piece in halves(tuple(spec), split)]


def each_block(shape, body):
    lead = shape[:-2]
    count = 1
    for n in lead:
        count *= n
    if count == 1:
        body((0,) * len(lead))
        return

    def step(k, carry):
        index = []
        for n in reversed(lead):
            index.append(k % n)
            k = k // n
        body(tuple(reversed(index)))
        return carry

    lax.fori_loop(0, count, step, 0)


def scatter_kernel(mlp_ref, rest_ref, out_ref, *scratch):
    buffers = scratch[:54]
    total, sibling, load_sems, send_sems, recv_sems, rest_sems = scratch[54:]
    coords, core = my_coords()
    loads = [
        pltpu.make_async_copy(
            mlp_ref.at[:, :, :, pl.ds(0, ROWS)], total.at[:, :, :, 0], load_sems.at[0]
        ),
        pltpu.make_async_copy(
            mlp_ref.at[:, :, :, pl.ds(ROWS, 96)], total.at[:, :, :, 1, pl.ds(0, 96)], load_sems.at[1]
        ),
        pltpu.make_async_copy(rest_ref.at[core], total.at[:, :, :, 1, pl.ds(96, 48)], load_sems.at[2]),
    ]
    for copy in loads:
        copy.start()
    ring_barrier(coords, core)
    give = sibling_copy(rest_ref.at[1 - core], sibling, rest_sems, 0, core)
    give.start()
    for copy in loads:
        copy.wait()
    give.wait()

    def join(index):
        place = (*index, 1, pl.ds(96, 48), slice(None))
        total[place] = half(total[place].astype(jnp.float32) + sibling[index].astype(jnp.float32))

    each_block((4, 4, 2, 48, D), join)
    sends = []

    def copy_of(part, phase, slot, piece, dst, axis, by):
        spec, rows = piece
        return pltpu.make_async_remote_copy(
            src_ref=total.at[region(spec, part, rows)],
            dst_ref=dst,
            send_sem=send_sems.at[part, phase, slot],
            recv_sem=recv_sems.at[part, phase, slot],
            device_id=device_of(shifted(coords, axis, by), core),
            device_id_type=MESH,
        )

    def send(*args):
        copy = copy_of(*args)
        copy.start()
        sends.append(copy)

    def add_piece(part, piece, *sources):
        spec, rows = piece
        shape = region_shape(spec, rows)
        base = region(spec, part, rows)

        def one(index):
            place = []
            position = 0
            for entry in base[:4]:
                if isinstance(entry, slice):
                    place.append(index[position])
                    position += 1
                elif isinstance(entry, pl.Slice):
                    place.append(entry.start + index[position])
                    position += 1
                else:
                    place.append(entry)
            place = (*place, base[4], slice(None))
            value = total[place].astype(jnp.float32)
            for source in sources:
                value = value + source[(*index, slice(None), slice(None))].astype(jnp.float32)
            total[place] = value.astype(jnp.bfloat16)

        each_block(shape, one)

    for phase in range(3):
        plans = []
        for part, order in enumerate(SCATTER_ORDERS):
            axis = order[phase]
            split = order[phase + 1] if phase < 2 else None

            def pieces_at(by, order=order, axis=axis, split=split):
                spec = [FULL if order.index(k) > phase else coords[k] for k in range(3)]
                spec[axis] = (coords[axis] + by) % 4
                return halves(tuple(spec), split)

            base = (part * 3 + phase) * 6
            bufs = buffers[base : base + 6]
            plans.append((axis, pieces_at, (bufs[0], bufs[1], bufs[2:4], bufs[4:6])))
        for part, (axis, pieces_at, bufs) in enumerate(plans):
            far_left, far_right, near_left, near_right = bufs
            send(part, phase, 0, pieces_at(2)[0], far_left, axis, 1)
            send(part, phase, 1, pieces_at(2)[1], far_right, axis, 3)
            send(part, phase, 2, pieces_at(1)[1], near_left[1], axis, 1)
            send(part, phase, 3, pieces_at(3)[0], near_right[0], axis, 3)
        for part, (axis, pieces_at, bufs) in enumerate(plans):
            far_left, far_right, near_left, near_right = bufs
            copy_of(part, phase, 0, pieces_at(2)[0], far_left, axis, 1).wait_recv()
            add_piece(part, pieces_at(1)[0], far_left)
            send(part, phase, 4, pieces_at(1)[0], near_left[0], axis, 1)
            copy_of(part, phase, 1, pieces_at(2)[1], far_right, axis, 3).wait_recv()
            add_piece(part, pieces_at(3)[1], far_right)
            send(part, phase, 5, pieces_at(3)[1], near_right[1], axis, 3)
        for part, (axis, pieces_at, bufs) in enumerate(plans):
            far_left, far_right, near_left, near_right = bufs
            copy_of(part, phase, 3, pieces_at(3)[0], near_right[0], axis, 3).wait_recv()
            copy_of(part, phase, 4, pieces_at(1)[0], near_left[0], axis, 1).wait_recv()
            add_piece(part, pieces_at(0)[0], near_left[0], near_right[0])
            copy_of(part, phase, 2, pieces_at(1)[1], near_left[1], axis, 1).wait_recv()
            copy_of(part, phase, 5, pieces_at(3)[1], near_right[1], axis, 3).wait_recv()
            add_piece(part, pieces_at(0)[1], near_left[1], near_right[1])
    for copy in sends:
        copy.wait_send()
    out_ref[...] = total[coords[0], coords[1], coords[2] // 2, coords[2] % 2]


def scatter_blocks(mlp, rest):
    scratch = []
    for order in SCATTER_ORDERS:
        for phase in range(3):
            h0, h1 = static_specs(order, phase)
            scratch += [pltpu.VMEM(shape, jnp.bfloat16) for shape in (h0, h1, h0, h1, h0, h1)]
    scratch += [
        pltpu.VMEM((4, 4, 2, 2, ROWS, D), jnp.bfloat16),
        pltpu.VMEM((4, 4, 2, 48, D), jnp.bfloat16),
        pltpu.SemaphoreType.DMA((3,)),
        pltpu.SemaphoreType.DMA((3, 3, 6)),
        pltpu.SemaphoreType.DMA((3, 3, 6)),
        pltpu.SemaphoreType.DMA((2, 1)),
    ]
    return pl.pallas_call(
        scatter_kernel,
        out_shape=jax.ShapeDtypeStruct((ROWS, D), jnp.bfloat16),
        in_specs=[pl.BlockSpec(memory_space=pl.ANY)] * 2,
        out_specs=pl.BlockSpec(memory_space=pltpu.VMEM),
        scratch_shapes=scratch,
        compiler_params=pltpu.CompilerParams(
            collective_id=1, has_side_effects=True, vmem_limit_bytes=56 * 2**20
        ),
    )(mlp, rest)


UNITS = 80
TILE_PAIRS = 8
TILE = TILE_PAIRS * UNITS
TILES = 32 // TILE_PAIRS
TOKENS = 256


def sibling_copy(src, dst, sems, slot, core):
    return pltpu.make_async_remote_copy(
        src_ref=src,
        dst_ref=dst,
        send_sem=sems.at[0, slot],
        recv_sem=sems.at[1, slot],
        device_id=(lax.axis_index("dp"), 1 - core),
        device_id_type=MESH,
    )


def mlp_kernel(
    h_ref, e_ref, gate_ref, up_ref, down_ref, out_ref, back_ref, grad_ref,
    h_all, e_all, out_acc, back_acc, parcel, arrived, sems,
):
    core = lax.axis_index("narrow")
    step = pl.program_id(0)

    @pl.when(step == 0)
    def _():
        barrier = pltpu.get_barrier_semaphore()
        pl.semaphore_signal(
            barrier, inc=1, device_id=(lax.axis_index("dp"), 1 - core), device_id_type=MESH
        )
        pl.semaphore_wait(barrier, 1)
        h_copy = sibling_copy(h_ref, h_all.at[core], sems, 0, core)
        e_copy = sibling_copy(e_ref, e_all.at[core], sems, 1, core)
        h_copy.start()
        e_copy.start()
        h_all[core] = h_ref[...]
        e_all[core] = e_ref[...]
        out_acc[...] = jnp.zeros_like(out_acc)
        back_acc[...] = jnp.zeros_like(back_acc)
        h_copy.wait()
        e_copy.wait()

    h = h_all[...].reshape(2 * TOKENS, D)
    e = e_all[...].reshape(2 * TOKENS, D)
    gate_w = gate_ref[...].reshape(TILE, D)
    up_w = up_ref[...].reshape(TILE, D)
    down_w = down_ref[...].reshape(TILE, D)
    gate = outer_cols(h, gate_w)
    up = outer_cols(h, up_w)
    sigma = jax.nn.sigmoid(gate)
    silu = gate * sigma
    hidden = half(silu * up)
    grad_hidden = outer_cols(e, down_w)
    out_acc[...] += product(hidden, down_w).reshape(2, TOKENS, D)
    grad_gate = half(grad_hidden * up * sigma * (1.0 + gate * (1.0 - sigma)))
    grad_up = half(grad_hidden * silu)
    back_acc[...] += (product(grad_gate, gate_w) + product(grad_up, up_w)).reshape(2, TOKENS, D)
    grad_ref[:, 0:UNITS] = half(inner_rows(grad_gate, h)).reshape(TILE_PAIRS, UNITS, D)
    grad_ref[:, UNITS : 2 * UNITS] = half(inner_rows(grad_up, h)).reshape(TILE_PAIRS, UNITS, D)
    grad_ref[:, 2 * UNITS :] = half(inner_rows(hidden, e)).reshape(TILE_PAIRS, UNITS, D)

    @pl.when(step == TILES - 1)
    def _():
        parcel[0] = half(out_acc[1 - core])
        parcel[1] = half(back_acc[1 - core])
        copy = sibling_copy(parcel, arrived, sems, 2, core)
        copy.start()
        copy.wait()
        out_ref[...] = out_acc[core] + arrived[0].astype(jnp.float32)
        back_ref[...] = back_acc[core] + arrived[1].astype(jnp.float32)


def mlp(normed_two, back_half, weights):
    whole = pl.BlockSpec((TOKENS, D), lambda i: (0, 0))
    return pl.pallas_call(
        mlp_kernel,
        grid=(TILES,),
        out_shape=(
            jax.ShapeDtypeStruct((TOKENS, D), jnp.float32),
            jax.ShapeDtypeStruct((TOKENS, D), jnp.float32),
            jax.ShapeDtypeStruct((32, 3 * UNITS, D), jnp.bfloat16),
        ),
        in_specs=[
            whole,
            whole,
            pl.BlockSpec((TILE_PAIRS, UNITS, D), lambda i: (i, 0, 0)),
            pl.BlockSpec((TILE_PAIRS, UNITS, D), lambda i: (i, 1, 0)),
            pl.BlockSpec((TILE_PAIRS, UNITS, D), lambda i: (i, 2, 0)),
        ],
        out_specs=(whole, whole, pl.BlockSpec((TILE_PAIRS, 3 * UNITS, D), lambda i: (i, 0, 0))),
        scratch_shapes=[
            pltpu.VMEM((2, TOKENS, D), jnp.bfloat16),
            pltpu.VMEM((2, TOKENS, D), jnp.bfloat16),
            pltpu.VMEM((2, TOKENS, D), jnp.float32),
            pltpu.VMEM((2, TOKENS, D), jnp.float32),
            pltpu.VMEM((2, TOKENS, D), jnp.bfloat16),
            pltpu.VMEM((2, TOKENS, D), jnp.bfloat16),
            pltpu.SemaphoreType.DMA((2, 3)),
        ],
        compiler_params=pltpu.CompilerParams(
            collective_id=2, has_side_effects=True, vmem_limit_bytes=58 * 2**20
        ),
    )(normed_two, back_half, weights, weights, weights)


def swap_pair(value):
    return lax.ppermute(value, "dp", [(i, i ^ 1) for i in range(64)])


def pack_pair(pieces, parity):
    wide, narrow, vector = pieces
    extra = jnp.concatenate(
        [narrow, jnp.pad(vector[None], ((0, 6), (0, D - 256 - vector.shape[0])))], axis=1
    )
    own = half(jnp.concatenate([wide, extra]))
    other = swap_pair(own)
    even = jnp.where(parity == 0, own, other).astype(jnp.float32)
    odd = jnp.where(parity == 0, other, own).astype(jnp.float32)

    def two(start, size, pad):
        return [even[start : start + size], odd[start : start + size], jnp.zeros((pad, D), jnp.float32)]

    rows = [
        *two(0, 38, 4),
        *two(38, 38, 4),
        *two(76, 38, 4),
        *two(114, 7, 2),
        *two(121, 7, 2),
        *two(128, 7, 2),
    ]
    block = half(jnp.concatenate(rows))
    return jnp.where(parity == 0, block[:ROWS], block[ROWS:])


SCALE = HEAD ** (-0.5)


def turn(values, sign):
    lane = lax.broadcasted_iota(jnp.int32, values.shape, 1)
    ahead = pltpu.roll(values, 96, 1)
    behind = pltpu.roll(values, 32, 1)
    return jnp.where(lane & 32 == 0, sign * ahead, -sign * behind)


def tiles_of(values):
    return [values[:, 128 * t : 128 * t + 128] for t in range(values.shape[1] // 128)]


def rotated(values, cosine, sine):
    return jnp.concatenate(
        [tile * cosine + turn(tile, -1.0) * sine for tile in tiles_of(values)], axis=1
    )


def rotated_back(values, cosine, sine):
    return jnp.concatenate(
        [tile * cosine + turn(tile * sine, 1.0) for tile in tiles_of(values)], axis=1
    )


def low_lanes(shape):
    return lax.broadcasted_iota(jnp.int32, shape, 1) < HEAD


def paired(both):
    swapped = pltpu.roll(both, 64, 1)
    low = low_lanes(both.shape)
    even = [half(jnp.where(low, v, 0.0)) for v in (both, swapped)]
    odd = [half(jnp.where(low, 0.0, v)) for v in (swapped, both)]
    kinds = [jnp.concatenate([even[a], odd[b]]) for a, b in ((0, 0), (0, 1), (1, 1))]
    return [kinds[0]] * 3 + [kinds[1]] + [kinds[2]] * 3


def gathered_place():
    row = lax.broadcasted_iota(jnp.int32, (1024, D), 0)
    feature = lax.broadcasted_iota(jnp.int32, (1024, D), 1)
    slot = row & 15
    odd = (slot >= 7).astype(jnp.int32)
    device = (((row >> 4) & 31) * 2 + odd) * 2 + (row >> 9)
    source = jnp.where(slot < 14, 7 * device + slot - 7 * odd, -1)
    return half((source == feature).astype(jnp.float32))


def vector_maps():
    device = lax.broadcasted_iota(jnp.int32, (128, 1024), 0)
    row = lax.broadcasted_iota(jnp.int32, (128, 1024), 1)
    target = (device & 1) * 512 + (device >> 2) * 16 + ((device >> 1) & 1) * 7
    pick = half((row == target).astype(jnp.float32))
    start = lax.broadcasted_iota(jnp.int32, (128, 2944), 0) * 23
    entry = lax.broadcasted_iota(jnp.int32, (128, 2944), 1)
    owner = half(((entry >= start) & (entry < start + 23)).astype(jnp.float32))
    return pick, owner


def slot_mask(slots):
    return lax.broadcasted_iota(jnp.int32, (128, 2944), 0) == slots


def forward_kernel(
    x_ref, cot_ref, rest_ref, len_ref, cos_ref, sin_ref, slot_ref,
    middle_ref, h2_ref, eb_ref, h1p_ref, q_ref, k_ref, v_ref, mixed_ref, probs_ref, vector_ref,
):
    place = gathered_place()
    pick, owner = vector_maps()
    stored = rest_ref[:, :, 32:48, 256:384].reshape(1024, 128)
    by_device = half(product(pick, stored))
    spread = inner_rows(by_device, owner)
    vector = jnp.sum(jnp.where(slot_mask(slot_ref[...]), spread, 0.0), axis=0, keepdims=True)
    vector_ref[...] = vector
    first_gain, second_gain = vector[:, :D], vector[:, D : 2 * D]
    query_bias, narrow_bias = vector[:, 2 * D : 3 * D], vector[:, 3 * D :]
    cosine, sine = cos_ref[...], sin_ref[...]
    inputs = x_ref[...].astype(jnp.float32)
    first_scale = lax.rsqrt(jnp.mean(inputs * inputs, axis=-1, keepdims=True) + NORM_EPSILON)
    normed = half(inputs * first_scale * first_gain)
    placed = half(outer_cols(normed, place))
    h1p_ref[...] = placed
    queries = product(placed, rest_ref[:, :, 0:16, :].reshape(1024, D)) + query_bias
    narrow = product(placed, rest_ref[:, :, 32:48, 0:256].reshape(1024, 256)) + narrow_bias
    q_ref[...] = half(rotated(queries, cosine, sine))
    keys = rotated(narrow[:, 0:128], cosine, sine)
    k_ref[...] = half(keys)
    values = narrow[:, 128:256]
    v_ref[...] = half(values)
    position = lax.broadcasted_iota(jnp.int32, (128, 256), 0)
    other = lax.broadcasted_iota(jnp.int32, (128, 256), 1) & 127
    causal = other <= position
    rows = []
    for b in range(2):
        here = slice(128 * b, 128 * b + 128)
        allowed = causal & (other < len_ref[here, :])
        key_tiles = paired(keys[here])
        value_tiles = paired(values[here])
        tiles = []
        for t in range(7):
            scores = outer_cols(q_ref[here, 128 * t : 128 * t + 128], key_tiles[t])
            scores = jnp.where(allowed, scores * SCALE, MASKED)
            parts = []
            for part in tiles_of(scores):
                shifted = jnp.exp(part - jnp.max(part, axis=-1, keepdims=True))
                parts.append(shifted / jnp.sum(shifted, axis=-1, keepdims=True))
            probs = jnp.concatenate(parts, axis=1)
            probs_ref[b, t] = probs
            tiles.append(half(product(half(probs), value_tiles[t])))
        rows.append(jnp.concatenate(tiles, axis=1))
    mixed = half(outer_cols(jnp.concatenate(rows), place))
    mixed_ref[...] = mixed
    middle = inputs + product(mixed, rest_ref[:, :, 16:32, :].reshape(1024, D))
    middle_ref[...] = middle
    second_scale = lax.rsqrt(jnp.mean(middle * middle, axis=-1, keepdims=True) + NORM_EPSILON)
    h2_ref[...] = half(middle * second_scale * second_gain)
    token = lax.broadcasted_iota(jnp.int32, (TOKENS, 1), 0) & 127
    live = (token < len_ref[...]).astype(jnp.float32)
    eb_ref[...] = half(cot_ref[...].astype(jnp.float32) * live)


def backward_kernel(
    x_ref, e_ref, rest_ref, len_ref, cos_ref, sin_ref, slot_ref,
    middle_ref, h1p_ref, q_ref, k_ref, v_ref, mixed_ref, probs_ref, vector_ref, fed_ref, dh2_ref,
    output_ref, input_grad_ref, grad_ref,
):
    place = gathered_place()
    pick, owner = vector_maps()
    vector = vector_ref[...]
    first_gain, second_gain = vector[:, :D], vector[:, D : 2 * D]
    cosine, sine = cos_ref[...], sin_ref[...]
    token = lax.broadcasted_iota(jnp.int32, (TOKENS, 1), 0) & 127
    live = (token < len_ref[...]).astype(jnp.float32)
    middle = middle_ref[...]
    output_ref[...] = half((middle + fed_ref[...]) * live)
    second_scale = lax.rsqrt(jnp.mean(middle * middle, axis=-1, keepdims=True) + NORM_EPSILON)
    second_normed = middle * second_scale
    dh2 = dh2_ref[...]
    second_gain_grad = jnp.sum(dh2 * second_normed, axis=0, keepdims=True)
    grad_middle = e_ref[...].astype(jnp.float32) + norm_back(
        dh2 * second_gain, second_normed, second_scale
    )
    branch = half(grad_middle)
    wide = rest_ref[:, :, 16:32, :].reshape(1024, D)
    grad_ref[:, :, 16:32, :] = half(inner_rows(mixed_ref[...], branch)).reshape(2, 32, 16, D)
    grad_mixed = half(product(half(outer_cols(branch, wide)), place))
    low = low_lanes((128, 128))
    query_rows, key_rows, value_rows = [], [], []
    for b in range(2):
        here = slice(128 * b, 128 * b + 128)
        key_tiles = paired(k_ref[here, :].astype(jnp.float32))
        value_tiles = paired(v_ref[here, :].astype(jnp.float32))
        tiles = []
        sums = [[jnp.zeros((128, 128), jnp.float32) for _ in range(4)] for _ in range(2)]
        for t in range(7):
            head = grad_mixed[here, 128 * t : 128 * t + 128]
            grad_probs = outer_cols(head, value_tiles[t])
            probs = probs_ref[b, t]
            parts = []
            for p, g in zip(tiles_of(probs), tiles_of(grad_probs)):
                parts.append(half(p * (g - jnp.sum(p * g, axis=-1, keepdims=True))))
            grad_scores = jnp.concatenate(parts, axis=1)
            tiles.append(product(grad_scores, key_tiles[t]) * SCALE)
            for which, (left, right) in enumerate(
                ((grad_scores, q_ref[here, 128 * t : 128 * t + 128]), (half(probs), head))
            ):
                both = inner_rows(left, right)
                even, odd = (2 * t) // 7, (2 * t + 1) // 7
                sums[which][even] += both[0:128]
                sums[which][2 + odd] += both[128:256]
        query_rows.append(jnp.concatenate(tiles, axis=1))
        joined = []
        for which in range(2):
            even0, even1, odd0, odd1 = sums[which]
            joined.append(
                jnp.where(low, even0 + pltpu.roll(odd0, 64, 1), odd1 + pltpu.roll(even1, 64, 1))
            )
        key_rows.append(joined[0] * SCALE)
        value_rows.append(joined[1])
    grad_query = half(rotated_back(jnp.concatenate(query_rows), cosine, sine))
    grad_key = half(rotated_back(jnp.concatenate(key_rows), cosine, sine))
    grad_narrow = jnp.concatenate([grad_key, half(jnp.concatenate(value_rows))], axis=1)
    placed = h1p_ref[...]
    grad_ref[:, :, 0:16, :] = half(inner_rows(placed, grad_query)).reshape(2, 32, 16, D)
    grad_ref[:, :, 32:48, 0:256] = half(inner_rows(placed, grad_narrow)).reshape(2, 32, 16, 256)
    bias_grad = jnp.sum(
        jnp.concatenate([grad_query, grad_narrow], axis=1).astype(jnp.float32), axis=0, keepdims=True
    )
    grad_placed = outer_cols(grad_query, rest_ref[:, :, 0:16, :].reshape(1024, D)) + outer_cols(
        grad_narrow, rest_ref[:, :, 32:48, 0:256].reshape(1024, 256)
    )
    high = half(grad_placed)
    remainder = half(grad_placed - high.astype(jnp.float32))
    grad_normed = product(high, place) + product(remainder, place)
    inputs = x_ref[...].astype(jnp.float32)
    first_scale = lax.rsqrt(jnp.mean(inputs * inputs, axis=-1, keepdims=True) + NORM_EPSILON)
    first_normed = inputs * first_scale
    first_gain_grad = jnp.sum(grad_normed * first_normed, axis=0, keepdims=True)
    input_grad_ref[...] = half(
        grad_middle + norm_back(grad_normed * first_gain, first_normed, first_scale)
    )
    vector_grad = jnp.concatenate([first_gain_grad, second_gain_grad, bias_grad], axis=1)
    spread = half(jnp.where(slot_mask(slot_ref[...]), vector_grad, 0.0))
    by_device = half(outer_cols(owner, spread))
    stored = half(inner_rows(pick, by_device))
    grad_ref[:, :, 32:48, 256:384] = stored.reshape(2, 32, 16, 128)
    grad_ref[:, :, 32:48, 384:] = jnp.zeros((2, 32, 16, D - 384), jnp.bfloat16)


def local_kernel(kernel, outs, *args):
    vmem = pl.BlockSpec(memory_space=pltpu.VMEM)
    return pl.pallas_call(
        kernel,
        out_shape=[jax.ShapeDtypeStruct(shape, dtype) for shape, dtype in outs],
        in_specs=[vmem] * len(args),
        out_specs=[vmem] * len(outs),
        compiler_params=pltpu.CompilerParams(vmem_limit_bytes=58 * 2**20),
    )(*args)


def layer(full, tokens, cotangent, lengths):
    rest, mlp_weights = full
    bf16, f32 = jnp.bfloat16, jnp.float32
    rest = rest.reshape(2, 32, 48, D)
    x = tokens.reshape(TOKENS, D)
    rows = jnp.repeat(lengths, 128)[:, None]
    cosine, sine = rotary_tables(128)
    cosine, sine = jnp.tile(cosine, (2, 2)), jnp.tile(sine, (2, 2))
    slots = (jnp.arange(2944, dtype=jnp.int32) % 23)[None]
    shared = (rest, rows, cosine, sine, slots)
    middle, h2, back, h1p, q, k, v, mixed, probs, vector = local_kernel(
        forward_kernel,
        (
            ((TOKENS, D), f32),
            ((TOKENS, D), bf16),
            ((TOKENS, D), bf16),
            ((TOKENS, 1024), bf16),
            ((TOKENS, D), bf16),
            ((TOKENS, 128), bf16),
            ((TOKENS, 128), bf16),
            ((TOKENS, 1024), bf16),
            ((2, 7, 128, 256), f32),
            ((1, 2944), f32),
        ),
        x,
        cotangent.reshape(TOKENS, D),
        *shared,
    )
    fed, dh2, grad_mlp = mlp(h2, back, mlp_weights)
    output, input_grad, grad_rest = local_kernel(
        backward_kernel,
        (((TOKENS, D), bf16), ((TOKENS, D), bf16), ((2, 32, 48, D), bf16)),
        x,
        back,
        *shared,
        middle,
        h1p,
        q,
        k,
        v,
        mixed,
        probs,
        vector,
        fed,
        dh2,
    )
    return (
        output.reshape(2, 1, 128, D),
        input_grad.reshape(2, 1, 128, D),
        grad_mlp,
        grad_rest.reshape(2, 4, 4, 2, 48, D),
    )


def half(value):
    return value.astype(jnp.bfloat16)


def mixing(gram):
    gram_half = half(gram)
    first = half(NEWTON_B * gram + NEWTON_C * product(gram_half, gram_half))
    cross = product(gram_half, first)
    after = (
        NEWTON_A * NEWTON_A * gram + 2.0 * NEWTON_A * cross + product(half(cross), first)
    )
    after_half = half(after)
    second = NEWTON_B * after + NEWTON_C * product(after_half, after_half)
    return half(
        NEWTON_A * (first.astype(jnp.float32) + second) + product(first, half(second))
    )


BLOCKS = [(i, j) for i in range(7) for j in range(i, 7)]


def muon_kernel(
    sent_ref, big_ref, square_ref, narrow_ref,
    rows, job, gram_out, gram_in, gram_all, gram, back, narrow_back, big_got, square_got, narrow_got,
    job_sems, sum_sems, all_sems, back_send, back_recv,
):
    coords, core = my_coords()
    z, y, x = coords
    me = y * 4 + x

    def plane(peer):
        return device_of((z, peer // 4, peer % 4), core)

    def line(other, other_core):
        return device_of((other, y, x), other_core)

    barrier = pltpu.get_barrier_semaphore()
    for k in range(1, 8):
        t = (z * 2 + core + k) % 8
        pl.semaphore_signal(barrier, inc=1, device_id=line(t // 2, t % 2), device_id_type=MESH)
    for k in range(1, 16):
        pl.semaphore_signal(barrier, inc=1, device_id=plane((me + k) % 16), device_id_type=MESH)
    pl.semaphore_wait(barrier, 22)

    def returned(src, dst, send_slot, slot, device):
        return pltpu.make_async_remote_copy(
            src_ref=src,
            dst_ref=dst,
            send_sem=back_send.at[send_slot],
            recv_sem=back_recv.at[slot],
            device_id=device,
            device_id_type=MESH,
        )

    def remote(src, dst, sems, slot, device):
        return pltpu.make_async_remote_copy(
            src_ref=src,
            dst_ref=dst,
            send_sem=sems.at[0, slot],
            recv_sem=sems.at[1, slot],
            device_id=device,
            device_id_type=MESH,
        )

    own = z * 2 + core

    def job_copy(k):
        t = (own + k) % 8
        return remote(sent_ref.at[t // 2], rows.at[own], job_sems, k, line(t // 2, t % 2))

    def job_arrival(k):
        t = (own + 8 - k) % 8
        return remote(sent_ref.at[0], rows.at[t], job_sems, k, line(t // 2, t % 2))

    for k in range(1, 8):
        job_copy(k).start()
    rows[own] = sent_ref[z]
    for k in range(1, 8):
        job_arrival(k).wait_recv()

    @pl.when(z < 3)
    def _():
        job[...] = rows[...]

    for job_core in range(2):

        @pl.when((z == 3) & (core == job_core))
        def _():
            job[:, 0:16] = rows[:, 16 * job_core : 16 * job_core + 16]
            job[:, 16:48] = jnp.zeros((8, 32, D), jnp.bfloat16)

    flat = job[...].reshape(384, D)
    narrow = rows[:, 32:48, 0:256].reshape(128, 256)
    gram[...] = inner_rows(flat, flat)
    for index, (i, j) in enumerate(BLOCKS):
        gram_out[index // 2, index % 2] = half(
            gram[128 * i : 128 * i + 128, 128 * j : 128 * j + 128]
        )
    for t in range(2):
        part = narrow[:, 128 * t : 128 * t + 128]
        gram_out[14, t] = half(inner_rows(part, part))
        gram_out[15, t] = jnp.zeros((128, 128), jnp.bfloat16)

    def sum_copy(k):
        peer = (me + k) % 16
        return remote(gram_out.at[peer], gram_in.at[me], sum_sems, k, plane(peer))

    def sum_arrival(k):
        peer = (me + 16 - k) % 16
        return remote(gram_out.at[0], gram_in.at[peer], sum_sems, k, plane(peer))

    for k in range(1, 16):
        sum_copy(k).start()
    gram_in[me] = gram_out[me]
    for k in range(1, 16):
        sum_arrival(k).wait_recv()
    for t in range(2):
        value = gram_in[0, t].astype(jnp.float32)
        for s in range(1, 16):
            value = value + gram_in[s, t].astype(jnp.float32)
        gram_all[me, t] = half(value)

    def all_copy(k, peer):
        return remote(gram_all.at[peer], gram_all.at[peer], all_sems, k, plane((me + k) % 16))

    for k in range(1, 16):
        all_copy(k, me).start()
    for k in range(1, 16):
        all_copy(k, (me + 16 - k) % 16).wait_recv()

    eye = lax.broadcasted_iota(jnp.int32, (128, 128), 0) == lax.broadcasted_iota(
        jnp.int32, (128, 128), 1
    )

    def diagonal(block):
        return jnp.sum(jnp.where(eye, block, 0.0))

    trace = 0.0
    for index, (i, j) in enumerate(BLOCKS):
        block = gram_all[index // 2, index % 2].astype(jnp.float32)
        gram[128 * i : 128 * i + 128, 128 * j : 128 * j + 128] = block
        if i == j:
            trace = trace + diagonal(block)
        else:
            gram[128 * j : 128 * j + 128, 128 * i : 128 * i + 128] = block.T

    def finish(total, matrix, values):
        inverse = 1.0 / (jnp.sqrt(jnp.full((1, 1), total)) + 1e-07)
        mixer = mixing(matrix * (inverse * inverse))
        scaled = values.astype(jnp.float32) * inverse
        return half(NEWTON_A * NEWTON_A * scaled + product(half(scaled), mixer))

    back[...] = finish(trace, gram[...], flat).reshape(8, 48, D)
    for t in range(2):
        matrix = gram_all[14, t].astype(jnp.float32)
        part = narrow[:, 128 * t : 128 * t + 128]
        narrow_back[t] = finish(diagonal(matrix), matrix, part).reshape(8, 16, 128)

    @pl.when(z < 3)
    def _():
        copies = []
        for k in range(1, 4):
            other = (z + k) % 4
            copies.append(
                returned(
                    back.at[other * 2 + core], big_got.at[z], k, z, line(other, core)
                )
            )
        for copy in copies:
            copy.start()
        big_got[z] = back[own]
        for copy in copies:
            copy.wait_send()

    @pl.when(z == 3)
    def _():
        copies = []
        for k in range(1, 8):
            t = (own + k) % 8
            device = line(t // 2, t % 2)
            copies.append(
                returned(back.at[t, pl.ds(0, 16)], square_got.at[core], k, 3 + core, device)
            )
            copies.append(
                returned(narrow_back.at[core, t], narrow_got.at[core], 8 + k, 5 + core, device)
            )
        for copy in copies:
            copy.start()
        square_got[core] = back[own, 0:16]
        narrow_got[core] = narrow_back[core, own]
        for copy in copies:
            copy.wait_send()

    for plane_z in range(3):

        @pl.when(z != plane_z)
        def _():
            returned(
                back.at[0], big_got.at[plane_z], 0, plane_z, line(plane_z, core)
            ).wait_recv()

    for job_core in range(2):

        @pl.when((z != 3) | (core != job_core))
        def _():
            device = line(3, job_core)
            returned(
                back.at[0, pl.ds(0, 16)], square_got.at[job_core], 0, 3 + job_core, device
            ).wait_recv()
            returned(
                narrow_back.at[0, 0], narrow_got.at[job_core], 0, 5 + job_core, device
            ).wait_recv()

    for k in range(1, 8):
        job_copy(k).wait_send()
    for k in range(1, 16):
        sum_copy(k).wait_send()
        all_copy(k, me).wait_send()
    big_ref[...] = big_got[...]
    square_ref[...] = square_got[...]
    narrow_ref[...] = narrow_got[...]


def muon(sent):
    vmem = pl.BlockSpec(memory_space=pltpu.VMEM)
    return pl.pallas_call(
        muon_kernel,
        out_shape=(
            jax.ShapeDtypeStruct((3, 48, D), jnp.bfloat16),
            jax.ShapeDtypeStruct((2, 16, D), jnp.bfloat16),
            jax.ShapeDtypeStruct((2, 16, 128), jnp.bfloat16),
        ),
        in_specs=[vmem],
        out_specs=(vmem,) * 3,
        scratch_shapes=[
            pltpu.VMEM((8, 48, D), jnp.bfloat16),
            pltpu.VMEM((8, 48, D), jnp.bfloat16),
            pltpu.VMEM((16, 2, 128, 128), jnp.bfloat16),
            pltpu.VMEM((16, 2, 128, 128), jnp.bfloat16),
            pltpu.VMEM((16, 2, 128, 128), jnp.bfloat16),
            pltpu.VMEM((D, D), jnp.float32),
            pltpu.VMEM((8, 48, D), jnp.bfloat16),
            pltpu.VMEM((2, 8, 16, 128), jnp.bfloat16),
            pltpu.VMEM((3, 48, D), jnp.bfloat16),
            pltpu.VMEM((2, 16, D), jnp.bfloat16),
            pltpu.VMEM((2, 16, 128), jnp.bfloat16),
            pltpu.SemaphoreType.DMA((2, 8)),
            pltpu.SemaphoreType.DMA((2, 16)),
            pltpu.SemaphoreType.DMA((2, 16)),
            pltpu.SemaphoreType.DMA((16,)),
            pltpu.SemaphoreType.DMA((7,)),
        ],
        compiler_params=pltpu.CompilerParams(
            collective_id=3, has_side_effects=True, vmem_limit_bytes=58 * 2**20
        ),
    )(sent)


def body(
    inputs,
    cotangent,
    lengths,
    query_weight,
    key_weight,
    value_weight,
    out_weight,
    gate_weight,
    up_weight,
    down_weight,
    vectors,
    query_prior,
    key_prior,
    value_prior,
    out_prior,
    gate_prior,
    up_prior,
    down_prior,
    first_prior,
    second_prior,
):
    axes = ("dp", "narrow")
    chip = lax.axis_index("dp")
    core = lax.axis_index("narrow")
    parity = chip % 2
    kv_width = key_weight.shape[1]
    own = pack_pair(
        (
            jnp.concatenate([gate_weight.T, up_weight.T, down_weight, query_weight, out_weight]),
            jnp.concatenate([key_weight, value_weight], axis=1),
            vectors,
        ),
        parity,
    )
    gathered, rest = gather_blocks(own)
    own_lengths = lax.dynamic_slice_in_dim(lengths, chip * 2 + core, 1, axis=1)[:, 0]
    block_output, input_grad, grad_mlp, grad_rest = layer(
        (rest, gathered.reshape(32, 2 * ROWS, D)), inputs[:, 0], cotangent[:, 0], own_lengths
    )
    reduced = scatter_blocks(grad_mlp.reshape(4, 4, 2, 3 * UNITS, D), grad_rest)
    partner = swap_pair(reduced)
    both = jnp.where(
        parity == 0, jnp.concatenate([reduced, partner]), jnp.concatenate([partner, reduced])
    ).astype(jnp.float32)

    def mine(start, size):
        return lax.dynamic_slice_in_dim(both, start + parity * size, size, axis=0)

    own_narrow = mine(272, 7)
    grad_vector = own_narrow[0, 2 * kv_width : 2 * kv_width + 23]
    owned = (
        mine(240, 7),
        own_narrow[:, :kv_width],
        own_narrow[:, kv_width : 2 * kv_width],
        mine(256, 7),
        mine(0, 38),
        mine(80, 38),
        mine(160, 38),
    )
    priors = (
        query_prior,
        key_prior,
        value_prior,
        out_prior,
        gate_prior.T,
        up_prior.T,
        down_prior,
    )
    masters = (
        query_weight,
        key_weight,
        value_weight,
        out_weight,
        gate_weight,
        up_weight,
        down_weight,
    )
    shapes = ((D, D), (D, kv_width), (D, kv_width), (D, D), (D, FF), (D, FF), (FF, D))
    lefts = (False, False, False, False, True, True, False)
    momenta = tuple((MOMENTUM * priors[k] + owned[k] for k in range(7)))

    def padded(value, count):
        return jnp.pad(value, ((0, count - value.shape[0]), (0, D - value.shape[1])))

    narrow_rows = jnp.concatenate([momenta[1], momenta[2]], axis=1)
    last = jnp.concatenate(
        [padded(momenta[0], 16), padded(momenta[3], 16), padded(narrow_rows, 16)]
    )
    sent = jnp.stack([padded(momenta[4], 48), padded(momenta[5], 48), padded(momenta[6], 48), last])
    big, square, thin = muon(half(sent))
    finals = (
        square[0, :7], thin[0, :7], thin[1, :7], square[1, :7], big[0, :38], big[1, :38], big[2, :38],
    )
    updated = []
    kept = []
    for k in range(7):
        current = finals[k].astype(jnp.float32)
        factor = MUON_RATE * 0.2 * math.sqrt(max(shapes[k][0], shapes[k][1]))
        if lefts[k]:
            current = current.T
        updated.append(masters[k] * (1.0 - MUON_RATE * MUON_DECAY) - factor * current)
        kept.append(momenta[k].T if lefts[k] else momenta[k])
    vector_first = BETA_FIRST * first_prior + (1.0 - BETA_FIRST) * grad_vector
    vector_second = BETA_SECOND * second_prior + (1.0 - BETA_SECOND) * grad_vector * grad_vector
    first_hat = vector_first / (1.0 - BETA_FIRST**STEP)
    second_hat = vector_second / (1.0 - BETA_SECOND**STEP)
    vector_new = vectors * (1.0 - ADAM_RATE * ADAM_DECAY) - ADAM_RATE * first_hat / (
        jnp.sqrt(second_hat) + ADAM_EPSILON
    )
    return (
        block_output,
        input_grad,
        *kept,
        *updated,
        vector_first,
        vector_second,
        vector_new,
    )


def solution(mesh):
    placed = (
        P(None, ("dp", "narrow"), None, None),
        P(None, ("dp", "narrow"), None, None),
        P(),
        P(("dp", "narrow"), None),
        P(("dp", "narrow"), None),
        P(("dp", "narrow"), None),
        P(("dp", "narrow"), None),
        P(None, ("dp", "narrow")),
        P(None, ("dp", "narrow")),
        P(("dp", "narrow"), None),
        P(("dp", "narrow")),
        P(("dp", "narrow"), None),
        P(("dp", "narrow"), None),
        P(("dp", "narrow"), None),
        P(("dp", "narrow"), None),
        P(None, ("dp", "narrow")),
        P(None, ("dp", "narrow")),
        P(("dp", "narrow"), None),
        P(("dp", "narrow")),
        P(("dp", "narrow")),
    )
    return jax.shard_map(
        body,
        mesh=mesh,
        in_specs=placed,
        out_specs=(
            P(None, ("dp", "narrow"), None, None),
            P(None, ("dp", "narrow"), None, None),
            P(("dp", "narrow"), None),
            P(("dp", "narrow"), None),
            P(("dp", "narrow"), None),
            P(("dp", "narrow"), None),
            P(None, ("dp", "narrow")),
            P(None, ("dp", "narrow")),
            P(("dp", "narrow"), None),
            P(("dp", "narrow"), None),
            P(("dp", "narrow"), None),
            P(("dp", "narrow"), None),
            P(("dp", "narrow"), None),
            P(None, ("dp", "narrow")),
            P(None, ("dp", "narrow")),
            P(("dp", "narrow"), None),
            P(("dp", "narrow")),
            P(("dp", "narrow")),
            P(("dp", "narrow")),
        ),
        check_vma=False,
    )
```

```python
import math

import jax
import jax.numpy as jnp
from jax import lax
from jax.experimental import pallas as pl
from jax.experimental.pallas import tpu as pltpu
from jax.sharding import PartitionSpec as P

D = 896
FF = 4864
HEADS = 14
KV_HEADS = 2
HEAD = 64
STEP = 10


NORM_EPSILON = 1e-06
ROPE_BASE = 1000000.0
MOMENTUM = 0.95
NEWTON_A = 3.4445
NEWTON_B = -4.775
NEWTON_C = 2.0315
MUON_RATE = 0.4
MUON_DECAY = 0.1
ADAM_RATE = 0.5
ADAM_DECAY = 0.01
BETA_FIRST = 0.9
BETA_SECOND = 0.999
ADAM_EPSILON = 1e-08
MASKED = -1e30


def product(left, right):
    return jnp.dot(left, right, preferred_element_type=jnp.float32)


def inner_rows(left, right):
    return lax.dot_general(
        left, right, (((0,), (0,)), ((), ())), preferred_element_type=jnp.float32
    )


def outer_cols(left, right):
    return lax.dot_general(
        left, right, (((1,), (1,)), ((), ())), preferred_element_type=jnp.float32
    )


def rotary_tables(length):
    half = HEAD // 2
    freqs = ROPE_BASE ** (-jnp.arange(half, dtype=jnp.float32) * 2.0 / HEAD)
    angles = jnp.arange(length, dtype=jnp.float32)[:, None] * freqs[None, :]
    angles = jnp.concatenate([angles, angles], axis=-1)
    return (jnp.cos(angles), jnp.sin(angles))


def norm_back(grad, normed, scale):
    return scale * (grad - normed * jnp.mean(grad * normed, axis=-1, keepdims=True))


def half(value):
    return value.astype(jnp.bfloat16)


MESH = pl.DeviceIdType.MESH
TOKENS = 256
FULL = (0, 4)
BF16 = jnp.bfloat16
F32 = jnp.float32
CHUNK = 48
PARTS = (
    (0, 0, CHUNK, (2, 1, 0), False),
    (0, CHUNK, CHUNK, (1, 0, 2), False),
    (1, 0, CHUNK, (0, 2, 1), True),
    (2, 0, 16, (2, 1, 0), True),
    (2, 16, 16, (1, 0, 2), True),
    (2, 32, 16, (0, 2, 1), True),
)
WIDE = (0, 1, 2)
THIN = (3, 4, 5)


def my_coords():
    dp = lax.axis_index("dp")
    return (dp // 16, (dp // 4) % 4, dp % 4), lax.axis_index("narrow")


def device_of(coords, core):
    return (coords[0] * 16 + coords[1] * 4 + coords[2], core)


def shifted(coords, axis, by):
    out = list(coords)
    out[axis] = (coords[axis] + by) % 4
    return tuple(out)


def facing(coords):
    return (coords[0], coords[1], 3 - coords[2])


def greet(coords, core):
    barrier = pltpu.get_barrier_semaphore()
    for axis in range(3):
        for by in (1, 3):
            pl.semaphore_signal(
                barrier, inc=1, device_id=device_of(shifted(coords, axis, by), core), device_id_type=MESH
            )
    pl.semaphore_signal(barrier, inc=1, device_id=device_of(coords, 1 - core), device_id_type=MESH)
    pl.semaphore_wait(barrier, 7)


def remote(src, dst, send_sem, recv_sem, device):
    return pltpu.make_async_remote_copy(
        src_ref=src,
        dst_ref=dst,
        send_sem=send_sem,
        recv_sem=recv_sem,
        device_id=device,
        device_id_type=MESH,
    )


def place_of(part, piece):
    spec, columns = piece
    _, first, rows, _, shared = PARTS[part]
    index = [pl.ds(*s) if isinstance(s, tuple) else s for s in spec[:2]]
    s = spec[2]
    if isinstance(s, tuple):
        index.append(pl.ds(s[0] // 2, s[1] // 2))
        index += [] if shared else [pl.ds(0, 2)]
    else:
        index.append(s // 2)
        index += [] if shared else [s % 2]
    columns = (0, D) if columns is None else columns
    return (*index, pl.ds(first, rows), pl.ds(*columns))


def shape_of(part, piece):
    return tuple(entry.size for entry in place_of(part, piece) if isinstance(entry, pl.Slice))


def halves(spec, axis):
    if axis is None:
        return [(spec, (0, 512)), (spec, (512, 384))]
    out = []
    for h in range(2):
        s = list(spec)
        s[axis] = (2 * h, 2)
        out.append((tuple(s), None))
    return out


class Plan:
    def __init__(self, part, coords, axis, spec, split):
        self.coords, self.axis, self.spec, self.split = coords, axis, spec, split
        self.exchange = PARTS[part][4] and axis == 2

    def pieces(self, by):
        spec = list(self.spec)
        spec[self.axis] = (self.coords[self.axis] + by) % 4
        return halves(tuple(spec), self.split)

    def facing(self):
        return ((*self.spec[:2], 3 - self.coords[2]), None)

    def own(self):
        return (self.spec, None)


def plan_of(part, stage, coords):
    order = PARTS[part][3]
    spec = tuple(FULL if k in order[:stage] else coords[k] for k in range(3))
    return Plan(part, coords, order[stage], spec, order[stage - 1] if stage else None)


class Gather:
    def __init__(self, arrays, coords, core, send_sems, recv_sems):
        self.arrays, self.coords, self.core = arrays, coords, core
        self.send_sems, self.recv_sems = send_sems, recv_sems

    def copy(self, part, phase, slot, piece, coords):
        array, prefix = self.arrays[PARTS[part][0]]
        ref = array.at[(*prefix, *place_of(part, piece))]
        sems = (self.send_sems.at[part, phase, slot], self.recv_sems.at[part, phase, slot])
        return remote(ref, ref, *sems, device_of(coords, self.core))

    def send(self, *args):
        self.copy(*args).start()

    def neighbours(self, plan):
        return shifted(self.coords, plan.axis, 1), shifted(self.coords, plan.axis, 3)

    def start(self, parts, phase):
        for part in parts:
            plan = plan_of(part, phase, self.coords)
            if plan.exchange:
                self.send(part, phase, 0, plan.own(), facing(self.coords))
                continue
            right, left = self.neighbours(plan)
            first, second = plan.pieces(0)
            self.send(part, phase, 0, first, right)
            self.send(part, phase, 1, second, left)
            self.send(part, phase, 2, second, right)
            self.send(part, phase, 3, first, left)

    def forward(self, parts, phase):
        for part in parts:
            plan = plan_of(part, phase, self.coords)
            if plan.exchange:
                continue
            right, left = self.neighbours(plan)
            piece = plan.pieces(3)[0]
            self.copy(part, phase, 0, piece, right).wait_recv()
            self.send(part, phase, 4, piece, right)
            piece = plan.pieces(1)[1]
            self.copy(part, phase, 1, piece, left).wait_recv()
            self.send(part, phase, 5, piece, left)

    def near(self, parts, phase):
        for part in parts:
            plan = plan_of(part, phase, self.coords)
            if plan.exchange:
                self.copy(part, phase, 0, plan.facing(), facing(self.coords)).wait_recv()
                continue
            right, left = self.neighbours(plan)
            self.copy(part, phase, 2, plan.pieces(3)[1], right).wait_recv()
            self.copy(part, phase, 3, plan.pieces(1)[0], left).wait_recv()

    def far(self, parts, phase):
        for part in parts:
            plan = plan_of(part, phase, self.coords)
            if plan.exchange:
                continue
            right, left = self.neighbours(plan)
            self.copy(part, phase, 4, plan.pieces(2)[0], right).wait_recv()
            self.copy(part, phase, 5, plan.pieces(2)[1], left).wait_recv()

    def finish(self, parts, phase):
        self.near(parts, phase)
        self.far(parts, phase)

    def drain(self):
        for part in range(6):
            for phase in range(3):
                plan = plan_of(part, phase, self.coords)
                if plan.exchange:
                    self.copy(part, phase, 0, plan.own(), facing(self.coords)).wait_send()
                    continue
                right, _ = self.neighbours(plan)
                for slot, which in enumerate((0, 1, 1, 0, 0, 1)):
                    self.copy(part, phase, slot, plan.pieces(0)[which], right).wait_send()


def each_block(shape, body):
    lead = shape[:-2]
    count = math.prod(lead)
    if count == 1:
        body((0,) * len(lead))
        return

    def step(k, carry):
        index = []
        for n in reversed(lead):
            index.append(k % n)
            k = k // n
        body(tuple(reversed(index)))
        return carry

    lax.fori_loop(0, count, step, 0)


class Scatter:
    def __init__(self, arrays, coords, core, buffers, send_sems, recv_sems):
        self.arrays, self.coords, self.core = arrays, coords, core
        self.buffers, self.send_sems, self.recv_sems = buffers, send_sems, recv_sems

    def copy(self, part, phase, slot, piece, coords):
        array, prefix = self.arrays[PARTS[part][0]]
        ref = array.at[(*prefix, *place_of(part, piece))]
        sems = (self.send_sems.at[part, phase, slot], self.recv_sems.at[part, phase, slot])
        return remote(ref, self.buffers[part, phase][slot], *sems, device_of(coords, self.core))

    def send(self, *args):
        self.copy(*args).start()

    def arrive(self, *args):
        self.copy(*args).wait_recv()

    def add(self, part, phase, piece, *slots):
        sources = [self.buffers[part, phase][slot] for slot in slots]
        base = place_of(part, piece)
        array, prefix = self.arrays[PARTS[part][0]]

        def one(index):
            spot, position = [], 0
            for entry in base[:-2]:
                if isinstance(entry, pl.Slice):
                    spot.append(entry.start + index[position])
                    position += 1
                else:
                    spot.append(entry)
            spot = (*prefix, *spot, *base[-2:])
            value = array[spot].astype(F32)
            for source in sources:
                value = value + source[(*index, slice(None), slice(None))].astype(F32)
            array[spot] = half(value)

        each_block(shape_of(part, piece), one)

    def neighbours(self, plan):
        return shifted(self.coords, plan.axis, 1), shifted(self.coords, plan.axis, 3)

    def start_far(self, parts, phase):
        for part in parts:
            plan = plan_of(part, phase, self.coords)
            if plan.exchange:
                continue
            right, left = self.neighbours(plan)
            self.send(part, phase, 0, plan.pieces(2)[0], right)
            self.send(part, phase, 1, plan.pieces(2)[1], left)

    def start_near(self, parts, phase):
        for part in parts:
            plan = plan_of(part, phase, self.coords)
            if plan.exchange:
                self.send(part, phase, 0, plan.facing(), facing(self.coords))
                continue
            right, left = self.neighbours(plan)
            self.send(part, phase, 2, plan.pieces(1)[1], right)
            self.send(part, phase, 3, plan.pieces(3)[0], left)

    def start(self, parts, phase):
        self.start_far(parts, phase)
        self.start_near(parts, phase)

    def forward(self, parts, phase):
        for part in parts:
            plan = plan_of(part, phase, self.coords)
            if plan.exchange:
                continue
            right, left = self.neighbours(plan)
            self.arrive(part, phase, 0, plan.pieces(2)[0], right)
            self.add(part, phase, plan.pieces(1)[0], 0)
            self.send(part, phase, 4, plan.pieces(1)[0], right)
            self.arrive(part, phase, 1, plan.pieces(2)[1], left)
            self.add(part, phase, plan.pieces(3)[1], 1)
            self.send(part, phase, 5, plan.pieces(3)[1], left)

    def finish(self, parts, phase):
        for part in parts:
            plan = plan_of(part, phase, self.coords)
            if plan.exchange:
                self.arrive(part, phase, 0, plan.facing(), facing(self.coords))
                self.add(part, phase, plan.own(), 0)
                continue
            right, left = self.neighbours(plan)
            self.arrive(part, phase, 3, plan.pieces(3)[0], left)
            self.arrive(part, phase, 4, plan.pieces(1)[0], right)
            self.add(part, phase, plan.pieces(0)[0], 4, 3)
            self.arrive(part, phase, 2, plan.pieces(1)[1], right)
            self.arrive(part, phase, 5, plan.pieces(3)[1], left)
            self.add(part, phase, plan.pieces(0)[1], 2, 5)

    def drain(self):
        for part in range(6):
            for phase in range(3):
                plan = plan_of(part, phase, self.coords)
                if plan.exchange:
                    self.copy(part, phase, 0, plan.own(), facing(self.coords)).wait_send()
                    continue
                right, _ = self.neighbours(plan)
                for slot, which in enumerate((0, 1, 1, 0, 0, 1)):
                    self.copy(part, phase, slot, plan.pieces(0)[which], right).wait_send()


def scatter_buffer_shapes():
    out = []
    for part in range(6):
        for phase in range(3):
            plan = plan_of(part, phase, (0, 0, 0))
            if plan.exchange:
                shapes = [shape_of(part, plan.own())]
            else:
                first, second = (shape_of(part, piece) for piece in plan.pieces(0))
                shapes = [first, second, second, first, first, second]
            out.append(((part, phase), shapes))
    return out


SCALE = HEAD ** (-0.5)


def turn(values, sign):
    lane = lax.broadcasted_iota(jnp.int32, values.shape, 1)
    ahead = pltpu.roll(values, 96, 1)
    behind = pltpu.roll(values, 32, 1)
    return jnp.where(lane & 32 == 0, sign * ahead, -sign * behind)


def tiles_of(values):
    return [values[:, 128 * t : 128 * t + 128] for t in range(values.shape[1] // 128)]


def rotated(values, cosine, sine):
    return jnp.concatenate(
        [tile * cosine + turn(tile, -1.0) * sine for tile in tiles_of(values)], axis=1
    )


def rotated_back(values, cosine, sine):
    return jnp.concatenate(
        [tile * cosine + turn(tile * sine, 1.0) for tile in tiles_of(values)], axis=1
    )


def low_lanes(shape):
    return lax.broadcasted_iota(jnp.int32, shape, 1) < HEAD


def paired(both):
    swapped = pltpu.roll(both, 64, 1)
    low = low_lanes(both.shape)
    even = [half(jnp.where(low, v, 0.0)) for v in (both, swapped)]
    odd = [half(jnp.where(low, 0.0, v)) for v in (swapped, both)]
    kinds = [jnp.concatenate([even[a], odd[b]]) for a, b in ((0, 0), (0, 1), (1, 1))]
    return [kinds[0]] * 3 + [kinds[1]] + [kinds[2]] * 3


def gathered_place():
    row = lax.broadcasted_iota(jnp.int32, (1024, D), 0)
    feature = lax.broadcasted_iota(jnp.int32, (1024, D), 1)
    slot = row & 15
    odd = (slot >= 7).astype(jnp.int32)
    device = (((row >> 4) & 31) * 2 + odd) * 2 + (row >> 9)
    source = jnp.where(slot < 14, 7 * device + slot - 7 * odd, -1)
    return half((source == feature).astype(jnp.float32))


def vector_maps():
    device = lax.broadcasted_iota(jnp.int32, (128, 1024), 0)
    row = lax.broadcasted_iota(jnp.int32, (128, 1024), 1)
    target = (device & 1) * 512 + (device >> 2) * 16 + ((device >> 1) & 1) * 7
    pick = half((row == target).astype(jnp.float32))
    start = lax.broadcasted_iota(jnp.int32, (128, 2944), 0) * 23
    entry = lax.broadcasted_iota(jnp.int32, (128, 2944), 1)
    owner = half(((entry >= start) & (entry < start + 23)).astype(jnp.float32))
    return pick, owner


def slot_mask(slots):
    return lax.broadcasted_iota(jnp.int32, (128, 2944), 0) == slots


def attention_forward(
    x_ref, rest_ref, len_ref, cos_ref, sin_ref, slot_ref,
    middle_ref, h1p_ref, q_ref, k_ref, v_ref, mixed_ref, probs_ref, vector_ref,
):
    place = gathered_place()
    pick, owner = vector_maps()
    stored = rest_ref[:, :, :, :, 32:48, 256:384].reshape(1024, 128)
    by_device = half(product(pick, stored))
    spread = inner_rows(by_device, owner)
    vector = jnp.sum(jnp.where(slot_mask(slot_ref[...]), spread, 0.0), axis=0, keepdims=True)
    vector_ref[...] = vector
    first_gain, second_gain = vector[:, :D], vector[:, D : 2 * D]
    query_bias, narrow_bias = vector[:, 2 * D : 3 * D], vector[:, 3 * D :]
    cosine, sine = cos_ref[...], sin_ref[...]
    inputs = x_ref[...].astype(jnp.float32)
    first_scale = lax.rsqrt(jnp.mean(inputs * inputs, axis=-1, keepdims=True) + NORM_EPSILON)
    normed = half(inputs * first_scale * first_gain)
    placed = half(outer_cols(normed, place))
    h1p_ref[...] = placed
    queries = product(placed, rest_ref[:, :, :, :, 0:16, :].reshape(1024, D)) + query_bias
    narrow = product(placed, rest_ref[:, :, :, :, 32:48, 0:256].reshape(1024, 256)) + narrow_bias
    q_ref[...] = half(rotated(queries, cosine, sine))
    keys = rotated(narrow[:, 0:128], cosine, sine)
    k_ref[...] = half(keys)
    values = narrow[:, 128:256]
    v_ref[...] = half(values)
    position = lax.broadcasted_iota(jnp.int32, (128, 256), 0)
    other = lax.broadcasted_iota(jnp.int32, (128, 256), 1) & 127
    causal = other <= position
    rows = []
    for b in range(2):
        here = slice(128 * b, 128 * b + 128)
        allowed = causal & (other < len_ref[here, :])
        key_tiles = paired(keys[here])
        value_tiles = paired(values[here])
        tiles = []
        for t in range(7):
            scores = outer_cols(q_ref[here, 128 * t : 128 * t + 128], key_tiles[t])
            scores = jnp.where(allowed, scores * SCALE, MASKED)
            parts = []
            for part in tiles_of(scores):
                shifted = jnp.exp(part - jnp.max(part, axis=-1, keepdims=True))
                parts.append(shifted / jnp.sum(shifted, axis=-1, keepdims=True))
            probs = jnp.concatenate(parts, axis=1)
            probs_ref[b, t] = probs
            tiles.append(half(product(half(probs), value_tiles[t])))
        rows.append(jnp.concatenate(tiles, axis=1))
    mixed = half(outer_cols(jnp.concatenate(rows), place))
    mixed_ref[...] = mixed
    middle = inputs + product(mixed, rest_ref[:, :, :, :, 16:32, :].reshape(1024, D))
    middle_ref[...] = middle
    second_scale = lax.rsqrt(jnp.mean(middle * middle, axis=-1, keepdims=True) + NORM_EPSILON)
    return half(middle * second_scale * second_gain)


def mlp_tile(weights, h, e, out_acc, back_acc):
    lead = weights.shape[:-2]
    units = 16 * math.prod(lead)
    gate_w, up_w, down_w = (
        weights[..., 16 * k : 16 * k + 16, :].reshape(units, D) for k in range(3)
    )
    gate = outer_cols(h, gate_w)
    up = outer_cols(h, up_w)
    sigma = jax.nn.sigmoid(gate)
    silu = gate * sigma
    hidden = half(silu * up)
    grad_hidden = outer_cols(e, down_w)
    out_acc[...] += product(hidden, down_w).reshape(2, TOKENS, D)
    grad_gate = half(grad_hidden * up * sigma * (1.0 + gate * (1.0 - sigma)))
    grad_up = half(grad_hidden * silu)
    back_acc[...] += (product(grad_gate, gate_w) + product(grad_up, up_w)).reshape(2, TOKENS, D)
    grads = (inner_rows(grad_gate, h), inner_rows(grad_up, h), inner_rows(hidden, e))
    return [half(grad).reshape(*lead, 16, D) for grad in grads]


def gather_kernel(
    wide_ref, tail_ref, x_ref, cot_ref, len_ref, cos_ref, sin_ref, slot_ref,
    middle_ref, e_ref, h1p_ref, q_ref, k_ref, v_ref, mixed_ref, probs_ref, vector_ref,
    output_ref, dh2_ref, grad_wide_ref, grad_shared_ref, rest_ref,
    wide, shared, rest, stage0, stage1, stage2, h_all, e_all, out_acc, back_acc, parcel, arrived, tail,
    local_sems, send_sems, recv_sems, twin_sems, store_sems,
):
    coords, core = my_coords()
    z, y, x = coords
    pair, odd = x // 2, x % 2
    load = pltpu.make_async_copy(wide_ref, wide.at[z, y, pair, odd], local_sems.at[0])
    load.start()
    greet(coords, core)
    twin = device_of(coords, 1 - core)

    def to_twin(src, dst, slot):
        return remote(src, dst, twin_sems.at[0, slot], twin_sems.at[1, slot], twin)

    gather = Gather(((wide, ()), (shared, ()), (rest, (core,))), coords, core, send_sems, recv_sems)
    partner = device_of((z, y, x + 1 - 2 * odd), core)
    tail_copy = remote(tail_ref, tail, twin_sems.at[0, 4], twin_sems.at[1, 4], partner)
    tail_copy.start()
    load.wait()
    gather.start((0, 1), 0)
    token = lax.broadcasted_iota(jnp.int32, (TOKENS, 1), 0) & 127
    live = (token < len_ref[...]).astype(F32)
    e_ref[...] = half(cot_ref[...].astype(F32) * live)
    e_all[core] = e_ref[...]
    e_copy = to_twin(e_ref, e_all.at[core], 0)
    e_copy.start()
    tail_copy.wait()
    both = half(tail_ref[...].astype(F32) + tail[...].astype(F32))
    shared[z, y, pair] = both[:CHUNK]
    rest[core, z, y, pair] = both[CHUNK:]
    gather.start(THIN, 0)
    gather.start((2,), 0)
    gather.forward(THIN, 0)
    gather.finish(THIN, 0)
    gather.start(THIN, 1)
    gather.forward(WIDE, 0)
    gather.forward(THIN, 1)
    gather.finish(THIN, 1)
    gather.start(THIN, 2)
    gather.finish(WIDE, 0)
    gather.start(WIDE, 1)
    gather.forward(THIN, 2)
    gather.finish(THIN, 2)
    rest_copy = to_twin(rest.at[core], rest.at[core], 1)
    rest_copy.start()
    gather.forward(WIDE, 1)
    gather.finish(WIDE, 1)
    gather.start(WIDE, 2)
    rest_copy.wait()
    rest_store = pltpu.make_async_copy(rest, rest_ref, local_sems.at[0])
    rest_store.start()
    h_all[core] = attention_forward(
        x_ref, rest, len_ref, cos_ref, sin_ref, slot_ref,
        middle_ref, h1p_ref, q_ref, k_ref, v_ref, mixed_ref, probs_ref, vector_ref,
    )
    h_copy = to_twin(h_all.at[core], h_all.at[core], 2)
    h_copy.start()
    out_acc[...] = jnp.zeros_like(out_acc)
    back_acc[...] = jnp.zeros_like(back_acc)
    e_copy.wait()
    h_copy.wait()
    stages = (stage0, stage1, stage2)

    def tile_places(j):
        return (
            (wide, grad_wide_ref, (j, slice(None), slice(None), slice(None), pl.ds(0, CHUNK))),
            (wide, grad_wide_ref, (slice(None), slice(None), j // 2, j % 2, pl.ds(CHUNK, CHUNK))),
            (shared, grad_shared_ref, (slice(None), j, slice(None), pl.ds(0, CHUNK))),
        )

    def step(k, carry):
        @pl.when(k == 1)
        def _():
            gather.near(WIDE, 2)

        @pl.when(k == 3)
        def _():
            gather.far(WIDE, 2)

        offset = jnp.where(k < 2, k, 5 - k)
        h = h_all[...].reshape(2 * TOKENS, D)
        e = e_all[...].reshape(2 * TOKENS, D)
        for t, axis in enumerate((0, 2, 1)):
            j = (coords[axis] + offset) % 4
            source, target, index = tile_places(j)[t]
            grads = mlp_tile(source[(*index, slice(None))], h, e, out_acc, back_acc)
            copy = pltpu.make_async_copy(
                stages[t], target.at[(*index, slice(None))], store_sems.at[t]
            )

            @pl.when(k > 0)
            def _():
                copy.wait()

            for place, grad in enumerate(grads):
                stages[t][..., 16 * place : 16 * place + 16, :] = grad
            copy.start()

        @pl.when(k == 0)
        def _():
            gather.forward(WIDE, 2)

        return carry

    lax.fori_loop(0, 4, step, 0)
    parcel[0] = half(out_acc[1 - core])
    parcel[1] = half(back_acc[1 - core])
    parcel_copy = to_twin(parcel, arrived, 3)
    parcel_copy.start()
    parcel_copy.wait()
    output_ref[...] = half(
        (middle_ref[...] + (out_acc[core] + arrived[0].astype(F32))) * live
    )
    dh2_ref[...] = back_acc[core] + arrived[1].astype(F32)
    for t in range(3):
        _, target, index = tile_places(0)[t]
        pltpu.make_async_copy(
            stages[t], target.at[(*index, slice(None))], store_sems.at[t]
        ).wait()
    rest_store.wait()
    gather.drain()


def attention_backward(
    between, x_ref, e_ref, rest_ref, cos_ref, sin_ref, slot_ref,
    middle_ref, h1p_ref, q_ref, k_ref, v_ref, mixed_ref, probs_ref, vector_ref, dh2_ref,
    input_grad_ref, grad_ref,
):
    place = gathered_place()
    pick, owner = vector_maps()
    vector = vector_ref[...]
    first_gain, second_gain = vector[:, :D], vector[:, D : 2 * D]
    cosine, sine = cos_ref[...], sin_ref[...]
    middle = middle_ref[...]
    second_scale = lax.rsqrt(jnp.mean(middle * middle, axis=-1, keepdims=True) + NORM_EPSILON)
    second_normed = middle * second_scale
    dh2 = dh2_ref[...]
    second_gain_grad = jnp.sum(dh2 * second_normed, axis=0, keepdims=True)
    grad_middle = e_ref[...].astype(jnp.float32) + norm_back(
        dh2 * second_gain, second_normed, second_scale
    )
    branch = half(grad_middle)
    wide = rest_ref[:, :, :, :, 16:32, :].reshape(1024, D)
    grad_ref[:, :, :, :, 16:32, :] = half(inner_rows(mixed_ref[...], branch)).reshape(2, 4, 4, 2, 16, D)
    grad_mixed = half(product(half(outer_cols(branch, wide)), place))
    low = low_lanes((128, 128))
    query_rows, key_rows, value_rows = [], [], []
    for b in range(2):
        if b == 1:
            between()
        here = slice(128 * b, 128 * b + 128)
        key_tiles = paired(k_ref[here, :].astype(jnp.float32))
        value_tiles = paired(v_ref[here, :].astype(jnp.float32))
        tiles = []
        sums = [[jnp.zeros((128, 128), jnp.float32) for _ in range(4)] for _ in range(2)]
        for t in range(7):
            head = grad_mixed[here, 128 * t : 128 * t + 128]
            grad_probs = outer_cols(head, value_tiles[t])
            probs = probs_ref[b, t]
            parts = []
            for p, g in zip(tiles_of(probs), tiles_of(grad_probs)):
                parts.append(half(p * (g - jnp.sum(p * g, axis=-1, keepdims=True))))
            grad_scores = jnp.concatenate(parts, axis=1)
            tiles.append(product(grad_scores, key_tiles[t]) * SCALE)
            for which, (left, right) in enumerate(
                ((grad_scores, q_ref[here, 128 * t : 128 * t + 128]), (half(probs), head))
            ):
                both = inner_rows(left, right)
                even, odd = (2 * t) // 7, (2 * t + 1) // 7
                sums[which][even] += both[0:128]
                sums[which][2 + odd] += both[128:256]
        query_rows.append(jnp.concatenate(tiles, axis=1))
        joined = []
        for which in range(2):
            even0, even1, odd0, odd1 = sums[which]
            joined.append(
                jnp.where(low, even0 + pltpu.roll(odd0, 64, 1), odd1 + pltpu.roll(even1, 64, 1))
            )
        key_rows.append(joined[0] * SCALE)
        value_rows.append(joined[1])
    grad_query = half(rotated_back(jnp.concatenate(query_rows), cosine, sine))
    grad_key = half(rotated_back(jnp.concatenate(key_rows), cosine, sine))
    grad_narrow = jnp.concatenate([grad_key, half(jnp.concatenate(value_rows))], axis=1)
    placed = h1p_ref[...]
    grad_ref[:, :, :, :, 0:16, :] = half(inner_rows(placed, grad_query)).reshape(2, 4, 4, 2, 16, D)
    grad_ref[:, :, :, :, 32:48, 0:256] = half(inner_rows(placed, grad_narrow)).reshape(2, 4, 4, 2, 16, 256)
    bias_grad = jnp.sum(
        jnp.concatenate([grad_query, grad_narrow], axis=1).astype(jnp.float32), axis=0, keepdims=True
    )
    grad_placed = outer_cols(grad_query, rest_ref[:, :, :, :, 0:16, :].reshape(1024, D)) + outer_cols(
        grad_narrow, rest_ref[:, :, :, :, 32:48, 0:256].reshape(1024, 256)
    )
    high = half(grad_placed)
    remainder = half(grad_placed - high.astype(jnp.float32))
    grad_normed = product(high, place) + product(remainder, place)
    inputs = x_ref[...].astype(jnp.float32)
    first_scale = lax.rsqrt(jnp.mean(inputs * inputs, axis=-1, keepdims=True) + NORM_EPSILON)
    first_normed = inputs * first_scale
    first_gain_grad = jnp.sum(grad_normed * first_normed, axis=0, keepdims=True)
    input_grad_ref[...] = half(
        grad_middle + norm_back(grad_normed * first_gain, first_normed, first_scale)
    )
    vector_grad = jnp.concatenate([first_gain_grad, second_gain_grad, bias_grad], axis=1)
    spread = half(jnp.where(slot_mask(slot_ref[...]), vector_grad, 0.0))
    by_device = half(outer_cols(owner, spread))
    stored = half(inner_rows(pick, by_device))
    grad_ref[:, :, :, :, 32:48, 256:384] = stored.reshape(2, 4, 4, 2, 16, 128)
    grad_ref[:, :, :, :, 32:48, 384:] = jnp.zeros((2, 4, 4, 2, 16, D - 384), jnp.bfloat16)


def scatter_kernel(
    grad_wide_ref, grad_shared_ref, x_ref, e_ref, rest_ref, cos_ref, sin_ref, slot_ref,
    middle_ref, h1p_ref, q_ref, k_ref, v_ref, mixed_ref, probs_ref, vector_ref, dh2_ref,
    input_grad_ref, out_ref,
    wide, shared, thin, joined, mine, theirs, load_sems, send_sems, recv_sems, twin_sems, pair_sems,
    *buffers,
):
    coords, core = my_coords()
    z, y, x = coords
    pair, odd = x // 2, x % 2
    named, position = {}, 0
    for key, shapes in scatter_buffer_shapes():
        named[key] = buffers[position : position + len(shapes)]
        position += len(shapes)
    scatter = Scatter(((wide, ()), (shared, ()), (thin, (core,))), coords, core, named, send_sems, recv_sems)

    def load(part, by):
        spec = [FULL] * 3
        axis = PARTS[part][3][2]
        spec[axis] = (coords[axis] + by) % 4
        place = place_of(part, (tuple(spec), None))
        source = (grad_wide_ref, grad_shared_ref)[PARTS[part][0]]
        target = (wide, shared)[PARTS[part][0]]
        return pltpu.make_async_copy(source.at[place], target.at[place], load_sems.at[part, by])

    for by in (2, 1, 3, 0):
        for part in WIDE:
            load(part, by).start()
    greet(coords, core)

    for part in WIDE:
        load(part, 2).wait()
        scatter.start_far((part,), 2)
    for part in WIDE:
        load(part, 1).wait()
        load(part, 3).wait()
        scatter.start_near((part,), 2)

    def between():
        scatter.forward(WIDE, 2)

    attention_backward(
        between, x_ref, e_ref, rest_ref, cos_ref, sin_ref, slot_ref,
        middle_ref, h1p_ref, q_ref, k_ref, v_ref, mixed_ref, probs_ref, vector_ref, dh2_ref,
        input_grad_ref, thin,
    )
    twin_copy = remote(
        thin.at[1 - core], joined, twin_sems.at[0], twin_sems.at[1], device_of(coords, 1 - core)
    )
    twin_copy.start()
    for part in WIDE:
        load(part, 0).wait()
    twin_copy.wait()

    def join(index):
        thin[(core, *index)] = half(thin[(core, *index)].astype(F32) + joined[index].astype(F32))

    each_block((4, 4, 2, CHUNK, D), join)
    scatter.start(THIN, 2)
    for part in WIDE:
        scatter.finish((part,), 2)
        scatter.start((part,), 1)
    scatter.forward(THIN, 2)
    scatter.finish(THIN, 2)
    scatter.start(THIN, 1)
    scatter.forward(WIDE, 1)
    scatter.forward(THIN, 1)
    for part in WIDE:
        scatter.finish((part,), 1)
        scatter.start((part,), 0)
    scatter.finish(THIN, 1)
    scatter.start(THIN, 0)
    scatter.forward(WIDE, 0)
    scatter.forward(THIN, 0)
    scatter.finish(WIDE, 0)
    scatter.finish(THIN, 0)
    mine[0] = shared[z, y, pair]
    mine[1] = thin[core, z, y, pair]
    partner = device_of((z, y, x + 1 - 2 * odd), core)
    pair_copy = remote(mine, theirs, pair_sems.at[0], pair_sems.at[1], partner)
    pair_copy.start()
    pair_copy.wait()
    out_ref[0] = wide[z, y, pair, odd, 0:CHUNK].astype(F32)
    out_ref[1] = wide[z, y, pair, odd, CHUNK : 2 * CHUNK].astype(F32)
    out_ref[2] = mine[0].astype(F32) + theirs[0].astype(F32)
    out_ref[3] = mine[1].astype(F32) + theirs[1].astype(F32)
    scatter.drain()


def layer(blocks, tokens, cotangent, lengths):
    vmem = pl.BlockSpec(memory_space=pltpu.VMEM)
    anywhere = pl.BlockSpec(memory_space=pl.ANY)
    x = tokens.reshape(TOKENS, D)
    rows = jnp.repeat(lengths, 128)[:, None]
    cosine, sine = rotary_tables(128)
    tables = (
        jnp.tile(cosine, (2, 2)),
        jnp.tile(sine, (2, 2)),
        (jnp.arange(2944, dtype=jnp.int32) % 23)[None],
    )

    def shapes(*pairs):
        return [jax.ShapeDtypeStruct(shape, dtype) for shape, dtype in pairs]

    kept = pl.pallas_call(
        gather_kernel,
        out_shape=shapes(
            ((TOKENS, D), F32),
            ((TOKENS, D), BF16),
            ((TOKENS, 1024), BF16),
            ((TOKENS, D), BF16),
            ((TOKENS, 128), BF16),
            ((TOKENS, 128), BF16),
            ((TOKENS, 1024), BF16),
            ((2, 7, 128, 256), F32),
            ((1, 2944), F32),
            ((TOKENS, D), BF16),
            ((TOKENS, D), F32),
            ((4, 4, 2, 2, 2 * CHUNK, D), BF16),
            ((4, 4, 2, CHUNK, D), BF16),
            ((2, 4, 4, 2, CHUNK, D), BF16),
        ),
        in_specs=[anywhere] + [vmem] * 7,
        out_specs=[vmem] * 11 + [anywhere] * 3,
        scratch_shapes=[
            pltpu.VMEM((4, 4, 2, 2, 2 * CHUNK, D), BF16),
            pltpu.VMEM((4, 4, 2, CHUNK, D), BF16),
            pltpu.VMEM((2, 4, 4, 2, CHUNK, D), BF16),
            pltpu.VMEM((4, 2, 2, CHUNK, D), BF16),
            pltpu.VMEM((4, 4, CHUNK, D), BF16),
            pltpu.VMEM((4, 2, CHUNK, D), BF16),
            pltpu.VMEM((2, TOKENS, D), BF16),
            pltpu.VMEM((2, TOKENS, D), BF16),
            pltpu.VMEM((2, TOKENS, D), F32),
            pltpu.VMEM((2, TOKENS, D), F32),
            pltpu.VMEM((2, TOKENS, D), BF16),
            pltpu.VMEM((2, TOKENS, D), BF16),
            pltpu.VMEM((2 * CHUNK, D), BF16),
            pltpu.SemaphoreType.DMA((3,)),
            pltpu.SemaphoreType.DMA((6, 3, 6)),
            pltpu.SemaphoreType.DMA((6, 3, 6)),
            pltpu.SemaphoreType.DMA((2, 5)),
            pltpu.SemaphoreType.DMA((3,)),
        ],
        compiler_params=pltpu.CompilerParams(
            collective_id=0, has_side_effects=True, vmem_limit_bytes=60 * 2**20
        ),
    )(*blocks, x, cotangent.reshape(TOKENS, D), rows, *tables)
    (middle, e, h1p, q, k, v, mixed, probs, vector, output, dh2, grad_wide, grad_shared, rest) = kept
    input_grad, grads = pl.pallas_call(
        scatter_kernel,
        out_shape=shapes(((TOKENS, D), BF16), ((4, CHUNK, D), F32)),
        in_specs=[anywhere] * 2 + [vmem] * 15,
        out_specs=[vmem] * 2,
        scratch_shapes=[
            pltpu.VMEM((4, 4, 2, 2, 2 * CHUNK, D), BF16),
            pltpu.VMEM((4, 4, 2, CHUNK, D), BF16),
            pltpu.VMEM((2, 4, 4, 2, CHUNK, D), BF16),
            pltpu.VMEM((4, 4, 2, CHUNK, D), BF16),
            pltpu.VMEM((2, CHUNK, D), BF16),
            pltpu.VMEM((2, CHUNK, D), BF16),
            pltpu.SemaphoreType.DMA((3, 4)),
            pltpu.SemaphoreType.DMA((6, 3, 6)),
            pltpu.SemaphoreType.DMA((6, 3, 6)),
            pltpu.SemaphoreType.DMA((2,)),
            pltpu.SemaphoreType.DMA((2,)),
        ]
        + [pltpu.VMEM(shape, BF16) for _, group in scatter_buffer_shapes() for shape in group],
        compiler_params=pltpu.CompilerParams(
            collective_id=1, has_side_effects=True, vmem_limit_bytes=62 * 2**20
        ),
    )(grad_wide, grad_shared, x, e, rest, *tables, middle, h1p, q, k, v, mixed, probs, vector, dh2)
    return output.reshape(2, 1, 128, D), input_grad.reshape(2, 1, 128, D), grads


def pack(units, query, out, narrow, vector, parity):
    wide = jnp.concatenate(
        [half(rows[16 * k : 16 * k + 16]) for k in range(2) for rows in units]
    )
    narrow = jnp.concatenate(
        [narrow, jnp.pad(vector[None], ((0, 6), (0, D - 256 - vector.shape[0])))], axis=1
    )

    def placed(rows, size):
        low = jnp.pad(rows, ((0, 16 - size), (0, 0)))
        high = jnp.pad(rows, ((size, 16 - 2 * size), (0, 0)))
        return jnp.where(parity == 0, low, high)

    shared = [placed(rows[32:38], 6) for rows in units] + [
        placed(rows, 7) for rows in (query, out, narrow)
    ]
    return wide, half(jnp.concatenate(shared))


def newton_schulz(gram, values):
    gram_half = half(gram)
    first = half(NEWTON_B * gram + NEWTON_C * product(gram_half, gram_half))
    cross = product(gram_half, first)
    after = NEWTON_A * NEWTON_A * gram + 2.0 * NEWTON_A * cross + product(half(cross), first)
    after_half = half(after)
    second = half(NEWTON_B * after + NEWTON_C * product(after_half, after_half))
    values = half(NEWTON_A * values + product(half(values), first))
    return half(NEWTON_A * values.astype(F32) + product(values, second))


BLOCKS = [(i, j) for i in range(7) for j in range(i, 7)]
JOB_ROWS = (48, 48, 48, 16, 16, 16, 16)


def muon_kernel(
    tall_ref, short_ref, tall_out_ref, short_out_ref,
    rows, gram_out, gram_twin, gram_half_sum, gram_in, gram_all, gram, back, tall_got, short_got,
    job_sems, twin_sems, sum_sems, all_sems, back_sems,
):
    coords, core = my_coords()
    z, y, x = coords
    job = z * 2 + y // 2
    source = z * 2 + y // 2
    member = (y % 2) * 4 + x
    twin = device_of(coords, 1 - core)

    def group(peer):
        return device_of((z, (y // 2) * 2 + peer // 4, peer % 4), core)

    def square(k):
        return device_of((k // 2, (k % 2) * 2 + y % 2, x), core)

    barrier = pltpu.get_barrier_semaphore()
    for k in range(1, 8):
        for device in (group((member + k) % 8), square((source + k) % 8)):
            pl.semaphore_signal(barrier, inc=1, device_id=device, device_id_type=MESH)
    pl.semaphore_signal(barrier, inc=1, device_id=twin, device_id_type=MESH)
    pl.semaphore_wait(barrier, 15)

    def copy(src, dst, sems, slot, device):
        return remote(src, dst, sems.at[0, slot], sems.at[1, slot], device)

    def mine(m, tall, short):
        return tall.at[m] if m < 3 else short.at[m - 3]

    def job_copy(m):
        return remote(
            mine(m, tall_ref, short_ref),
            rows.at[source, pl.ds(0, JOB_ROWS[m])],
            job_sems.at[0, m],
            job_sems.at[1, source],
            square(m),
        )

    for m in range(7):

        @pl.when(job != m)
        def _():
            job_copy(m).start()

    for kind in range(2):
        count = (48, 16)[kind]

        @pl.when((job >= 3 * kind) & (job < 3 + 4 * kind))
        def _():
            if kind == 1:
                rows[:, 16:48] = jnp.zeros((8, 32, D), BF16)
                rows[source, 0:16] = short_ref[job - 3]
            else:
                rows[source] = tall_ref[job]
            for k in range(1, 8):
                other = (source + k) % 8
                arrival = rows.at[other, pl.ds(0, count)]
                remote(
                    arrival, arrival, job_sems.at[0, 0], job_sems.at[1, other], square(other)
                ).wait_recv()

    @pl.when(job < 7)
    def _():
        flat = rows[...].reshape(384, D)
        gram[...] = inner_rows(flat, flat)
        for index, (i, j) in enumerate(BLOCKS):
            gram_out[index // 16, index % 16] = half(
                gram[128 * i : 128 * i + 128, 128 * j : 128 * j + 128]
            )
        gram_out[1, 12:16] = jnp.zeros((4, 128, 128), BF16)
        twin_copy = copy(gram_out.at[1 - core], gram_twin, twin_sems, 0, twin)
        twin_copy.start()
        twin_copy.wait()
        gram_half_sum[...] = half(gram_out[core].astype(F32) + gram_twin[...].astype(F32))

        def sum_copy(k):
            peer = (member + k) % 8
            return copy(
                gram_half_sum.at[pl.ds(2 * peer, 2)], gram_in.at[k], sum_sems, k, group(peer)
            )

        for k in range(1, 8):
            sum_copy(k).start()
        total = gram_half_sum[pl.ds(2 * member, 2)].astype(F32)
        for k in range(1, 8):
            sum_copy(k).wait_recv()
            total = total + gram_in[k].astype(F32)
        gram_all[core, pl.ds(2 * member, 2)] = half(total)

        def all_copy(k, owner):
            ref = gram_all.at[core, pl.ds(2 * owner, 2)]
            return copy(ref, ref, all_sems, k, group((member + k) % 8))

        for k in range(1, 8):
            all_copy(k, member).start()
        for k in range(1, 8):
            all_copy(k, (member + 8 - k) % 8).wait_recv()
        last_copy = copy(gram_all.at[core], gram_all.at[core], twin_sems, 1, twin)
        last_copy.start()
        last_copy.wait()

        eye = lax.broadcasted_iota(jnp.int32, (128, 128), 0) == lax.broadcasted_iota(
            jnp.int32, (128, 128), 1
        )
        trace = 0.0
        for index, (i, j) in enumerate(BLOCKS):
            block = gram_all[index // 16, index % 16].astype(F32)
            gram[128 * i : 128 * i + 128, 128 * j : 128 * j + 128] = block
            if i == j:
                trace = trace + jnp.sum(jnp.where(eye, block, 0.0))
            else:
                gram[128 * j : 128 * j + 128, 128 * i : 128 * i + 128] = block.T
        inverse = 1.0 / (jnp.sqrt(jnp.full((1, 1), trace)) + 1e-07)
        moved = newton_schulz(
            gram[...] * (inverse * inverse), rows[...].reshape(384, D).astype(F32) * inverse
        )
        back[...] = moved.reshape(8, 48, D)
        for k in range(1, 8):
            sum_copy(k).wait_send()
            all_copy(k, member).wait_send()

    for m in range(7):

        @pl.when(job == m)
        def _():
            copies = []
            for k in range(1, 8):
                other = (source + k) % 8
                copies.append(
                    remote(
                        back.at[other, pl.ds(0, JOB_ROWS[m])],
                        mine(m, tall_got, short_got),
                        back_sems.at[0, k],
                        back_sems.at[1, m],
                        square(other),
                    )
                )
            for item in copies:
                item.start()
            if m < 3:
                tall_got[m] = back[source]
            else:
                short_got[m - 3] = back[source, 0:16]
            for item in copies:
                item.wait_send()

    for m in range(7):

        @pl.when(job != m)
        def _():
            arrival = mine(m, tall_got, short_got)
            remote(arrival, arrival, back_sems.at[0, 0], back_sems.at[1, m], square(m)).wait_recv()
            job_copy(m).wait_send()

    tall_out_ref[...] = tall_got[...]
    short_out_ref[...] = short_got[...]


def muon(tall, short):
    vmem = pl.BlockSpec(memory_space=pltpu.VMEM)
    return pl.pallas_call(
        muon_kernel,
        out_shape=(
            jax.ShapeDtypeStruct((3, 48, D), BF16),
            jax.ShapeDtypeStruct((4, 16, D), BF16),
        ),
        in_specs=[vmem] * 2,
        out_specs=(vmem,) * 2,
        scratch_shapes=[
            pltpu.VMEM((8, 48, D), BF16),
            pltpu.VMEM((2, 16, 128, 128), BF16),
            pltpu.VMEM((16, 128, 128), BF16),
            pltpu.VMEM((16, 128, 128), BF16),
            pltpu.VMEM((8, 2, 128, 128), BF16),
            pltpu.VMEM((2, 16, 128, 128), BF16),
            pltpu.VMEM((D, D), F32),
            pltpu.VMEM((8, 48, D), BF16),
            pltpu.VMEM((3, 48, D), BF16),
            pltpu.VMEM((4, 16, D), BF16),
            pltpu.SemaphoreType.DMA((2, 8)),
            pltpu.SemaphoreType.DMA((2, 2)),
            pltpu.SemaphoreType.DMA((2, 8)),
            pltpu.SemaphoreType.DMA((2, 8)),
            pltpu.SemaphoreType.DMA((2, 8)),
        ],
        compiler_params=pltpu.CompilerParams(
            collective_id=3, has_side_effects=True, vmem_limit_bytes=58 * 2**20
        ),
    )(tall, short)


def body(
    inputs,
    cotangent,
    lengths,
    query_weight,
    key_weight,
    value_weight,
    out_weight,
    gate_weight,
    up_weight,
    down_weight,
    vectors,
    query_prior,
    key_prior,
    value_prior,
    out_prior,
    gate_prior,
    up_prior,
    down_prior,
    first_prior,
    second_prior,
):
    chip = lax.axis_index("dp")
    core = lax.axis_index("narrow")
    parity = chip % 2
    kv_width = key_weight.shape[1]
    blocks = pack(
        (gate_weight.T, up_weight.T, down_weight),
        query_weight,
        out_weight,
        jnp.concatenate([key_weight, value_weight], axis=1),
        vectors,
        parity,
    )
    own_lengths = lax.dynamic_slice_in_dim(lengths, chip * 2 + core, 1, axis=1)[:, 0]
    block_output, input_grad, grads = layer(blocks, inputs[:, 0], cotangent[:, 0], own_lengths)
    units = grads[:3].reshape(3, 3, 16, D)
    thin = grads[3]

    def mine(which, size):
        if size == 7:
            return lax.dynamic_slice_in_dim(thin, 16 * which + parity * 7, 7, axis=0)
        last = lax.dynamic_slice_in_dim(units[2, which], parity * 6, 6, axis=0)
        return jnp.concatenate([units[0, which], units[1, which], last])

    own_narrow = mine(2, 7)
    grad_vector = own_narrow[0, 2 * kv_width : 2 * kv_width + 23]
    owned = (
        mine(0, 7),
        own_narrow[:, :kv_width],
        own_narrow[:, kv_width : 2 * kv_width],
        mine(1, 7),
        mine(0, 38),
        mine(1, 38),
        mine(2, 38),
    )
    priors = (
        query_prior,
        key_prior,
        value_prior,
        out_prior,
        gate_prior.T,
        up_prior.T,
        down_prior,
    )
    masters = (
        query_weight,
        key_weight,
        value_weight,
        out_weight,
        gate_weight,
        up_weight,
        down_weight,
    )
    shapes = ((D, D), (D, kv_width), (D, kv_width), (D, D), (D, FF), (D, FF), (FF, D))
    lefts = (False, False, False, False, True, True, False)
    momenta = tuple((MOMENTUM * priors[k] + owned[k] for k in range(7)))

    def padded(value, count):
        return jnp.pad(value, ((0, count - value.shape[0]), (0, D - value.shape[1])))

    tall, short = muon(
        half(jnp.stack([padded(momenta[k], 48) for k in (4, 5, 6)])),
        half(jnp.stack([padded(momenta[k], 16) for k in (0, 3, 1, 2)])),
    )
    finals = (
        short[0, :7], short[2, :7, :128], short[3, :7, :128], short[1, :7], tall[0, :38], tall[1, :38],
        tall[2, :38],
    )
    updated = []
    kept = []
    for k in range(7):
        current = finals[k].astype(jnp.float32)
        factor = MUON_RATE * 0.2 * math.sqrt(max(shapes[k][0], shapes[k][1]))
        if lefts[k]:
            current = current.T
        updated.append(masters[k] * (1.0 - MUON_RATE * MUON_DECAY) - factor * current)
        kept.append(momenta[k].T if lefts[k] else momenta[k])
    vector_first = BETA_FIRST * first_prior + (1.0 - BETA_FIRST) * grad_vector
    vector_second = BETA_SECOND * second_prior + (1.0 - BETA_SECOND) * grad_vector * grad_vector
    first_hat = vector_first / (1.0 - BETA_FIRST**STEP)
    second_hat = vector_second / (1.0 - BETA_SECOND**STEP)
    vector_new = vectors * (1.0 - ADAM_RATE * ADAM_DECAY) - ADAM_RATE * first_hat / (
        jnp.sqrt(second_hat) + ADAM_EPSILON
    )
    return (
        block_output,
        input_grad,
        *kept,
        *updated,
        vector_first,
        vector_second,
        vector_new,
    )


def solution(mesh):
    placed = (
        P(None, ("dp", "narrow"), None, None),
        P(None, ("dp", "narrow"), None, None),
        P(),
        P(("dp", "narrow"), None),
        P(("dp", "narrow"), None),
        P(("dp", "narrow"), None),
        P(("dp", "narrow"), None),
        P(None, ("dp", "narrow")),
        P(None, ("dp", "narrow")),
        P(("dp", "narrow"), None),
        P(("dp", "narrow")),
        P(("dp", "narrow"), None),
        P(("dp", "narrow"), None),
        P(("dp", "narrow"), None),
        P(("dp", "narrow"), None),
        P(None, ("dp", "narrow")),
        P(None, ("dp", "narrow")),
        P(("dp", "narrow"), None),
        P(("dp", "narrow")),
        P(("dp", "narrow")),
    )
    return jax.shard_map(
        body,
        mesh=mesh,
        in_specs=placed,
        out_specs=(
            P(None, ("dp", "narrow"), None, None),
            P(None, ("dp", "narrow"), None, None),
            P(("dp", "narrow"), None),
            P(("dp", "narrow"), None),
            P(("dp", "narrow"), None),
            P(("dp", "narrow"), None),
            P(None, ("dp", "narrow")),
            P(None, ("dp", "narrow")),
            P(("dp", "narrow"), None),
            P(("dp", "narrow"), None),
            P(("dp", "narrow"), None),
            P(("dp", "narrow"), None),
            P(("dp", "narrow"), None),
            P(None, ("dp", "narrow")),
            P(None, ("dp", "narrow")),
            P(("dp", "narrow"), None),
            P(("dp", "narrow")),
            P(("dp", "narrow")),
            P(("dp", "narrow")),
        ),
        check_vma=False,
    )
```

```python
import math

import jax
import jax.numpy as jnp
import numpy as np
from jax import lax
from jax.experimental import pallas as pl
from jax.experimental.pallas import tpu as pltpu
from jax.sharding import PartitionSpec as P

D = 896
FF = 4864
HEADS = 14
KV_HEADS = 2
HEAD = 64
STEP = 10


NORM_EPSILON = 1e-06
ROPE_BASE = 1000000.0
MOMENTUM = 0.95
NEWTON_A = 3.4445
NEWTON_B = -4.775
NEWTON_C = 2.0315
MUON_RATE = 0.4
MUON_DECAY = 0.1
ADAM_RATE = 0.5
ADAM_DECAY = 0.01
BETA_FIRST = 0.9
BETA_SECOND = 0.999
ADAM_EPSILON = 1e-08
MASKED = -1e30


def product(left, right):
    return jnp.dot(left, right, preferred_element_type=jnp.float32)


def inner_rows(left, right):
    return lax.dot_general(
        left, right, (((0,), (0,)), ((), ())), preferred_element_type=jnp.float32
    )


def outer_cols(left, right):
    return lax.dot_general(
        left, right, (((1,), (1,)), ((), ())), preferred_element_type=jnp.float32
    )


def norm_back(grad, normed, scale):
    return scale * (grad - normed * jnp.mean(grad * normed, axis=-1, keepdims=True))


def half(value):
    return value.astype(jnp.bfloat16)


MESH = pl.DeviceIdType.MESH
TOKENS = 256
FULL = (0, 4)
BF16 = jnp.bfloat16
F32 = jnp.float32
CHUNK = 48
PARTS = (
    (0, 0, CHUNK, (2, 1, 0), False),
    (0, CHUNK, CHUNK, (1, 0, 2), False),
    (1, 0, CHUNK, (0, 2, 1), True),
    (2, 0, 16, (2, 1, 0), True),
    (2, 16, 16, (1, 0, 2), True),
    (2, 32, 16, (0, 2, 1), True),
)
WIDE = (0, 1, 2)
THIN = (3, 4, 5)


def my_coords():
    dp = lax.axis_index("dp")
    return (dp // 16, (dp // 4) % 4, dp % 4), lax.axis_index("narrow")


def device_of(coords, core):
    return (coords[0] * 16 + coords[1] * 4 + coords[2], core)


def shifted(coords, axis, by):
    out = list(coords)
    out[axis] = (coords[axis] + by) % 4
    return tuple(out)


def facing(coords):
    return (coords[0], coords[1], 3 - coords[2])


def greet(coords, core):
    barrier = pltpu.get_barrier_semaphore()
    for axis in range(3):
        for by in (1, 2, 3):
            pl.semaphore_signal(
                barrier, inc=1, device_id=device_of(shifted(coords, axis, by), core), device_id_type=MESH
            )
    pl.semaphore_signal(barrier, inc=1, device_id=device_of(coords, 1 - core), device_id_type=MESH)
    pl.semaphore_wait(barrier, 10)


def remote(src, dst, send_sem, recv_sem, device):
    return pltpu.make_async_remote_copy(
        src_ref=src,
        dst_ref=dst,
        send_sem=send_sem,
        recv_sem=recv_sem,
        device_id=device,
        device_id_type=MESH,
    )


def place_of(part, piece):
    spec, columns = piece
    _, first, rows, _, shared = PARTS[part]
    index = [pl.ds(*s) if isinstance(s, tuple) else s for s in spec[:2]]
    s = spec[2]
    if isinstance(s, tuple):
        index.append(pl.ds(s[0] // 2, s[1] // 2))
        index += [] if shared else [pl.ds(0, 2)]
    else:
        index.append(s // 2)
        index += [] if shared else [s % 2]
    columns = (0, D) if columns is None else columns
    return (*index, pl.ds(first, rows), pl.ds(*columns))


def shape_of(part, piece):
    return tuple(entry.size for entry in place_of(part, piece) if isinstance(entry, pl.Slice))


def halves(spec, axis):
    if axis is None:
        return [(spec, (0, 512)), (spec, (512, 384))]
    out = []
    for h in range(2):
        s = list(spec)
        s[axis] = (2 * h, 2)
        out.append((tuple(s), None))
    return out


class Plan:
    def __init__(self, part, stage, coords, axis, spec, split):
        self.coords, self.axis, self.spec, self.split = coords, axis, spec, split
        self.exchange = PARTS[part][4] and axis == 2
        self.direct = not self.exchange and stage == 0

    def whole(self, by):
        spec = list(self.spec)
        spec[self.axis] = (self.coords[self.axis] + by) % 4
        return (tuple(spec), None)

    def at(self, by):
        return shifted(self.coords, self.axis, by)

    def pieces(self, by):
        spec = list(self.spec)
        spec[self.axis] = (self.coords[self.axis] + by) % 4
        return halves(tuple(spec), self.split)

    def facing(self):
        return ((*self.spec[:2], 3 - self.coords[2]), None)

    def own(self):
        return (self.spec, None)


def plan_of(part, stage, coords):
    order = PARTS[part][3]
    spec = tuple(FULL if k in order[:stage] else coords[k] for k in range(3))
    return Plan(part, stage, coords, order[stage], spec, order[stage - 1] if stage else None)


class Gather:
    def __init__(self, arrays, coords, core, send_sems, recv_sems):
        self.arrays, self.coords, self.core = arrays, coords, core
        self.send_sems, self.recv_sems = send_sems, recv_sems

    def copy(self, part, phase, slot, piece, coords):
        array, prefix = self.arrays[PARTS[part][0]]
        ref = array.at[(*prefix, *place_of(part, piece))]
        sems = (self.send_sems.at[part, phase, slot], self.recv_sems.at[part, phase, slot])
        return remote(ref, ref, *sems, device_of(coords, self.core))

    def send(self, *args):
        self.copy(*args).start()

    def neighbours(self, plan):
        return shifted(self.coords, plan.axis, 1), shifted(self.coords, plan.axis, 3)

    def start(self, parts, phase):
        for part in parts:
            plan = plan_of(part, phase, self.coords)
            if plan.exchange:
                self.send(part, phase, 0, plan.own(), facing(self.coords))
                continue
            if plan.direct:
                for by in (1, 3, 2):
                    self.send(part, phase, by, plan.own(), plan.at(by))
                continue
            right, left = self.neighbours(plan)
            first, second = plan.pieces(0)
            self.send(part, phase, 0, first, right)
            self.send(part, phase, 1, second, left)
            self.send(part, phase, 2, second, right)
            self.send(part, phase, 3, first, left)

    def forward(self, parts, phase):
        for part in parts:
            plan = plan_of(part, phase, self.coords)
            if plan.exchange or plan.direct:
                continue
            right, left = self.neighbours(plan)
            piece = plan.pieces(3)[0]
            self.copy(part, phase, 0, piece, right).wait_recv()
            self.send(part, phase, 4, piece, right)
            piece = plan.pieces(1)[1]
            self.copy(part, phase, 1, piece, left).wait_recv()
            self.send(part, phase, 5, piece, left)

    def near(self, parts, phase):
        for part in parts:
            plan = plan_of(part, phase, self.coords)
            if plan.exchange:
                self.copy(part, phase, 0, plan.facing(), facing(self.coords)).wait_recv()
                continue
            if plan.direct:
                for by in (1, 3):
                    self.copy(part, phase, by, plan.whole(4 - by), plan.at(by)).wait_recv()
                continue
            right, left = self.neighbours(plan)
            self.copy(part, phase, 2, plan.pieces(3)[1], right).wait_recv()
            self.copy(part, phase, 3, plan.pieces(1)[0], left).wait_recv()

    def far(self, parts, phase):
        for part in parts:
            plan = plan_of(part, phase, self.coords)
            if plan.exchange:
                continue
            if plan.direct:
                self.copy(part, phase, 2, plan.whole(2), plan.at(2)).wait_recv()
                continue
            right, left = self.neighbours(plan)
            self.copy(part, phase, 4, plan.pieces(2)[0], right).wait_recv()
            self.copy(part, phase, 5, plan.pieces(2)[1], left).wait_recv()

    def finish(self, parts, phase):
        self.near(parts, phase)
        self.far(parts, phase)

    def drain(self):
        for part in range(6):
            for phase in range(3):
                plan = plan_of(part, phase, self.coords)
                if plan.exchange:
                    self.copy(part, phase, 0, plan.own(), facing(self.coords)).wait_send()
                    continue
                if plan.direct:
                    for by in (1, 3, 2):
                        self.copy(part, phase, by, plan.own(), plan.at(by)).wait_send()
                    continue
                right, _ = self.neighbours(plan)
                for slot, which in enumerate((0, 1, 1, 0, 0, 1)):
                    self.copy(part, phase, slot, plan.pieces(0)[which], right).wait_send()


def each_block(shape, body):
    lead = shape[:-2]
    count = math.prod(lead)
    if count == 1:
        body((0,) * len(lead))
        return

    def step(k, carry):
        index = []
        for n in reversed(lead):
            index.append(k % n)
            k = k // n
        body(tuple(reversed(index)))
        return carry

    lax.fori_loop(0, count, step, 0)


class Scatter:
    def __init__(self, arrays, coords, core, buffers, send_sems, recv_sems, done):
        self.arrays, self.coords, self.core, self.done = arrays, coords, core, done
        self.buffers, self.send_sems, self.recv_sems = buffers, send_sems, recv_sems

    def copy(self, part, phase, slot, piece, coords):
        array, prefix = self.arrays[PARTS[part][0]]
        ref = array.at[(*prefix, *place_of(part, piece))]
        sems = (self.send_sems.at[part, phase, slot], self.recv_sems.at[part, phase, slot])
        return remote(ref, self.buffers[part, phase][slot], *sems, device_of(coords, self.core))

    def send(self, *args):
        if args[:3] not in self.done:
            self.copy(*args).start()

    def arrive(self, *args):
        if args[:3] not in self.done:
            self.copy(*args).wait_recv()

    def add(self, part, phase, piece, *slots):
        sources = [self.buffers[part, phase][slot] for slot in slots]
        base = place_of(part, piece)
        array, prefix = self.arrays[PARTS[part][0]]

        def one(index):
            spot, position = [], 0
            for entry in base[:-2]:
                if isinstance(entry, pl.Slice):
                    spot.append(entry.start + index[position])
                    position += 1
                else:
                    spot.append(entry)
            spot = (*prefix, *spot, *base[-2:])
            value = array[spot].astype(F32)
            for source in sources:
                value = value + source[(*index, slice(None), slice(None))].astype(F32)
            array[spot] = half(value)

        each_block(shape_of(part, piece), one)

    def neighbours(self, plan):
        return shifted(self.coords, plan.axis, 1), shifted(self.coords, plan.axis, 3)

    def start_far(self, parts, phase):
        for part in parts:
            plan = plan_of(part, phase, self.coords)
            if plan.exchange or plan.direct:
                continue
            right, left = self.neighbours(plan)
            self.send(part, phase, 0, plan.pieces(2)[0], right)
            self.send(part, phase, 1, plan.pieces(2)[1], left)

    def start_near(self, parts, phase):
        for part in parts:
            plan = plan_of(part, phase, self.coords)
            if plan.exchange:
                self.send(part, phase, 0, plan.facing(), facing(self.coords))
                continue
            if plan.direct:
                for by in (1, 3, 2):
                    self.send(part, phase, by, plan.whole(by), plan.at(by))
                continue
            right, left = self.neighbours(plan)
            self.send(part, phase, 2, plan.pieces(1)[1], right)
            self.send(part, phase, 3, plan.pieces(3)[0], left)

    def start(self, parts, phase):
        self.start_far(parts, phase)
        self.start_near(parts, phase)

    def forward(self, parts, phase):
        for part in parts:
            plan = plan_of(part, phase, self.coords)
            if plan.exchange or plan.direct:
                continue
            right, left = self.neighbours(plan)
            self.arrive(part, phase, 0, plan.pieces(2)[0], right)
            self.add(part, phase, plan.pieces(1)[0], 0)
            self.send(part, phase, 4, plan.pieces(1)[0], right)
            self.arrive(part, phase, 1, plan.pieces(2)[1], left)
            self.add(part, phase, plan.pieces(3)[1], 1)
            self.send(part, phase, 5, plan.pieces(3)[1], left)

    def finish(self, parts, phase):
        for part in parts:
            plan = plan_of(part, phase, self.coords)
            if plan.exchange:
                self.arrive(part, phase, 0, plan.facing(), facing(self.coords))
                self.add(part, phase, plan.own(), 0)
                continue
            if plan.direct:
                for by in (1, 3, 2):
                    self.arrive(part, phase, by, plan.whole(by), plan.at(by))
                self.add(part, phase, plan.own(), 1, 3, 2)
                continue
            right, left = self.neighbours(plan)
            self.arrive(part, phase, 3, plan.pieces(3)[0], left)
            self.arrive(part, phase, 4, plan.pieces(1)[0], right)
            self.add(part, phase, plan.pieces(0)[0], 4, 3)
            self.arrive(part, phase, 2, plan.pieces(1)[1], right)
            self.arrive(part, phase, 5, plan.pieces(3)[1], left)
            self.add(part, phase, plan.pieces(0)[1], 2, 5)

    def drain(self):
        for part in range(6):
            for phase in range(3):
                plan = plan_of(part, phase, self.coords)
                if plan.exchange:
                    self.copy(part, phase, 0, plan.own(), facing(self.coords)).wait_send()
                    continue
                if plan.direct:
                    for by in (1, 3, 2):
                        self.copy(part, phase, by, plan.whole(by), plan.at(by)).wait_send()
                    continue
                right, _ = self.neighbours(plan)
                for slot, which in enumerate((0, 1, 1, 0, 0, 1)):
                    if (part, phase, slot) in self.done:
                        continue
                    self.copy(part, phase, slot, plan.pieces(0)[which], right).wait_send()


EARLY = tuple((part, 2, slot) for part in WIDE for slot in (2, 3))


def scatter_buffer_shapes():
    out = []
    for part in range(6):
        for phase in range(3):
            plan = plan_of(part, phase, (0, 0, 0))
            if plan.exchange:
                shapes = [shape_of(part, plan.own())]
            elif plan.direct:
                shapes = [None] + [shape_of(part, plan.own())] * 3
            else:
                first, second = (shape_of(part, piece) for piece in plan.pieces(0))
                shapes = [first, second, second, first, first, second]
            out.append(((part, phase), shapes))
    return out


SCALE = HEAD ** (-0.5)


def turn(values, sign):
    lane = lax.broadcasted_iota(jnp.int32, values.shape, 1)
    ahead = pltpu.roll(values, 96, 1)
    behind = pltpu.roll(values, 32, 1)
    return jnp.where(lane & 32 == 0, sign * ahead, -sign * behind)


def tiles_of(values):
    return [values[:, 128 * t : 128 * t + 128] for t in range(values.shape[1] // 128)]


def rotated(values, cosine, sine):
    return jnp.concatenate(
        [tile * cosine + turn(tile, -1.0) * sine for tile in tiles_of(values)], axis=1
    )


def rotated_back(values, cosine, sine):
    return jnp.concatenate(
        [tile * cosine + turn(tile * sine, 1.0) for tile in tiles_of(values)], axis=1
    )


def low_lanes(shape):
    return lax.broadcasted_iota(jnp.int32, shape, 1) < HEAD


def paired(both):
    swapped = pltpu.roll(both, 64, 1)
    low = low_lanes(both.shape)
    even = [half(jnp.where(low, v, 0.0)) for v in (both, swapped)]
    odd = [half(jnp.where(low, 0.0, v)) for v in (swapped, both)]
    kinds = [jnp.concatenate([even[a], odd[b]]) for a, b in ((0, 0), (0, 1), (1, 1))]
    return [kinds[0]] * 3 + [kinds[1]] + [kinds[2]] * 3


def gathered_place():
    row = lax.broadcasted_iota(jnp.int32, (1024, D), 0)
    feature = lax.broadcasted_iota(jnp.int32, (1024, D), 1)
    slot = row & 15
    odd = (slot >= 7).astype(jnp.int32)
    device = (((row >> 4) & 31) * 2 + odd) * 2 + (row >> 9)
    source = jnp.where(slot < 14, 7 * device + slot - 7 * odd, -1)
    return half((source == feature).astype(jnp.float32))


def vector_maps():
    device = lax.broadcasted_iota(jnp.int32, (128, 1024), 0)
    row = lax.broadcasted_iota(jnp.int32, (128, 1024), 1)
    target = (device & 1) * 512 + (device >> 2) * 16 + ((device >> 1) & 1) * 7
    pick = half((row == target).astype(jnp.float32))
    start = lax.broadcasted_iota(jnp.int32, (128, 2944), 0) * 23
    entry = lax.broadcasted_iota(jnp.int32, (128, 2944), 1)
    owner = half(((entry >= start) & (entry < start + 23)).astype(jnp.float32))
    return pick, owner


def slot_mask(slots):
    return lax.broadcasted_iota(jnp.int32, (128, 2944), 0) == slots


def attention_forward(
    x_ref, rest_ref, len_ref, cos_ref, sin_ref, slot_ref,
    middle_ref, h1p_ref, q_ref, k_ref, v_ref, mixed_ref, probs_ref, vector_ref,
):
    place = gathered_place()
    pick, owner = vector_maps()
    stored = rest_ref[:, :, :, :, 32:48, 256:384].reshape(1024, 128)
    by_device = half(product(pick, stored))
    spread = inner_rows(by_device, owner)
    vector = jnp.sum(jnp.where(slot_mask(slot_ref[...]), spread, 0.0), axis=0, keepdims=True)
    vector_ref[...] = vector
    first_gain, second_gain = vector[:, :D], vector[:, D : 2 * D]
    query_bias, narrow_bias = vector[:, 2 * D : 3 * D], vector[:, 3 * D :]
    cosine, sine = cos_ref[...], sin_ref[...]
    inputs = x_ref[...].astype(jnp.float32)
    first_scale = lax.rsqrt(jnp.mean(inputs * inputs, axis=-1, keepdims=True) + NORM_EPSILON)
    normed = half(inputs * first_scale * first_gain)
    placed = half(outer_cols(normed, place))
    h1p_ref[...] = placed
    queries = product(placed, rest_ref[:, :, :, :, 0:16, :].reshape(1024, D)) + query_bias
    narrow = product(placed, rest_ref[:, :, :, :, 32:48, 0:256].reshape(1024, 256)) + narrow_bias
    q_ref[...] = half(rotated(queries, cosine, sine))
    keys = rotated(narrow[:, 0:128], cosine, sine)
    k_ref[...] = half(keys)
    values = narrow[:, 128:256]
    v_ref[...] = half(values)
    position = lax.broadcasted_iota(jnp.int32, (128, 256), 0)
    other = lax.broadcasted_iota(jnp.int32, (128, 256), 1) & 127
    causal = other <= position
    rows = []
    for b in range(2):
        here = slice(128 * b, 128 * b + 128)
        length = len_ref[b : b + 1, :]
        allowed = causal & (other < jnp.concatenate([length, length], axis=1))
        key_tiles = paired(keys[here])
        value_tiles = paired(values[here])
        tiles = []
        for t in range(7):
            scores = outer_cols(q_ref[here, 128 * t : 128 * t + 128], key_tiles[t])
            scores = jnp.where(allowed, scores * SCALE, MASKED)
            parts = []
            for part in tiles_of(scores):
                shifted = jnp.exp(part - jnp.max(part, axis=-1, keepdims=True))
                parts.append(shifted / jnp.sum(shifted, axis=-1, keepdims=True))
            probs = jnp.concatenate(parts, axis=1)
            probs_ref[b, t] = probs
            tiles.append(half(product(half(probs), value_tiles[t])))
        rows.append(jnp.concatenate(tiles, axis=1))
    mixed = half(outer_cols(jnp.concatenate(rows), place))
    mixed_ref[...] = mixed
    middle = inputs + product(mixed, rest_ref[:, :, :, :, 16:32, :].reshape(1024, D))
    middle_ref[...] = middle
    second_scale = lax.rsqrt(jnp.mean(middle * middle, axis=-1, keepdims=True) + NORM_EPSILON)
    return half(middle * second_scale * second_gain)


def mlp_tile(weights, h, e, out_acc, back_acc):
    lead = weights.shape[:-2]
    units = 16 * math.prod(lead)
    gate_w, up_w, down_w = (
        weights[..., 16 * k : 16 * k + 16, :].reshape(units, D) for k in range(3)
    )
    gate = outer_cols(h, gate_w)
    up = outer_cols(h, up_w)
    sigma = jax.nn.sigmoid(gate)
    silu = gate * sigma
    hidden = half(silu * up)
    grad_hidden = outer_cols(e, down_w)
    out_acc[...] += product(hidden, down_w).reshape(2, TOKENS, D)
    grad_gate = half(grad_hidden * up * sigma * (1.0 + gate * (1.0 - sigma)))
    grad_up = half(grad_hidden * silu)
    back_acc[...] += (product(grad_gate, gate_w) + product(grad_up, up_w)).reshape(2, TOKENS, D)
    grads = (inner_rows(grad_gate, h), inner_rows(grad_up, h), inner_rows(hidden, e))
    return [half(grad).reshape(*lead, 16, D) for grad in grads]


KEPT = 17


def gather_kernel(
    gate_ref, up_ref, down_ref, query_ref, out_ref, narrow_ref,
    x_ref, cot_ref, len_ref, cos_ref, sin_ref, slot_ref, *refs,
):
    coords, core = my_coords()
    z, y, x = coords
    pair, odd = x // 2, x % 2
    results, (grad_wide_ref, grad_shared_ref, rest_ref) = refs[:KEPT], refs[KEPT : KEPT + 3]
    held = refs[KEPT + 3 : 2 * KEPT + 3]
    (
        wide, shared, rest, stage0, stage1, stage2, h_all, e_all, out_acc, back_acc, parcel, arrived,
        tail, tail_own, tail_wide,
        local_sems, send_sems, recv_sems, twin_sems, store_sems, early_sems, kept_sems,
    ) = refs[2 * KEPT + 3 :]
    (
        middle_ref, e_ref, h1p_ref, q_ref, k_ref, v_ref, mixed_ref, probs_ref, vector_ref,
        output_ref, dh2_ref,
    ) = held[:11]
    early = held[11:]

    def keep(first, last):
        return [
            pltpu.make_async_copy(held[n], results[n], kept_sems.at[n]) for n in range(first, last)
        ]

    units = (gate_ref, up_ref, down_ref)
    for n, ref in enumerate(units):
        for k in range(2):
            wide[z, y, pair, odd, CHUNK * k + 16 * n : CHUNK * k + 16 * n + 16] = half(
                ref[16 * k : 16 * k + 16]
            )
    tail_wide[...] = jnp.zeros_like(tail_wide)
    for parity in range(2):

        @pl.when(odd == parity)
        def _():
            for n, ref in enumerate(units):
                start = 16 * n + 6 * parity
                tail_wide[start : start + 6] = ref[32:38]
            for n, ref in enumerate((query_ref, out_ref)):
                start = CHUNK + 16 * n + 7 * parity
                tail_wide[start : start + 7] = ref[...]
            start = CHUNK + 32 + 7 * parity
            tail_wide[start : start + 7, 0:384] = narrow_ref[...]

    tail_own[...] = half(tail_wide[...])
    greet(coords, core)
    twin = device_of(coords, 1 - core)

    def to_twin(src, dst, slot):
        return remote(src, dst, twin_sems.at[0, slot], twin_sems.at[1, slot], twin)

    gather = Gather(((wide, ()), (shared, ()), (rest, (core,))), coords, core, send_sems, recv_sems)
    partner = device_of((z, y, x + 1 - 2 * odd), core)
    tail_copy = remote(tail_own, tail, twin_sems.at[0, 4], twin_sems.at[1, 4], partner)
    tail_copy.start()
    gather.start((0, 1), 0)
    token = lax.broadcasted_iota(jnp.int32, (128, 1), 0)
    live = jnp.concatenate([(token < len_ref[b : b + 1, 0:1]).astype(F32) for b in range(2)])
    e_ref[...] = half(cot_ref[...].astype(F32) * live)
    e_all[core] = e_ref[...]
    e_copy = to_twin(e_ref, e_all.at[core], 0)
    e_copy.start()
    tail_copy.wait()
    both = half(tail_wide[...] + tail[...].astype(F32))
    shared[z, y, pair] = both[:CHUNK]
    rest[core, z, y, pair] = both[CHUNK:]
    gather.start(THIN, 0)
    gather.start((2,), 0)
    gather.forward(THIN, 0)
    gather.finish(THIN, 0)
    gather.start(THIN, 1)
    gather.forward(WIDE, 0)
    gather.forward(THIN, 1)
    gather.finish(THIN, 1)
    gather.start(THIN, 2)
    gather.finish(WIDE, 0)
    gather.start(WIDE, 1)
    gather.forward(THIN, 2)
    gather.finish(THIN, 2)
    rest_copy = to_twin(rest.at[core], rest.at[core], 1)
    rest_copy.start()
    gather.forward(WIDE, 1)
    gather.finish(WIDE, 1)
    gather.start(WIDE, 2)
    rest_copy.wait()
    rest_store = pltpu.make_async_copy(rest, rest_ref, local_sems.at[0])
    rest_store.start()
    h_all[core] = attention_forward(
        x_ref, rest, len_ref, cos_ref, sin_ref, slot_ref,
        middle_ref, h1p_ref, q_ref, k_ref, v_ref, mixed_ref, probs_ref, vector_ref,
    )
    h_copy = to_twin(h_all.at[core], h_all.at[core], 2)
    h_copy.start()
    for copy in keep(0, 9):
        copy.start()
    out_acc[...] = jnp.zeros_like(out_acc)
    back_acc[...] = jnp.zeros_like(back_acc)
    e_copy.wait()
    h_copy.wait()
    stages = (stage0, stage1, stage2)

    def early_copy(t, slot):
        axis = PARTS[t][3][2]
        which = 3 - slot
        place = [slice(None)] * (len(stages[t].shape) - 1)
        place[1 if t == 2 else 0] = pl.ds(which, 1) if t == 2 else pl.ds(2 * which, 2)
        return remote(
            stages[t].at[(slot - 1) % 2].at[tuple(place)],
            early[2 * t + slot - 2],
            early_sems.at[0, t, slot - 2],
            early_sems.at[1, t, slot - 2],
            device_of(shifted(coords, axis, 1 if slot == 2 else 3), core),
        )

    def tile_places(j):
        return (
            (wide, grad_wide_ref, (j, slice(None), slice(None), slice(None), pl.ds(0, CHUNK))),
            (wide, grad_wide_ref, (slice(None), slice(None), j // 2, j % 2, pl.ds(CHUNK, CHUNK))),
            (shared, grad_shared_ref, (slice(None), j, slice(None), pl.ds(0, CHUNK))),
        )

    def step(k, carry):
        @pl.when(k == 1)
        def _():
            gather.near(WIDE, 2)

        @pl.when(k == 3)
        def _():
            gather.far(WIDE, 2)

        offset = jnp.where(k < 2, k, 5 - k)
        h = h_all[...].reshape(2 * TOKENS, D)
        e = e_all[...].reshape(2 * TOKENS, D)
        for t, axis in enumerate((0, 2, 1)):
            j = (coords[axis] + offset) % 4
            source, target, index = tile_places(j)[t]
            grads = mlp_tile(source[(*index, slice(None))], h, e, out_acc, back_acc)
            copy = pltpu.make_async_copy(
                stages[t].at[k % 2], target.at[(*index, slice(None))], store_sems.at[t, k % 2]
            )

            @pl.when(k > 1)
            def _():
                copy.wait()

            @pl.when(k == 3)
            def _():
                early_copy(t, 2).wait_send()

            for place, grad in enumerate(grads):
                stages[t][k % 2, ..., 16 * place : 16 * place + 16, :] = grad
            copy.start()

            @pl.when(k == 1)
            def _():
                early_copy(t, 2).start()

            @pl.when(k == 2)
            def _():
                early_copy(t, 3).start()

        @pl.when(k == 0)
        def _():
            gather.forward(WIDE, 2)

        return carry

    lax.fori_loop(0, 4, step, 0)
    parcel[0] = half(out_acc[1 - core])
    parcel[1] = half(back_acc[1 - core])
    parcel_copy = to_twin(parcel, arrived, 3)
    parcel_copy.start()
    parcel_copy.wait()
    output_ref[...] = half(
        (middle_ref[...] + (out_acc[core] + arrived[0].astype(F32))) * live
    )
    dh2_ref[...] = back_acc[core] + arrived[1].astype(F32)
    for copy in keep(9, 11):
        copy.start()
    for t in range(3):
        _, target, index = tile_places(0)[t]
        for which in range(2):
            pltpu.make_async_copy(
                stages[t].at[which], target.at[(*index, slice(None))], store_sems.at[t, which]
            ).wait()
        early_copy(t, 3).wait_send()
        early_copy(t, 2).wait_recv()
        early_copy(t, 3).wait_recv()
        for copy in keep(11 + 2 * t, 13 + 2 * t):
            copy.start()
    rest_store.wait()
    for copy in keep(0, KEPT):
        copy.wait()
    gather.drain()


def attention_backward(
    between, x_ref, e_ref, rest_ref, cos_ref, sin_ref, slot_ref,
    middle_ref, h1p_ref, q_ref, k_ref, v_ref, mixed_ref, probs_ref, vector_ref, dh2_ref,
    input_grad_ref, grad_ref,
):
    place = gathered_place()
    pick, owner = vector_maps()
    vector = vector_ref[...]
    first_gain, second_gain = vector[:, :D], vector[:, D : 2 * D]
    cosine, sine = cos_ref[...], sin_ref[...]
    middle = middle_ref[...]
    second_scale = lax.rsqrt(jnp.mean(middle * middle, axis=-1, keepdims=True) + NORM_EPSILON)
    second_normed = middle * second_scale
    dh2 = dh2_ref[...]
    second_gain_grad = jnp.sum(dh2 * second_normed, axis=0, keepdims=True)
    grad_middle = e_ref[...].astype(jnp.float32) + norm_back(
        dh2 * second_gain, second_normed, second_scale
    )
    branch = half(grad_middle)
    wide = rest_ref[:, :, :, :, 16:32, :].reshape(1024, D)
    grad_ref[:, :, :, :, 16:32, :] = half(inner_rows(mixed_ref[...], branch)).reshape(2, 4, 4, 2, 16, D)
    grad_mixed = half(product(half(outer_cols(branch, wide)), place))
    low = low_lanes((128, 128))
    query_rows, key_rows, value_rows = [], [], []
    for b in range(2):
        here = slice(128 * b, 128 * b + 128)
        key_tiles = paired(k_ref[here, :].astype(jnp.float32))
        value_tiles = paired(v_ref[here, :].astype(jnp.float32))
        tiles = []
        sums = [[jnp.zeros((128, 128), jnp.float32) for _ in range(4)] for _ in range(2)]
        for t in range(7):
            head = grad_mixed[here, 128 * t : 128 * t + 128]
            grad_probs = outer_cols(head, value_tiles[t])
            probs = probs_ref[b, t]
            parts = []
            for p, g in zip(tiles_of(probs), tiles_of(grad_probs)):
                parts.append(half(p * (g - jnp.sum(p * g, axis=-1, keepdims=True))))
            grad_scores = jnp.concatenate(parts, axis=1)
            tiles.append(product(grad_scores, key_tiles[t]) * SCALE)
            for which, (left, right) in enumerate(
                ((grad_scores, q_ref[here, 128 * t : 128 * t + 128]), (half(probs), head))
            ):
                both = inner_rows(left, right)
                even, odd = (2 * t) // 7, (2 * t + 1) // 7
                sums[which][even] += both[0:128]
                sums[which][2 + odd] += both[128:256]
        query_rows.append(jnp.concatenate(tiles, axis=1))
        joined = []
        for which in range(2):
            even0, even1, odd0, odd1 = sums[which]
            joined.append(
                jnp.where(low, even0 + pltpu.roll(odd0, 64, 1), odd1 + pltpu.roll(even1, 64, 1))
            )
        key_rows.append(joined[0] * SCALE)
        value_rows.append(joined[1])
    between()
    grad_query = half(rotated_back(jnp.concatenate(query_rows), cosine, sine))
    grad_key = half(rotated_back(jnp.concatenate(key_rows), cosine, sine))
    grad_narrow = jnp.concatenate([grad_key, half(jnp.concatenate(value_rows))], axis=1)
    placed = h1p_ref[...]
    grad_ref[:, :, :, :, 0:16, :] = half(inner_rows(placed, grad_query)).reshape(2, 4, 4, 2, 16, D)
    grad_ref[:, :, :, :, 32:48, 0:256] = half(inner_rows(placed, grad_narrow)).reshape(2, 4, 4, 2, 16, 256)
    bias_grad = jnp.sum(
        jnp.concatenate([grad_query, grad_narrow], axis=1).astype(jnp.float32), axis=0, keepdims=True
    )
    grad_placed = outer_cols(grad_query, rest_ref[:, :, :, :, 0:16, :].reshape(1024, D)) + outer_cols(
        grad_narrow, rest_ref[:, :, :, :, 32:48, 0:256].reshape(1024, 256)
    )
    high = half(grad_placed)
    remainder = half(grad_placed - high.astype(jnp.float32))
    grad_normed = product(high, place) + product(remainder, place)
    inputs = x_ref[...].astype(jnp.float32)
    first_scale = lax.rsqrt(jnp.mean(inputs * inputs, axis=-1, keepdims=True) + NORM_EPSILON)
    first_normed = inputs * first_scale
    first_gain_grad = jnp.sum(grad_normed * first_normed, axis=0, keepdims=True)
    input_grad_ref[...] = half(
        grad_middle + norm_back(grad_normed * first_gain, first_normed, first_scale)
    )
    vector_grad = jnp.concatenate([first_gain_grad, second_gain_grad, bias_grad], axis=1)
    spread = half(jnp.where(slot_mask(slot_ref[...]), vector_grad, 0.0))
    by_device = half(outer_cols(owner, spread))
    stored = half(inner_rows(pick, by_device))
    grad_ref[:, :, :, :, 32:48, 256:384] = stored.reshape(2, 4, 4, 2, 16, 128)
    grad_ref[:, :, :, :, 32:48, 384:] = jnp.zeros((2, 4, 4, 2, 16, D - 384), jnp.bfloat16)


LOADED = ("x", "e", "rest", "middle", "h1p", "q", "k", "v", "mixed", "probs", "vector", "dh2")


def scatter_kernel(
    cos_ref, sin_ref, slot_ref, grad_wide_ref, grad_shared_ref, *refs,
):
    coords, core = my_coords()
    z, y, x = coords
    pair, odd = x // 2, x % 2
    count = len(LOADED) + len(EARLY)
    sources, (input_grad_ref, out_ref) = refs[:count], refs[count : count + 2]
    held = refs[count + 2 : 2 * count + 2]
    (
        wide, shared, thin, joined, mine, theirs,
        load_sems, send_sems, recv_sems, twin_sems, pair_sems, held_sems,
    ) = refs[2 * count + 2 : 2 * count + 14]
    buffers = refs[2 * count + 14 :]
    (
        x_ref, e_ref, rest_ref, middle_ref, h1p_ref, q_ref, k_ref, v_ref, mixed_ref, probs_ref,
        vector_ref, dh2_ref,
    ) = held[: len(LOADED)]
    fetches = [
        pltpu.make_async_copy(sources[n], held[n], held_sems.at[n]) for n in range(count)
    ]
    named, position = {}, 0
    early = dict(zip(EARLY, held[len(LOADED) :]))
    for key, shapes in scatter_buffer_shapes():
        named[key] = []
        for slot in range(len(shapes)):
            if (*key, slot) in early:
                named[key].append(early[(*key, slot)])
            elif shapes[slot] is None:
                named[key].append(None)
            else:
                named[key].append(buffers[position])
                position += 1
    scatter = Scatter(((wide, ()), (shared, ()), (thin, (core,))), coords, core, named, send_sems, recv_sems, EARLY)

    def load(part, by):
        spec = [FULL] * 3
        axis = PARTS[part][3][2]
        spec[axis] = (coords[axis] + by) % 4
        place = place_of(part, (tuple(spec), None))
        source = (grad_wide_ref, grad_shared_ref)[PARTS[part][0]]
        target = (wide, shared)[PARTS[part][0]]
        return pltpu.make_async_copy(source.at[place], target.at[place], load_sems.at[part, by])

    for by in (2, 1, 3, 0):
        for part in WIDE:
            load(part, by).start()
    for copy in fetches:
        copy.start()
    greet(coords, core)

    for part in WIDE:
        load(part, 2).wait()
        scatter.start_far((part,), 2)
    for part in WIDE:
        load(part, 1).wait()
        load(part, 3).wait()

    def between():
        scatter.forward(WIDE, 2)

    for copy in fetches:
        copy.wait()
    attention_backward(
        between, x_ref, e_ref, rest_ref, cos_ref, sin_ref, slot_ref,
        middle_ref, h1p_ref, q_ref, k_ref, v_ref, mixed_ref, probs_ref, vector_ref, dh2_ref,
        input_grad_ref, thin,
    )
    twin_copy = remote(
        thin.at[1 - core], joined, twin_sems.at[0], twin_sems.at[1], device_of(coords, 1 - core)
    )
    twin_copy.start()
    for part in WIDE:
        load(part, 0).wait()
    twin_copy.wait()

    def join(index):
        thin[(core, *index)] = half(thin[(core, *index)].astype(F32) + joined[index].astype(F32))

    each_block((4, 4, 2, CHUNK, D), join)
    scatter.start(THIN, 2)
    for part in WIDE:
        scatter.finish((part,), 2)
        scatter.start((part,), 1)
    scatter.forward(THIN, 2)
    scatter.finish(THIN, 2)
    scatter.start(THIN, 1)
    scatter.forward(WIDE, 1)
    scatter.forward(THIN, 1)
    for part in WIDE:
        scatter.finish((part,), 1)
        scatter.start((part,), 0)
    scatter.finish(THIN, 1)
    scatter.start(THIN, 0)
    scatter.forward(WIDE, 0)
    scatter.forward(THIN, 0)
    scatter.finish(WIDE, 0)
    scatter.finish(THIN, 0)
    mine[0] = shared[z, y, pair]
    mine[1] = thin[core, z, y, pair]
    partner = device_of((z, y, x + 1 - 2 * odd), core)
    pair_copy = remote(mine, theirs, pair_sems.at[0], pair_sems.at[1], partner)
    pair_copy.start()
    pair_copy.wait()
    out_ref[0] = wide[z, y, pair, odd, 0:CHUNK].astype(F32)
    out_ref[1] = wide[z, y, pair, odd, CHUNK : 2 * CHUNK].astype(F32)
    out_ref[2] = mine[0].astype(F32) + theirs[0].astype(F32)
    out_ref[3] = mine[1].astype(F32) + theirs[1].astype(F32)
    scatter.drain()


def layer(weights, tokens, cotangent, lengths):
    vmem = pl.BlockSpec(memory_space=pltpu.VMEM)
    anywhere = pl.BlockSpec(memory_space=pl.ANY)
    x = tokens.reshape(TOKENS, D)
    freqs = ROPE_BASE ** (-np.arange(HEAD // 2) * 2.0 / HEAD)
    angles = np.tile(np.arange(128)[:, None] * freqs[None, :], (2, 4))
    tables = (
        np.cos(angles).astype(np.float32),
        np.sin(angles).astype(np.float32),
        (np.arange(2944, dtype=np.int32) % 23)[None],
    )
    buffers = dict(scatter_buffer_shapes())
    kept = [
        ((TOKENS, D), F32),
        ((TOKENS, D), BF16),
        ((TOKENS, 1024), BF16),
        ((TOKENS, D), BF16),
        ((TOKENS, 128), BF16),
        ((TOKENS, 128), BF16),
        ((TOKENS, 1024), BF16),
        ((2, 7, 128, 256), F32),
        ((1, 2944), F32),
        ((TOKENS, D), BF16),
        ((TOKENS, D), F32),
    ] + [(buffers[part, stage][slot], BF16) for part, stage, slot in EARLY]
    large = [
        ((4, 4, 2, 2, 2 * CHUNK, D), BF16),
        ((4, 4, 2, CHUNK, D), BF16),
        ((2, 4, 4, 2, CHUNK, D), BF16),
    ]

    def shapes(pairs):
        return [jax.ShapeDtypeStruct(shape, dtype) for shape, dtype in pairs]

    def scratch(pairs):
        return [pltpu.VMEM(shape, dtype) for shape, dtype in pairs]

    results = pl.pallas_call(
        gather_kernel,
        out_shape=shapes(kept + large),
        in_specs=[vmem] * 12,
        out_specs=[anywhere] * (KEPT + 3),
        scratch_shapes=scratch(
            kept
            + large
            + [
                ((2, 4, 2, 2, CHUNK, D), BF16),
                ((2, 4, 4, CHUNK, D), BF16),
                ((2, 4, 2, CHUNK, D), BF16),
                ((2, TOKENS, D), BF16),
                ((2, TOKENS, D), BF16),
                ((2, TOKENS, D), F32),
                ((2, TOKENS, D), F32),
                ((2, TOKENS, D), BF16),
                ((2, TOKENS, D), BF16),
                ((2 * CHUNK, D), BF16),
                ((2 * CHUNK, D), BF16),
                ((2 * CHUNK, D), F32),
            ]
        )
        + [
            pltpu.SemaphoreType.DMA((3,)),
            pltpu.SemaphoreType.DMA((6, 3, 6)),
            pltpu.SemaphoreType.DMA((6, 3, 6)),
            pltpu.SemaphoreType.DMA((2, 5)),
            pltpu.SemaphoreType.DMA((3, 2)),
            pltpu.SemaphoreType.DMA((2, 3, 2)),
            pltpu.SemaphoreType.DMA((KEPT,)),
        ],
        compiler_params=pltpu.CompilerParams(
            collective_id=0, has_side_effects=True, vmem_limit_bytes=61 * 2**20
        ),
    )(*weights, x, cotangent.reshape(TOKENS, D), lengths, *tables)
    middle, e, h1p, q, k, v, mixed, probs, vector, output, dh2 = results[:11]
    early = results[11:KEPT]
    grad_wide, grad_shared, rest = results[KEPT:]
    loaded = dict(
        x=x, e=e, rest=rest, middle=middle, h1p=h1p, q=q, k=k, v=v, mixed=mixed, probs=probs,
        vector=vector, dh2=dh2,
    )
    fetched = [loaded[name] for name in LOADED] + list(early)
    input_grad, grads = pl.pallas_call(
        scatter_kernel,
        out_shape=shapes([((TOKENS, D), BF16), ((4, CHUNK, D), F32)]),
        in_specs=[vmem] * 3 + [anywhere] * (2 + len(fetched)),
        out_specs=[vmem] * 2,
        scratch_shapes=scratch(
            [(value.shape, value.dtype) for value in fetched]
            + large[:2]
            + [
                ((2, 4, 4, 2, CHUNK, D), BF16),
                ((4, 4, 2, CHUNK, D), BF16),
                ((2, CHUNK, D), BF16),
                ((2, CHUNK, D), BF16),
            ]
        )
        + [
            pltpu.SemaphoreType.DMA((3, 4)),
            pltpu.SemaphoreType.DMA((6, 3, 6)),
            pltpu.SemaphoreType.DMA((6, 3, 6)),
            pltpu.SemaphoreType.DMA((2,)),
            pltpu.SemaphoreType.DMA((2,)),
            pltpu.SemaphoreType.DMA((len(fetched),)),
        ]
        + [
            pltpu.VMEM(shape, BF16)
            for key, group in buffers.items()
            for slot, shape in enumerate(group)
            if shape is not None and (*key, slot) not in EARLY
        ],
        compiler_params=pltpu.CompilerParams(
            collective_id=1, has_side_effects=True, vmem_limit_bytes=62 * 2**20
        ),
    )(*tables, grad_wide, grad_shared, *fetched)
    return output.reshape(2, 1, 128, D), input_grad.reshape(2, 1, 128, D), grads


def newton_schulz(gram, values):
    gram_half = half(gram)
    first = half(NEWTON_B * gram + NEWTON_C * product(gram_half, gram_half))
    cross = product(gram_half, first)
    after = NEWTON_A * NEWTON_A * gram + 2.0 * NEWTON_A * cross + product(half(cross), first)
    after_half = half(after)
    second = half(NEWTON_B * after + NEWTON_C * product(after_half, after_half))
    values = half(NEWTON_A * values + product(half(values), first))
    return half(NEWTON_A * values.astype(F32) + product(values, second))


BLOCKS = [(i, j) for i in range(7) for j in range(i, 7)]
JOB_ROWS = (48, 48, 48, 16, 16, 16, 16)


def muon_kernel(
    tall_ref, short_ref, tall_out_ref, short_out_ref,
    rows, gram_out, gram_twin, gram_half_sum, gram_in, gram_all, gram, back, tall_got, short_got,
    job_sems, twin_sems, sum_sems, all_sems, back_sems,
):
    coords, core = my_coords()
    z, y, x = coords
    job = z * 2 + y // 2
    source = z * 2 + y // 2
    member = (y % 2) * 4 + x
    twin = device_of(coords, 1 - core)

    def group(peer):
        return device_of((z, (y // 2) * 2 + peer // 4, peer % 4), core)

    def square(k):
        return device_of((k // 2, (k % 2) * 2 + y % 2, x), core)

    barrier = pltpu.get_barrier_semaphore()
    for k in range(1, 8):
        for device in (group((member + k) % 8), square((source + k) % 8)):
            pl.semaphore_signal(barrier, inc=1, device_id=device, device_id_type=MESH)
    pl.semaphore_signal(barrier, inc=1, device_id=twin, device_id_type=MESH)
    pl.semaphore_wait(barrier, 15)

    def copy(src, dst, sems, slot, device):
        return remote(src, dst, sems.at[0, slot], sems.at[1, slot], device)

    def mine(m, tall, short):
        return tall.at[m] if m < 3 else short.at[m - 3]

    def job_copy(m):
        return remote(
            mine(m, tall_ref, short_ref),
            rows.at[source, pl.ds(0, JOB_ROWS[m])],
            job_sems.at[0, m],
            job_sems.at[1, source],
            square(m),
        )

    for m in range(7):

        @pl.when(job != m)
        def _():
            job_copy(m).start()

    for kind in range(2):
        count = (48, 16)[kind]

        @pl.when((job >= 3 * kind) & (job < 3 + 4 * kind))
        def _():
            if kind == 1:
                rows[:, 16:48] = jnp.zeros((8, 32, D), BF16)
                rows[source, 0:16] = short_ref[job - 3]
            else:
                rows[source] = tall_ref[job]
            for k in range(1, 8):
                other = (source + k) % 8
                arrival = rows.at[other, pl.ds(0, count)]
                remote(
                    arrival, arrival, job_sems.at[0, 0], job_sems.at[1, other], square(other)
                ).wait_recv()

    @pl.when(job < 7)
    def _():
        flat = rows[...].reshape(384, D)
        gram[...] = inner_rows(flat, flat)
        for index, (i, j) in enumerate(BLOCKS):
            gram_out[index // 16, index % 16] = half(
                gram[128 * i : 128 * i + 128, 128 * j : 128 * j + 128]
            )
        gram_out[1, 12:16] = jnp.zeros((4, 128, 128), BF16)
        twin_copy = copy(gram_out.at[1 - core], gram_twin, twin_sems, 0, twin)
        twin_copy.start()
        twin_copy.wait()
        gram_half_sum[...] = half(gram_out[core].astype(F32) + gram_twin[...].astype(F32))

        def sum_copy(k):
            peer = (member + k) % 8
            return copy(
                gram_half_sum.at[pl.ds(2 * peer, 2)], gram_in.at[k], sum_sems, k, group(peer)
            )

        for k in range(1, 8):
            sum_copy(k).start()
        total = gram_half_sum[pl.ds(2 * member, 2)].astype(F32)
        for k in range(1, 8):
            sum_copy(k).wait_recv()
            total = total + gram_in[k].astype(F32)
        gram_all[core, pl.ds(2 * member, 2)] = half(total)

        def all_copy(k, owner):
            ref = gram_all.at[core, pl.ds(2 * owner, 2)]
            return copy(ref, ref, all_sems, k, group((member + k) % 8))

        for k in range(1, 8):
            all_copy(k, member).start()
        for k in range(1, 8):
            all_copy(k, (member + 8 - k) % 8).wait_recv()
        last_copy = copy(gram_all.at[core], gram_all.at[core], twin_sems, 1, twin)
        last_copy.start()
        last_copy.wait()

        eye = lax.broadcasted_iota(jnp.int32, (128, 128), 0) == lax.broadcasted_iota(
            jnp.int32, (128, 128), 1
        )
        trace = 0.0
        for index, (i, j) in enumerate(BLOCKS):
            block = gram_all[index // 16, index % 16].astype(F32)
            gram[128 * i : 128 * i + 128, 128 * j : 128 * j + 128] = block
            if i == j:
                trace = trace + jnp.sum(jnp.where(eye, block, 0.0))
            else:
                gram[128 * j : 128 * j + 128, 128 * i : 128 * i + 128] = block.T
        inverse = 1.0 / (jnp.sqrt(jnp.full((1, 1), trace)) + 1e-07)
        moved = newton_schulz(
            gram[...] * (inverse * inverse), rows[...].reshape(384, D).astype(F32) * inverse
        )
        back[...] = moved.reshape(8, 48, D)
        for k in range(1, 8):
            sum_copy(k).wait_send()
            all_copy(k, member).wait_send()

    for m in range(7):

        @pl.when(job == m)
        def _():
            copies = []
            for k in range(1, 8):
                other = (source + k) % 8
                copies.append(
                    remote(
                        back.at[other, pl.ds(0, JOB_ROWS[m])],
                        mine(m, tall_got, short_got),
                        back_sems.at[0, k],
                        back_sems.at[1, m],
                        square(other),
                    )
                )
            for item in copies:
                item.start()
            if m < 3:
                tall_got[m] = back[source]
            else:
                short_got[m - 3] = back[source, 0:16]
            for item in copies:
                item.wait_send()

    for m in range(7):

        @pl.when(job != m)
        def _():
            arrival = mine(m, tall_got, short_got)
            remote(arrival, arrival, back_sems.at[0, 0], back_sems.at[1, m], square(m)).wait_recv()
            job_copy(m).wait_send()

    tall_out_ref[...] = tall_got[...]
    short_out_ref[...] = short_got[...]


def muon(tall, short):
    vmem = pl.BlockSpec(memory_space=pltpu.VMEM)
    return pl.pallas_call(
        muon_kernel,
        out_shape=(
            jax.ShapeDtypeStruct((3, 48, D), BF16),
            jax.ShapeDtypeStruct((4, 16, D), BF16),
        ),
        in_specs=[vmem] * 2,
        out_specs=(vmem,) * 2,
        scratch_shapes=[
            pltpu.VMEM((8, 48, D), BF16),
            pltpu.VMEM((2, 16, 128, 128), BF16),
            pltpu.VMEM((16, 128, 128), BF16),
            pltpu.VMEM((16, 128, 128), BF16),
            pltpu.VMEM((8, 2, 128, 128), BF16),
            pltpu.VMEM((2, 16, 128, 128), BF16),
            pltpu.VMEM((D, D), F32),
            pltpu.VMEM((8, 48, D), BF16),
            pltpu.VMEM((3, 48, D), BF16),
            pltpu.VMEM((4, 16, D), BF16),
            pltpu.SemaphoreType.DMA((2, 8)),
            pltpu.SemaphoreType.DMA((2, 2)),
            pltpu.SemaphoreType.DMA((2, 8)),
            pltpu.SemaphoreType.DMA((2, 8)),
            pltpu.SemaphoreType.DMA((2, 8)),
        ],
        compiler_params=pltpu.CompilerParams(
            collective_id=3, has_side_effects=True, vmem_limit_bytes=58 * 2**20
        ),
    )(tall, short)


def body(
    inputs,
    cotangent,
    lengths,
    query_weight,
    key_weight,
    value_weight,
    out_weight,
    gate_weight,
    up_weight,
    down_weight,
    vectors,
    query_prior,
    key_prior,
    value_prior,
    out_prior,
    gate_prior,
    up_prior,
    down_prior,
    first_prior,
    second_prior,
):
    chip = lax.axis_index("dp")
    core = lax.axis_index("narrow")
    parity = chip % 2
    kv_width = key_weight.shape[1]
    narrow_rows = jnp.concatenate(
        [key_weight, value_weight, jnp.pad(vectors[None], ((0, 6), (0, 128 - vectors.shape[0])))],
        axis=1,
    )
    weights = (
        gate_weight.T, up_weight.T, down_weight, query_weight, out_weight, narrow_rows
    )
    own_lengths = lax.dynamic_slice_in_dim(lengths, chip * 2 + core, 1, axis=1)
    own_lengths = jnp.broadcast_to(own_lengths, (2, 128))
    block_output, input_grad, grads = layer(weights, inputs[:, 0], cotangent[:, 0], own_lengths)
    units = grads[:3].reshape(3, 3, 16, D)
    thin = grads[3]

    def mine(which, size):
        if size == 7:
            return lax.dynamic_slice_in_dim(thin, 16 * which + parity * 7, 7, axis=0)
        last = lax.dynamic_slice_in_dim(units[2, which], parity * 6, 6, axis=0)
        return jnp.concatenate([units[0, which], units[1, which], last])

    own_narrow = mine(2, 7)
    grad_vector = own_narrow[0, 2 * kv_width : 2 * kv_width + 23]
    owned = (
        mine(0, 7),
        own_narrow[:, :kv_width],
        own_narrow[:, kv_width : 2 * kv_width],
        mine(1, 7),
        mine(0, 38),
        mine(1, 38),
        mine(2, 38),
    )
    priors = (
        query_prior,
        key_prior,
        value_prior,
        out_prior,
        gate_prior.T,
        up_prior.T,
        down_prior,
    )
    masters = (
        query_weight,
        key_weight,
        value_weight,
        out_weight,
        gate_weight,
        up_weight,
        down_weight,
    )
    shapes = ((D, D), (D, kv_width), (D, kv_width), (D, D), (D, FF), (D, FF), (FF, D))
    lefts = (False, False, False, False, True, True, False)
    momenta = tuple((MOMENTUM * priors[k] + owned[k] for k in range(7)))

    def padded(value, count):
        return jnp.pad(value, ((0, count - value.shape[0]), (0, D - value.shape[1])))

    tall, short = muon(
        half(jnp.stack([padded(momenta[k], 48) for k in (4, 5, 6)])),
        half(jnp.stack([padded(momenta[k], 16) for k in (0, 3, 1, 2)])),
    )
    finals = (
        short[0, :7], short[2, :7, :128], short[3, :7, :128], short[1, :7], tall[0, :38], tall[1, :38],
        tall[2, :38],
    )
    updated = []
    kept = []
    for k in range(7):
        current = finals[k].astype(jnp.float32)
        factor = MUON_RATE * 0.2 * math.sqrt(max(shapes[k][0], shapes[k][1]))
        if lefts[k]:
            current = current.T
        updated.append(masters[k] * (1.0 - MUON_RATE * MUON_DECAY) - factor * current)
        kept.append(momenta[k].T if lefts[k] else momenta[k])
    vector_first = BETA_FIRST * first_prior + (1.0 - BETA_FIRST) * grad_vector
    vector_second = BETA_SECOND * second_prior + (1.0 - BETA_SECOND) * grad_vector * grad_vector
    first_hat = vector_first / (1.0 - BETA_FIRST**STEP)
    second_hat = vector_second / (1.0 - BETA_SECOND**STEP)
    vector_new = vectors * (1.0 - ADAM_RATE * ADAM_DECAY) - ADAM_RATE * first_hat / (
        jnp.sqrt(second_hat) + ADAM_EPSILON
    )
    return (
        block_output,
        input_grad,
        *kept,
        *updated,
        vector_first,
        vector_second,
        vector_new,
    )


def solution(mesh):
    placed = (
        P(None, ("dp", "narrow"), None, None),
        P(None, ("dp", "narrow"), None, None),
        P(),
        P(("dp", "narrow"), None),
        P(("dp", "narrow"), None),
        P(("dp", "narrow"), None),
        P(("dp", "narrow"), None),
        P(None, ("dp", "narrow")),
        P(None, ("dp", "narrow")),
        P(("dp", "narrow"), None),
        P(("dp", "narrow")),
        P(("dp", "narrow"), None),
        P(("dp", "narrow"), None),
        P(("dp", "narrow"), None),
        P(("dp", "narrow"), None),
        P(None, ("dp", "narrow")),
        P(None, ("dp", "narrow")),
        P(("dp", "narrow"), None),
        P(("dp", "narrow")),
        P(("dp", "narrow")),
    )
    return jax.shard_map(
        body,
        mesh=mesh,
        in_specs=placed,
        out_specs=(
            P(None, ("dp", "narrow"), None, None),
            P(None, ("dp", "narrow"), None, None),
            P(("dp", "narrow"), None),
            P(("dp", "narrow"), None),
            P(("dp", "narrow"), None),
            P(("dp", "narrow"), None),
            P(None, ("dp", "narrow")),
            P(None, ("dp", "narrow")),
            P(("dp", "narrow"), None),
            P(("dp", "narrow"), None),
            P(("dp", "narrow"), None),
            P(("dp", "narrow"), None),
            P(("dp", "narrow"), None),
            P(None, ("dp", "narrow")),
            P(None, ("dp", "narrow")),
            P(("dp", "narrow"), None),
            P(("dp", "narrow")),
            P(("dp", "narrow")),
            P(("dp", "narrow")),
        ),
        check_vma=False,
    )
```

```python
import math

import jax
import jax.numpy as jnp
import numpy as np
from jax import lax
from jax.experimental import pallas as pl
from jax.experimental.pallas import tpu as pltpu
from jax.sharding import PartitionSpec as P

D = 896
FF = 4864
HEADS = 14
KV_HEADS = 2
HEAD = 64
STEP = 10


NORM_EPSILON = 1e-06
ROPE_BASE = 1000000.0
MOMENTUM = 0.95
NEWTON_A = 3.4445
NEWTON_B = -4.775
NEWTON_C = 2.0315
MUON_RATE = 0.4
MUON_DECAY = 0.1
ADAM_RATE = 0.5
ADAM_DECAY = 0.01
BETA_FIRST = 0.9
BETA_SECOND = 0.999
ADAM_EPSILON = 1e-08
MASKED = -1e30


def product(left, right):
    return jnp.dot(left, right, preferred_element_type=jnp.float32)


def inner_rows(left, right):
    return lax.dot_general(
        left, right, (((0,), (0,)), ((), ())), preferred_element_type=jnp.float32
    )


def outer_cols(left, right):
    return lax.dot_general(
        left, right, (((1,), (1,)), ((), ())), preferred_element_type=jnp.float32
    )


def norm_back(grad, normed, scale):
    return scale * (grad - normed * jnp.mean(grad * normed, axis=-1, keepdims=True))


def half(value):
    return value.astype(jnp.bfloat16)


MESH = pl.DeviceIdType.MESH
TOKENS = 256
FULL = (0, 4)
BF16 = jnp.bfloat16
F32 = jnp.float32
CHUNK = 48
PARTS = (
    (0, 0, CHUNK, (2, 1, 0), False, (0, D)),
    (0, CHUNK, CHUNK, (1, 0, 2), False, (0, D)),
    (1, 0, CHUNK, (0, 2, 1), True, (0, D)),
    (2, 0, 16, (2, 1, 0), True, (0, D)),
    (2, 16, 16, (1, 0, 2), True, (0, 512)),
    (2, 16, 16, (0, 2, 1), True, (512, 384)),
    (2, 32, 16, (0, 2, 1), True, (0, 384)),
)
WIDE = (0, 1, 2)
THIN = (3, 4, 5, 6)


def my_coords():
    dp = lax.axis_index("dp")
    return (dp // 16, (dp // 4) % 4, dp % 4), lax.axis_index("narrow")


def device_of(coords, core):
    return (coords[0] * 16 + coords[1] * 4 + coords[2], core)


def shifted(coords, axis, by):
    out = list(coords)
    out[axis] = (coords[axis] + by) % 4
    return tuple(out)


def facing(coords):
    return (coords[0], coords[1], 3 - coords[2])


def greet(coords, core):
    barrier = pltpu.get_barrier_semaphore()
    for axis in range(3):
        for by in (1, 2, 3):
            pl.semaphore_signal(
                barrier, inc=1, device_id=device_of(shifted(coords, axis, by), core), device_id_type=MESH
            )
    pl.semaphore_signal(barrier, inc=1, device_id=device_of(coords, 1 - core), device_id_type=MESH)
    pl.semaphore_wait(barrier, 10)


def remote(src, dst, send_sem, recv_sem, device):
    return pltpu.make_async_remote_copy(
        src_ref=src,
        dst_ref=dst,
        send_sem=send_sem,
        recv_sem=recv_sem,
        device_id=device,
        device_id_type=MESH,
    )


def place_of(part, spec):
    _, first, rows, _, shared, columns = PARTS[part]
    index = [pl.ds(*s) if isinstance(s, tuple) else s for s in spec[:2]]
    s = spec[2]
    if isinstance(s, tuple):
        index.append(pl.ds(s[0] // 2, s[1] // 2))
        index += [] if shared else [pl.ds(0, 2)]
    else:
        index.append(s // 2)
        index += [] if shared else [s % 2]
    return (*index, pl.ds(first, rows), pl.ds(*columns))


def shape_of(part, spec):
    return tuple(entry.size for entry in place_of(part, spec) if isinstance(entry, pl.Slice))


class Plan:
    def __init__(self, part, stage, coords, axis, spec, split):
        self.coords, self.axis, self.spec, self.split = coords, axis, spec, split
        self.exchange = PARTS[part][4] and axis == 2
        self.direct = not self.exchange and stage == 0

    def at(self, by):
        return shifted(self.coords, self.axis, by)

    def whole(self, by):
        spec = list(self.spec)
        spec[self.axis] = (self.coords[self.axis] + by) % 4
        return tuple(spec)

    def pieces(self, by):
        out = []
        for h in range(2):
            spec = list(self.whole(by))
            spec[self.split] = (2 * h, 2)
            out.append(tuple(spec))
        return out

    def facing(self):
        return (*self.spec[:2], 3 - self.coords[2])

    def own(self):
        return self.spec


def plan_of(part, stage, coords):
    order = PARTS[part][3]
    spec = tuple(FULL if k in order[:stage] else coords[k] for k in range(3))
    return Plan(part, stage, coords, order[stage], spec, order[stage - 1] if stage else None)


class Gather:
    def __init__(self, arrays, coords, core, send_sems, recv_sems):
        self.arrays, self.coords, self.core = arrays, coords, core
        self.send_sems, self.recv_sems = send_sems, recv_sems

    def copy(self, part, phase, slot, piece, coords):
        array, prefix = self.arrays[PARTS[part][0]]
        ref = array.at[(*prefix, *place_of(part, piece))]
        sems = (self.send_sems.at[part, phase, slot], self.recv_sems.at[part, phase, slot])
        return remote(ref, ref, *sems, device_of(coords, self.core))

    def send(self, *args):
        self.copy(*args).start()

    def neighbours(self, plan):
        return shifted(self.coords, plan.axis, 1), shifted(self.coords, plan.axis, 3)

    def start(self, parts, phase):
        for part in parts:
            plan = plan_of(part, phase, self.coords)
            if plan.exchange:
                self.send(part, phase, 0, plan.own(), facing(self.coords))
                continue
            if plan.direct:
                for by in (1, 3, 2):
                    self.send(part, phase, by, plan.own(), plan.at(by))
                continue
            right, left = self.neighbours(plan)
            first, second = plan.pieces(0)
            self.send(part, phase, 0, first, right)
            self.send(part, phase, 1, second, left)
            self.send(part, phase, 2, second, right)
            self.send(part, phase, 3, first, left)

    def forward(self, parts, phase):
        for part in parts:
            plan = plan_of(part, phase, self.coords)
            if plan.exchange or plan.direct:
                continue
            right, left = self.neighbours(plan)
            piece = plan.pieces(3)[0]
            self.copy(part, phase, 0, piece, right).wait_recv()
            self.send(part, phase, 4, piece, right)
            piece = plan.pieces(1)[1]
            self.copy(part, phase, 1, piece, left).wait_recv()
            self.send(part, phase, 5, piece, left)

    def near(self, parts, phase):
        for part in parts:
            plan = plan_of(part, phase, self.coords)
            if plan.exchange:
                self.copy(part, phase, 0, plan.facing(), facing(self.coords)).wait_recv()
                continue
            if plan.direct:
                for by in (1, 3):
                    self.copy(part, phase, by, plan.whole(4 - by), plan.at(by)).wait_recv()
                continue
            right, left = self.neighbours(plan)
            self.copy(part, phase, 2, plan.pieces(3)[1], right).wait_recv()
            self.copy(part, phase, 3, plan.pieces(1)[0], left).wait_recv()

    def far(self, parts, phase):
        for part in parts:
            plan = plan_of(part, phase, self.coords)
            if plan.exchange:
                continue
            if plan.direct:
                self.copy(part, phase, 2, plan.whole(2), plan.at(2)).wait_recv()
                continue
            right, left = self.neighbours(plan)
            self.copy(part, phase, 4, plan.pieces(2)[0], right).wait_recv()
            self.copy(part, phase, 5, plan.pieces(2)[1], left).wait_recv()

    def finish(self, parts, phase):
        self.near(parts, phase)
        self.far(parts, phase)

    def drain(self):
        for part in range(len(PARTS)):
            for phase in range(3):
                plan = plan_of(part, phase, self.coords)
                if plan.exchange:
                    self.copy(part, phase, 0, plan.own(), facing(self.coords)).wait_send()
                    continue
                if plan.direct:
                    for by in (1, 3, 2):
                        self.copy(part, phase, by, plan.own(), plan.at(by)).wait_send()
                    continue
                right, _ = self.neighbours(plan)
                for slot, which in enumerate((0, 1, 1, 0, 0, 1)):
                    self.copy(part, phase, slot, plan.pieces(0)[which], right).wait_send()


def each_block(shape, body):
    lead = shape[:-2]
    count = math.prod(lead)
    if count == 1:
        body((0,) * len(lead))
        return

    def step(k, carry):
        index = []
        for n in reversed(lead):
            index.append(k % n)
            k = k // n
        body(tuple(reversed(index)))
        return carry

    lax.fori_loop(0, count, step, 0)


class Scatter:
    def __init__(self, arrays, coords, core, buffers, send_sems, recv_sems, done):
        self.arrays, self.coords, self.core, self.done = arrays, coords, core, done
        self.buffers, self.send_sems, self.recv_sems = buffers, send_sems, recv_sems

    def copy(self, part, phase, slot, piece, coords):
        array, prefix = self.arrays[PARTS[part][0]]
        ref = array.at[(*prefix, *place_of(part, piece))]
        sems = (self.send_sems.at[part, phase, slot], self.recv_sems.at[part, phase, slot])
        return remote(ref, self.buffers[part, phase][slot], *sems, device_of(coords, self.core))

    def send(self, *args):
        if args[:3] not in self.done:
            self.copy(*args).start()

    def arrive(self, *args):
        if args[:3] not in self.done:
            self.copy(*args).wait_recv()

    def add(self, part, phase, piece, *slots):
        sources = [self.buffers[part, phase][slot] for slot in slots]
        base = place_of(part, piece)
        array, prefix = self.arrays[PARTS[part][0]]

        def one(index):
            spot, position = [], 0
            for entry in base[:-2]:
                if isinstance(entry, pl.Slice):
                    spot.append(entry.start + index[position])
                    position += 1
                else:
                    spot.append(entry)
            spot = (*prefix, *spot, *base[-2:])
            value = array[spot].astype(F32)
            for source in sources:
                value = value + source[(*index, slice(None), slice(None))].astype(F32)
            array[spot] = half(value)

        each_block(shape_of(part, piece), one)

    def neighbours(self, plan):
        return shifted(self.coords, plan.axis, 1), shifted(self.coords, plan.axis, 3)

    def start_far(self, parts, phase):
        for part in parts:
            plan = plan_of(part, phase, self.coords)
            if plan.exchange or plan.direct:
                continue
            right, left = self.neighbours(plan)
            self.send(part, phase, 0, plan.pieces(2)[0], right)
            self.send(part, phase, 1, plan.pieces(2)[1], left)

    def start_near(self, parts, phase):
        for part in parts:
            plan = plan_of(part, phase, self.coords)
            if plan.exchange:
                self.send(part, phase, 0, plan.facing(), facing(self.coords))
                continue
            if plan.direct:
                for by in (1, 3, 2):
                    self.send(part, phase, by, plan.whole(by), plan.at(by))
                continue
            right, left = self.neighbours(plan)
            self.send(part, phase, 2, plan.pieces(1)[1], right)
            self.send(part, phase, 3, plan.pieces(3)[0], left)

    def start(self, parts, phase):
        self.start_far(parts, phase)
        self.start_near(parts, phase)

    def forward(self, parts, phase):
        for part in parts:
            plan = plan_of(part, phase, self.coords)
            if plan.exchange or plan.direct:
                continue
            right, left = self.neighbours(plan)
            self.arrive(part, phase, 0, plan.pieces(2)[0], right)
            self.add(part, phase, plan.pieces(1)[0], 0)
            self.send(part, phase, 4, plan.pieces(1)[0], right)
            self.arrive(part, phase, 1, plan.pieces(2)[1], left)
            self.add(part, phase, plan.pieces(3)[1], 1)
            self.send(part, phase, 5, plan.pieces(3)[1], left)

    def finish(self, parts, phase):
        for part in parts:
            plan = plan_of(part, phase, self.coords)
            if plan.exchange:
                self.arrive(part, phase, 0, plan.facing(), facing(self.coords))
                self.add(part, phase, plan.own(), 0)
                continue
            if plan.direct:
                for by in (1, 3, 2):
                    self.arrive(part, phase, by, plan.whole(by), plan.at(by))
                self.add(part, phase, plan.own(), 1, 3, 2)
                continue
            right, left = self.neighbours(plan)
            self.arrive(part, phase, 3, plan.pieces(3)[0], left)
            self.arrive(part, phase, 4, plan.pieces(1)[0], right)
            self.add(part, phase, plan.pieces(0)[0], 4, 3)
            self.arrive(part, phase, 2, plan.pieces(1)[1], right)
            self.arrive(part, phase, 5, plan.pieces(3)[1], left)
            self.add(part, phase, plan.pieces(0)[1], 2, 5)

    def drain(self):
        for part in range(len(PARTS)):
            for phase in range(3):
                plan = plan_of(part, phase, self.coords)
                if plan.exchange:
                    self.copy(part, phase, 0, plan.own(), facing(self.coords)).wait_send()
                    continue
                if plan.direct:
                    for by in (1, 3, 2):
                        self.copy(part, phase, by, plan.whole(by), plan.at(by)).wait_send()
                    continue
                right, _ = self.neighbours(plan)
                for slot, which in enumerate((0, 1, 1, 0, 0, 1)):
                    if (part, phase, slot) in self.done:
                        continue
                    self.copy(part, phase, slot, plan.pieces(0)[which], right).wait_send()


EARLY = tuple((part, 2, slot) for part in WIDE for slot in (2, 3))


def scatter_buffer_shapes():
    out = []
    for part in range(len(PARTS)):
        for phase in range(3):
            plan = plan_of(part, phase, (0, 0, 0))
            if plan.exchange:
                shapes = [shape_of(part, plan.own())]
            elif plan.direct:
                shapes = [None] + [shape_of(part, plan.own())] * 3
            else:
                first, second = (shape_of(part, piece) for piece in plan.pieces(0))
                shapes = [first, second, second, first, first, second]
            out.append(((part, phase), shapes))
    return out


SCALE = HEAD ** (-0.5)


def turn(values, sign):
    lane = lax.broadcasted_iota(jnp.int32, values.shape, 1)
    ahead = pltpu.roll(values, 96, 1)
    behind = pltpu.roll(values, 32, 1)
    return jnp.where(lane & 32 == 0, sign * ahead, -sign * behind)


def tiles_of(values):
    return [values[:, 128 * t : 128 * t + 128] for t in range(values.shape[1] // 128)]


def rotated(values, cosine, sine):
    return jnp.concatenate(
        [tile * cosine + turn(tile, -1.0) * sine for tile in tiles_of(values)], axis=1
    )


def rotated_back(values, cosine, sine):
    return jnp.concatenate(
        [tile * cosine + turn(tile * sine, 1.0) for tile in tiles_of(values)], axis=1
    )


def low_lanes(shape):
    return lax.broadcasted_iota(jnp.int32, shape, 1) < HEAD


def paired(both):
    swapped = pltpu.roll(both, 64, 1)
    low = low_lanes(both.shape)
    even = [half(jnp.where(low, v, 0.0)) for v in (both, swapped)]
    odd = [half(jnp.where(low, 0.0, v)) for v in (swapped, both)]
    kinds = [jnp.concatenate([even[a], odd[b]]) for a, b in ((0, 0), (0, 1), (1, 1))]
    return [kinds[0]] * 3 + [kinds[1]] + [kinds[2]] * 3


def gathered_place():
    row = lax.broadcasted_iota(jnp.int32, (1024, D), 0)
    feature = lax.broadcasted_iota(jnp.int32, (1024, D), 1)
    slot = row & 15
    odd = (slot >= 7).astype(jnp.int32)
    device = (((row >> 4) & 31) * 2 + odd) * 2 + (row >> 9)
    source = jnp.where(slot < 14, 7 * device + slot - 7 * odd, -1)
    return half((source == feature).astype(jnp.float32))


def vector_maps():
    device = lax.broadcasted_iota(jnp.int32, (128, 1024), 0)
    row = lax.broadcasted_iota(jnp.int32, (128, 1024), 1)
    target = (device & 1) * 512 + (device >> 2) * 16 + ((device >> 1) & 1) * 7
    pick = half((row == target).astype(jnp.float32))
    start = lax.broadcasted_iota(jnp.int32, (128, 2944), 0) * 23
    entry = lax.broadcasted_iota(jnp.int32, (128, 2944), 1)
    owner = half(((entry >= start) & (entry < start + 23)).astype(jnp.float32))
    return pick, owner


def slot_mask(slots):
    return lax.broadcasted_iota(jnp.int32, (128, 2944), 0) == slots


def live_tokens(len_ref):
    token = lax.broadcasted_iota(jnp.int32, (128, 1), 0)
    return jnp.concatenate([(token < len_ref[b : b + 1, 0:1]).astype(F32) for b in range(2)])


def attention_forward(
    x_ref, rest_ref, len_ref, cos_ref, sin_ref, slot_ref,
    middle_ref, h1p_ref, q_ref, k_ref, v_ref, mixed_ref, probs_ref, vector_ref,
):
    place = gathered_place()
    pick, owner = vector_maps()
    stored = rest_ref[:, :, :, :, 32:48, 256:384].reshape(1024, 128)
    by_device = half(product(pick, stored))
    spread = inner_rows(by_device, owner)
    vector = jnp.sum(jnp.where(slot_mask(slot_ref[...]), spread, 0.0), axis=0, keepdims=True)
    vector_ref[...] = vector
    first_gain, second_gain = vector[:, :D], vector[:, D : 2 * D]
    query_bias, narrow_bias = vector[:, 2 * D : 3 * D], vector[:, 3 * D :]
    cosine, sine = cos_ref[...], sin_ref[...]
    inputs = x_ref[...].astype(jnp.float32)
    first_scale = lax.rsqrt(jnp.mean(inputs * inputs, axis=-1, keepdims=True) + NORM_EPSILON)
    normed = half(inputs * first_scale * first_gain)
    placed = half(outer_cols(normed, place))
    h1p_ref[...] = placed
    queries = product(placed, rest_ref[:, :, :, :, 0:16, :].reshape(1024, D)) + query_bias
    narrow = product(placed, rest_ref[:, :, :, :, 32:48, 0:256].reshape(1024, 256)) + narrow_bias
    q_ref[...] = half(rotated(queries, cosine, sine))
    keys = rotated(narrow[:, 0:128], cosine, sine)
    k_ref[...] = half(keys)
    values = narrow[:, 128:256]
    v_ref[...] = half(values)
    position = lax.broadcasted_iota(jnp.int32, (128, 256), 0)
    other = lax.broadcasted_iota(jnp.int32, (128, 256), 1) & 127
    causal = other <= position
    rows = []
    for b in range(2):
        here = slice(128 * b, 128 * b + 128)
        length = len_ref[b : b + 1, :]
        allowed = causal & (other < jnp.concatenate([length, length], axis=1))
        key_tiles = paired(keys[here])
        value_tiles = paired(values[here])
        tiles = []
        for t in range(7):
            scores = outer_cols(q_ref[here, 128 * t : 128 * t + 128], key_tiles[t])
            scores = jnp.where(allowed, scores * SCALE, MASKED)
            parts = []
            for part in tiles_of(scores):
                shifted = jnp.exp(part - jnp.max(part, axis=-1, keepdims=True))
                parts.append(shifted / jnp.sum(shifted, axis=-1, keepdims=True))
            probs = jnp.concatenate(parts, axis=1)
            probs_ref[b, t] = probs
            tiles.append(half(product(half(probs), value_tiles[t])))
        rows.append(jnp.concatenate(tiles, axis=1))
    mixed = half(outer_cols(jnp.concatenate(rows), place))
    mixed_ref[...] = mixed
    middle = inputs + product(mixed, rest_ref[:, :, :, :, 16:32, :].reshape(1024, D))
    middle_ref[...] = middle
    second_scale = lax.rsqrt(jnp.mean(middle * middle, axis=-1, keepdims=True) + NORM_EPSILON)
    return half(middle * second_scale * second_gain)


def mlp_tile(weights, h, e, sums):
    lead = weights.shape[:-2]
    units = 16 * math.prod(lead)
    gate_w, up_w, down_w = (
        weights[..., 16 * k : 16 * k + 16, :].reshape(units, D) for k in range(3)
    )
    gate = outer_cols(h, gate_w)
    up = outer_cols(h, up_w)
    sigma = jax.nn.sigmoid(gate)
    silu = gate * sigma
    hidden = half(silu * up)
    grad_hidden = outer_cols(e, down_w)
    sums[0] += product(hidden, down_w).reshape(2, TOKENS, D)
    grad_gate = half(grad_hidden * up * sigma * (1.0 + gate * (1.0 - sigma)))
    grad_up = half(grad_hidden * silu)
    sums[1] += (product(grad_gate, gate_w) + product(grad_up, up_w)).reshape(2, TOKENS, D)
    grads = (inner_rows(grad_gate, h), inner_rows(grad_up, h), inner_rows(hidden, e))
    return [half(grad).reshape(*lead, 16, D) for grad in grads]


KEPT = 17


def gather_kernel(
    gate_ref, up_ref, down_ref, query_ref, out_ref, narrow_ref,
    x_ref, cot_ref, len_ref, cos_ref, sin_ref, slot_ref, *refs,
):
    coords, core = my_coords()
    z, y, x = coords
    pair, odd = x // 2, x % 2
    results, (grad_wide_ref, grad_shared_ref, rest_ref) = refs[:KEPT], refs[KEPT : KEPT + 3]
    held = refs[KEPT + 3 : 2 * KEPT + 1]
    (
        wide, shared, rest, stage0, stage1, stage2, h_all, e_all, sums, parcel, tail, tail_own, tail_wide,
        local_sems, send_sems, recv_sems, twin_sems, store_sems, early_sems, kept_sems,
    ) = refs[2 * KEPT + 1 :]
    middle_ref, e_ref, h1p_ref, q_ref, k_ref, v_ref, mixed_ref, probs_ref, vector_ref = held[:9]
    early = held[9:]
    kept = [*held[:9], sums.at[:, core], parcel, *early]

    def keep(first, last):
        return [
            pltpu.make_async_copy(kept[n], results[n], kept_sems.at[n]) for n in range(first, last)
        ]

    units = (gate_ref, up_ref, down_ref)
    for n, ref in enumerate(units):
        for k in range(2):
            wide[z, y, pair, odd, CHUNK * k + 16 * n : CHUNK * k + 16 * n + 16] = half(
                ref[16 * k : 16 * k + 16]
            )
    tail_wide[...] = jnp.zeros_like(tail_wide)
    for parity in range(2):

        @pl.when(odd == parity)
        def _():
            for n, ref in enumerate(units):
                start = 16 * n + 6 * parity
                tail_wide[start : start + 6] = ref[32:38]
            for n, ref in enumerate((query_ref, out_ref)):
                start = CHUNK + 16 * n + 7 * parity
                tail_wide[start : start + 7] = ref[...]
            start = CHUNK + 32 + 7 * parity
            tail_wide[start : start + 7, 0:384] = narrow_ref[...]

    tail_own[...] = half(tail_wide[...])
    greet(coords, core)
    twin = device_of(coords, 1 - core)

    def to_twin(src, dst, slot):
        return remote(src, dst, twin_sems.at[0, slot], twin_sems.at[1, slot], twin)

    gather = Gather(((wide, ()), (shared, ()), (rest, (core,))), coords, core, send_sems, recv_sems)
    partner = device_of((z, y, x + 1 - 2 * odd), core)
    tail_copy = remote(tail_own, tail, twin_sems.at[0, 4], twin_sems.at[1, 4], partner)
    tail_copy.start()
    gather.start((0, 1), 0)
    e_ref[...] = half(cot_ref[...].astype(F32) * live_tokens(len_ref))
    e_all[core] = e_ref[...]
    e_copy = to_twin(e_ref, e_all.at[core], 0)
    e_copy.start()
    tail_copy.wait()
    both = half(tail_wide[...] + tail[...].astype(F32))
    shared[z, y, pair] = both[:CHUNK]
    rest[core, z, y, pair] = both[CHUNK:]
    gather.start(THIN, 0)
    gather.start((2,), 0)
    gather.forward(THIN, 0)
    gather.finish(THIN, 0)
    gather.start(THIN, 1)
    gather.forward(WIDE, 0)
    gather.forward(THIN, 1)
    gather.finish(THIN, 1)
    gather.start(THIN, 2)
    gather.finish(WIDE, 0)
    gather.start(WIDE, 1)
    gather.forward(THIN, 2)
    gather.finish(THIN, 2)
    rest_copy = to_twin(rest.at[core], rest.at[core], 1)
    rest_copy.start()
    gather.forward(WIDE, 1)
    gather.finish(WIDE, 1)
    gather.start(WIDE, 2)
    rest_copy.wait()
    rest_store = pltpu.make_async_copy(rest, rest_ref, local_sems.at[0])
    rest_store.start()
    h_all[core] = attention_forward(
        x_ref, rest, len_ref, cos_ref, sin_ref, slot_ref,
        middle_ref, h1p_ref, q_ref, k_ref, v_ref, mixed_ref, probs_ref, vector_ref,
    )
    h_copy = to_twin(h_all.at[core], h_all.at[core], 2)
    h_copy.start()
    for copy in keep(0, 9):
        copy.start()
    sums[...] = jnp.zeros_like(sums)
    e_copy.wait()
    h_copy.wait()
    stages = (stage0, stage1, stage2)

    def early_copy(t, slot):
        axis = PARTS[t][3][2]
        which = 3 - slot
        place = [slice(None)] * (len(stages[t].shape) - 1)
        place[1 if t == 2 else 0] = pl.ds(which, 1) if t == 2 else pl.ds(2 * which, 2)
        return remote(
            stages[t].at[(slot - 1) % 2].at[tuple(place)],
            early[2 * t + slot - 2],
            early_sems.at[0, t, slot - 2],
            early_sems.at[1, t, slot - 2],
            device_of(shifted(coords, axis, 1 if slot == 2 else 3), core),
        )

    def tile_places(j):
        return (
            (wide, grad_wide_ref, (j, slice(None), slice(None), slice(None), pl.ds(0, CHUNK))),
            (wide, grad_wide_ref, (slice(None), slice(None), j // 2, j % 2, pl.ds(CHUNK, CHUNK))),
            (shared, grad_shared_ref, (slice(None), j, slice(None), pl.ds(0, CHUNK))),
        )

    def step(k, carry):
        @pl.when(k == 1)
        def _():
            gather.near(WIDE, 2)

        @pl.when(k == 3)
        def _():
            gather.far(WIDE, 2)

        offset = jnp.where(k < 2, k, 5 - k)
        h = h_all[...].reshape(2 * TOKENS, D)
        e = e_all[...].reshape(2 * TOKENS, D)
        for t, axis in enumerate((0, 2, 1)):
            j = (coords[axis] + offset) % 4
            source, target, index = tile_places(j)[t]
            grads = mlp_tile(source[(*index, slice(None))], h, e, sums)
            copy = pltpu.make_async_copy(
                stages[t].at[k % 2], target.at[(*index, slice(None))], store_sems.at[t, k % 2]
            )

            @pl.when(k > 1)
            def _():
                copy.wait()

            @pl.when(k == 3)
            def _():
                early_copy(t, 2).wait_send()

            for place, grad in enumerate(grads):
                stages[t][k % 2, ..., 16 * place : 16 * place + 16, :] = grad
            copy.start()

            @pl.when(k == 1)
            def _():
                early_copy(t, 2).start()

            @pl.when(k == 2)
            def _():
                early_copy(t, 3).start()

        @pl.when(k == 0)
        def _():
            gather.forward(WIDE, 2)

        return carry

    lax.fori_loop(0, 4, step, 0)
    parcel[...] = half(sums[:, 1 - core])
    for copy in keep(9, 11):
        copy.start()
    for t in range(3):
        _, target, index = tile_places(0)[t]
        for which in range(2):
            pltpu.make_async_copy(
                stages[t].at[which], target.at[(*index, slice(None))], store_sems.at[t, which]
            ).wait()
        early_copy(t, 3).wait_send()
        early_copy(t, 2).wait_recv()
        early_copy(t, 3).wait_recv()
        for copy in keep(11 + 2 * t, 13 + 2 * t):
            copy.start()
    rest_store.wait()
    for copy in keep(0, KEPT):
        copy.wait()
    gather.drain()


def attention_backward(
    between, x_ref, e_ref, rest_ref, cos_ref, sin_ref, slot_ref,
    middle_ref, h1p_ref, q_ref, k_ref, v_ref, mixed_ref, probs_ref, vector_ref, dh2_ref,
    input_grad_ref, grad_ref,
):
    place = gathered_place()
    pick, owner = vector_maps()
    vector = vector_ref[...]
    first_gain, second_gain = vector[:, :D], vector[:, D : 2 * D]
    cosine, sine = cos_ref[...], sin_ref[...]
    middle = middle_ref[...]
    second_scale = lax.rsqrt(jnp.mean(middle * middle, axis=-1, keepdims=True) + NORM_EPSILON)
    second_normed = middle * second_scale
    dh2 = dh2_ref[...]
    second_gain_grad = jnp.sum(dh2 * second_normed, axis=0, keepdims=True)
    grad_middle = e_ref[...].astype(jnp.float32) + norm_back(
        dh2 * second_gain, second_normed, second_scale
    )
    branch = half(grad_middle)
    wide = rest_ref[:, :, :, :, 16:32, :].reshape(1024, D)
    grad_ref[:, :, :, :, 16:32, :] = half(inner_rows(mixed_ref[...], branch)).reshape(2, 4, 4, 2, 16, D)
    grad_mixed = half(product(half(outer_cols(branch, wide)), place))
    low = low_lanes((128, 128))
    query_rows, key_rows, value_rows = [], [], []
    for b in range(2):
        here = slice(128 * b, 128 * b + 128)
        key_tiles = paired(k_ref[here, :].astype(jnp.float32))
        value_tiles = paired(v_ref[here, :].astype(jnp.float32))
        tiles = []
        sums = [[jnp.zeros((128, 128), jnp.float32) for _ in range(4)] for _ in range(2)]
        for t in range(7):
            head = grad_mixed[here, 128 * t : 128 * t + 128]
            grad_probs = outer_cols(head, value_tiles[t])
            probs = probs_ref[b, t]
            parts = []
            for p, g in zip(tiles_of(probs), tiles_of(grad_probs)):
                parts.append(half(p * (g - jnp.sum(p * g, axis=-1, keepdims=True))))
            grad_scores = jnp.concatenate(parts, axis=1)
            tiles.append(product(grad_scores, key_tiles[t]) * SCALE)
            for which, (left, right) in enumerate(
                ((grad_scores, q_ref[here, 128 * t : 128 * t + 128]), (half(probs), head))
            ):
                both = inner_rows(left, right)
                even, odd = (2 * t) // 7, (2 * t + 1) // 7
                sums[which][even] += both[0:128]
                sums[which][2 + odd] += both[128:256]
        query_rows.append(jnp.concatenate(tiles, axis=1))
        joined = []
        for which in range(2):
            even0, even1, odd0, odd1 = sums[which]
            joined.append(
                jnp.where(low, even0 + pltpu.roll(odd0, 64, 1), odd1 + pltpu.roll(even1, 64, 1))
            )
        key_rows.append(joined[0] * SCALE)
        value_rows.append(joined[1])
    between()
    grad_query = half(rotated_back(jnp.concatenate(query_rows), cosine, sine))
    grad_key = half(rotated_back(jnp.concatenate(key_rows), cosine, sine))
    grad_narrow = jnp.concatenate([grad_key, half(jnp.concatenate(value_rows))], axis=1)
    placed = h1p_ref[...]
    grad_ref[:, :, :, :, 0:16, :] = half(inner_rows(placed, grad_query)).reshape(2, 4, 4, 2, 16, D)
    grad_ref[:, :, :, :, 32:48, 0:256] = half(inner_rows(placed, grad_narrow)).reshape(2, 4, 4, 2, 16, 256)
    bias_grad = jnp.sum(
        jnp.concatenate([grad_query, grad_narrow], axis=1).astype(jnp.float32), axis=0, keepdims=True
    )
    grad_placed = outer_cols(grad_query, rest_ref[:, :, :, :, 0:16, :].reshape(1024, D)) + outer_cols(
        grad_narrow, rest_ref[:, :, :, :, 32:48, 0:256].reshape(1024, 256)
    )
    high = half(grad_placed)
    remainder = half(grad_placed - high.astype(jnp.float32))
    grad_normed = product(high, place) + product(remainder, place)
    inputs = x_ref[...].astype(jnp.float32)
    first_scale = lax.rsqrt(jnp.mean(inputs * inputs, axis=-1, keepdims=True) + NORM_EPSILON)
    first_normed = inputs * first_scale
    first_gain_grad = jnp.sum(grad_normed * first_normed, axis=0, keepdims=True)
    input_grad_ref[...] = half(
        grad_middle + norm_back(grad_normed * first_gain, first_normed, first_scale)
    )
    vector_grad = jnp.concatenate([first_gain_grad, second_gain_grad, bias_grad], axis=1)
    spread = half(jnp.where(slot_mask(slot_ref[...]), vector_grad, 0.0))
    by_device = half(outer_cols(owner, spread))
    stored = half(inner_rows(pick, by_device))
    grad_ref[:, :, :, :, 32:48, 256:384] = stored.reshape(2, 4, 4, 2, 16, 128)
    grad_ref[:, :, :, :, 32:48, 384:] = jnp.zeros((2, 4, 4, 2, 16, D - 384), jnp.bfloat16)


LOADED = (
    "parcel", "own", "middle", "e", "x", "rest", "h1p", "q", "k", "v", "mixed", "probs", "vector",
)


def scatter_kernel(
    len_ref, cos_ref, sin_ref, slot_ref, grad_wide_ref, grad_shared_ref, *refs,
):
    coords, core = my_coords()
    z, y, x = coords
    pair, odd = x // 2, x % 2
    count = len(LOADED) + len(EARLY)
    sources, (output_ref, input_grad_ref, out_ref) = refs[:count], refs[count : count + 3]
    held = refs[count + 3 : 2 * count + 3]
    (
        wide, shared, thin, joined, mine, theirs, arrived, dh2_ref,
        load_sems, send_sems, recv_sems, twin_sems, pair_sems, held_sems,
    ) = refs[2 * count + 3 : 2 * count + 17]
    buffers = refs[2 * count + 17 :]
    (
        parcel_ref, own_ref, middle_ref, e_ref, x_ref, rest_ref, h1p_ref, q_ref, k_ref, v_ref,
        mixed_ref, probs_ref, vector_ref,
    ) = held[: len(LOADED)]
    fetches = [
        pltpu.make_async_copy(sources[n], held[n], held_sems.at[n]) for n in range(count)
    ]
    named, position = {}, 0
    early = dict(zip(EARLY, held[len(LOADED) :]))
    for key, shapes in scatter_buffer_shapes():
        named[key] = []
        for slot in range(len(shapes)):
            if (*key, slot) in early:
                named[key].append(early[(*key, slot)])
            elif shapes[slot] is None:
                named[key].append(None)
            else:
                named[key].append(buffers[position])
                position += 1
    scatter = Scatter(((wide, ()), (shared, ()), (thin, (core,))), coords, core, named, send_sems, recv_sems, EARLY)

    def load(part, by):
        spec = [FULL] * 3
        axis = PARTS[part][3][2]
        spec[axis] = (coords[axis] + by) % 4
        place = place_of(part, tuple(spec))
        source = (grad_wide_ref, grad_shared_ref)[PARTS[part][0]]
        target = (wide, shared)[PARTS[part][0]]
        return pltpu.make_async_copy(source.at[place], target.at[place], load_sems.at[part, by])

    for by in (2, 1, 3, 0):
        for part in WIDE:
            load(part, by).start()
    for copy in fetches:
        copy.start()
    greet(coords, core)

    for part in WIDE:
        load(part, 2).wait()
        scatter.start_far((part,), 2)
    for part in WIDE:
        load(part, 1).wait()
        load(part, 3).wait()

    def between():
        scatter.forward(WIDE, 2)

    for copy in fetches[:3]:
        copy.wait()
    parcel_copy = remote(
        parcel_ref, arrived, twin_sems.at[0, 1], twin_sems.at[1, 1], device_of(coords, 1 - core)
    )
    parcel_copy.start()
    for copy in fetches[3:]:
        copy.wait()
    parcel_copy.wait()
    output_ref[...] = half(
        (middle_ref[...] + (own_ref[0] + arrived[0].astype(F32))) * live_tokens(len_ref)
    )
    dh2_ref[...] = own_ref[1] + arrived[1].astype(F32)
    attention_backward(
        between, x_ref, e_ref, rest_ref, cos_ref, sin_ref, slot_ref,
        middle_ref, h1p_ref, q_ref, k_ref, v_ref, mixed_ref, probs_ref, vector_ref, dh2_ref,
        input_grad_ref, thin,
    )
    twin_copy = remote(
        thin.at[1 - core], joined, twin_sems.at[0, 0], twin_sems.at[1, 0], device_of(coords, 1 - core)
    )
    twin_copy.start()
    for part in WIDE:
        load(part, 0).wait()
    twin_copy.wait()

    def join(index):
        thin[(core, *index)] = half(thin[(core, *index)].astype(F32) + joined[index].astype(F32))

    each_block((4, 4, 2, CHUNK, D), join)
    scatter.start(THIN, 2)
    for part in WIDE:
        scatter.finish((part,), 2)
        scatter.start((part,), 1)
    scatter.forward(THIN, 2)
    scatter.finish(THIN, 2)
    scatter.start(THIN, 1)
    scatter.forward(WIDE, 1)
    scatter.forward(THIN, 1)
    for part in WIDE:
        scatter.finish((part,), 1)
        scatter.start((part,), 0)
    scatter.finish(THIN, 1)
    scatter.start(THIN, 0)
    scatter.forward(WIDE, 0)
    scatter.forward(THIN, 0)
    scatter.finish(WIDE, 0)
    scatter.finish(THIN, 0)
    mine[0] = shared[z, y, pair]
    mine[1] = thin[core, z, y, pair]
    partner = device_of((z, y, x + 1 - 2 * odd), core)
    pair_copy = remote(mine, theirs, pair_sems.at[0], pair_sems.at[1], partner)
    pair_copy.start()
    pair_copy.wait()
    out_ref[0] = wide[z, y, pair, odd, 0:CHUNK].astype(F32)
    out_ref[1] = wide[z, y, pair, odd, CHUNK : 2 * CHUNK].astype(F32)
    out_ref[2] = mine[0].astype(F32) + theirs[0].astype(F32)
    out_ref[3] = mine[1].astype(F32) + theirs[1].astype(F32)
    scatter.drain()


def layer(weights, tokens, cotangent, lengths):
    vmem = pl.BlockSpec(memory_space=pltpu.VMEM)
    anywhere = pl.BlockSpec(memory_space=pl.ANY)
    x = tokens.reshape(TOKENS, D)
    freqs = ROPE_BASE ** (-np.arange(HEAD // 2) * 2.0 / HEAD)
    angles = np.tile(np.arange(128)[:, None] * freqs[None, :], (2, 4))
    tables = (
        np.cos(angles).astype(np.float32),
        np.sin(angles).astype(np.float32),
        (np.arange(2944, dtype=np.int32) % 23)[None],
    )
    buffers = dict(scatter_buffer_shapes())
    kept = [
        ((TOKENS, D), F32),
        ((TOKENS, D), BF16),
        ((TOKENS, 1024), BF16),
        ((TOKENS, D), BF16),
        ((TOKENS, 128), BF16),
        ((TOKENS, 128), BF16),
        ((TOKENS, 1024), BF16),
        ((2, 7, 128, 256), F32),
        ((1, 2944), F32),
        ((2, TOKENS, D), F32),
        ((2, TOKENS, D), BF16),
    ] + [(buffers[part, stage][slot], BF16) for part, stage, slot in EARLY]
    large = [
        ((4, 4, 2, 2, 2 * CHUNK, D), BF16),
        ((4, 4, 2, CHUNK, D), BF16),
        ((2, 4, 4, 2, CHUNK, D), BF16),
    ]

    def shapes(pairs):
        return [jax.ShapeDtypeStruct(shape, dtype) for shape, dtype in pairs]

    def scratch(pairs):
        return [pltpu.VMEM(shape, dtype) for shape, dtype in pairs]

    results = pl.pallas_call(
        gather_kernel,
        out_shape=shapes(kept + large),
        in_specs=[vmem] * 12,
        out_specs=[anywhere] * (KEPT + 3),
        scratch_shapes=scratch(
            kept[:9]
            + kept[11:]
            + large
            + [
                ((2, 4, 2, 2, CHUNK, D), BF16),
                ((2, 4, 4, CHUNK, D), BF16),
                ((2, 4, 2, CHUNK, D), BF16),
                ((2, TOKENS, D), BF16),
                ((2, TOKENS, D), BF16),
                ((2, 2, TOKENS, D), F32),
                ((2, TOKENS, D), BF16),
                ((2 * CHUNK, D), BF16),
                ((2 * CHUNK, D), BF16),
                ((2 * CHUNK, D), F32),
            ]
        )
        + [
            pltpu.SemaphoreType.DMA((3,)),
            pltpu.SemaphoreType.DMA((len(PARTS), 3, 6)),
            pltpu.SemaphoreType.DMA((len(PARTS), 3, 6)),
            pltpu.SemaphoreType.DMA((2, 5)),
            pltpu.SemaphoreType.DMA((3, 2)),
            pltpu.SemaphoreType.DMA((2, 3, 2)),
            pltpu.SemaphoreType.DMA((KEPT,)),
        ],
        compiler_params=pltpu.CompilerParams(
            collective_id=0, has_side_effects=True, vmem_limit_bytes=61 * 2**20
        ),
    )(*weights, x, cotangent.reshape(TOKENS, D), lengths, *tables)
    middle, e, h1p, q, k, v, mixed, probs, vector, own, parcel = results[:11]
    early = results[11:KEPT]
    grad_wide, grad_shared, rest = results[KEPT:]
    loaded = dict(
        x=x, e=e, rest=rest, middle=middle, h1p=h1p, q=q, k=k, v=v, mixed=mixed, probs=probs,
        vector=vector, own=own, parcel=parcel,
    )
    fetched = [loaded[name] for name in LOADED] + list(early)
    output, input_grad, grads = pl.pallas_call(
        scatter_kernel,
        out_shape=shapes([((TOKENS, D), BF16), ((TOKENS, D), BF16), ((4, CHUNK, D), F32)]),
        in_specs=[vmem] * 4 + [anywhere] * (2 + len(fetched)),
        out_specs=[vmem] * 3,
        scratch_shapes=scratch(
            [(value.shape, value.dtype) for value in fetched]
            + large[:2]
            + [
                ((2, 4, 4, 2, CHUNK, D), BF16),
                ((4, 4, 2, CHUNK, D), BF16),
                ((2, CHUNK, D), BF16),
                ((2, CHUNK, D), BF16),
                ((2, TOKENS, D), BF16),
                ((TOKENS, D), F32),
            ]
        )
        + [
            pltpu.SemaphoreType.DMA((3, 4)),
            pltpu.SemaphoreType.DMA((len(PARTS), 3, 6)),
            pltpu.SemaphoreType.DMA((len(PARTS), 3, 6)),
            pltpu.SemaphoreType.DMA((2, 2)),
            pltpu.SemaphoreType.DMA((2,)),
            pltpu.SemaphoreType.DMA((len(fetched),)),
        ]
        + [
            pltpu.VMEM(shape, BF16)
            for key, group in buffers.items()
            for slot, shape in enumerate(group)
            if shape is not None and (*key, slot) not in EARLY
        ],
        compiler_params=pltpu.CompilerParams(
            collective_id=1, has_side_effects=True, vmem_limit_bytes=62 * 2**20
        ),
    )(lengths, *tables, grad_wide, grad_shared, *fetched)
    return output.reshape(2, 1, 128, D), input_grad.reshape(2, 1, 128, D), grads


def newton_schulz(gram, values):
    gram_half = half(gram)
    first = half(NEWTON_B * gram + NEWTON_C * product(gram_half, gram_half))
    cross = product(gram_half, first)
    after = NEWTON_A * NEWTON_A * gram + 2.0 * NEWTON_A * cross + product(half(cross), first)
    after_half = half(after)
    second = half(NEWTON_B * after + NEWTON_C * product(after_half, after_half))
    values = half(NEWTON_A * values + product(half(values), first))
    return half(NEWTON_A * values.astype(F32) + product(values, second))


BLOCKS = [(i, j) for i in range(7) for j in range(i, 7)]
JOB_ROWS = (48, 48, 48, 16, 16, 16, 16)


def own_momenta(grads_ref, priors, momenta, odd):
    for parity in range(2):

        @pl.when(odd == parity)
        def _():
            for n in range(3):
                for k, (start, size) in enumerate(((0, 16), (16, 16), (32, 6))):
                    base = 16 * n + (6 * parity if k == 2 else 0)
                    momenta[n][start : start + size] = (
                        MOMENTUM * priors[n][start : start + size] + grads_ref[k, base : base + size]
                    )
            for n in range(4):
                base = 16 * min(n, 2) + 7 * parity
                lanes = slice(0, D) if n < 2 else slice(128 * n - 256, 128 * n - 128)
                momenta[3 + n][...] = (
                    MOMENTUM * priors[3 + n][...] + grads_ref[3, base : base + 7, lanes]
                )


def update_kernel(grads_ref, tall_ref, short_ref, *refs):
    priors, masters, (first_ref, second_ref, vector_ref) = refs[:7], refs[7:14], refs[14:17]
    momenta, updated, vector_outs = refs[17:24], refs[24:31], refs[31:34]
    odd = lax.axis_index("dp") % 2
    own_momenta(grads_ref, priors, momenta, odd)
    for n in range(7):
        size = FF if n < 3 else D
        got = tall_ref[n].astype(F32)[:38] if n < 3 else short_ref[n - 3].astype(F32)[:7]
        got = got[:, :128] if n > 4 else got
        updated[n][...] = masters[n][...] * (1.0 - MUON_RATE * MUON_DECAY) - (
            MUON_RATE * 0.2 * math.sqrt(size) * got
        )
    for parity in range(2):

        @pl.when(odd == parity)
        def _():
            start = 32 + 7 * parity
            grad = grads_ref[3, start : start + 1, 256:384][:, :23]
            first = BETA_FIRST * first_ref[...] + (1.0 - BETA_FIRST) * grad
            second = BETA_SECOND * second_ref[...] + (1.0 - BETA_SECOND) * grad * grad
            first_hat = first / (1.0 - BETA_FIRST**STEP)
            second_hat = second / (1.0 - BETA_SECOND**STEP)
            vector_outs[0][...] = first
            vector_outs[1][...] = second
            vector_outs[2][...] = vector_ref[...] * (1.0 - ADAM_RATE * ADAM_DECAY) - (
                ADAM_RATE * first_hat / (jnp.sqrt(second_hat) + ADAM_EPSILON)
            )


def muon_kernel(
    grads_ref, prior0, prior1, prior2, prior3, prior4, prior5, prior6, tall_out_ref, short_out_ref,
    momentum0, momentum1, momentum2, momentum3, momentum4, momentum5, momentum6,
    tall_wide, short_wide, tall_ref, short_ref, rows, gram_out, gram_twin, gram_half_sum, gram_in, gram_all, gram, back, tall_got, short_got,
    job_sems, twin_sems, sum_sems, all_sems, back_sems,
):
    priors = (prior0, prior1, prior2, prior3, prior4, prior5, prior6)
    momenta = (momentum0, momentum1, momentum2, momentum3, momentum4, momentum5, momentum6)
    coords, core = my_coords()
    z, y, x = coords
    job = z * 2 + y // 2
    source = z * 2 + y // 2
    member = (y % 2) * 4 + x
    tall_wide[...] = jnp.zeros_like(tall_wide)
    short_wide[...] = jnp.zeros_like(short_wide)
    own_momenta(grads_ref, priors, momenta, x % 2)
    for n in range(3):
        tall_wide[n, 0:38] = momenta[n][...]
    for n in range(4):
        short_wide[n, 0:7, 0 : D if n < 2 else 128] = momenta[3 + n][...]
    tall_ref[...] = half(tall_wide[...])
    short_ref[...] = half(short_wide[...])
    twin = device_of(coords, 1 - core)

    def group(peer):
        return device_of((z, (y // 2) * 2 + peer // 4, peer % 4), core)

    def square(k):
        return device_of((k // 2, (k % 2) * 2 + y % 2, x), core)

    barrier = pltpu.get_barrier_semaphore()
    for k in range(1, 8):
        for device in (group((member + k) % 8), square((source + k) % 8)):
            pl.semaphore_signal(barrier, inc=1, device_id=device, device_id_type=MESH)
    pl.semaphore_signal(barrier, inc=1, device_id=twin, device_id_type=MESH)
    pl.semaphore_wait(barrier, 15)

    def copy(src, dst, sems, slot, device):
        return remote(src, dst, sems.at[0, slot], sems.at[1, slot], device)

    def mine(m, tall, short):
        return tall.at[m] if m < 3 else short.at[m - 3]

    def job_copy(m):
        return remote(
            mine(m, tall_ref, short_ref),
            rows.at[source, pl.ds(0, JOB_ROWS[m])],
            job_sems.at[0, m],
            job_sems.at[1, source],
            square(m),
        )

    for m in range(7):

        @pl.when(job != m)
        def _():
            job_copy(m).start()

    for kind in range(2):
        count = (48, 16)[kind]

        @pl.when((job >= 3 * kind) & (job < 3 + 4 * kind))
        def _():
            if kind == 1:
                rows[:, 16:48] = jnp.zeros((8, 32, D), BF16)
                rows[source, 0:16] = short_ref[job - 3]
            else:
                rows[source] = tall_ref[job]
            for k in range(1, 8):
                other = (source + k) % 8
                arrival = rows.at[other, pl.ds(0, count)]
                remote(
                    arrival, arrival, job_sems.at[0, 0], job_sems.at[1, other], square(other)
                ).wait_recv()

    @pl.when(job < 7)
    def _():
        flat = rows[...].reshape(384, D)
        gram[...] = inner_rows(flat, flat)
        for index, (i, j) in enumerate(BLOCKS):
            gram_out[index // 16, index % 16] = half(
                gram[128 * i : 128 * i + 128, 128 * j : 128 * j + 128]
            )
        gram_out[1, 12:16] = jnp.zeros((4, 128, 128), BF16)
        twin_copy = copy(gram_out.at[1 - core], gram_twin, twin_sems, 0, twin)
        twin_copy.start()
        twin_copy.wait()
        gram_half_sum[...] = half(gram_out[core].astype(F32) + gram_twin[...].astype(F32))

        def sum_copy(k):
            peer = (member + k) % 8
            return copy(
                gram_half_sum.at[pl.ds(2 * peer, 2)], gram_in.at[k], sum_sems, k, group(peer)
            )

        for k in range(1, 8):
            sum_copy(k).start()
        total = gram_half_sum[pl.ds(2 * member, 2)].astype(F32)
        for k in range(1, 8):
            sum_copy(k).wait_recv()
            total = total + gram_in[k].astype(F32)
        gram_all[core, pl.ds(2 * member, 2)] = half(total)

        def all_copy(k, owner):
            ref = gram_all.at[core, pl.ds(2 * owner, 2)]
            return copy(ref, ref, all_sems, k, group((member + k) % 8))

        for k in range(1, 8):
            all_copy(k, member).start()
        for k in range(1, 8):
            all_copy(k, (member + 8 - k) % 8).wait_recv()
        last_copy = copy(gram_all.at[core], gram_all.at[core], twin_sems, 1, twin)
        last_copy.start()
        last_copy.wait()

        eye = lax.broadcasted_iota(jnp.int32, (128, 128), 0) == lax.broadcasted_iota(
            jnp.int32, (128, 128), 1
        )
        trace = 0.0
        for index, (i, j) in enumerate(BLOCKS):
            block = gram_all[index // 16, index % 16].astype(F32)
            gram[128 * i : 128 * i + 128, 128 * j : 128 * j + 128] = block
            if i == j:
                trace = trace + jnp.sum(jnp.where(eye, block, 0.0))
            else:
                gram[128 * j : 128 * j + 128, 128 * i : 128 * i + 128] = block.T
        inverse = 1.0 / (jnp.sqrt(jnp.full((1, 1), trace)) + 1e-07)
        moved = newton_schulz(
            gram[...] * (inverse * inverse), rows[...].reshape(384, D).astype(F32) * inverse
        )
        back[...] = moved.reshape(8, 48, D)
        for k in range(1, 8):
            sum_copy(k).wait_send()
            all_copy(k, member).wait_send()

    for m in range(7):

        @pl.when(job == m)
        def _():
            copies = []
            for k in range(1, 8):
                other = (source + k) % 8
                copies.append(
                    remote(
                        back.at[other, pl.ds(0, JOB_ROWS[m])],
                        mine(m, tall_got, short_got),
                        back_sems.at[0, k],
                        back_sems.at[1, m],
                        square(other),
                    )
                )
            for item in copies:
                item.start()
            if m < 3:
                tall_got[m] = back[source]
            else:
                short_got[m - 3] = back[source, 0:16]
            for item in copies:
                item.wait_send()

    for m in range(7):

        @pl.when(job != m)
        def _():
            arrival = mine(m, tall_got, short_got)
            remote(arrival, arrival, back_sems.at[0, 0], back_sems.at[1, m], square(m)).wait_recv()
            job_copy(m).wait_send()

    tall_out_ref[...] = tall_got[...]
    short_out_ref[...] = short_got[...]


def muon(grads, priors, masters, vectors):
    vmem = pl.BlockSpec(memory_space=pltpu.VMEM)
    tall, short = pl.pallas_call(
        muon_kernel,
        out_shape=(
            jax.ShapeDtypeStruct((3, 48, D), BF16),
            jax.ShapeDtypeStruct((4, 16, D), BF16),
        ),
        in_specs=[vmem] * 8,
        out_specs=[vmem] * 2,
        scratch_shapes=[
            *(pltpu.VMEM(value.shape, F32) for value in priors),
            pltpu.VMEM((3, 48, D), F32),
            pltpu.VMEM((4, 16, D), F32),
            pltpu.VMEM((3, 48, D), BF16),
            pltpu.VMEM((4, 16, D), BF16),
            pltpu.VMEM((8, 48, D), BF16),
            pltpu.VMEM((2, 16, 128, 128), BF16),
            pltpu.VMEM((16, 128, 128), BF16),
            pltpu.VMEM((16, 128, 128), BF16),
            pltpu.VMEM((8, 2, 128, 128), BF16),
            pltpu.VMEM((2, 16, 128, 128), BF16),
            pltpu.VMEM((D, D), F32),
            pltpu.VMEM((8, 48, D), BF16),
            pltpu.VMEM((3, 48, D), BF16),
            pltpu.VMEM((4, 16, D), BF16),
            pltpu.SemaphoreType.DMA((2, 8)),
            pltpu.SemaphoreType.DMA((2, 2)),
            pltpu.SemaphoreType.DMA((2, 8)),
            pltpu.SemaphoreType.DMA((2, 8)),
            pltpu.SemaphoreType.DMA((2, 8)),
        ],
        compiler_params=pltpu.CompilerParams(
            collective_id=3, has_side_effects=True, vmem_limit_bytes=58 * 2**20
        ),
    )(grads, *priors)
    outs = [*priors, *masters, *vectors]
    return pl.pallas_call(
        update_kernel,
        out_shape=[jax.ShapeDtypeStruct(value.shape, F32) for value in outs],
        in_specs=[vmem] * 20,
        out_specs=[vmem] * 17,
    )(grads, tall, short, *outs)


def body(
    inputs,
    cotangent,
    lengths,
    query_weight,
    key_weight,
    value_weight,
    out_weight,
    gate_weight,
    up_weight,
    down_weight,
    vectors,
    query_prior,
    key_prior,
    value_prior,
    out_prior,
    gate_prior,
    up_prior,
    down_prior,
    first_prior,
    second_prior,
):
    chip = lax.axis_index("dp")
    core = lax.axis_index("narrow")
    narrow_rows = jnp.concatenate(
        [key_weight, value_weight, jnp.pad(vectors[None], ((0, 6), (0, 128 - vectors.shape[0])))],
        axis=1,
    )
    weights = (
        gate_weight.T, up_weight.T, down_weight, query_weight, out_weight, narrow_rows
    )
    own_lengths = lax.dynamic_slice_in_dim(lengths, chip * 2 + core, 1, axis=1)
    own_lengths = jnp.broadcast_to(own_lengths, (2, 128))
    block_output, input_grad, grads = layer(weights, inputs[:, 0], cotangent[:, 0], own_lengths)
    results = muon(
        grads,
        (gate_prior.T, up_prior.T, down_prior, query_prior, out_prior, key_prior, value_prior),
        (gate_weight.T, up_weight.T, down_weight, query_weight, out_weight, key_weight, value_weight),
        (first_prior[None], second_prior[None], vectors[None]),
    )

    def ordered(gate, up, down, query, out, key, value):
        return query, key, value, out, gate.T, up.T, down

    return (
        block_output,
        input_grad,
        *ordered(*results[:7]),
        *ordered(*results[7:14]),
        *(value[0] for value in results[14:]),
    )


def solution(mesh):
    placed = (
        P(None, ("dp", "narrow"), None, None),
        P(None, ("dp", "narrow"), None, None),
        P(),
        P(("dp", "narrow"), None),
        P(("dp", "narrow"), None),
        P(("dp", "narrow"), None),
        P(("dp", "narrow"), None),
        P(None, ("dp", "narrow")),
        P(None, ("dp", "narrow")),
        P(("dp", "narrow"), None),
        P(("dp", "narrow")),
        P(("dp", "narrow"), None),
        P(("dp", "narrow"), None),
        P(("dp", "narrow"), None),
        P(("dp", "narrow"), None),
        P(None, ("dp", "narrow")),
        P(None, ("dp", "narrow")),
        P(("dp", "narrow"), None),
        P(("dp", "narrow")),
        P(("dp", "narrow")),
    )
    return jax.shard_map(
        body,
        mesh=mesh,
        in_specs=placed,
        out_specs=(
            P(None, ("dp", "narrow"), None, None),
            P(None, ("dp", "narrow"), None, None),
            P(("dp", "narrow"), None),
            P(("dp", "narrow"), None),
            P(("dp", "narrow"), None),
            P(("dp", "narrow"), None),
            P(None, ("dp", "narrow")),
            P(None, ("dp", "narrow")),
            P(("dp", "narrow"), None),
            P(("dp", "narrow"), None),
            P(("dp", "narrow"), None),
            P(("dp", "narrow"), None),
            P(("dp", "narrow"), None),
            P(None, ("dp", "narrow")),
            P(None, ("dp", "narrow")),
            P(("dp", "narrow"), None),
            P(("dp", "narrow")),
            P(("dp", "narrow")),
            P(("dp", "narrow")),
        ),
        check_vma=False,
    )
```

```python
import math

import jax
import jax.numpy as jnp
import numpy as np
from jax import lax
from jax.experimental import pallas as pl
from jax.experimental.pallas import tpu as pltpu
from jax.sharding import PartitionSpec as P

D = 896
FF = 4864
HEADS = 14
KV_HEADS = 2
HEAD = 64
STEP = 10


NORM_EPSILON = 1e-06
ROPE_BASE = 1000000.0
MOMENTUM = 0.95
NEWTON_A = 3.4445
NEWTON_B = -4.775
NEWTON_C = 2.0315
MUON_RATE = 0.4
MUON_DECAY = 0.1
ADAM_RATE = 0.5
ADAM_DECAY = 0.01
BETA_FIRST = 0.9
BETA_SECOND = 0.999
ADAM_EPSILON = 1e-08
MASKED = -1e30


def product(left, right):
    return jnp.dot(left, right, preferred_element_type=jnp.float32)


def inner_rows(left, right):
    return lax.dot_general(
        left, right, (((0,), (0,)), ((), ())), preferred_element_type=jnp.float32
    )


def outer_cols(left, right):
    return lax.dot_general(
        left, right, (((1,), (1,)), ((), ())), preferred_element_type=jnp.float32
    )


def norm_back(grad, normed, scale):
    return scale * (grad - normed * jnp.mean(grad * normed, axis=-1, keepdims=True))


def half(value):
    return value.astype(jnp.bfloat16)


MESH = pl.DeviceIdType.MESH
TOKENS = 256
FULL = (0, 4)
BF16 = jnp.bfloat16
F32 = jnp.float32
CHUNK = 48
PARTS = (
    (0, 0, CHUNK, (2, 1, 0), False, (0, D)),
    (0, CHUNK, CHUNK, (1, 0, 2), False, (0, D)),
    (1, 0, CHUNK, (0, 2, 1), True, (0, D)),
    (2, 0, 16, (2, 1, 0), True, (0, D)),
    (2, 16, 16, (1, 0, 2), True, (0, 512)),
    (2, 16, 16, (0, 2, 1), True, (512, 384)),
    (2, 32, 16, (0, 2, 1), True, (0, 384)),
    (0, 0, CHUNK, (2, 1, 0), False, (0, 768)),
    (0, CHUNK, CHUNK, (1, 0, 2), False, (0, 768)),
    (0, 0, CHUNK, (2, 0, 1), False, (768, 128)),
    (0, CHUNK, CHUNK, (0, 2, 1), False, (768, 128)),
)
WIDE = (0, 1, 2)
THIN = (3, 4, 5, 6)
MAIN, SIDE = (7, 8, 2), (9, 10)
SUMMED = MAIN + SIDE


def my_coords():
    dp = lax.axis_index("dp")
    return (dp // 16, (dp // 4) % 4, dp % 4), lax.axis_index("narrow")


def device_of(coords, core):
    return (coords[0] * 16 + coords[1] * 4 + coords[2], core)


def shifted(coords, axis, by):
    out = list(coords)
    out[axis] = (coords[axis] + by) % 4
    return tuple(out)


def facing(coords):
    return (coords[0], coords[1], 3 - coords[2])


def greet(coords, core):
    barrier = pltpu.get_barrier_semaphore()
    for axis in range(3):
        for by in (1, 2, 3):
            pl.semaphore_signal(
                barrier, inc=1, device_id=device_of(shifted(coords, axis, by), core), device_id_type=MESH
            )
    pl.semaphore_signal(barrier, inc=1, device_id=device_of(coords, 1 - core), device_id_type=MESH)
    pl.semaphore_wait(barrier, 10)


def remote(src, dst, send_sem, recv_sem, device):
    return pltpu.make_async_remote_copy(
        src_ref=src,
        dst_ref=dst,
        send_sem=send_sem,
        recv_sem=recv_sem,
        device_id=device,
        device_id_type=MESH,
    )


def place_of(part, spec):
    _, first, rows, _, shared, columns = PARTS[part]
    index = [pl.ds(*s) if isinstance(s, tuple) else s for s in spec[:2]]
    s = spec[2]
    if isinstance(s, tuple):
        index.append(pl.ds(s[0] // 2, s[1] // 2))
        index += [] if shared else [pl.ds(0, 2)]
    else:
        index.append(s // 2)
        index += [] if shared else [s % 2]
    return (*index, pl.ds(first, rows), pl.ds(*columns))


def shape_of(part, spec):
    return tuple(entry.size for entry in place_of(part, spec) if isinstance(entry, pl.Slice))


class Plan:
    def __init__(self, part, stage, coords, axis, spec, split):
        self.coords, self.axis, self.spec, self.split = coords, axis, spec, split
        self.exchange = PARTS[part][4] and axis == 2
        self.direct = not self.exchange and stage == 0

    def at(self, by):
        return shifted(self.coords, self.axis, by)

    def whole(self, by):
        spec = list(self.spec)
        spec[self.axis] = (self.coords[self.axis] + by) % 4
        return tuple(spec)

    def pieces(self, by):
        out = []
        for h in range(2):
            spec = list(self.whole(by))
            spec[self.split] = (2 * h, 2)
            out.append(tuple(spec))
        return out

    def facing(self):
        return (*self.spec[:2], 3 - self.coords[2])

    def own(self):
        return self.spec


def plan_of(part, stage, coords):
    order = PARTS[part][3]
    spec = tuple(FULL if k in order[:stage] else coords[k] for k in range(3))
    return Plan(part, stage, coords, order[stage], spec, order[stage - 1] if stage else None)


class Gather:
    def __init__(self, arrays, coords, core, send_sems, recv_sems):
        self.arrays, self.coords, self.core = arrays, coords, core
        self.send_sems, self.recv_sems = send_sems, recv_sems

    def copy(self, part, phase, slot, piece, coords):
        array, prefix = self.arrays[PARTS[part][0]]
        ref = array.at[(*prefix, *place_of(part, piece))]
        sems = (self.send_sems.at[part, phase, slot], self.recv_sems.at[part, phase, slot])
        return remote(ref, ref, *sems, device_of(coords, self.core))

    def send(self, *args):
        self.copy(*args).start()

    def neighbours(self, plan):
        return shifted(self.coords, plan.axis, 1), shifted(self.coords, plan.axis, 3)

    def start(self, parts, phase):
        for part in parts:
            plan = plan_of(part, phase, self.coords)
            if plan.exchange:
                self.send(part, phase, 0, plan.own(), facing(self.coords))
                continue
            if plan.direct:
                for by in (1, 3, 2):
                    self.send(part, phase, by, plan.own(), plan.at(by))
                continue
            right, left = self.neighbours(plan)
            first, second = plan.pieces(0)
            self.send(part, phase, 0, first, right)
            self.send(part, phase, 1, second, left)
            self.send(part, phase, 2, second, right)
            self.send(part, phase, 3, first, left)

    def forward(self, parts, phase):
        for part in parts:
            plan = plan_of(part, phase, self.coords)
            if plan.exchange or plan.direct:
                continue
            right, left = self.neighbours(plan)
            piece = plan.pieces(3)[0]
            self.copy(part, phase, 0, piece, right).wait_recv()
            self.send(part, phase, 4, piece, right)
            piece = plan.pieces(1)[1]
            self.copy(part, phase, 1, piece, left).wait_recv()
            self.send(part, phase, 5, piece, left)

    def near(self, parts, phase):
        for part in parts:
            plan = plan_of(part, phase, self.coords)
            if plan.exchange:
                self.copy(part, phase, 0, plan.facing(), facing(self.coords)).wait_recv()
                continue
            if plan.direct:
                for by in (1, 3):
                    self.copy(part, phase, by, plan.whole(4 - by), plan.at(by)).wait_recv()
                continue
            right, left = self.neighbours(plan)
            self.copy(part, phase, 2, plan.pieces(3)[1], right).wait_recv()
            self.copy(part, phase, 3, plan.pieces(1)[0], left).wait_recv()

    def far(self, parts, phase):
        for part in parts:
            plan = plan_of(part, phase, self.coords)
            if plan.exchange:
                continue
            if plan.direct:
                self.copy(part, phase, 2, plan.whole(2), plan.at(2)).wait_recv()
                continue
            right, left = self.neighbours(plan)
            self.copy(part, phase, 4, plan.pieces(2)[0], right).wait_recv()
            self.copy(part, phase, 5, plan.pieces(2)[1], left).wait_recv()

    def finish(self, parts, phase):
        self.near(parts, phase)
        self.far(parts, phase)

    def drain(self):
        for part in WIDE + THIN:
            for phase in range(3):
                plan = plan_of(part, phase, self.coords)
                if plan.exchange:
                    self.copy(part, phase, 0, plan.own(), facing(self.coords)).wait_send()
                    continue
                if plan.direct:
                    for by in (1, 3, 2):
                        self.copy(part, phase, by, plan.own(), plan.at(by)).wait_send()
                    continue
                right, _ = self.neighbours(plan)
                for slot, which in enumerate((0, 1, 1, 0, 0, 1)):
                    self.copy(part, phase, slot, plan.pieces(0)[which], right).wait_send()


def each_block(shape, body):
    lead = shape[:-2]
    count = math.prod(lead)
    if count == 1:
        body((0,) * len(lead))
        return

    def step(k, carry):
        index = []
        for n in reversed(lead):
            index.append(k % n)
            k = k // n
        body(tuple(reversed(index)))
        return carry

    lax.fori_loop(0, count, step, 0)


class Scatter:
    def __init__(self, arrays, coords, core, buffers, send_sems, recv_sems, done):
        self.arrays, self.coords, self.core, self.done = arrays, coords, core, done
        self.buffers, self.send_sems, self.recv_sems = buffers, send_sems, recv_sems

    def copy(self, part, phase, slot, piece, coords):
        array, prefix = self.arrays[PARTS[part][0]]
        ref = array.at[(*prefix, *place_of(part, piece))]
        sems = (self.send_sems.at[part, phase, slot], self.recv_sems.at[part, phase, slot])
        return remote(ref, self.buffers[part, phase][slot], *sems, device_of(coords, self.core))

    def send(self, *args):
        if args[:3] not in self.done:
            self.copy(*args).start()

    def arrive(self, *args):
        if args[:3] not in self.done:
            self.copy(*args).wait_recv()

    def add(self, part, phase, piece, *slots):
        sources = [self.buffers[part, phase][slot] for slot in slots]
        base = place_of(part, piece)
        array, prefix = self.arrays[PARTS[part][0]]

        def one(index):
            spot, position = [], 0
            for entry in base[:-2]:
                if isinstance(entry, pl.Slice):
                    spot.append(entry.start + index[position])
                    position += 1
                else:
                    spot.append(entry)
            spot = (*prefix, *spot, *base[-2:])
            value = array[spot].astype(F32)
            for source in sources:
                value = value + source[(*index, slice(None), slice(None))].astype(F32)
            array[spot] = half(value)

        each_block(shape_of(part, piece), one)

    def neighbours(self, plan):
        return shifted(self.coords, plan.axis, 1), shifted(self.coords, plan.axis, 3)

    def start_far(self, parts, phase):
        for part in parts:
            plan = plan_of(part, phase, self.coords)
            if plan.exchange or plan.direct:
                continue
            right, left = self.neighbours(plan)
            self.send(part, phase, 0, plan.pieces(2)[0], right)
            self.send(part, phase, 1, plan.pieces(2)[1], left)

    def start_near(self, parts, phase):
        for part in parts:
            plan = plan_of(part, phase, self.coords)
            if plan.exchange:
                self.send(part, phase, 0, plan.facing(), facing(self.coords))
                continue
            if plan.direct:
                for by in (1, 3, 2):
                    self.send(part, phase, by, plan.whole(by), plan.at(by))
                continue
            right, left = self.neighbours(plan)
            self.send(part, phase, 2, plan.pieces(1)[1], right)
            self.send(part, phase, 3, plan.pieces(3)[0], left)

    def start(self, parts, phase):
        self.start_far(parts, phase)
        self.start_near(parts, phase)

    def forward(self, parts, phase):
        for part in parts:
            plan = plan_of(part, phase, self.coords)
            if plan.exchange or plan.direct:
                continue
            right, left = self.neighbours(plan)
            self.arrive(part, phase, 0, plan.pieces(2)[0], right)
            self.add(part, phase, plan.pieces(1)[0], 0)
            self.send(part, phase, 4, plan.pieces(1)[0], right)
            self.arrive(part, phase, 1, plan.pieces(2)[1], left)
            self.add(part, phase, plan.pieces(3)[1], 1)
            self.send(part, phase, 5, plan.pieces(3)[1], left)

    def finish(self, parts, phase):
        for part in parts:
            plan = plan_of(part, phase, self.coords)
            if plan.exchange:
                self.arrive(part, phase, 0, plan.facing(), facing(self.coords))
                self.add(part, phase, plan.own(), 0)
                continue
            if plan.direct:
                for by in (1, 3, 2):
                    self.arrive(part, phase, by, plan.whole(by), plan.at(by))
                self.add(part, phase, plan.own(), 1, 3, 2)
                continue
            right, left = self.neighbours(plan)
            self.arrive(part, phase, 3, plan.pieces(3)[0], left)
            self.arrive(part, phase, 4, plan.pieces(1)[0], right)
            self.add(part, phase, plan.pieces(0)[0], 4, 3)
            self.arrive(part, phase, 2, plan.pieces(1)[1], right)
            self.arrive(part, phase, 5, plan.pieces(3)[1], left)
            self.add(part, phase, plan.pieces(0)[1], 2, 5)

    def drain(self):
        for part in SUMMED + THIN:
            for phase in range(3):
                plan = plan_of(part, phase, self.coords)
                if plan.exchange:
                    self.copy(part, phase, 0, plan.own(), facing(self.coords)).wait_send()
                    continue
                if plan.direct:
                    for by in (1, 3, 2):
                        self.copy(part, phase, by, plan.whole(by), plan.at(by)).wait_send()
                    continue
                right, _ = self.neighbours(plan)
                for slot, which in enumerate((0, 1, 1, 0, 0, 1)):
                    if (part, phase, slot) in self.done:
                        continue
                    self.copy(part, phase, slot, plan.pieces(0)[which], right).wait_send()


EARLY = tuple((part, 2, slot) for part in MAIN for slot in (2, 3))


def scatter_buffer_shapes():
    out = []
    for part in SUMMED + THIN:
        for phase in range(3):
            plan = plan_of(part, phase, (0, 0, 0))
            if plan.exchange:
                shapes = [shape_of(part, plan.own())]
            elif plan.direct:
                shapes = [None] + [shape_of(part, plan.own())] * 3
            else:
                first, second = (shape_of(part, piece) for piece in plan.pieces(0))
                shapes = [first, second, second, first, first, second]
            out.append(((part, phase), shapes))
    return out


SCALE = HEAD ** (-0.5)


def turn(values, sign):
    lane = lax.broadcasted_iota(jnp.int32, values.shape, 1)
    ahead = pltpu.roll(values, 96, 1)
    behind = pltpu.roll(values, 32, 1)
    return jnp.where(lane & 32 == 0, sign * ahead, -sign * behind)


def tiles_of(values):
    return [values[:, 128 * t : 128 * t + 128] for t in range(values.shape[1] // 128)]


def rotated(values, cosine, sine):
    return jnp.concatenate(
        [tile * cosine + turn(tile, -1.0) * sine for tile in tiles_of(values)], axis=1
    )


def rotated_back(values, cosine, sine):
    return jnp.concatenate(
        [tile * cosine + turn(tile * sine, 1.0) for tile in tiles_of(values)], axis=1
    )


def low_lanes(shape):
    return lax.broadcasted_iota(jnp.int32, shape, 1) < HEAD


def paired(both):
    swapped = pltpu.roll(both, 64, 1)
    low = low_lanes(both.shape)
    even = [half(jnp.where(low, v, 0.0)) for v in (both, swapped)]
    odd = [half(jnp.where(low, 0.0, v)) for v in (swapped, both)]
    kinds = [jnp.concatenate([even[a], odd[b]]) for a, b in ((0, 0), (0, 1), (1, 1))]
    return [kinds[0]] * 3 + [kinds[1]] + [kinds[2]] * 3


def gathered_place():
    row = lax.broadcasted_iota(jnp.int32, (1024, D), 0)
    feature = lax.broadcasted_iota(jnp.int32, (1024, D), 1)
    slot = row & 15
    odd = (slot >= 7).astype(jnp.int32)
    device = (((row >> 4) & 31) * 2 + odd) * 2 + (row >> 9)
    source = jnp.where(slot < 14, 7 * device + slot - 7 * odd, -1)
    return half((source == feature).astype(jnp.float32))


def vector_maps():
    device = lax.broadcasted_iota(jnp.int32, (128, 1024), 0)
    row = lax.broadcasted_iota(jnp.int32, (128, 1024), 1)
    target = (device & 1) * 512 + (device >> 2) * 16 + ((device >> 1) & 1) * 7
    pick = half((row == target).astype(jnp.float32))
    start = lax.broadcasted_iota(jnp.int32, (128, 2944), 0) * 23
    entry = lax.broadcasted_iota(jnp.int32, (128, 2944), 1)
    owner = half(((entry >= start) & (entry < start + 23)).astype(jnp.float32))
    return pick, owner


def slot_mask(slots):
    return lax.broadcasted_iota(jnp.int32, (128, 2944), 0) == slots


def live_tokens(len_ref):
    token = lax.broadcasted_iota(jnp.int32, (128, 1), 0)
    return jnp.concatenate([(token < len_ref[b : b + 1, 0:1]).astype(F32) for b in range(2)])


def attention_forward(
    x_ref, rest_ref, len_ref, cos_ref, sin_ref, slot_ref,
    middle_ref, h1p_ref, q_ref, k_ref, v_ref, mixed_ref, probs_ref, vector_ref,
):
    place = gathered_place()
    pick, owner = vector_maps()
    stored = rest_ref[:, :, :, :, 32:48, 256:384].reshape(1024, 128)
    by_device = half(product(pick, stored))
    spread = inner_rows(by_device, owner)
    vector = jnp.sum(jnp.where(slot_mask(slot_ref[...]), spread, 0.0), axis=0, keepdims=True)
    vector_ref[...] = vector
    first_gain, second_gain = vector[:, :D], vector[:, D : 2 * D]
    query_bias, narrow_bias = vector[:, 2 * D : 3 * D], vector[:, 3 * D :]
    cosine, sine = cos_ref[...], sin_ref[...]
    inputs = x_ref[...].astype(jnp.float32)
    first_scale = lax.rsqrt(jnp.mean(inputs * inputs, axis=-1, keepdims=True) + NORM_EPSILON)
    normed = half(inputs * first_scale * first_gain)
    placed = half(outer_cols(normed, place))
    h1p_ref[...] = placed
    queries = product(placed, rest_ref[:, :, :, :, 0:16, :].reshape(1024, D)) + query_bias
    narrow = product(placed, rest_ref[:, :, :, :, 32:48, 0:256].reshape(1024, 256)) + narrow_bias
    q_ref[...] = half(rotated(queries, cosine, sine))
    keys = rotated(narrow[:, 0:128], cosine, sine)
    k_ref[...] = half(keys)
    values = narrow[:, 128:256]
    v_ref[...] = half(values)
    position = lax.broadcasted_iota(jnp.int32, (128, 256), 0)
    other = lax.broadcasted_iota(jnp.int32, (128, 256), 1) & 127
    causal = other <= position
    rows = []
    for b in range(2):
        here = slice(128 * b, 128 * b + 128)
        length = len_ref[b : b + 1, :]
        allowed = causal & (other < jnp.concatenate([length, length], axis=1))
        key_tiles = paired(keys[here])
        value_tiles = paired(values[here])
        tiles = []
        for t in range(7):
            scores = outer_cols(q_ref[here, 128 * t : 128 * t + 128], key_tiles[t])
            scores = jnp.where(allowed, scores * SCALE, MASKED)
            parts = []
            for part in tiles_of(scores):
                shifted = jnp.exp(part - jnp.max(part, axis=-1, keepdims=True))
                parts.append(shifted / jnp.sum(shifted, axis=-1, keepdims=True))
            probs = jnp.concatenate(parts, axis=1)
            probs_ref[b, t] = probs
            tiles.append(half(product(half(probs), value_tiles[t])))
        rows.append(jnp.concatenate(tiles, axis=1))
    mixed = half(outer_cols(jnp.concatenate(rows), place))
    mixed_ref[...] = mixed
    middle = inputs + product(mixed, rest_ref[:, :, :, :, 16:32, :].reshape(1024, D))
    middle_ref[...] = middle
    second_scale = lax.rsqrt(jnp.mean(middle * middle, axis=-1, keepdims=True) + NORM_EPSILON)
    return half(middle * second_scale * second_gain)


def mlp_tile(weights, h, e, sums):
    lead = weights.shape[:-2]
    units = 16 * math.prod(lead)
    gate_w, up_w, down_w = (
        weights[..., 16 * k : 16 * k + 16, :].reshape(units, D) for k in range(3)
    )
    gate = outer_cols(h, gate_w)
    up = outer_cols(h, up_w)
    sigma = jax.nn.sigmoid(gate)
    silu = gate * sigma
    hidden = half(silu * up)
    grad_hidden = outer_cols(e, down_w)
    sums[0] += product(hidden, down_w).reshape(2, TOKENS, D)
    grad_gate = half(grad_hidden * up * sigma * (1.0 + gate * (1.0 - sigma)))
    grad_up = half(grad_hidden * silu)
    sums[1] += (product(grad_gate, gate_w) + product(grad_up, up_w)).reshape(2, TOKENS, D)
    grads = (inner_rows(grad_gate, h), inner_rows(grad_up, h), inner_rows(hidden, e))
    return [half(grad).reshape(*lead, 16, D) for grad in grads]


KEPT = 17


def gather_kernel(
    gate_ref, up_ref, down_ref, query_ref, out_ref, narrow_ref,
    x_ref, cot_ref, len_ref, cos_ref, sin_ref, slot_ref, *refs,
):
    coords, core = my_coords()
    z, y, x = coords
    pair, odd = x // 2, x % 2
    results, (grad_wide_ref, grad_shared_ref, rest_ref) = refs[:KEPT], refs[KEPT : KEPT + 3]
    held = refs[KEPT + 3 : 2 * KEPT + 1]
    (
        wide, shared, rest, stage0, stage1, stage2, h_all, e_all, sums, parcel, tail, tail_own, tail_wide,
        local_sems, send_sems, recv_sems, twin_sems, store_sems, early_sems, kept_sems,
    ) = refs[2 * KEPT + 1 :]
    middle_ref, e_ref, h1p_ref, q_ref, k_ref, v_ref, mixed_ref, probs_ref, vector_ref = held[:9]
    early = held[9:]
    kept = [*held[:9], sums.at[:, core], parcel, *early]

    def keep(first, last):
        return [
            pltpu.make_async_copy(kept[n], results[n], kept_sems.at[n]) for n in range(first, last)
        ]

    units = (gate_ref, up_ref, down_ref)
    for n, ref in enumerate(units):
        for k in range(2):
            wide[z, y, pair, odd, CHUNK * k + 16 * n : CHUNK * k + 16 * n + 16] = half(
                ref[16 * k : 16 * k + 16]
            )
    tail_wide[...] = jnp.zeros_like(tail_wide)
    for parity in range(2):

        @pl.when(odd == parity)
        def _():
            for n, ref in enumerate(units):
                start = 16 * n + 6 * parity
                tail_wide[start : start + 6] = ref[32:38]
            for n, ref in enumerate((query_ref, out_ref)):
                start = CHUNK + 16 * n + 7 * parity
                tail_wide[start : start + 7] = ref[...]
            start = CHUNK + 32 + 7 * parity
            tail_wide[start : start + 7, 0:384] = narrow_ref[...]

    tail_own[...] = half(tail_wide[...])
    greet(coords, core)
    twin = device_of(coords, 1 - core)

    def to_twin(src, dst, slot):
        return remote(src, dst, twin_sems.at[0, slot], twin_sems.at[1, slot], twin)

    gather = Gather(((wide, ()), (shared, ()), (rest, (core,))), coords, core, send_sems, recv_sems)
    partner = device_of((z, y, x + 1 - 2 * odd), core)
    tail_copy = remote(tail_own, tail, twin_sems.at[0, 4], twin_sems.at[1, 4], partner)
    tail_copy.start()
    gather.start((0, 1), 0)
    e_ref[...] = half(cot_ref[...].astype(F32) * live_tokens(len_ref))
    e_all[core] = e_ref[...]
    e_copy = to_twin(e_ref, e_all.at[core], 0)
    e_copy.start()
    tail_copy.wait()
    both = half(tail_wide[...] + tail[...].astype(F32))
    shared[z, y, pair] = both[:CHUNK]
    rest[core, z, y, pair] = both[CHUNK:]
    gather.start(THIN, 0)
    gather.start((2,), 0)
    gather.forward(THIN, 0)
    gather.finish(THIN, 0)
    gather.start(THIN, 1)
    gather.forward(WIDE, 0)
    gather.forward(THIN, 1)
    gather.finish(THIN, 1)
    gather.start(THIN, 2)
    gather.finish(WIDE, 0)
    gather.start(WIDE, 1)
    gather.forward(THIN, 2)
    gather.finish(THIN, 2)
    rest_copy = to_twin(rest.at[core], rest.at[core], 1)
    rest_copy.start()
    gather.forward(WIDE, 1)
    gather.finish(WIDE, 1)
    gather.start(WIDE, 2)
    rest_copy.wait()
    rest_store = pltpu.make_async_copy(rest, rest_ref, local_sems.at[0])
    rest_store.start()
    h_all[core] = attention_forward(
        x_ref, rest, len_ref, cos_ref, sin_ref, slot_ref,
        middle_ref, h1p_ref, q_ref, k_ref, v_ref, mixed_ref, probs_ref, vector_ref,
    )
    h_copy = to_twin(h_all.at[core], h_all.at[core], 2)
    h_copy.start()
    for copy in keep(0, 9):
        copy.start()
    sums[...] = jnp.zeros_like(sums)
    e_copy.wait()
    h_copy.wait()
    stages = (stage0, stage1, stage2)

    def early_copy(t, slot):
        axis = PARTS[t][3][2]
        which = 3 - slot
        place = [slice(None)] * (len(stages[t].shape) - 1)
        place[1 if t == 2 else 0] = pl.ds(which, 1) if t == 2 else pl.ds(2 * which, 2)
        place[-1] = pl.ds(*PARTS[MAIN[t]][5])
        return remote(
            stages[t].at[(slot - 1) % 2].at[tuple(place)],
            early[2 * t + slot - 2],
            early_sems.at[0, t, slot - 2],
            early_sems.at[1, t, slot - 2],
            device_of(shifted(coords, axis, 1 if slot == 2 else 3), core),
        )

    def tile_places(j):
        return (
            (wide, grad_wide_ref, (j, slice(None), slice(None), slice(None), pl.ds(0, CHUNK))),
            (wide, grad_wide_ref, (slice(None), slice(None), j // 2, j % 2, pl.ds(CHUNK, CHUNK))),
            (shared, grad_shared_ref, (slice(None), j, slice(None), pl.ds(0, CHUNK))),
        )

    def step(k, carry):
        @pl.when(k == 1)
        def _():
            gather.near(WIDE, 2)

        @pl.when(k == 3)
        def _():
            gather.far(WIDE, 2)

        offset = jnp.where(k < 2, k, 5 - k)
        h = h_all[...].reshape(2 * TOKENS, D)
        e = e_all[...].reshape(2 * TOKENS, D)
        for t, axis in enumerate((0, 2, 1)):
            j = (coords[axis] + offset) % 4
            source, target, index = tile_places(j)[t]
            grads = mlp_tile(source[(*index, slice(None))], h, e, sums)
            copy = pltpu.make_async_copy(
                stages[t].at[k % 2], target.at[(*index, slice(None))], store_sems.at[t, k % 2]
            )

            @pl.when(k > 1)
            def _():
                copy.wait()

            @pl.when(k == 3)
            def _():
                early_copy(t, 2).wait_send()

            for place, grad in enumerate(grads):
                stages[t][k % 2, ..., 16 * place : 16 * place + 16, :] = grad
            copy.start()

            @pl.when(k == 1)
            def _():
                early_copy(t, 2).start()

            @pl.when(k == 2)
            def _():
                early_copy(t, 3).start()

        @pl.when(k == 0)
        def _():
            gather.forward(WIDE, 2)

        return carry

    lax.fori_loop(0, 4, step, 0)
    parcel[...] = half(sums[:, 1 - core])
    for copy in keep(9, 11):
        copy.start()
    for t in range(3):
        _, target, index = tile_places(0)[t]
        for which in range(2):
            pltpu.make_async_copy(
                stages[t].at[which], target.at[(*index, slice(None))], store_sems.at[t, which]
            ).wait()
        early_copy(t, 3).wait_send()
        early_copy(t, 2).wait_recv()
        early_copy(t, 3).wait_recv()
        for copy in keep(11 + 2 * t, 13 + 2 * t):
            copy.start()
    rest_store.wait()
    for copy in keep(0, KEPT):
        copy.wait()
    gather.drain()


def attention_backward(
    between, x_ref, e_ref, rest_ref, cos_ref, sin_ref, slot_ref,
    middle_ref, h1p_ref, q_ref, k_ref, v_ref, mixed_ref, probs_ref, vector_ref, dh2_ref,
    input_grad_ref, grad_ref,
):
    place = gathered_place()
    pick, owner = vector_maps()
    vector = vector_ref[...]
    first_gain, second_gain = vector[:, :D], vector[:, D : 2 * D]
    cosine, sine = cos_ref[...], sin_ref[...]
    middle = middle_ref[...]
    second_scale = lax.rsqrt(jnp.mean(middle * middle, axis=-1, keepdims=True) + NORM_EPSILON)
    second_normed = middle * second_scale
    dh2 = dh2_ref[...]
    second_gain_grad = jnp.sum(dh2 * second_normed, axis=0, keepdims=True)
    grad_middle = e_ref[...].astype(jnp.float32) + norm_back(
        dh2 * second_gain, second_normed, second_scale
    )
    branch = half(grad_middle)
    wide = rest_ref[:, :, :, :, 16:32, :].reshape(1024, D)
    grad_ref[:, :, :, :, 16:32, :] = half(inner_rows(mixed_ref[...], branch)).reshape(2, 4, 4, 2, 16, D)
    grad_mixed = half(product(half(outer_cols(branch, wide)), place))
    low = low_lanes((128, 128))
    query_rows, key_rows, value_rows = [], [], []
    for b in range(2):
        here = slice(128 * b, 128 * b + 128)
        key_tiles = paired(k_ref[here, :].astype(jnp.float32))
        value_tiles = paired(v_ref[here, :].astype(jnp.float32))
        tiles = []
        sums = [[jnp.zeros((128, 128), jnp.float32) for _ in range(4)] for _ in range(2)]
        for t in range(7):
            head = grad_mixed[here, 128 * t : 128 * t + 128]
            grad_probs = outer_cols(head, value_tiles[t])
            probs = probs_ref[b, t]
            parts = []
            for p, g in zip(tiles_of(probs), tiles_of(grad_probs)):
                parts.append(half(p * (g - jnp.sum(p * g, axis=-1, keepdims=True))))
            grad_scores = jnp.concatenate(parts, axis=1)
            tiles.append(product(grad_scores, key_tiles[t]) * SCALE)
            for which, (left, right) in enumerate(
                ((grad_scores, q_ref[here, 128 * t : 128 * t + 128]), (half(probs), head))
            ):
                both = inner_rows(left, right)
                even, odd = (2 * t) // 7, (2 * t + 1) // 7
                sums[which][even] += both[0:128]
                sums[which][2 + odd] += both[128:256]
        query_rows.append(jnp.concatenate(tiles, axis=1))
        joined = []
        for which in range(2):
            even0, even1, odd0, odd1 = sums[which]
            joined.append(
                jnp.where(low, even0 + pltpu.roll(odd0, 64, 1), odd1 + pltpu.roll(even1, 64, 1))
            )
        key_rows.append(joined[0] * SCALE)
        value_rows.append(joined[1])
    between()
    grad_query = half(rotated_back(jnp.concatenate(query_rows), cosine, sine))
    grad_key = half(rotated_back(jnp.concatenate(key_rows), cosine, sine))
    grad_narrow = jnp.concatenate([grad_key, half(jnp.concatenate(value_rows))], axis=1)
    placed = h1p_ref[...]
    grad_ref[:, :, :, :, 0:16, :] = half(inner_rows(placed, grad_query)).reshape(2, 4, 4, 2, 16, D)
    grad_ref[:, :, :, :, 32:48, 0:256] = half(inner_rows(placed, grad_narrow)).reshape(2, 4, 4, 2, 16, 256)
    bias_grad = jnp.sum(
        jnp.concatenate([grad_query, grad_narrow], axis=1).astype(jnp.float32), axis=0, keepdims=True
    )
    grad_placed = outer_cols(grad_query, rest_ref[:, :, :, :, 0:16, :].reshape(1024, D)) + outer_cols(
        grad_narrow, rest_ref[:, :, :, :, 32:48, 0:256].reshape(1024, 256)
    )
    high = half(grad_placed)
    remainder = half(grad_placed - high.astype(jnp.float32))
    grad_normed = product(high, place) + product(remainder, place)
    inputs = x_ref[...].astype(jnp.float32)
    first_scale = lax.rsqrt(jnp.mean(inputs * inputs, axis=-1, keepdims=True) + NORM_EPSILON)
    first_normed = inputs * first_scale
    first_gain_grad = jnp.sum(grad_normed * first_normed, axis=0, keepdims=True)
    input_grad_ref[...] = half(
        grad_middle + norm_back(grad_normed * first_gain, first_normed, first_scale)
    )
    vector_grad = jnp.concatenate([first_gain_grad, second_gain_grad, bias_grad], axis=1)
    spread = half(jnp.where(slot_mask(slot_ref[...]), vector_grad, 0.0))
    by_device = half(outer_cols(owner, spread))
    stored = half(inner_rows(pick, by_device))
    grad_ref[:, :, :, :, 32:48, 256:384] = stored.reshape(2, 4, 4, 2, 16, 128)
    grad_ref[:, :, :, :, 32:48, 384:] = jnp.zeros((2, 4, 4, 2, 16, D - 384), jnp.bfloat16)


LOADED = (
    "parcel", "own", "middle", "e", "x", "rest", "h1p", "q", "k", "v", "mixed", "probs", "vector",
)


def scatter_kernel(
    len_ref, cos_ref, sin_ref, slot_ref, grad_wide_ref, grad_shared_ref, *refs,
):
    coords, core = my_coords()
    z, y, x = coords
    pair, odd = x // 2, x % 2
    count = len(LOADED) + len(EARLY)
    sources, (output_ref, input_grad_ref, out_ref) = refs[:count], refs[count : count + 3]
    held = refs[count + 3 : 2 * count + 3]
    (
        wide, shared, thin, joined, mine, theirs, arrived, dh2_ref,
        load_sems, send_sems, recv_sems, twin_sems, pair_sems, held_sems,
    ) = refs[2 * count + 3 : 2 * count + 17]
    buffers = refs[2 * count + 17 :]
    (
        parcel_ref, own_ref, middle_ref, e_ref, x_ref, rest_ref, h1p_ref, q_ref, k_ref, v_ref,
        mixed_ref, probs_ref, vector_ref,
    ) = held[: len(LOADED)]
    fetches = [
        pltpu.make_async_copy(sources[n], held[n], held_sems.at[n]) for n in range(count)
    ]
    named, position = {}, 0
    early = dict(zip(EARLY, held[len(LOADED) :]))
    for key, shapes in scatter_buffer_shapes():
        named[key] = []
        for slot in range(len(shapes)):
            if (*key, slot) in early:
                named[key].append(early[(*key, slot)])
            elif shapes[slot] is None:
                named[key].append(None)
            else:
                named[key].append(buffers[position])
                position += 1
    scatter = Scatter(((wide, ()), (shared, ()), (thin, (core,))), coords, core, named, send_sems, recv_sems, EARLY)

    def load(part, by):
        spec = [FULL] * 3
        axis = PARTS[part][3][2]
        spec[axis] = (coords[axis] + by) % 4
        place = place_of(part, tuple(spec))
        source = (grad_wide_ref, grad_shared_ref)[PARTS[part][0]]
        target = (wide, shared)[PARTS[part][0]]
        return pltpu.make_async_copy(source.at[place], target.at[place], load_sems.at[part, by])

    for by in (2, 1, 3, 0):
        for part in SUMMED:
            load(part, by).start()
    for copy in fetches:
        copy.start()
    greet(coords, core)

    for part in SUMMED:
        load(part, 2).wait()
        scatter.start_far((part,), 2)
    for part in SUMMED:
        load(part, 1).wait()
        load(part, 3).wait()
    scatter.start_near(SIDE, 2)

    def between():
        scatter.forward(SUMMED, 2)

    for copy in fetches[:3]:
        copy.wait()
    parcel_copy = remote(
        parcel_ref, arrived, twin_sems.at[0, 1], twin_sems.at[1, 1], device_of(coords, 1 - core)
    )
    parcel_copy.start()
    for copy in fetches[3:]:
        copy.wait()
    parcel_copy.wait()
    output_ref[...] = half(
        (middle_ref[...] + (own_ref[0] + arrived[0].astype(F32))) * live_tokens(len_ref)
    )
    dh2_ref[...] = own_ref[1] + arrived[1].astype(F32)
    attention_backward(
        between, x_ref, e_ref, rest_ref, cos_ref, sin_ref, slot_ref,
        middle_ref, h1p_ref, q_ref, k_ref, v_ref, mixed_ref, probs_ref, vector_ref, dh2_ref,
        input_grad_ref, thin,
    )
    twin_copy = remote(
        thin.at[1 - core], joined, twin_sems.at[0, 0], twin_sems.at[1, 0], device_of(coords, 1 - core)
    )
    twin_copy.start()
    for part in SUMMED:
        load(part, 0).wait()
    twin_copy.wait()

    def join(index):
        thin[(core, *index)] = half(thin[(core, *index)].astype(F32) + joined[index].astype(F32))

    each_block((4, 4, 2, CHUNK, D), join)
    scatter.start(THIN, 2)
    for part in SUMMED:
        scatter.finish((part,), 2)
        scatter.start((part,), 1)
    scatter.forward(THIN, 2)
    scatter.finish(THIN, 2)
    scatter.start(THIN, 1)
    scatter.forward(SUMMED, 1)
    scatter.forward(THIN, 1)
    for part in SUMMED:
        scatter.finish((part,), 1)
        scatter.start((part,), 0)
    scatter.finish(THIN, 1)
    scatter.start(THIN, 0)
    scatter.forward(SUMMED, 0)
    scatter.forward(THIN, 0)
    scatter.finish(SUMMED, 0)
    scatter.finish(THIN, 0)
    mine[0] = shared[z, y, pair]
    mine[1] = thin[core, z, y, pair]
    partner = device_of((z, y, x + 1 - 2 * odd), core)
    pair_copy = remote(mine, theirs, pair_sems.at[0], pair_sems.at[1], partner)
    pair_copy.start()
    pair_copy.wait()
    out_ref[0] = wide[z, y, pair, odd, 0:CHUNK].astype(F32)
    out_ref[1] = wide[z, y, pair, odd, CHUNK : 2 * CHUNK].astype(F32)
    out_ref[2] = mine[0].astype(F32) + theirs[0].astype(F32)
    out_ref[3] = mine[1].astype(F32) + theirs[1].astype(F32)
    scatter.drain()


def layer(weights, tokens, cotangent, lengths):
    vmem = pl.BlockSpec(memory_space=pltpu.VMEM)
    anywhere = pl.BlockSpec(memory_space=pl.ANY)
    x = tokens.reshape(TOKENS, D)
    freqs = ROPE_BASE ** (-np.arange(HEAD // 2) * 2.0 / HEAD)
    angles = np.tile(np.arange(128)[:, None] * freqs[None, :], (2, 4))
    tables = (
        np.cos(angles).astype(np.float32),
        np.sin(angles).astype(np.float32),
        (np.arange(2944, dtype=np.int32) % 23)[None],
    )
    buffers = dict(scatter_buffer_shapes())
    kept = [
        ((TOKENS, D), F32),
        ((TOKENS, D), BF16),
        ((TOKENS, 1024), BF16),
        ((TOKENS, D), BF16),
        ((TOKENS, 128), BF16),
        ((TOKENS, 128), BF16),
        ((TOKENS, 1024), BF16),
        ((2, 7, 128, 256), F32),
        ((1, 2944), F32),
        ((2, TOKENS, D), F32),
        ((2, TOKENS, D), BF16),
    ] + [(buffers[part, stage][slot], BF16) for part, stage, slot in EARLY]
    large = [
        ((4, 4, 2, 2, 2 * CHUNK, D), BF16),
        ((4, 4, 2, CHUNK, D), BF16),
        ((2, 4, 4, 2, CHUNK, D), BF16),
    ]

    def shapes(pairs):
        return [jax.ShapeDtypeStruct(shape, dtype) for shape, dtype in pairs]

    def scratch(pairs):
        return [pltpu.VMEM(shape, dtype) for shape, dtype in pairs]

    results = pl.pallas_call(
        gather_kernel,
        out_shape=shapes(kept + large),
        in_specs=[vmem] * 12,
        out_specs=[anywhere] * (KEPT + 3),
        scratch_shapes=scratch(
            kept[:9]
            + kept[11:]
            + large
            + [
                ((2, 4, 2, 2, CHUNK, D), BF16),
                ((2, 4, 4, CHUNK, D), BF16),
                ((2, 4, 2, CHUNK, D), BF16),
                ((2, TOKENS, D), BF16),
                ((2, TOKENS, D), BF16),
                ((2, 2, TOKENS, D), F32),
                ((2, TOKENS, D), BF16),
                ((2 * CHUNK, D), BF16),
                ((2 * CHUNK, D), BF16),
                ((2 * CHUNK, D), F32),
            ]
        )
        + [
            pltpu.SemaphoreType.DMA((3,)),
            pltpu.SemaphoreType.DMA((len(PARTS), 3, 6)),
            pltpu.SemaphoreType.DMA((len(PARTS), 3, 6)),
            pltpu.SemaphoreType.DMA((2, 5)),
            pltpu.SemaphoreType.DMA((3, 2)),
            pltpu.SemaphoreType.DMA((2, 3, 2)),
            pltpu.SemaphoreType.DMA((KEPT,)),
        ],
        compiler_params=pltpu.CompilerParams(
            collective_id=0, has_side_effects=True, vmem_limit_bytes=61 * 2**20
        ),
    )(*weights, x, cotangent.reshape(TOKENS, D), lengths, *tables)
    middle, e, h1p, q, k, v, mixed, probs, vector, own, parcel = results[:11]
    early = results[11:KEPT]
    grad_wide, grad_shared, rest = results[KEPT:]
    loaded = dict(
        x=x, e=e, rest=rest, middle=middle, h1p=h1p, q=q, k=k, v=v, mixed=mixed, probs=probs,
        vector=vector, own=own, parcel=parcel,
    )
    fetched = [loaded[name] for name in LOADED] + list(early)
    output, input_grad, grads = pl.pallas_call(
        scatter_kernel,
        out_shape=shapes([((TOKENS, D), BF16), ((TOKENS, D), BF16), ((4, CHUNK, D), F32)]),
        in_specs=[vmem] * 4 + [anywhere] * (2 + len(fetched)),
        out_specs=[vmem] * 3,
        scratch_shapes=scratch(
            [(value.shape, value.dtype) for value in fetched]
            + large[:2]
            + [
                ((2, 4, 4, 2, CHUNK, D), BF16),
                ((4, 4, 2, CHUNK, D), BF16),
                ((2, CHUNK, D), BF16),
                ((2, CHUNK, D), BF16),
                ((2, TOKENS, D), BF16),
                ((TOKENS, D), F32),
            ]
        )
        + [
            pltpu.SemaphoreType.DMA((len(PARTS), 4)),
            pltpu.SemaphoreType.DMA((len(PARTS), 3, 6)),
            pltpu.SemaphoreType.DMA((len(PARTS), 3, 6)),
            pltpu.SemaphoreType.DMA((2, 2)),
            pltpu.SemaphoreType.DMA((2,)),
            pltpu.SemaphoreType.DMA((len(fetched),)),
        ]
        + [
            pltpu.VMEM(shape, BF16)
            for key, group in buffers.items()
            for slot, shape in enumerate(group)
            if shape is not None and (*key, slot) not in EARLY
        ],
        compiler_params=pltpu.CompilerParams(
            collective_id=1, has_side_effects=True, vmem_limit_bytes=62 * 2**20
        ),
    )(lengths, *tables, grad_wide, grad_shared, *fetched)
    return output.reshape(2, 1, 128, D), input_grad.reshape(2, 1, 128, D), grads


def newton_schulz(gram, values):
    gram_half = half(gram)
    first = half(NEWTON_B * gram + NEWTON_C * product(gram_half, gram_half))
    cross = product(gram_half, first)
    after = NEWTON_A * NEWTON_A * gram + 2.0 * NEWTON_A * cross + product(half(cross), first)
    after_half = half(after)
    second = half(NEWTON_B * after + NEWTON_C * product(after_half, after_half))
    values = half(NEWTON_A * values + product(half(values), first))
    return half(NEWTON_A * values.astype(F32) + product(values, second))


BLOCKS = [(i, j) for i in range(7) for j in range(i, 7)]
JOB_ROWS = (48, 48, 48, 16, 16, 16, 16)


def own_momenta(grads_ref, priors, momenta, odd):
    for parity in range(2):

        @pl.when(odd == parity)
        def _():
            for n in range(3):
                for k, (start, size) in enumerate(((0, 16), (16, 16), (32, 6))):
                    base = 16 * n + (6 * parity if k == 2 else 0)
                    momenta[n][start : start + size] = (
                        MOMENTUM * priors[n][start : start + size] + grads_ref[k, base : base + size]
                    )
            for n in range(4):
                base = 16 * min(n, 2) + 7 * parity
                lanes = slice(0, D) if n < 2 else slice(128 * n - 256, 128 * n - 128)
                momenta[3 + n][...] = (
                    MOMENTUM * priors[3 + n][...] + grads_ref[3, base : base + 7, lanes]
                )


def update_kernel(grads_ref, tall_ref, short_ref, *refs):
    priors, masters, (first_ref, second_ref, vector_ref) = refs[:7], refs[7:14], refs[14:17]
    momenta, updated, vector_outs = refs[17:24], refs[24:31], refs[31:34]
    odd = lax.axis_index("dp") % 2
    own_momenta(grads_ref, priors, momenta, odd)
    for n in range(7):
        size = FF if n < 3 else D
        got = tall_ref[n].astype(F32)[:38] if n < 3 else short_ref[n - 3].astype(F32)[:7]
        got = got[:, :128] if n > 4 else got
        updated[n][...] = masters[n][...] * (1.0 - MUON_RATE * MUON_DECAY) - (
            MUON_RATE * 0.2 * math.sqrt(size) * got
        )
    for parity in range(2):

        @pl.when(odd == parity)
        def _():
            start = 32 + 7 * parity
            grad = grads_ref[3, start : start + 1, 256:384][:, :23]
            first = BETA_FIRST * first_ref[...] + (1.0 - BETA_FIRST) * grad
            second = BETA_SECOND * second_ref[...] + (1.0 - BETA_SECOND) * grad * grad
            first_hat = first / (1.0 - BETA_FIRST**STEP)
            second_hat = second / (1.0 - BETA_SECOND**STEP)
            vector_outs[0][...] = first
            vector_outs[1][...] = second
            vector_outs[2][...] = vector_ref[...] * (1.0 - ADAM_RATE * ADAM_DECAY) - (
                ADAM_RATE * first_hat / (jnp.sqrt(second_hat) + ADAM_EPSILON)
            )


def muon_kernel(
    grads_ref, prior0, prior1, prior2, prior3, prior4, prior5, prior6, tall_out_ref, short_out_ref,
    momentum0, momentum1, momentum2, momentum3, momentum4, momentum5, momentum6,
    tall_wide, short_wide, tall_ref, short_ref, rows, gram_out, gram_twin, gram_half_sum, gram_in, gram_all, gram, back, tall_got, short_got,
    job_sems, twin_sems, sum_sems, all_sems, back_sems,
):
    priors = (prior0, prior1, prior2, prior3, prior4, prior5, prior6)
    momenta = (momentum0, momentum1, momentum2, momentum3, momentum4, momentum5, momentum6)
    coords, core = my_coords()
    z, y, x = coords
    job = z * 2 + y // 2
    source = z * 2 + y // 2
    member = (y % 2) * 4 + x
    tall_wide[...] = jnp.zeros_like(tall_wide)
    short_wide[...] = jnp.zeros_like(short_wide)
    own_momenta(grads_ref, priors, momenta, x % 2)
    for n in range(3):
        tall_wide[n, 0:38] = momenta[n][...]
    for n in range(4):
        short_wide[n, 0:7, 0 : D if n < 2 else 128] = momenta[3 + n][...]
    tall_ref[...] = half(tall_wide[...])
    short_ref[...] = half(short_wide[...])
    twin = device_of(coords, 1 - core)

    def group(peer):
        return device_of((z, (y // 2) * 2 + peer // 4, peer % 4), core)

    def square(k):
        return device_of((k // 2, (k % 2) * 2 + y % 2, x), core)

    barrier = pltpu.get_barrier_semaphore()
    for k in range(1, 8):
        for device in (group((member + k) % 8), square((source + k) % 8)):
            pl.semaphore_signal(barrier, inc=1, device_id=device, device_id_type=MESH)
    pl.semaphore_signal(barrier, inc=1, device_id=twin, device_id_type=MESH)
    pl.semaphore_wait(barrier, 15)

    def copy(src, dst, sems, slot, device):
        return remote(src, dst, sems.at[0, slot], sems.at[1, slot], device)

    def mine(m, tall, short):
        return tall.at[m] if m < 3 else short.at[m - 3]

    def job_copy(m):
        return remote(
            mine(m, tall_ref, short_ref),
            rows.at[source, pl.ds(0, JOB_ROWS[m])],
            job_sems.at[0, m],
            job_sems.at[1, source],
            square(m),
        )

    for m in range(7):

        @pl.when(job != m)
        def _():
            job_copy(m).start()

    for kind in range(2):
        count = (48, 16)[kind]

        @pl.when((job >= 3 * kind) & (job < 3 + 4 * kind))
        def _():
            if kind == 1:
                rows[:, 16:48] = jnp.zeros((8, 32, D), BF16)
                rows[source, 0:16] = short_ref[job - 3]
            else:
                rows[source] = tall_ref[job]
            for k in range(1, 8):
                other = (source + k) % 8
                arrival = rows.at[other, pl.ds(0, count)]
                remote(
                    arrival, arrival, job_sems.at[0, 0], job_sems.at[1, other], square(other)
                ).wait_recv()

    @pl.when(job < 7)
    def _():
        flat = rows[...].reshape(384, D)
        gram[...] = inner_rows(flat, flat)
        for index, (i, j) in enumerate(BLOCKS):
            gram_out[index // 16, index % 16] = half(
                gram[128 * i : 128 * i + 128, 128 * j : 128 * j + 128]
            )
        gram_out[1, 12:16] = jnp.zeros((4, 128, 128), BF16)
        twin_copy = copy(gram_out.at[1 - core], gram_twin, twin_sems, 0, twin)
        twin_copy.start()
        twin_copy.wait()
        gram_half_sum[...] = half(gram_out[core].astype(F32) + gram_twin[...].astype(F32))

        def sum_copy(k):
            peer = (member + k) % 8
            return copy(
                gram_half_sum.at[pl.ds(2 * peer, 2)], gram_in.at[k], sum_sems, k, group(peer)
            )

        for k in range(1, 8):
            sum_copy(k).start()
        total = gram_half_sum[pl.ds(2 * member, 2)].astype(F32)
        for k in range(1, 8):
            sum_copy(k).wait_recv()
            total = total + gram_in[k].astype(F32)
        gram_all[core, pl.ds(2 * member, 2)] = half(total)

        def all_copy(k, owner):
            ref = gram_all.at[core, pl.ds(2 * owner, 2)]
            return copy(ref, ref, all_sems, k, group((member + k) % 8))

        for k in range(1, 8):
            all_copy(k, member).start()
        for k in range(1, 8):
            all_copy(k, (member + 8 - k) % 8).wait_recv()
        last_copy = copy(gram_all.at[core], gram_all.at[core], twin_sems, 1, twin)
        last_copy.start()
        last_copy.wait()

        eye = lax.broadcasted_iota(jnp.int32, (128, 128), 0) == lax.broadcasted_iota(
            jnp.int32, (128, 128), 1
        )
        trace = 0.0
        for index, (i, j) in enumerate(BLOCKS):
            block = gram_all[index // 16, index % 16].astype(F32)
            gram[128 * i : 128 * i + 128, 128 * j : 128 * j + 128] = block
            if i == j:
                trace = trace + jnp.sum(jnp.where(eye, block, 0.0))
            else:
                gram[128 * j : 128 * j + 128, 128 * i : 128 * i + 128] = block.T
        inverse = 1.0 / (jnp.sqrt(jnp.full((1, 1), trace)) + 1e-07)
        moved = newton_schulz(
            gram[...] * (inverse * inverse), rows[...].reshape(384, D).astype(F32) * inverse
        )
        back[...] = moved.reshape(8, 48, D)
        for k in range(1, 8):
            sum_copy(k).wait_send()
            all_copy(k, member).wait_send()

    for m in range(7):

        @pl.when(job == m)
        def _():
            copies = []
            for k in range(1, 8):
                other = (source + k) % 8
                copies.append(
                    remote(
                        back.at[other, pl.ds(0, JOB_ROWS[m])],
                        mine(m, tall_got, short_got),
                        back_sems.at[0, k],
                        back_sems.at[1, m],
                        square(other),
                    )
                )
            for item in copies:
                item.start()
            if m < 3:
                tall_got[m] = back[source]
            else:
                short_got[m - 3] = back[source, 0:16]
            for item in copies:
                item.wait_send()

    for m in range(7):

        @pl.when(job != m)
        def _():
            arrival = mine(m, tall_got, short_got)
            remote(arrival, arrival, back_sems.at[0, 0], back_sems.at[1, m], square(m)).wait_recv()
            job_copy(m).wait_send()

    tall_out_ref[...] = tall_got[...]
    short_out_ref[...] = short_got[...]


def muon(grads, priors, masters, vectors):
    vmem = pl.BlockSpec(memory_space=pltpu.VMEM)
    tall, short = pl.pallas_call(
        muon_kernel,
        out_shape=(
            jax.ShapeDtypeStruct((3, 48, D), BF16),
            jax.ShapeDtypeStruct((4, 16, D), BF16),
        ),
        in_specs=[vmem] * 8,
        out_specs=[vmem] * 2,
        scratch_shapes=[
            *(pltpu.VMEM(value.shape, F32) for value in priors),
            pltpu.VMEM((3, 48, D), F32),
            pltpu.VMEM((4, 16, D), F32),
            pltpu.VMEM((3, 48, D), BF16),
            pltpu.VMEM((4, 16, D), BF16),
            pltpu.VMEM((8, 48, D), BF16),
            pltpu.VMEM((2, 16, 128, 128), BF16),
            pltpu.VMEM((16, 128, 128), BF16),
            pltpu.VMEM((16, 128, 128), BF16),
            pltpu.VMEM((8, 2, 128, 128), BF16),
            pltpu.VMEM((2, 16, 128, 128), BF16),
            pltpu.VMEM((D, D), F32),
            pltpu.VMEM((8, 48, D), BF16),
            pltpu.VMEM((3, 48, D), BF16),
            pltpu.VMEM((4, 16, D), BF16),
            pltpu.SemaphoreType.DMA((2, 8)),
            pltpu.SemaphoreType.DMA((2, 2)),
            pltpu.SemaphoreType.DMA((2, 8)),
            pltpu.SemaphoreType.DMA((2, 8)),
            pltpu.SemaphoreType.DMA((2, 8)),
        ],
        compiler_params=pltpu.CompilerParams(
            collective_id=3, has_side_effects=True, vmem_limit_bytes=58 * 2**20
        ),
    )(grads, *priors)
    outs = [*priors, *masters, *vectors]
    return pl.pallas_call(
        update_kernel,
        out_shape=[jax.ShapeDtypeStruct(value.shape, F32) for value in outs],
        in_specs=[vmem] * 20,
        out_specs=[vmem] * 17,
    )(grads, tall, short, *outs)


def body(
    inputs,
    cotangent,
    lengths,
    query_weight,
    key_weight,
    value_weight,
    out_weight,
    gate_weight,
    up_weight,
    down_weight,
    vectors,
    query_prior,
    key_prior,
    value_prior,
    out_prior,
    gate_prior,
    up_prior,
    down_prior,
    first_prior,
    second_prior,
):
    chip = lax.axis_index("dp")
    core = lax.axis_index("narrow")
    narrow_rows = jnp.concatenate(
        [key_weight, value_weight, jnp.pad(vectors[None], ((0, 6), (0, 128 - vectors.shape[0])))],
        axis=1,
    )
    weights = (
        gate_weight.T, up_weight.T, down_weight, query_weight, out_weight, narrow_rows
    )
    own_lengths = lax.dynamic_slice_in_dim(lengths, chip * 2 + core, 1, axis=1)
    own_lengths = jnp.broadcast_to(own_lengths, (2, 128))
    block_output, input_grad, grads = layer(weights, inputs[:, 0], cotangent[:, 0], own_lengths)
    results = muon(
        grads,
        (gate_prior.T, up_prior.T, down_prior, query_prior, out_prior, key_prior, value_prior),
        (gate_weight.T, up_weight.T, down_weight, query_weight, out_weight, key_weight, value_weight),
        (first_prior[None], second_prior[None], vectors[None]),
    )

    def ordered(gate, up, down, query, out, key, value):
        return query, key, value, out, gate.T, up.T, down

    return (
        block_output,
        input_grad,
        *ordered(*results[:7]),
        *ordered(*results[7:14]),
        *(value[0] for value in results[14:]),
    )


def solution(mesh):
    placed = (
        P(None, ("dp", "narrow"), None, None),
        P(None, ("dp", "narrow"), None, None),
        P(),
        P(("dp", "narrow"), None),
        P(("dp", "narrow"), None),
        P(("dp", "narrow"), None),
        P(("dp", "narrow"), None),
        P(None, ("dp", "narrow")),
        P(None, ("dp", "narrow")),
        P(("dp", "narrow"), None),
        P(("dp", "narrow")),
        P(("dp", "narrow"), None),
        P(("dp", "narrow"), None),
        P(("dp", "narrow"), None),
        P(("dp", "narrow"), None),
        P(None, ("dp", "narrow")),
        P(None, ("dp", "narrow")),
        P(("dp", "narrow"), None),
        P(("dp", "narrow")),
        P(("dp", "narrow")),
    )
    return jax.shard_map(
        body,
        mesh=mesh,
        in_specs=placed,
        out_specs=(
            P(None, ("dp", "narrow"), None, None),
            P(None, ("dp", "narrow"), None, None),
            P(("dp", "narrow"), None),
            P(("dp", "narrow"), None),
            P(("dp", "narrow"), None),
            P(("dp", "narrow"), None),
            P(None, ("dp", "narrow")),
            P(None, ("dp", "narrow")),
            P(("dp", "narrow"), None),
            P(("dp", "narrow"), None),
            P(("dp", "narrow"), None),
            P(("dp", "narrow"), None),
            P(("dp", "narrow"), None),
            P(None, ("dp", "narrow")),
            P(None, ("dp", "narrow")),
            P(("dp", "narrow"), None),
            P(("dp", "narrow")),
            P(("dp", "narrow")),
            P(("dp", "narrow")),
        ),
        check_vma=False,
    )
```

```python
import math

import jax
import jax.numpy as jnp
import numpy as np
from jax import lax
from jax.experimental import pallas as pl
from jax.experimental.pallas import tpu as pltpu
from jax.sharding import PartitionSpec as P

D = 896
FF = 4864
HEADS = 14
KV_HEADS = 2
HEAD = 64
STEP = 10


NORM_EPSILON = 1e-06
ROPE_BASE = 1000000.0
MOMENTUM = 0.95
NEWTON_A = 3.4445
NEWTON_B = -4.775
NEWTON_C = 2.0315
MUON_RATE = 0.4
MUON_DECAY = 0.1
ADAM_RATE = 0.5
ADAM_DECAY = 0.01
BETA_FIRST = 0.9
BETA_SECOND = 0.999
ADAM_EPSILON = 1e-08
MASKED = -1e30


def product(left, right):
    return jnp.dot(left, right, preferred_element_type=jnp.float32)


def inner_rows(left, right):
    return lax.dot_general(
        left, right, (((0,), (0,)), ((), ())), preferred_element_type=jnp.float32
    )


def outer_cols(left, right):
    return lax.dot_general(
        left, right, (((1,), (1,)), ((), ())), preferred_element_type=jnp.float32
    )


def norm_back(grad, normed, scale):
    return scale * (grad - normed * jnp.mean(grad * normed, axis=-1, keepdims=True))


def half(value):
    return value.astype(jnp.bfloat16)


MESH = pl.DeviceIdType.MESH
TOKENS = 256
FULL = (0, 4)
BF16 = jnp.bfloat16
F32 = jnp.float32
CHUNK = 48
PARTS = (
    (0, 0, CHUNK, (2, 1, 0), False, (0, D)),
    (0, CHUNK, CHUNK, (1, 0, 2), False, (0, D)),
    (1, 0, CHUNK, (0, 2, 1), True, (0, D)),
    (2, 0, 16, (2, 1, 0), True, (0, D)),
    (2, 16, 16, (1, 0, 2), True, (0, 512)),
    (2, 16, 16, (0, 2, 1), True, (512, 384)),
    (2, 32, 16, (0, 2, 1), True, (0, 384)),
    (0, 0, CHUNK, (2, 1, 0), False, (0, 768)),
    (0, CHUNK, CHUNK, (1, 0, 2), False, (0, 768)),
    (0, 0, CHUNK, (2, 0, 1), False, (768, 128)),
    (0, CHUNK, CHUNK, (0, 2, 1), False, (768, 128)),
)
WIDE = (0, 1, 2)
THIN = (3, 4, 5, 6)
MAIN, SIDE = (7, 8, 2), (9, 10)
SUMMED = MAIN + SIDE


def my_coords():
    dp = lax.axis_index("dp")
    return (dp // 16, (dp // 4) % 4, dp % 4), lax.axis_index("narrow")


def device_of(coords, core):
    return (coords[0] * 16 + coords[1] * 4 + coords[2], core)


def shifted(coords, axis, by):
    out = list(coords)
    out[axis] = (coords[axis] + by) % 4
    return tuple(out)


def facing(coords):
    return (coords[0], coords[1], 3 - coords[2])


def greet(coords, core):
    barrier = pltpu.get_barrier_semaphore()
    for axis in range(3):
        for by in (1, 2, 3):
            pl.semaphore_signal(
                barrier, inc=1, device_id=device_of(shifted(coords, axis, by), core), device_id_type=MESH
            )
    pl.semaphore_signal(barrier, inc=1, device_id=device_of(coords, 1 - core), device_id_type=MESH)
    pl.semaphore_wait(barrier, 10)


def remote(src, dst, send_sem, recv_sem, device):
    return pltpu.make_async_remote_copy(
        src_ref=src,
        dst_ref=dst,
        send_sem=send_sem,
        recv_sem=recv_sem,
        device_id=device,
        device_id_type=MESH,
    )


def place_of(part, spec):
    _, first, rows, _, shared, columns = PARTS[part]
    index = [pl.ds(*s) if isinstance(s, tuple) else s for s in spec[:2]]
    s = spec[2]
    if isinstance(s, tuple):
        index.append(pl.ds(s[0] // 2, s[1] // 2))
        index += [] if shared else [pl.ds(0, 2)]
    else:
        index.append(s // 2)
        index += [] if shared else [s % 2]
    return (*index, pl.ds(first, rows), pl.ds(*columns))


def shape_of(part, spec):
    return tuple(entry.size for entry in place_of(part, spec) if isinstance(entry, pl.Slice))


class Plan:
    def __init__(self, part, stage, coords, axis, spec, split):
        self.coords, self.axis, self.spec, self.split = coords, axis, spec, split
        self.exchange = PARTS[part][4] and axis == 2
        self.direct = not self.exchange and stage == 0

    def at(self, by):
        return shifted(self.coords, self.axis, by)

    def whole(self, by):
        spec = list(self.spec)
        spec[self.axis] = (self.coords[self.axis] + by) % 4
        return tuple(spec)

    def pieces(self, by):
        out = []
        for h in range(2):
            spec = list(self.whole(by))
            spec[self.split] = (2 * h, 2)
            out.append(tuple(spec))
        return out

    def facing(self):
        return (*self.spec[:2], 3 - self.coords[2])

    def own(self):
        return self.spec


def plan_of(part, stage, coords):
    order = PARTS[part][3]
    spec = tuple(FULL if k in order[:stage] else coords[k] for k in range(3))
    return Plan(part, stage, coords, order[stage], spec, order[stage - 1] if stage else None)


class Gather:
    def __init__(self, arrays, coords, core, send_sems, recv_sems):
        self.arrays, self.coords, self.core = arrays, coords, core
        self.send_sems, self.recv_sems = send_sems, recv_sems

    def copy(self, part, phase, slot, piece, coords):
        array, prefix = self.arrays[PARTS[part][0]]
        ref = array.at[(*prefix, *place_of(part, piece))]
        sems = (self.send_sems.at[part, phase, slot], self.recv_sems.at[part, phase, slot])
        return remote(ref, ref, *sems, device_of(coords, self.core))

    def send(self, *args):
        self.copy(*args).start()

    def neighbours(self, plan):
        return shifted(self.coords, plan.axis, 1), shifted(self.coords, plan.axis, 3)

    def start(self, parts, phase):
        for part in parts:
            plan = plan_of(part, phase, self.coords)
            if plan.exchange:
                self.send(part, phase, 0, plan.own(), facing(self.coords))
                continue
            if plan.direct:
                for by in (1, 3, 2):
                    self.send(part, phase, by, plan.own(), plan.at(by))
                continue
            right, left = self.neighbours(plan)
            first, second = plan.pieces(0)
            self.send(part, phase, 0, first, right)
            self.send(part, phase, 1, second, left)
            self.send(part, phase, 2, second, right)
            self.send(part, phase, 3, first, left)

    def forward(self, parts, phase):
        for part in parts:
            plan = plan_of(part, phase, self.coords)
            if plan.exchange or plan.direct:
                continue
            right, left = self.neighbours(plan)
            piece = plan.pieces(3)[0]
            self.copy(part, phase, 0, piece, right).wait_recv()
            self.send(part, phase, 4, piece, right)
            piece = plan.pieces(1)[1]
            self.copy(part, phase, 1, piece, left).wait_recv()
            self.send(part, phase, 5, piece, left)

    def near(self, parts, phase):
        for part in parts:
            plan = plan_of(part, phase, self.coords)
            if plan.exchange:
                self.copy(part, phase, 0, plan.facing(), facing(self.coords)).wait_recv()
                continue
            if plan.direct:
                for by in (1, 3):
                    self.copy(part, phase, by, plan.whole(4 - by), plan.at(by)).wait_recv()
                continue
            right, left = self.neighbours(plan)
            self.copy(part, phase, 2, plan.pieces(3)[1], right).wait_recv()
            self.copy(part, phase, 3, plan.pieces(1)[0], left).wait_recv()

    def far(self, parts, phase):
        for part in parts:
            plan = plan_of(part, phase, self.coords)
            if plan.exchange:
                continue
            if plan.direct:
                self.copy(part, phase, 2, plan.whole(2), plan.at(2)).wait_recv()
                continue
            right, left = self.neighbours(plan)
            self.copy(part, phase, 4, plan.pieces(2)[0], right).wait_recv()
            self.copy(part, phase, 5, plan.pieces(2)[1], left).wait_recv()

    def finish(self, parts, phase):
        self.near(parts, phase)
        self.far(parts, phase)

    def drain(self):
        for part in WIDE + THIN:
            for phase in range(3):
                plan = plan_of(part, phase, self.coords)
                if plan.exchange:
                    self.copy(part, phase, 0, plan.own(), facing(self.coords)).wait_send()
                    continue
                if plan.direct:
                    for by in (1, 3, 2):
                        self.copy(part, phase, by, plan.own(), plan.at(by)).wait_send()
                    continue
                right, _ = self.neighbours(plan)
                for slot, which in enumerate((0, 1, 1, 0, 0, 1)):
                    self.copy(part, phase, slot, plan.pieces(0)[which], right).wait_send()


def each_block(shape, body):
    lead = shape[:-2]
    count = math.prod(lead)
    if count == 1:
        body((0,) * len(lead))
        return

    def step(k, carry):
        index = []
        for n in reversed(lead):
            index.append(k % n)
            k = k // n
        body(tuple(reversed(index)))
        return carry

    lax.fori_loop(0, count, step, 0)


class Scatter:
    def __init__(self, arrays, coords, core, buffers, send_sems, recv_sems, done):
        self.arrays, self.coords, self.core, self.done = arrays, coords, core, done
        self.buffers, self.send_sems, self.recv_sems = buffers, send_sems, recv_sems

    def copy(self, part, phase, slot, piece, coords):
        array, prefix = self.arrays[PARTS[part][0]]
        ref = array.at[(*prefix, *place_of(part, piece))]
        sems = (self.send_sems.at[part, phase, slot], self.recv_sems.at[part, phase, slot])
        return remote(ref, self.buffers[part, phase][slot], *sems, device_of(coords, self.core))

    def send(self, *args):
        if args[:3] not in self.done:
            self.copy(*args).start()

    def arrive(self, *args):
        if args[:3] not in self.done:
            self.copy(*args).wait_recv()

    def add(self, part, phase, piece, *slots):
        sources = [self.buffers[part, phase][slot] for slot in slots]
        base = place_of(part, piece)
        array, prefix = self.arrays[PARTS[part][0]]

        def one(index):
            spot, position = [], 0
            for entry in base[:-2]:
                if isinstance(entry, pl.Slice):
                    spot.append(entry.start + index[position])
                    position += 1
                else:
                    spot.append(entry)
            spot = (*prefix, *spot, *base[-2:])
            value = array[spot].astype(F32)
            for source in sources:
                value = value + source[(*index, slice(None), slice(None))].astype(F32)
            array[spot] = half(value)

        each_block(shape_of(part, piece), one)

    def neighbours(self, plan):
        return shifted(self.coords, plan.axis, 1), shifted(self.coords, plan.axis, 3)

    def start_far(self, parts, phase):
        for part in parts:
            plan = plan_of(part, phase, self.coords)
            if plan.exchange or plan.direct:
                continue
            right, left = self.neighbours(plan)
            self.send(part, phase, 0, plan.pieces(2)[0], right)
            self.send(part, phase, 1, plan.pieces(2)[1], left)

    def start_near(self, parts, phase):
        for part in parts:
            plan = plan_of(part, phase, self.coords)
            if plan.exchange:
                self.send(part, phase, 0, plan.facing(), facing(self.coords))
                continue
            if plan.direct:
                for by in (1, 3, 2):
                    self.send(part, phase, by, plan.whole(by), plan.at(by))
                continue
            right, left = self.neighbours(plan)
            self.send(part, phase, 2, plan.pieces(1)[1], right)
            self.send(part, phase, 3, plan.pieces(3)[0], left)

    def start(self, parts, phase):
        self.start_far(parts, phase)
        self.start_near(parts, phase)

    def forward(self, parts, phase):
        for part in parts:
            plan = plan_of(part, phase, self.coords)
            if plan.exchange or plan.direct:
                continue
            right, left = self.neighbours(plan)
            self.arrive(part, phase, 0, plan.pieces(2)[0], right)
            self.add(part, phase, plan.pieces(1)[0], 0)
            self.send(part, phase, 4, plan.pieces(1)[0], right)
            self.arrive(part, phase, 1, plan.pieces(2)[1], left)
            self.add(part, phase, plan.pieces(3)[1], 1)
            self.send(part, phase, 5, plan.pieces(3)[1], left)

    def finish(self, parts, phase):
        for part in parts:
            plan = plan_of(part, phase, self.coords)
            if plan.exchange:
                self.arrive(part, phase, 0, plan.facing(), facing(self.coords))
                self.add(part, phase, plan.own(), 0)
                continue
            if plan.direct:
                for by in (1, 3, 2):
                    self.arrive(part, phase, by, plan.whole(by), plan.at(by))
                self.add(part, phase, plan.own(), 1, 3, 2)
                continue
            right, left = self.neighbours(plan)
            self.arrive(part, phase, 3, plan.pieces(3)[0], left)
            self.arrive(part, phase, 4, plan.pieces(1)[0], right)
            self.add(part, phase, plan.pieces(0)[0], 4, 3)
            self.arrive(part, phase, 2, plan.pieces(1)[1], right)
            self.arrive(part, phase, 5, plan.pieces(3)[1], left)
            self.add(part, phase, plan.pieces(0)[1], 2, 5)

    def drain(self):
        for part in SUMMED + THIN:
            for phase in range(3):
                plan = plan_of(part, phase, self.coords)
                if plan.exchange:
                    self.copy(part, phase, 0, plan.own(), facing(self.coords)).wait_send()
                    continue
                if plan.direct:
                    for by in (1, 3, 2):
                        self.copy(part, phase, by, plan.whole(by), plan.at(by)).wait_send()
                    continue
                right, _ = self.neighbours(plan)
                for slot, which in enumerate((0, 1, 1, 0, 0, 1)):
                    if (part, phase, slot) in self.done:
                        continue
                    self.copy(part, phase, slot, plan.pieces(0)[which], right).wait_send()


EARLY = tuple((part, 2, slot) for part in MAIN for slot in (2, 3))


def scatter_buffer_shapes():
    out = []
    for part in SUMMED + THIN:
        for phase in range(3):
            plan = plan_of(part, phase, (0, 0, 0))
            if plan.exchange:
                shapes = [shape_of(part, plan.own())]
            elif plan.direct:
                shapes = [None] + [shape_of(part, plan.own())] * 3
            else:
                first, second = (shape_of(part, piece) for piece in plan.pieces(0))
                shapes = [first, second, second, first, first, second]
            out.append(((part, phase), shapes))
    return out


SCALE = HEAD ** (-0.5)


def turn(values, sign):
    lane = lax.broadcasted_iota(jnp.int32, values.shape, 1)
    ahead = pltpu.roll(values, 96, 1)
    behind = pltpu.roll(values, 32, 1)
    return jnp.where(lane & 32 == 0, sign * ahead, -sign * behind)


def tiles_of(values):
    return [values[:, 128 * t : 128 * t + 128] for t in range(values.shape[1] // 128)]


def rotated(values, cosine, sine):
    return jnp.concatenate(
        [tile * cosine + turn(tile, -1.0) * sine for tile in tiles_of(values)], axis=1
    )


def rotated_back(values, cosine, sine):
    return jnp.concatenate(
        [tile * cosine + turn(tile * sine, 1.0) for tile in tiles_of(values)], axis=1
    )


def low_lanes(shape):
    return lax.broadcasted_iota(jnp.int32, shape, 1) < HEAD


def paired(both):
    swapped = pltpu.roll(both, 64, 1)
    low = low_lanes(both.shape)
    even = [half(jnp.where(low, v, 0.0)) for v in (both, swapped)]
    odd = [half(jnp.where(low, 0.0, v)) for v in (swapped, both)]
    kinds = [jnp.concatenate([even[a], odd[b]]) for a, b in ((0, 0), (0, 1), (1, 1))]
    return [kinds[0]] * 3 + [kinds[1]] + [kinds[2]] * 3


def gathered_place():
    row = lax.broadcasted_iota(jnp.int32, (1024, D), 0)
    feature = lax.broadcasted_iota(jnp.int32, (1024, D), 1)
    slot = row & 15
    odd = (slot >= 7).astype(jnp.int32)
    device = (((row >> 4) & 31) * 2 + odd) * 2 + (row >> 9)
    source = jnp.where(slot < 14, 7 * device + slot - 7 * odd, -1)
    return half((source == feature).astype(jnp.float32))


def vector_maps():
    device = lax.broadcasted_iota(jnp.int32, (128, 1024), 0)
    row = lax.broadcasted_iota(jnp.int32, (128, 1024), 1)
    target = (device & 1) * 512 + (device >> 2) * 16 + ((device >> 1) & 1) * 7
    pick = half((row == target).astype(jnp.float32))
    start = lax.broadcasted_iota(jnp.int32, (128, 2944), 0) * 23
    entry = lax.broadcasted_iota(jnp.int32, (128, 2944), 1)
    owner = half(((entry >= start) & (entry < start + 23)).astype(jnp.float32))
    return pick, owner


def slot_mask(slots):
    return lax.broadcasted_iota(jnp.int32, (128, 2944), 0) == slots


def own_lengths(len_ref, coords, core):
    own = (coords[0] * 16 + coords[1] * 4 + coords[2]) * 2 + core
    lane = lax.broadcasted_iota(jnp.int32, (2, 128), 1)
    length = jnp.sum(jnp.where(lane == own, len_ref[...].astype(F32), 0.0), axis=1, keepdims=True)
    return jnp.broadcast_to(length, (2, 128))


def live_tokens(lengths):
    token = lax.broadcasted_iota(jnp.int32, (128, 1), 0).astype(F32)
    return jnp.concatenate([(token < lengths[b : b + 1, 0:1]).astype(F32) for b in range(2)])


def attention_forward(
    x_ref, rest_ref, lengths, cos_ref, sin_ref, slot_ref,
    middle_ref, h1p_ref, q_ref, k_ref, v_ref, mixed_ref, probs_ref, vector_ref,
):
    place = gathered_place()
    pick, owner = vector_maps()
    stored = rest_ref[:, :, :, :, 32:48, 256:384].reshape(1024, 128)
    by_device = half(product(pick, stored))
    spread = inner_rows(by_device, owner)
    vector = jnp.sum(jnp.where(slot_mask(slot_ref[...]), spread, 0.0), axis=0, keepdims=True)
    vector_ref[...] = vector
    first_gain, second_gain = vector[:, :D], vector[:, D : 2 * D]
    query_bias, narrow_bias = vector[:, 2 * D : 3 * D], vector[:, 3 * D :]
    cosine, sine = cos_ref[...], sin_ref[...]
    inputs = x_ref[...].astype(jnp.float32)
    first_scale = lax.rsqrt(jnp.mean(inputs * inputs, axis=-1, keepdims=True) + NORM_EPSILON)
    normed = half(inputs * first_scale * first_gain)
    placed = half(outer_cols(normed, place))
    h1p_ref[...] = placed
    queries = product(placed, rest_ref[:, :, :, :, 0:16, :].reshape(1024, D)) + query_bias
    narrow = product(placed, rest_ref[:, :, :, :, 32:48, 0:256].reshape(1024, 256)) + narrow_bias
    q_ref[...] = half(rotated(queries, cosine, sine))
    keys = rotated(narrow[:, 0:128], cosine, sine)
    k_ref[...] = half(keys)
    values = narrow[:, 128:256]
    v_ref[...] = half(values)
    position = lax.broadcasted_iota(jnp.int32, (128, 256), 0)
    other = lax.broadcasted_iota(jnp.int32, (128, 256), 1) & 127
    causal = other <= position
    other = other.astype(F32)
    rows = []
    for b in range(2):
        here = slice(128 * b, 128 * b + 128)
        length = lengths[b : b + 1, :]
        allowed = causal & (other < jnp.concatenate([length, length], axis=1))
        key_tiles = paired(keys[here])
        value_tiles = paired(values[here])
        tiles = []
        for t in range(7):
            scores = outer_cols(q_ref[here, 128 * t : 128 * t + 128], key_tiles[t])
            scores = jnp.where(allowed, scores * SCALE, MASKED)
            parts = []
            for part in tiles_of(scores):
                shifted = jnp.exp(part - jnp.max(part, axis=-1, keepdims=True))
                parts.append(shifted * (1.0 / jnp.sum(shifted, axis=-1, keepdims=True)))
            probs = jnp.concatenate(parts, axis=1)
            probs_ref[b, t] = probs
            tiles.append(half(product(half(probs), value_tiles[t])))
        rows.append(jnp.concatenate(tiles, axis=1))
    mixed = half(outer_cols(jnp.concatenate(rows), place))
    mixed_ref[...] = mixed
    middle = inputs + product(mixed, rest_ref[:, :, :, :, 16:32, :].reshape(1024, D))
    middle_ref[...] = middle
    second_scale = lax.rsqrt(jnp.mean(middle * middle, axis=-1, keepdims=True) + NORM_EPSILON)
    return half(middle * second_scale * second_gain)


def mlp_tile(weights, h, e, sums):
    lead = weights.shape[:-2]
    units = 16 * math.prod(lead)
    gate_w, up_w, down_w = (
        weights[..., 16 * k : 16 * k + 16, :].reshape(units, D) for k in range(3)
    )
    gate = outer_cols(h, gate_w)
    up = outer_cols(h, up_w)
    sigma = 0.5 * jnp.tanh(0.5 * gate) + 0.5
    silu = gate * sigma
    hidden = half(silu * up)
    grad_hidden = outer_cols(e, down_w)
    sums[0] += product(hidden, down_w).reshape(2, TOKENS, D)
    grad_gate = half(grad_hidden * up * (sigma + silu * (1.0 - sigma)))
    grad_up = half(grad_hidden * silu)
    sums[1] += (product(grad_gate, gate_w) + product(grad_up, up_w)).reshape(2, TOKENS, D)
    grads = (inner_rows(grad_gate, h), inner_rows(grad_up, h), inner_rows(hidden, e))
    return [half(grad).reshape(*lead, 16, D) for grad in grads]


KEPT = 17


def gather_kernel(
    gate_ref, up_ref, down_ref, query_ref, out_ref, key_ref, value_ref, own_vector_ref,
    x_ref, cot_ref, len_ref, cos_ref, sin_ref, slot_ref, *refs,
):
    coords, core = my_coords()
    z, y, x = coords
    pair, odd = x // 2, x % 2
    lengths = own_lengths(len_ref, coords, core)
    results, (grad_wide_ref, grad_shared_ref, rest_ref) = refs[:KEPT], refs[KEPT : KEPT + 3]
    held = refs[KEPT + 3 : 2 * KEPT + 1]
    (
        wide, shared, rest, stage0, stage1, stage2, h_all, e_all, sums, parcel, tail, tail_own, tail_wide,
        local_sems, send_sems, recv_sems, twin_sems, store_sems, early_sems, kept_sems,
    ) = refs[2 * KEPT + 1 :]
    middle_ref, e_ref, h1p_ref, q_ref, k_ref, v_ref, mixed_ref, probs_ref, vector_ref = held[:9]
    early = held[9:]
    kept = [*held[:9], sums.at[:, core], parcel, *early]

    def keep(first, last):
        return [
            pltpu.make_async_copy(kept[n], results[n], kept_sems.at[n]) for n in range(first, last)
        ]

    units = (gate_ref, up_ref, down_ref)
    for n, ref in enumerate(units):
        for k in range(2):
            wide[z, y, pair, odd, CHUNK * k + 16 * n : CHUNK * k + 16 * n + 16] = half(
                ref[16 * k : 16 * k + 16]
            )
    tail_wide[...] = jnp.zeros_like(tail_wide)
    for parity in range(2):

        @pl.when(odd == parity)
        def _():
            for n, ref in enumerate(units):
                start = 16 * n + 6 * parity
                tail_wide[start : start + 6] = ref[32:38]
            for n, ref in enumerate((query_ref, out_ref)):
                start = CHUNK + 16 * n + 7 * parity
                tail_wide[start : start + 7] = ref[...]
            start = CHUNK + 32 + 7 * parity
            tail_wide[start : start + 7, 0:128] = key_ref[...]
            tail_wide[start : start + 7, 128:256] = value_ref[...]
            tail_wide[start : start + 1, 256:384] = jnp.concatenate(
                [own_vector_ref[...], jnp.zeros((1, 105), F32)], axis=1
            )

    tail_own[...] = half(tail_wide[...])
    greet(coords, core)
    twin = device_of(coords, 1 - core)

    def to_twin(src, dst, slot):
        return remote(src, dst, twin_sems.at[0, slot], twin_sems.at[1, slot], twin)

    gather = Gather(((wide, ()), (shared, ()), (rest, (core,))), coords, core, send_sems, recv_sems)
    partner = device_of((z, y, x + 1 - 2 * odd), core)
    tail_copy = remote(tail_own, tail, twin_sems.at[0, 4], twin_sems.at[1, 4], partner)
    tail_copy.start()
    gather.start((0, 1), 0)
    e_ref[...] = half(cot_ref[...].astype(F32) * live_tokens(lengths))
    e_all[core] = e_ref[...]
    e_copy = to_twin(e_ref, e_all.at[core], 0)
    e_copy.start()
    tail_copy.wait()
    both = half(tail_wide[...] + tail[...].astype(F32))
    shared[z, y, pair] = both[:CHUNK]
    rest[core, z, y, pair] = both[CHUNK:]
    gather.start(THIN, 0)
    gather.start((2,), 0)
    gather.forward(THIN, 0)
    gather.finish(THIN, 0)
    gather.start(THIN, 1)
    gather.forward(WIDE, 0)
    gather.forward(THIN, 1)
    gather.finish(THIN, 1)
    gather.start(THIN, 2)
    gather.finish(WIDE, 0)
    gather.start(WIDE, 1)
    gather.forward(THIN, 2)
    gather.finish(THIN, 2)
    rest_copy = to_twin(rest.at[core], rest.at[core], 1)
    rest_copy.start()
    gather.forward(WIDE, 1)
    gather.finish(WIDE, 1)
    gather.start(WIDE, 2)
    rest_copy.wait()
    rest_store = pltpu.make_async_copy(rest, rest_ref, local_sems.at[0])
    rest_store.start()
    h_all[core] = attention_forward(
        x_ref, rest, lengths, cos_ref, sin_ref, slot_ref,
        middle_ref, h1p_ref, q_ref, k_ref, v_ref, mixed_ref, probs_ref, vector_ref,
    )
    h_copy = to_twin(h_all.at[core], h_all.at[core], 2)
    h_copy.start()
    for copy in keep(0, 9):
        copy.start()
    sums[...] = jnp.zeros_like(sums)
    e_copy.wait()
    h_copy.wait()
    stages = (stage0, stage1, stage2)

    def early_copy(t, slot):
        axis = PARTS[t][3][2]
        which = 3 - slot
        place = [slice(None)] * (len(stages[t].shape) - 1)
        place[1 if t == 2 else 0] = pl.ds(which, 1) if t == 2 else pl.ds(2 * which, 2)
        place[-1] = pl.ds(*PARTS[MAIN[t]][5])
        return remote(
            stages[t].at[(slot - 1) % 2].at[tuple(place)],
            early[2 * t + slot - 2],
            early_sems.at[0, t, slot - 2],
            early_sems.at[1, t, slot - 2],
            device_of(shifted(coords, axis, 1 if slot == 2 else 3), core),
        )

    def tile_places(j):
        return (
            (wide, grad_wide_ref, (j, slice(None), slice(None), slice(None), pl.ds(0, CHUNK))),
            (wide, grad_wide_ref, (slice(None), slice(None), j // 2, j % 2, pl.ds(CHUNK, CHUNK))),
            (shared, grad_shared_ref, (slice(None), j, slice(None), pl.ds(0, CHUNK))),
        )

    def step(k, carry):
        @pl.when(k == 1)
        def _():
            gather.near(WIDE, 2)

        @pl.when(k == 3)
        def _():
            gather.far(WIDE, 2)

        offset = jnp.where(k < 2, k, 5 - k)
        h = h_all[...].reshape(2 * TOKENS, D)
        e = e_all[...].reshape(2 * TOKENS, D)
        for t, axis in enumerate((0, 2, 1)):
            j = (coords[axis] + offset) % 4
            source, target, index = tile_places(j)[t]
            grads = mlp_tile(source[(*index, slice(None))], h, e, sums)
            copy = pltpu.make_async_copy(
                stages[t].at[k % 2], target.at[(*index, slice(None))], store_sems.at[t, k % 2]
            )

            @pl.when(k > 1)
            def _():
                copy.wait()

            @pl.when(k == 3)
            def _():
                early_copy(t, 2).wait_send()

            for place, grad in enumerate(grads):
                stages[t][k % 2, ..., 16 * place : 16 * place + 16, :] = grad
            copy.start()

            @pl.when(k == 1)
            def _():
                early_copy(t, 2).start()

            @pl.when(k == 2)
            def _():
                early_copy(t, 3).start()

        @pl.when(k == 0)
        def _():
            gather.forward(WIDE, 2)

        return carry

    lax.fori_loop(0, 4, step, 0)
    parcel[...] = half(sums[:, 1 - core])
    for copy in keep(9, 11):
        copy.start()
    for t in range(3):
        _, target, index = tile_places(0)[t]
        for which in range(2):
            pltpu.make_async_copy(
                stages[t].at[which], target.at[(*index, slice(None))], store_sems.at[t, which]
            ).wait()
        early_copy(t, 3).wait_send()
        early_copy(t, 2).wait_recv()
        early_copy(t, 3).wait_recv()
        for copy in keep(11 + 2 * t, 13 + 2 * t):
            copy.start()
    rest_store.wait()
    for copy in keep(0, KEPT):
        copy.wait()
    gather.drain()


def attention_backward(
    between, x_ref, e_ref, rest_ref, cos_ref, sin_ref, slot_ref,
    middle_ref, h1p_ref, q_ref, k_ref, v_ref, mixed_ref, probs_ref, vector_ref, dh2_ref,
    input_grad_ref, grad_ref,
):
    place = gathered_place()
    pick, owner = vector_maps()
    vector = vector_ref[...]
    first_gain, second_gain = vector[:, :D], vector[:, D : 2 * D]
    cosine, sine = cos_ref[...], sin_ref[...]
    middle = middle_ref[...]
    second_scale = lax.rsqrt(jnp.mean(middle * middle, axis=-1, keepdims=True) + NORM_EPSILON)
    second_normed = middle * second_scale
    dh2 = dh2_ref[...]
    second_gain_grad = jnp.sum(dh2 * second_normed, axis=0, keepdims=True)
    grad_middle = e_ref[...].astype(jnp.float32) + norm_back(
        dh2 * second_gain, second_normed, second_scale
    )
    branch = half(grad_middle)
    wide = rest_ref[:, :, :, :, 16:32, :].reshape(1024, D)
    grad_ref[:, :, :, :, 16:32, :] = half(inner_rows(mixed_ref[...], branch)).reshape(2, 4, 4, 2, 16, D)
    grad_mixed = half(product(half(outer_cols(branch, wide)), place))
    low = low_lanes((128, 128))
    query_rows, key_rows, value_rows = [], [], []
    for b in range(2):
        here = slice(128 * b, 128 * b + 128)
        key_tiles = paired(k_ref[here, :].astype(jnp.float32))
        value_tiles = paired(v_ref[here, :].astype(jnp.float32))
        tiles = []
        sums = [[jnp.zeros((128, 128), jnp.float32) for _ in range(4)] for _ in range(2)]
        for t in range(7):
            head = grad_mixed[here, 128 * t : 128 * t + 128]
            grad_probs = outer_cols(head, value_tiles[t])
            probs = probs_ref[b, t]
            parts = []
            for p, g in zip(tiles_of(probs), tiles_of(grad_probs)):
                parts.append(half(p * (g - jnp.sum(p * g, axis=-1, keepdims=True))))
            grad_scores = jnp.concatenate(parts, axis=1)
            tiles.append(product(grad_scores, key_tiles[t]) * SCALE)
            for which, (left, right) in enumerate(
                ((grad_scores, q_ref[here, 128 * t : 128 * t + 128]), (half(probs), head))
            ):
                both = inner_rows(left, right)
                even, odd = (2 * t) // 7, (2 * t + 1) // 7
                sums[which][even] += both[0:128]
                sums[which][2 + odd] += both[128:256]
        query_rows.append(jnp.concatenate(tiles, axis=1))
        joined = []
        for which in range(2):
            even0, even1, odd0, odd1 = sums[which]
            joined.append(
                jnp.where(low, even0 + pltpu.roll(odd0, 64, 1), odd1 + pltpu.roll(even1, 64, 1))
            )
        key_rows.append(joined[0] * SCALE)
        value_rows.append(joined[1])
    between()
    grad_query = half(rotated_back(jnp.concatenate(query_rows), cosine, sine))
    grad_key = half(rotated_back(jnp.concatenate(key_rows), cosine, sine))
    grad_narrow = jnp.concatenate([grad_key, half(jnp.concatenate(value_rows))], axis=1)
    placed = h1p_ref[...]
    grad_ref[:, :, :, :, 0:16, :] = half(inner_rows(placed, grad_query)).reshape(2, 4, 4, 2, 16, D)
    grad_ref[:, :, :, :, 32:48, 0:256] = half(inner_rows(placed, grad_narrow)).reshape(2, 4, 4, 2, 16, 256)
    bias_grad = jnp.sum(
        jnp.concatenate([grad_query, grad_narrow], axis=1).astype(jnp.float32), axis=0, keepdims=True
    )
    grad_placed = outer_cols(grad_query, rest_ref[:, :, :, :, 0:16, :].reshape(1024, D)) + outer_cols(
        grad_narrow, rest_ref[:, :, :, :, 32:48, 0:256].reshape(1024, 256)
    )
    high = half(grad_placed)
    remainder = half(grad_placed - high.astype(jnp.float32))
    grad_normed = product(high, place) + product(remainder, place)
    inputs = x_ref[...].astype(jnp.float32)
    first_scale = lax.rsqrt(jnp.mean(inputs * inputs, axis=-1, keepdims=True) + NORM_EPSILON)
    first_normed = inputs * first_scale
    first_gain_grad = jnp.sum(grad_normed * first_normed, axis=0, keepdims=True)
    input_grad_ref[...] = half(
        grad_middle + norm_back(grad_normed * first_gain, first_normed, first_scale)
    )
    vector_grad = jnp.concatenate([first_gain_grad, second_gain_grad, bias_grad], axis=1)
    spread = half(jnp.where(slot_mask(slot_ref[...]), vector_grad, 0.0))
    by_device = half(outer_cols(owner, spread))
    stored = half(inner_rows(pick, by_device))
    grad_ref[:, :, :, :, 32:48, 256:384] = stored.reshape(2, 4, 4, 2, 16, 128)
    grad_ref[:, :, :, :, 32:48, 384:] = jnp.zeros((2, 4, 4, 2, 16, D - 384), jnp.bfloat16)


LOADED = (
    "parcel", "own", "middle", "e", "x", "rest", "h1p", "q", "k", "v", "mixed", "probs", "vector",
)


def scatter_kernel(
    len_ref, cos_ref, sin_ref, slot_ref, grad_wide_ref, grad_shared_ref, *refs,
):
    coords, core = my_coords()
    z, y, x = coords
    pair, odd = x // 2, x % 2
    count = len(LOADED) + len(EARLY)
    sources, (output_ref, input_grad_ref, out_ref) = refs[:count], refs[count : count + 3]
    held = refs[count + 3 : 2 * count + 3]
    (
        wide, shared, thin, joined, mine, theirs, arrived, dh2_ref,
        load_sems, send_sems, recv_sems, twin_sems, pair_sems, held_sems,
    ) = refs[2 * count + 3 : 2 * count + 17]
    buffers = refs[2 * count + 17 :]
    (
        parcel_ref, own_ref, middle_ref, e_ref, x_ref, rest_ref, h1p_ref, q_ref, k_ref, v_ref,
        mixed_ref, probs_ref, vector_ref,
    ) = held[: len(LOADED)]
    fetches = [
        pltpu.make_async_copy(sources[n], held[n], held_sems.at[n]) for n in range(count)
    ]
    named, position = {}, 0
    early = dict(zip(EARLY, held[len(LOADED) :]))
    for key, shapes in scatter_buffer_shapes():
        named[key] = []
        for slot in range(len(shapes)):
            if (*key, slot) in early:
                named[key].append(early[(*key, slot)])
            elif shapes[slot] is None:
                named[key].append(None)
            else:
                named[key].append(buffers[position])
                position += 1
    scatter = Scatter(((wide, ()), (shared, ()), (thin, (core,))), coords, core, named, send_sems, recv_sems, EARLY)

    def load(part, by):
        spec = [FULL] * 3
        axis = PARTS[part][3][2]
        spec[axis] = (coords[axis] + by) % 4
        place = place_of(part, tuple(spec))
        source = (grad_wide_ref, grad_shared_ref)[PARTS[part][0]]
        target = (wide, shared)[PARTS[part][0]]
        return pltpu.make_async_copy(source.at[place], target.at[place], load_sems.at[part, by])

    for by in (2, 1, 3, 0):
        for part in SUMMED:
            load(part, by).start()
    for copy in fetches:
        copy.start()
    greet(coords, core)

    for part in SUMMED:
        load(part, 2).wait()
        scatter.start_far((part,), 2)
    for part in SUMMED:
        load(part, 1).wait()
        load(part, 3).wait()
    scatter.start_near(SIDE, 2)

    def between():
        scatter.forward(SUMMED, 2)

    for copy in fetches[:3]:
        copy.wait()
    parcel_copy = remote(
        parcel_ref, arrived, twin_sems.at[0, 1], twin_sems.at[1, 1], device_of(coords, 1 - core)
    )
    parcel_copy.start()
    for copy in fetches[3:]:
        copy.wait()
    parcel_copy.wait()
    output_ref[...] = half(
        (middle_ref[...] + (own_ref[0] + arrived[0].astype(F32))) * live_tokens(own_lengths(len_ref, coords, core))
    )
    dh2_ref[...] = own_ref[1] + arrived[1].astype(F32)
    attention_backward(
        between, x_ref, e_ref, rest_ref, cos_ref, sin_ref, slot_ref,
        middle_ref, h1p_ref, q_ref, k_ref, v_ref, mixed_ref, probs_ref, vector_ref, dh2_ref,
        input_grad_ref, thin,
    )
    twin_copy = remote(
        thin.at[1 - core], joined, twin_sems.at[0, 0], twin_sems.at[1, 0], device_of(coords, 1 - core)
    )
    twin_copy.start()
    for part in SUMMED:
        load(part, 0).wait()
    twin_copy.wait()

    def join(index):
        thin[(core, *index)] = half(thin[(core, *index)].astype(F32) + joined[index].astype(F32))

    each_block((4, 4, 2, CHUNK, D), join)
    scatter.start(THIN, 2)
    for part in SUMMED:
        scatter.finish((part,), 2)
        scatter.start((part,), 1)
    scatter.forward(THIN, 2)
    scatter.finish(THIN, 2)
    scatter.start(THIN, 1)
    scatter.forward(SUMMED, 1)
    scatter.forward(THIN, 1)
    for part in SUMMED:
        scatter.finish((part,), 1)
        scatter.start((part,), 0)
    scatter.finish(THIN, 1)
    scatter.start(THIN, 0)
    scatter.forward(SUMMED, 0)
    scatter.forward(THIN, 0)
    scatter.finish(SUMMED, 0)
    scatter.finish(THIN, 0)
    mine[0] = shared[z, y, pair]
    mine[1] = thin[core, z, y, pair]
    partner = device_of((z, y, x + 1 - 2 * odd), core)
    pair_copy = remote(mine, theirs, pair_sems.at[0], pair_sems.at[1], partner)
    pair_copy.start()
    pair_copy.wait()
    out_ref[0] = wide[z, y, pair, odd, 0:CHUNK].astype(F32)
    out_ref[1] = wide[z, y, pair, odd, CHUNK : 2 * CHUNK].astype(F32)
    out_ref[2] = mine[0].astype(F32) + theirs[0].astype(F32)
    out_ref[3] = mine[1].astype(F32) + theirs[1].astype(F32)
    scatter.drain()


def layer(weights, tokens, cotangent, lengths):
    vmem = pl.BlockSpec(memory_space=pltpu.VMEM)
    anywhere = pl.BlockSpec(memory_space=pl.ANY)
    x = tokens.reshape(TOKENS, D)
    freqs = ROPE_BASE ** (-np.arange(HEAD // 2) * 2.0 / HEAD)
    angles = np.tile(np.arange(128)[:, None] * freqs[None, :], (2, 4))
    tables = (
        np.cos(angles).astype(np.float32),
        np.sin(angles).astype(np.float32),
        (np.arange(2944, dtype=np.int32) % 23)[None],
    )
    buffers = dict(scatter_buffer_shapes())
    kept = [
        ((TOKENS, D), F32),
        ((TOKENS, D), BF16),
        ((TOKENS, 1024), BF16),
        ((TOKENS, D), BF16),
        ((TOKENS, 128), BF16),
        ((TOKENS, 128), BF16),
        ((TOKENS, 1024), BF16),
        ((2, 7, 128, 256), F32),
        ((1, 2944), F32),
        ((2, TOKENS, D), F32),
        ((2, TOKENS, D), BF16),
    ] + [(buffers[part, stage][slot], BF16) for part, stage, slot in EARLY]
    large = [
        ((4, 4, 2, 2, 2 * CHUNK, D), BF16),
        ((4, 4, 2, CHUNK, D), BF16),
        ((2, 4, 4, 2, CHUNK, D), BF16),
    ]

    def shapes(pairs):
        return [jax.ShapeDtypeStruct(shape, dtype) for shape, dtype in pairs]

    def scratch(pairs):
        return [pltpu.VMEM(shape, dtype) for shape, dtype in pairs]

    results = pl.pallas_call(
        gather_kernel,
        out_shape=shapes(kept + large),
        in_specs=[vmem] * 14,
        out_specs=[anywhere] * (KEPT + 3),
        scratch_shapes=scratch(
            kept[:9]
            + kept[11:]
            + large
            + [
                ((2, 4, 2, 2, CHUNK, D), BF16),
                ((2, 4, 4, CHUNK, D), BF16),
                ((2, 4, 2, CHUNK, D), BF16),
                ((2, TOKENS, D), BF16),
                ((2, TOKENS, D), BF16),
                ((2, 2, TOKENS, D), F32),
                ((2, TOKENS, D), BF16),
                ((2 * CHUNK, D), BF16),
                ((2 * CHUNK, D), BF16),
                ((2 * CHUNK, D), F32),
            ]
        )
        + [
            pltpu.SemaphoreType.DMA((3,)),
            pltpu.SemaphoreType.DMA((len(PARTS), 3, 6)),
            pltpu.SemaphoreType.DMA((len(PARTS), 3, 6)),
            pltpu.SemaphoreType.DMA((2, 5)),
            pltpu.SemaphoreType.DMA((3, 2)),
            pltpu.SemaphoreType.DMA((2, 3, 2)),
            pltpu.SemaphoreType.DMA((KEPT,)),
        ],
        compiler_params=pltpu.CompilerParams(
            collective_id=0, has_side_effects=True, vmem_limit_bytes=61 * 2**20
        ),
    )(*weights, x, cotangent.reshape(TOKENS, D), lengths, *tables)
    middle, e, h1p, q, k, v, mixed, probs, vector, own, parcel = results[:11]
    early = results[11:KEPT]
    grad_wide, grad_shared, rest = results[KEPT:]
    loaded = dict(
        x=x, e=e, rest=rest, middle=middle, h1p=h1p, q=q, k=k, v=v, mixed=mixed, probs=probs,
        vector=vector, own=own, parcel=parcel,
    )
    fetched = [loaded[name] for name in LOADED] + list(early)
    output, input_grad, grads = pl.pallas_call(
        scatter_kernel,
        out_shape=shapes([((TOKENS, D), BF16), ((TOKENS, D), BF16), ((4, CHUNK, D), F32)]),
        in_specs=[vmem] * 4 + [anywhere] * (2 + len(fetched)),
        out_specs=[vmem] * 3,
        scratch_shapes=scratch(
            [(value.shape, value.dtype) for value in fetched]
            + large[:2]
            + [
                ((2, 4, 4, 2, CHUNK, D), BF16),
                ((4, 4, 2, CHUNK, D), BF16),
                ((2, CHUNK, D), BF16),
                ((2, CHUNK, D), BF16),
                ((2, TOKENS, D), BF16),
                ((TOKENS, D), F32),
            ]
        )
        + [
            pltpu.SemaphoreType.DMA((len(PARTS), 4)),
            pltpu.SemaphoreType.DMA((len(PARTS), 3, 6)),
            pltpu.SemaphoreType.DMA((len(PARTS), 3, 6)),
            pltpu.SemaphoreType.DMA((2, 2)),
            pltpu.SemaphoreType.DMA((2,)),
            pltpu.SemaphoreType.DMA((len(fetched),)),
        ]
        + [
            pltpu.VMEM(shape, BF16)
            for key, group in buffers.items()
            for slot, shape in enumerate(group)
            if shape is not None and (*key, slot) not in EARLY
        ],
        compiler_params=pltpu.CompilerParams(
            collective_id=1, has_side_effects=True, vmem_limit_bytes=62 * 2**20
        ),
    )(lengths, *tables, grad_wide, grad_shared, *fetched)
    return output, input_grad, grads


def newton_schulz(gram, values):
    gram_half = half(gram)
    first = half(NEWTON_B * gram + NEWTON_C * product(gram_half, gram_half))
    cross = product(gram_half, first)
    after = NEWTON_A * NEWTON_A * gram + 2.0 * NEWTON_A * cross + product(half(cross), first)
    after_half = half(after)
    second = half(NEWTON_B * after + NEWTON_C * product(after_half, after_half))
    values = half(NEWTON_A * values + product(half(values), first))
    return half(NEWTON_A * values.astype(F32) + product(values, second))


BLOCKS = [(i, j) for i in range(7) for j in range(i, 7)]
JOB_ROWS = (48, 48, 48, 16, 16, 16, 16)


def own_momenta(grads_ref, priors, momenta, odd):
    for parity in range(2):

        @pl.when(odd == parity)
        def _():
            for n in range(3):
                for k, (start, size) in enumerate(((0, 16), (16, 16), (32, 6))):
                    base = 16 * n + (6 * parity if k == 2 else 0)
                    momenta[n][start : start + size] = (
                        MOMENTUM * priors[n][start : start + size] + grads_ref[k, base : base + size]
                    )
            for n in range(4):
                base = 16 * min(n, 2) + 7 * parity
                lanes = slice(0, D) if n < 2 else slice(128 * n - 256, 128 * n - 128)
                momenta[3 + n][...] = (
                    MOMENTUM * priors[3 + n][...] + grads_ref[3, base : base + 7, lanes]
                )


def update_kernel(output_ref, input_grad_ref, grads_ref, tall_ref, short_ref, *refs):
    priors, masters, (first_ref, second_ref, vector_ref) = refs[:7], refs[7:14], refs[14:17]
    momenta, updated, vector_outs = refs[17:24], refs[24:31], refs[31:34]
    refs[34][...] = output_ref[...]
    refs[35][...] = input_grad_ref[...]
    odd = lax.axis_index("dp") % 2
    own_momenta(grads_ref, priors, momenta, odd)
    for n in range(7):
        size = FF if n < 3 else D
        got = tall_ref[n].astype(F32)[:38] if n < 3 else short_ref[n - 3].astype(F32)[:7]
        got = got[:, :128] if n > 4 else got
        updated[n][...] = masters[n][...] * (1.0 - MUON_RATE * MUON_DECAY) - (
            MUON_RATE * 0.2 * math.sqrt(size) * got
        )
    for parity in range(2):

        @pl.when(odd == parity)
        def _():
            start = 32 + 7 * parity
            grad = grads_ref[3, start : start + 1, 256:384][:, :23]
            first = BETA_FIRST * first_ref[...] + (1.0 - BETA_FIRST) * grad
            second = BETA_SECOND * second_ref[...] + (1.0 - BETA_SECOND) * grad * grad
            first_hat = first / (1.0 - BETA_FIRST**STEP)
            second_hat = second / (1.0 - BETA_SECOND**STEP)
            vector_outs[0][...] = first
            vector_outs[1][...] = second
            vector_outs[2][...] = vector_ref[...] * (1.0 - ADAM_RATE * ADAM_DECAY) - (
                ADAM_RATE * first_hat / (jnp.sqrt(second_hat) + ADAM_EPSILON)
            )


def muon_kernel(
    grads_ref, prior0, prior1, prior2, prior3, prior4, prior5, prior6, tall_out_ref, short_out_ref,
    momentum0, momentum1, momentum2, momentum3, momentum4, momentum5, momentum6,
    tall_wide, short_wide, tall_ref, short_ref, rows, gram_out, gram_twin, gram_half_sum, gram_in, gram_all, gram, back, tall_got, short_got,
    job_sems, twin_sems, sum_sems, all_sems, back_sems,
):
    priors = (prior0, prior1, prior2, prior3, prior4, prior5, prior6)
    momenta = (momentum0, momentum1, momentum2, momentum3, momentum4, momentum5, momentum6)
    coords, core = my_coords()
    z, y, x = coords
    job = z * 2 + y // 2
    source = z * 2 + y // 2
    member = (y % 2) * 4 + x
    tall_wide[...] = jnp.zeros_like(tall_wide)
    short_wide[...] = jnp.zeros_like(short_wide)
    own_momenta(grads_ref, priors, momenta, x % 2)
    for n in range(3):
        tall_wide[n, 0:38] = momenta[n][...]
    for n in range(4):
        short_wide[n, 0:7, 0 : D if n < 2 else 128] = momenta[3 + n][...]
    tall_ref[...] = half(tall_wide[...])
    short_ref[...] = half(short_wide[...])
    twin = device_of(coords, 1 - core)

    def group(peer):
        return device_of((z, (y // 2) * 2 + peer // 4, peer % 4), core)

    def square(k):
        return device_of((k // 2, (k % 2) * 2 + y % 2, x), core)

    barrier = pltpu.get_barrier_semaphore()
    for k in range(1, 8):
        for device in (group((member + k) % 8), square((source + k) % 8)):
            pl.semaphore_signal(barrier, inc=1, device_id=device, device_id_type=MESH)
    pl.semaphore_signal(barrier, inc=1, device_id=twin, device_id_type=MESH)
    pl.semaphore_wait(barrier, 15)

    def copy(src, dst, sems, slot, device):
        return remote(src, dst, sems.at[0, slot], sems.at[1, slot], device)

    def mine(m, tall, short):
        return tall.at[m] if m < 3 else short.at[m - 3]

    def job_copy(m):
        return remote(
            mine(m, tall_ref, short_ref),
            rows.at[source, pl.ds(0, JOB_ROWS[m])],
            job_sems.at[0, m],
            job_sems.at[1, source],
            square(m),
        )

    for m in range(7):

        @pl.when(job != m)
        def _():
            job_copy(m).start()

    for kind in range(2):
        count = (48, 16)[kind]

        @pl.when((job >= 3 * kind) & (job < 3 + 4 * kind))
        def _():
            if kind == 1:
                rows[:, 16:48] = jnp.zeros((8, 32, D), BF16)
                rows[source, 0:16] = short_ref[job - 3]
            else:
                rows[source] = tall_ref[job]
            for k in range(1, 8):
                other = (source + k) % 8
                arrival = rows.at[other, pl.ds(0, count)]
                remote(
                    arrival, arrival, job_sems.at[0, 0], job_sems.at[1, other], square(other)
                ).wait_recv()

    @pl.when(job < 7)
    def _():
        flat = rows[...].reshape(384, D)
        gram[...] = inner_rows(flat, flat)
        for index, (i, j) in enumerate(BLOCKS):
            gram_out[index // 16, index % 16] = half(
                gram[128 * i : 128 * i + 128, 128 * j : 128 * j + 128]
            )
        gram_out[1, 12:16] = jnp.zeros((4, 128, 128), BF16)
        twin_copy = copy(gram_out.at[1 - core], gram_twin, twin_sems, 0, twin)
        twin_copy.start()
        twin_copy.wait()
        gram_half_sum[...] = half(gram_out[core].astype(F32) + gram_twin[...].astype(F32))

        def sum_copy(k):
            peer = (member + k) % 8
            return copy(
                gram_half_sum.at[pl.ds(2 * peer, 2)], gram_in.at[k], sum_sems, k, group(peer)
            )

        for k in range(1, 8):
            sum_copy(k).start()
        total = gram_half_sum[pl.ds(2 * member, 2)].astype(F32)
        for k in range(1, 8):
            sum_copy(k).wait_recv()
            total = total + gram_in[k].astype(F32)
        gram_all[core, pl.ds(2 * member, 2)] = half(total)

        def all_copy(k, owner):
            ref = gram_all.at[core, pl.ds(2 * owner, 2)]
            return copy(ref, ref, all_sems, k, group((member + k) % 8))

        for k in range(1, 8):
            all_copy(k, member).start()
        for k in range(1, 8):
            all_copy(k, (member + 8 - k) % 8).wait_recv()
        last_copy = copy(gram_all.at[core], gram_all.at[core], twin_sems, 1, twin)
        last_copy.start()
        last_copy.wait()

        eye = lax.broadcasted_iota(jnp.int32, (128, 128), 0) == lax.broadcasted_iota(
            jnp.int32, (128, 128), 1
        )
        trace = 0.0
        for index, (i, j) in enumerate(BLOCKS):
            block = gram_all[index // 16, index % 16].astype(F32)
            gram[128 * i : 128 * i + 128, 128 * j : 128 * j + 128] = block
            if i == j:
                trace = trace + jnp.sum(jnp.where(eye, block, 0.0))
            else:
                gram[128 * j : 128 * j + 128, 128 * i : 128 * i + 128] = block.T
        inverse = 1.0 / (jnp.sqrt(jnp.full((1, 1), trace)) + 1e-07)
        moved = newton_schulz(
            gram[...] * (inverse * inverse), rows[...].reshape(384, D).astype(F32) * inverse
        )
        back[...] = moved.reshape(8, 48, D)
        for k in range(1, 8):
            sum_copy(k).wait_send()
            all_copy(k, member).wait_send()

    for m in range(7):

        @pl.when(job == m)
        def _():
            copies = []
            for k in range(1, 8):
                other = (source + k) % 8
                copies.append(
                    remote(
                        back.at[other, pl.ds(0, JOB_ROWS[m])],
                        mine(m, tall_got, short_got),
                        back_sems.at[0, k],
                        back_sems.at[1, m],
                        square(other),
                    )
                )
            for item in copies:
                item.start()
            if m < 3:
                tall_got[m] = back[source]
            else:
                short_got[m - 3] = back[source, 0:16]
            for item in copies:
                item.wait_send()

    for m in range(7):

        @pl.when(job != m)
        def _():
            arrival = mine(m, tall_got, short_got)
            remote(arrival, arrival, back_sems.at[0, 0], back_sems.at[1, m], square(m)).wait_recv()
            job_copy(m).wait_send()

    tall_out_ref[...] = tall_got[...]
    short_out_ref[...] = short_got[...]


def muon(results, grads, priors, masters, vectors):
    vmem = pl.BlockSpec(memory_space=pltpu.VMEM)
    tall, short = pl.pallas_call(
        muon_kernel,
        out_shape=(
            jax.ShapeDtypeStruct((3, 48, D), BF16),
            jax.ShapeDtypeStruct((4, 16, D), BF16),
        ),
        in_specs=[vmem] * 8,
        out_specs=[vmem] * 2,
        scratch_shapes=[
            *(pltpu.VMEM(value.shape, F32) for value in priors),
            pltpu.VMEM((3, 48, D), F32),
            pltpu.VMEM((4, 16, D), F32),
            pltpu.VMEM((3, 48, D), BF16),
            pltpu.VMEM((4, 16, D), BF16),
            pltpu.VMEM((8, 48, D), BF16),
            pltpu.VMEM((2, 16, 128, 128), BF16),
            pltpu.VMEM((16, 128, 128), BF16),
            pltpu.VMEM((16, 128, 128), BF16),
            pltpu.VMEM((8, 2, 128, 128), BF16),
            pltpu.VMEM((2, 16, 128, 128), BF16),
            pltpu.VMEM((D, D), F32),
            pltpu.VMEM((8, 48, D), BF16),
            pltpu.VMEM((3, 48, D), BF16),
            pltpu.VMEM((4, 16, D), BF16),
            pltpu.SemaphoreType.DMA((2, 8)),
            pltpu.SemaphoreType.DMA((2, 2)),
            pltpu.SemaphoreType.DMA((2, 8)),
            pltpu.SemaphoreType.DMA((2, 8)),
            pltpu.SemaphoreType.DMA((2, 8)),
        ],
        compiler_params=pltpu.CompilerParams(
            collective_id=3, has_side_effects=True, vmem_limit_bytes=58 * 2**20
        ),
    )(grads, *priors)
    outs = [*priors, *masters, *vectors]
    return pl.pallas_call(
        update_kernel,
        out_shape=[jax.ShapeDtypeStruct(value.shape, value.dtype) for value in [*outs, *results]],
        in_specs=[vmem] * 22,
        out_specs=[vmem] * 19,
    )(*results, grads, tall, short, *outs)


def body(
    inputs,
    cotangent,
    lengths,
    query_weight,
    key_weight,
    value_weight,
    out_weight,
    gate_weight,
    up_weight,
    down_weight,
    vectors,
    query_prior,
    key_prior,
    value_prior,
    out_prior,
    gate_prior,
    up_prior,
    down_prior,
    first_prior,
    second_prior,
):
    weights = (
        gate_weight.T, up_weight.T, down_weight, query_weight, out_weight, key_weight, value_weight,
        vectors[None],
    )
    block_output, input_grad, grads = layer(weights, inputs[:, 0], cotangent[:, 0], lengths)
    results = muon(
        (block_output, input_grad),
        grads,
        (gate_prior.T, up_prior.T, down_prior, query_prior, out_prior, key_prior, value_prior),
        (gate_weight.T, up_weight.T, down_weight, query_weight, out_weight, key_weight, value_weight),
        (first_prior[None], second_prior[None], vectors[None]),
    )

    def ordered(gate, up, down, query, out, key, value):
        return query, key, value, out, gate.T, up.T, down

    return (
        *(value.reshape(2, 1, 128, D) for value in results[17:]),
        *ordered(*results[:7]),
        *ordered(*results[7:14]),
        *(value[0] for value in results[14:17]),
    )


def solution(mesh):
    placed = (
        P(None, ("dp", "narrow"), None, None),
        P(None, ("dp", "narrow"), None, None),
        P(),
        P(("dp", "narrow"), None),
        P(("dp", "narrow"), None),
        P(("dp", "narrow"), None),
        P(("dp", "narrow"), None),
        P(None, ("dp", "narrow")),
        P(None, ("dp", "narrow")),
        P(("dp", "narrow"), None),
        P(("dp", "narrow")),
        P(("dp", "narrow"), None),
        P(("dp", "narrow"), None),
        P(("dp", "narrow"), None),
        P(("dp", "narrow"), None),
        P(None, ("dp", "narrow")),
        P(None, ("dp", "narrow")),
        P(("dp", "narrow"), None),
        P(("dp", "narrow")),
        P(("dp", "narrow")),
    )
    return jax.shard_map(
        body,
        mesh=mesh,
        in_specs=placed,
        out_specs=(
            P(None, ("dp", "narrow"), None, None),
            P(None, ("dp", "narrow"), None, None),
            P(("dp", "narrow"), None),
            P(("dp", "narrow"), None),
            P(("dp", "narrow"), None),
            P(("dp", "narrow"), None),
            P(None, ("dp", "narrow")),
            P(None, ("dp", "narrow")),
            P(("dp", "narrow"), None),
            P(("dp", "narrow"), None),
            P(("dp", "narrow"), None),
            P(("dp", "narrow"), None),
            P(("dp", "narrow"), None),
            P(None, ("dp", "narrow")),
            P(None, ("dp", "narrow")),
            P(("dp", "narrow"), None),
            P(("dp", "narrow")),
            P(("dp", "narrow")),
            P(("dp", "narrow")),
        ),
        check_vma=False,
    )
```

```python
import math

import jax
import jax.numpy as jnp
import numpy as np
from jax import lax
from jax.experimental import pallas as pl
from jax.experimental.pallas import tpu as pltpu
from jax.sharding import PartitionSpec as P

D = 896
FF = 4864
HEADS = 14
KV_HEADS = 2
HEAD = 64
STEP = 10


NORM_EPSILON = 1e-06
ROPE_BASE = 1000000.0
MOMENTUM = 0.95
NEWTON_A = 3.4445
NEWTON_B = -4.775
NEWTON_C = 2.0315
MUON_RATE = 0.4
MUON_DECAY = 0.1
ADAM_RATE = 0.5
ADAM_DECAY = 0.01
BETA_FIRST = 0.9
BETA_SECOND = 0.999
ADAM_EPSILON = 1e-08
MASKED = -1e30


def product(left, right):
    return jnp.dot(left, right, preferred_element_type=jnp.float32)


def inner_rows(left, right):
    return lax.dot_general(
        left, right, (((0,), (0,)), ((), ())), preferred_element_type=jnp.float32
    )


def outer_cols(left, right):
    return lax.dot_general(
        left, right, (((1,), (1,)), ((), ())), preferred_element_type=jnp.float32
    )


def norm_back(grad, normed, scale):
    return scale * (grad - normed * jnp.mean(grad * normed, axis=-1, keepdims=True))


def half(value):
    return value.astype(jnp.bfloat16)


MESH = pl.DeviceIdType.MESH
TOKENS = 256
FULL = (0, 4)
BF16 = jnp.bfloat16
F32 = jnp.float32
CHUNK = 48
PARTS = (
    (0, 0, CHUNK, (2, 1, 0), False, (0, D)),
    (0, CHUNK, CHUNK, (1, 0, 2), False, (0, D)),
    (1, 0, CHUNK, (0, 2, 1), True, (0, D)),
    (2, 0, 16, (2, 1, 0), True, (0, D)),
    (2, 16, 16, (1, 0, 2), True, (0, 512)),
    (2, 16, 16, (0, 2, 1), True, (512, 384)),
    (2, 32, 16, (0, 2, 1), True, (0, 384)),
    (0, 0, CHUNK, (2, 1, 0), False, (0, 768)),
    (0, CHUNK, CHUNK, (1, 0, 2), False, (0, 768)),
    (0, 0, CHUNK, (2, 0, 1), False, (768, 128)),
    (0, CHUNK, CHUNK, (0, 2, 1), False, (768, 128)),
)
WIDE = (0, 1, 2)
THIN = (3, 4, 5, 6)
MAIN, SIDE = (7, 8, 2), (9, 10)
SUMMED = MAIN + SIDE


def my_coords():
    dp = lax.axis_index("dp")
    return (dp // 16, (dp // 4) % 4, dp % 4), lax.axis_index("narrow")


def device_of(coords, core):
    return (coords[0] * 16 + coords[1] * 4 + coords[2], core)


def shifted(coords, axis, by):
    out = list(coords)
    out[axis] = (coords[axis] + by) % 4
    return tuple(out)


def facing(coords):
    return (coords[0], coords[1], 3 - coords[2])


def greet(coords, core):
    barrier = pltpu.get_barrier_semaphore()
    for axis in range(3):
        for by in (1, 2, 3):
            pl.semaphore_signal(
                barrier, inc=1, device_id=device_of(shifted(coords, axis, by), core), device_id_type=MESH
            )
    pl.semaphore_signal(barrier, inc=1, device_id=device_of(coords, 1 - core), device_id_type=MESH)
    pl.semaphore_wait(barrier, 10)


def remote(src, dst, send_sem, recv_sem, device):
    return pltpu.make_async_remote_copy(
        src_ref=src,
        dst_ref=dst,
        send_sem=send_sem,
        recv_sem=recv_sem,
        device_id=device,
        device_id_type=MESH,
    )


def place_of(part, spec):
    _, first, rows, _, shared, columns = PARTS[part]
    index = [pl.ds(*s) if isinstance(s, tuple) else s for s in spec[:2]]
    s = spec[2]
    if isinstance(s, tuple):
        index.append(pl.ds(s[0] // 2, s[1] // 2))
        index += [] if shared else [pl.ds(0, 2)]
    else:
        index.append(s // 2)
        index += [] if shared else [s % 2]
    return (*index, pl.ds(first, rows), pl.ds(*columns))


def shape_of(part, spec):
    return tuple(entry.size for entry in place_of(part, spec) if isinstance(entry, pl.Slice))


class Plan:
    def __init__(self, part, stage, coords, axis, spec, split):
        self.coords, self.axis, self.spec, self.split = coords, axis, spec, split
        self.exchange = PARTS[part][4] and axis == 2
        self.direct = not self.exchange and stage == 0

    def at(self, by):
        return shifted(self.coords, self.axis, by)

    def whole(self, by):
        spec = list(self.spec)
        spec[self.axis] = (self.coords[self.axis] + by) % 4
        return tuple(spec)

    def pieces(self, by):
        out = []
        for h in range(2):
            spec = list(self.whole(by))
            spec[self.split] = (2 * h, 2)
            out.append(tuple(spec))
        return out

    def facing(self):
        return (*self.spec[:2], 3 - self.coords[2])

    def own(self):
        return self.spec


def plan_of(part, stage, coords):
    order = PARTS[part][3]
    spec = tuple(FULL if k in order[:stage] else coords[k] for k in range(3))
    return Plan(part, stage, coords, order[stage], spec, order[stage - 1] if stage else None)


class Gather:
    def __init__(self, arrays, coords, core, send_sems, recv_sems):
        self.arrays, self.coords, self.core = arrays, coords, core
        self.send_sems, self.recv_sems = send_sems, recv_sems

    def copy(self, part, phase, slot, piece, coords):
        array, prefix = self.arrays[PARTS[part][0]]
        ref = array.at[(*prefix, *place_of(part, piece))]
        sems = (self.send_sems.at[part, phase, slot], self.recv_sems.at[part, phase, slot])
        return remote(ref, ref, *sems, device_of(coords, self.core))

    def send(self, *args):
        self.copy(*args).start()

    def neighbours(self, plan):
        return shifted(self.coords, plan.axis, 1), shifted(self.coords, plan.axis, 3)

    def start(self, parts, phase):
        for part in parts:
            plan = plan_of(part, phase, self.coords)
            if plan.exchange:
                self.send(part, phase, 0, plan.own(), facing(self.coords))
                continue
            if plan.direct:
                for by in (1, 3, 2):
                    self.send(part, phase, by, plan.own(), plan.at(by))
                continue
            right, left = self.neighbours(plan)
            first, second = plan.pieces(0)
            self.send(part, phase, 0, first, right)
            self.send(part, phase, 1, second, left)
            self.send(part, phase, 2, second, right)
            self.send(part, phase, 3, first, left)

    def forward(self, parts, phase):
        for part in parts:
            plan = plan_of(part, phase, self.coords)
            if plan.exchange or plan.direct:
                continue
            right, left = self.neighbours(plan)
            piece = plan.pieces(3)[0]
            self.copy(part, phase, 0, piece, right).wait_recv()
            self.send(part, phase, 4, piece, right)
            piece = plan.pieces(1)[1]
            self.copy(part, phase, 1, piece, left).wait_recv()
            self.send(part, phase, 5, piece, left)

    def near(self, parts, phase):
        for part in parts:
            plan = plan_of(part, phase, self.coords)
            if plan.exchange:
                self.copy(part, phase, 0, plan.facing(), facing(self.coords)).wait_recv()
                continue
            if plan.direct:
                for by in (1, 3):
                    self.copy(part, phase, by, plan.whole(4 - by), plan.at(by)).wait_recv()
                continue
            right, left = self.neighbours(plan)
            self.copy(part, phase, 2, plan.pieces(3)[1], right).wait_recv()
            self.copy(part, phase, 3, plan.pieces(1)[0], left).wait_recv()

    def far(self, parts, phase):
        for part in parts:
            plan = plan_of(part, phase, self.coords)
            if plan.exchange:
                continue
            if plan.direct:
                self.copy(part, phase, 2, plan.whole(2), plan.at(2)).wait_recv()
                continue
            right, left = self.neighbours(plan)
            self.copy(part, phase, 4, plan.pieces(2)[0], right).wait_recv()
            self.copy(part, phase, 5, plan.pieces(2)[1], left).wait_recv()

    def finish(self, parts, phase):
        self.near(parts, phase)
        self.far(parts, phase)

    def drain(self):
        for part in WIDE + THIN:
            for phase in range(3):
                plan = plan_of(part, phase, self.coords)
                if plan.exchange:
                    self.copy(part, phase, 0, plan.own(), facing(self.coords)).wait_send()
                    continue
                if plan.direct:
                    for by in (1, 3, 2):
                        self.copy(part, phase, by, plan.own(), plan.at(by)).wait_send()
                    continue
                right, _ = self.neighbours(plan)
                for slot, which in enumerate((0, 1, 1, 0, 0, 1)):
                    self.copy(part, phase, slot, plan.pieces(0)[which], right).wait_send()


def each_block(shape, body):
    lead = shape[:-2]
    count = math.prod(lead)
    if count == 1:
        body((0,) * len(lead))
        return

    def step(k, carry):
        index = []
        for n in reversed(lead):
            index.append(k % n)
            k = k // n
        body(tuple(reversed(index)))
        return carry

    lax.fori_loop(0, count, step, 0)


class Scatter:
    def __init__(self, arrays, coords, core, buffers, send_sems, recv_sems, done):
        self.arrays, self.coords, self.core, self.done = arrays, coords, core, done
        self.buffers, self.send_sems, self.recv_sems = buffers, send_sems, recv_sems

    def copy(self, part, phase, slot, piece, coords):
        array, prefix = self.arrays[PARTS[part][0]]
        ref = array.at[(*prefix, *place_of(part, piece))]
        sems = (self.send_sems.at[part, phase, slot], self.recv_sems.at[part, phase, slot])
        return remote(ref, self.buffers[part, phase][slot], *sems, device_of(coords, self.core))

    def send(self, *args):
        if args[:3] not in self.done:
            self.copy(*args).start()

    def arrive(self, *args):
        if args[:3] not in self.done:
            self.copy(*args).wait_recv()

    def add(self, part, phase, piece, *slots):
        sources = [self.buffers[part, phase][slot] for slot in slots]
        base = place_of(part, piece)
        array, prefix = self.arrays[PARTS[part][0]]

        def one(index):
            spot, position = [], 0
            for entry in base[:-2]:
                if isinstance(entry, pl.Slice):
                    spot.append(entry.start + index[position])
                    position += 1
                else:
                    spot.append(entry)
            spot = (*prefix, *spot, *base[-2:])
            value = array[spot].astype(F32)
            for source in sources:
                value = value + source[(*index, slice(None), slice(None))].astype(F32)
            array[spot] = half(value)

        each_block(shape_of(part, piece), one)

    def neighbours(self, plan):
        return shifted(self.coords, plan.axis, 1), shifted(self.coords, plan.axis, 3)

    def start_far(self, parts, phase):
        for part in parts:
            plan = plan_of(part, phase, self.coords)
            if plan.exchange or plan.direct:
                continue
            right, left = self.neighbours(plan)
            self.send(part, phase, 0, plan.pieces(2)[0], right)
            self.send(part, phase, 1, plan.pieces(2)[1], left)

    def start_near(self, parts, phase):
        for part in parts:
            plan = plan_of(part, phase, self.coords)
            if plan.exchange:
                self.send(part, phase, 0, plan.facing(), facing(self.coords))
                continue
            if plan.direct:
                for by in (1, 3, 2):
                    self.send(part, phase, by, plan.whole(by), plan.at(by))
                continue
            right, left = self.neighbours(plan)
            self.send(part, phase, 2, plan.pieces(1)[1], right)
            self.send(part, phase, 3, plan.pieces(3)[0], left)

    def start(self, parts, phase):
        self.start_far(parts, phase)
        self.start_near(parts, phase)

    def forward(self, parts, phase):
        for part in parts:
            plan = plan_of(part, phase, self.coords)
            if plan.exchange or plan.direct:
                continue
            right, left = self.neighbours(plan)
            self.arrive(part, phase, 0, plan.pieces(2)[0], right)
            self.add(part, phase, plan.pieces(1)[0], 0)
            self.send(part, phase, 4, plan.pieces(1)[0], right)
            self.arrive(part, phase, 1, plan.pieces(2)[1], left)
            self.add(part, phase, plan.pieces(3)[1], 1)
            self.send(part, phase, 5, plan.pieces(3)[1], left)

    def finish(self, parts, phase):
        for part in parts:
            plan = plan_of(part, phase, self.coords)
            if plan.exchange:
                self.arrive(part, phase, 0, plan.facing(), facing(self.coords))
                self.add(part, phase, plan.own(), 0)
                continue
            if plan.direct:
                for by in (1, 3, 2):
                    self.arrive(part, phase, by, plan.whole(by), plan.at(by))
                self.add(part, phase, plan.own(), 1, 3, 2)
                continue
            right, left = self.neighbours(plan)
            self.arrive(part, phase, 3, plan.pieces(3)[0], left)
            self.arrive(part, phase, 4, plan.pieces(1)[0], right)
            self.add(part, phase, plan.pieces(0)[0], 4, 3)
            self.arrive(part, phase, 2, plan.pieces(1)[1], right)
            self.arrive(part, phase, 5, plan.pieces(3)[1], left)
            self.add(part, phase, plan.pieces(0)[1], 2, 5)

    def drain(self):
        for part in SUMMED + THIN:
            for phase in range(3):
                plan = plan_of(part, phase, self.coords)
                if plan.exchange:
                    self.copy(part, phase, 0, plan.own(), facing(self.coords)).wait_send()
                    continue
                if plan.direct:
                    for by in (1, 3, 2):
                        self.copy(part, phase, by, plan.whole(by), plan.at(by)).wait_send()
                    continue
                right, _ = self.neighbours(plan)
                for slot, which in enumerate((0, 1, 1, 0, 0, 1)):
                    if (part, phase, slot) in self.done:
                        continue
                    self.copy(part, phase, slot, plan.pieces(0)[which], right).wait_send()


EARLY = tuple((part, 2, slot) for part in MAIN for slot in (2, 3))


def scatter_buffer_shapes():
    out = []
    for part in SUMMED + THIN:
        for phase in range(3):
            plan = plan_of(part, phase, (0, 0, 0))
            if plan.exchange:
                shapes = [shape_of(part, plan.own())]
            elif plan.direct:
                shapes = [None] + [shape_of(part, plan.own())] * 3
            else:
                first, second = (shape_of(part, piece) for piece in plan.pieces(0))
                shapes = [first, second, second, first, first, second]
            out.append(((part, phase), shapes))
    return out


SCALE = HEAD ** (-0.5)


def turn(values, sign):
    lane = lax.broadcasted_iota(jnp.int32, values.shape, 1)
    ahead = pltpu.roll(values, 96, 1)
    behind = pltpu.roll(values, 32, 1)
    return jnp.where(lane & 32 == 0, sign * ahead, -sign * behind)


def tiles_of(values):
    return [values[:, 128 * t : 128 * t + 128] for t in range(values.shape[1] // 128)]


def rotated(values, cosine, sine):
    return jnp.concatenate(
        [tile * cosine + turn(tile, -1.0) * sine for tile in tiles_of(values)], axis=1
    )


def rotated_back(values, cosine, sine):
    return jnp.concatenate(
        [tile * cosine + turn(tile * sine, 1.0) for tile in tiles_of(values)], axis=1
    )


def low_lanes(shape):
    return lax.broadcasted_iota(jnp.int32, shape, 1) < HEAD


def paired(both):
    swapped = pltpu.roll(both, 64, 1)
    low = low_lanes(both.shape)
    even = [half(jnp.where(low, v, 0.0)) for v in (both, swapped)]
    odd = [half(jnp.where(low, 0.0, v)) for v in (swapped, both)]
    kinds = [jnp.concatenate([even[a], odd[b]]) for a, b in ((0, 0), (0, 1), (1, 1))]
    return [kinds[0]] * 3 + [kinds[1]] + [kinds[2]] * 3


def gathered_place():
    row = lax.broadcasted_iota(jnp.int32, (1024, D), 0)
    feature = lax.broadcasted_iota(jnp.int32, (1024, D), 1)
    slot = row & 15
    odd = (slot >= 7).astype(jnp.int32)
    device = (((row >> 4) & 31) * 2 + odd) * 2 + (row >> 9)
    source = jnp.where(slot < 14, 7 * device + slot - 7 * odd, -1)
    return half((source == feature).astype(jnp.float32))


def vector_maps():
    device = lax.broadcasted_iota(jnp.int32, (128, 1024), 0)
    row = lax.broadcasted_iota(jnp.int32, (128, 1024), 1)
    target = (device & 1) * 512 + (device >> 2) * 16 + ((device >> 1) & 1) * 7
    pick = half((row == target).astype(jnp.float32))
    start = lax.broadcasted_iota(jnp.int32, (128, 2944), 0) * 23
    entry = lax.broadcasted_iota(jnp.int32, (128, 2944), 1)
    owner = half(((entry >= start) & (entry < start + 23)).astype(jnp.float32))
    return pick, owner


def slot_mask(slots):
    return lax.broadcasted_iota(jnp.int32, (128, 2944), 0) == slots


def own_lengths(len_ref, coords, core):
    own = (coords[0] * 16 + coords[1] * 4 + coords[2]) * 2 + core
    lane = lax.broadcasted_iota(jnp.int32, (2, 128), 1)
    length = jnp.sum(jnp.where(lane == own, len_ref[...].astype(F32), 0.0), axis=1, keepdims=True)
    return jnp.broadcast_to(length, (2, 128))


def live_tokens(lengths):
    token = lax.broadcasted_iota(jnp.int32, (128, 1), 0).astype(F32)
    return jnp.concatenate([(token < lengths[b : b + 1, 0:1]).astype(F32) for b in range(2)])


def attention_forward(
    x_ref, rest_ref, lengths, cos_ref, sin_ref, slot_ref,
    middle_ref, h1p_ref, q_ref, k_ref, v_ref, mixed_ref, probs_ref, vector_ref,
):
    place = gathered_place()
    pick, owner = vector_maps()
    stored = rest_ref[:, :, :, :, 32:48, 256:384].reshape(1024, 128)
    by_device = half(product(pick, stored))
    spread = inner_rows(by_device, owner)
    vector = jnp.sum(jnp.where(slot_mask(slot_ref[...]), spread, 0.0), axis=0, keepdims=True)
    vector_ref[...] = vector
    first_gain, second_gain = vector[:, :D], vector[:, D : 2 * D]
    query_bias, narrow_bias = vector[:, 2 * D : 3 * D], vector[:, 3 * D :]
    cosine, sine = cos_ref[...], sin_ref[...]
    inputs = x_ref[...].astype(jnp.float32)
    first_scale = lax.rsqrt(jnp.mean(inputs * inputs, axis=-1, keepdims=True) + NORM_EPSILON)
    normed = half(inputs * first_scale * first_gain)
    placed = half(outer_cols(normed, place))
    h1p_ref[...] = placed
    queries = product(placed, rest_ref[:, :, :, :, 0:16, :].reshape(1024, D)) + query_bias
    narrow = product(placed, rest_ref[:, :, :, :, 32:48, 0:256].reshape(1024, 256)) + narrow_bias
    q_ref[...] = half(rotated(queries, cosine, sine))
    keys = rotated(narrow[:, 0:128], cosine, sine)
    k_ref[...] = half(keys)
    values = narrow[:, 128:256]
    v_ref[...] = half(values)
    position = lax.broadcasted_iota(jnp.int32, (128, 256), 0)
    other = lax.broadcasted_iota(jnp.int32, (128, 256), 1) & 127
    causal = other <= position
    other = other.astype(F32)
    rows = []
    for b in range(2):
        here = slice(128 * b, 128 * b + 128)
        length = lengths[b : b + 1, :]
        allowed = causal & (other < jnp.concatenate([length, length], axis=1))
        key_tiles = paired(keys[here])
        value_tiles = paired(values[here])
        tiles = []
        for t in range(7):
            scores = outer_cols(q_ref[here, 128 * t : 128 * t + 128], key_tiles[t])
            scores = jnp.where(allowed, scores * SCALE, MASKED)
            parts = []
            for part in tiles_of(scores):
                shifted = jnp.exp(part - jnp.max(part, axis=-1, keepdims=True))
                parts.append(shifted * (1.0 / jnp.sum(shifted, axis=-1, keepdims=True)))
            probs = jnp.concatenate(parts, axis=1)
            probs_ref[b, t] = probs
            tiles.append(half(product(half(probs), value_tiles[t])))
        rows.append(jnp.concatenate(tiles, axis=1))
    mixed = half(outer_cols(jnp.concatenate(rows), place))
    mixed_ref[...] = mixed
    middle = inputs + product(mixed, rest_ref[:, :, :, :, 16:32, :].reshape(1024, D))
    middle_ref[...] = middle
    second_scale = lax.rsqrt(jnp.mean(middle * middle, axis=-1, keepdims=True) + NORM_EPSILON)
    return half(middle * second_scale * second_gain)


def mlp_tile(weights, h, e, sums):
    lead = weights.shape[:-2]
    units = 16 * math.prod(lead)
    gate_w, up_w, down_w = (
        weights[..., 16 * k : 16 * k + 16, :].reshape(units, D) for k in range(3)
    )
    gate = outer_cols(h, gate_w)
    up = outer_cols(h, up_w)
    sigma = 0.5 * jnp.tanh(0.5 * gate) + 0.5
    silu = gate * sigma
    hidden = half(silu * up)
    grad_hidden = outer_cols(e, down_w)
    sums[0] += product(hidden, down_w).reshape(2, TOKENS, D)
    grad_gate = half(grad_hidden * up * (sigma + silu * (1.0 - sigma)))
    grad_up = half(grad_hidden * silu)
    sums[1] += (product(grad_gate, gate_w) + product(grad_up, up_w)).reshape(2, TOKENS, D)
    grads = (inner_rows(grad_gate, h), inner_rows(grad_up, h), inner_rows(hidden, e))
    return [half(grad).reshape(*lead, 16, D) for grad in grads]


KEPT = 17


def gather_kernel(
    gate_ref, up_ref, down_ref, query_ref, out_ref, key_ref, value_ref, own_vector_ref,
    x_ref, cot_ref, len_ref, cos_ref, sin_ref, slot_ref, *refs,
):
    coords, core = my_coords()
    z, y, x = coords
    pair, odd = x // 2, x % 2
    lengths = own_lengths(len_ref, coords, core)
    results, (grad_wide_ref, grad_shared_ref, rest_ref) = refs[:KEPT], refs[KEPT : KEPT + 3]
    held = refs[KEPT + 3 : 2 * KEPT + 1]
    (
        wide, shared, rest, stage0, stage1, stage2, h_all, e_all, sums, parcel, tail, tail_own, tail_wide,
        local_sems, send_sems, recv_sems, twin_sems, store_sems, early_sems, kept_sems,
    ) = refs[2 * KEPT + 1 :]
    middle_ref, e_ref, h1p_ref, q_ref, k_ref, v_ref, mixed_ref, probs_ref, vector_ref = held[:9]
    early = held[9:]
    kept = [*held[:9], sums.at[:, core], parcel, *early]

    def keep(first, last):
        return [
            pltpu.make_async_copy(kept[n], results[n], kept_sems.at[n]) for n in range(first, last)
        ]

    units = (gate_ref, up_ref, down_ref)
    for n, ref in enumerate(units):
        for k in range(2):
            wide[z, y, pair, odd, CHUNK * k + 16 * n : CHUNK * k + 16 * n + 16] = half(
                ref[16 * k : 16 * k + 16]
            )
    tail_wide[...] = jnp.zeros_like(tail_wide)
    for parity in range(2):

        @pl.when(odd == parity)
        def _():
            for n, ref in enumerate(units):
                start = 16 * n + 6 * parity
                tail_wide[start : start + 6] = ref[32:38]
            for n, ref in enumerate((query_ref, out_ref)):
                start = CHUNK + 16 * n + 7 * parity
                tail_wide[start : start + 7] = ref[...]
            start = CHUNK + 32 + 7 * parity
            tail_wide[start : start + 7, 0:128] = key_ref[...]
            tail_wide[start : start + 7, 128:256] = value_ref[...]
            tail_wide[start : start + 1, 256:384] = jnp.concatenate(
                [own_vector_ref[...], jnp.zeros((1, 105), F32)], axis=1
            )

    tail_own[...] = half(tail_wide[...])
    greet(coords, core)
    twin = device_of(coords, 1 - core)

    def to_twin(src, dst, slot):
        return remote(src, dst, twin_sems.at[0, slot], twin_sems.at[1, slot], twin)

    gather = Gather(((wide, ()), (shared, ()), (rest, (core,))), coords, core, send_sems, recv_sems)
    partner = device_of((z, y, x + 1 - 2 * odd), core)
    tail_copy = remote(tail_own, tail, twin_sems.at[0, 4], twin_sems.at[1, 4], partner)
    tail_copy.start()
    gather.start((0, 1), 0)
    e_ref[...] = half(cot_ref[...].astype(F32) * live_tokens(lengths))
    e_all[core] = e_ref[...]
    e_copy = to_twin(e_ref, e_all.at[core], 0)
    e_copy.start()
    tail_copy.wait()
    both = half(tail_wide[...] + tail[...].astype(F32))
    shared[z, y, pair] = both[:CHUNK]
    rest[core, z, y, pair] = both[CHUNK:]
    gather.start(THIN, 0)
    gather.start((2,), 0)
    gather.forward(THIN, 0)
    gather.finish(THIN, 0)
    gather.start(THIN, 1)
    gather.forward(WIDE, 0)
    gather.forward(THIN, 1)
    gather.finish(THIN, 1)
    gather.start(THIN, 2)
    gather.finish(WIDE, 0)
    gather.start(WIDE, 1)
    gather.forward(THIN, 2)
    gather.finish(THIN, 2)
    rest_copy = to_twin(rest.at[core], rest.at[core], 1)
    rest_copy.start()
    gather.forward(WIDE, 1)
    gather.finish(WIDE, 1)
    gather.start(WIDE, 2)
    rest_copy.wait()
    rest_store = pltpu.make_async_copy(rest, rest_ref, local_sems.at[0])
    rest_store.start()
    h_all[core] = attention_forward(
        x_ref, rest, lengths, cos_ref, sin_ref, slot_ref,
        middle_ref, h1p_ref, q_ref, k_ref, v_ref, mixed_ref, probs_ref, vector_ref,
    )
    h_copy = to_twin(h_all.at[core], h_all.at[core], 2)
    h_copy.start()
    for copy in keep(0, 9):
        copy.start()
    sums[...] = jnp.zeros_like(sums)
    e_copy.wait()
    h_copy.wait()
    stages = (stage0, stage1, stage2)

    def early_copy(t, slot):
        axis = PARTS[t][3][2]
        which = 3 - slot
        place = [slice(None)] * (len(stages[t].shape) - 1)
        place[1 if t == 2 else 0] = pl.ds(which, 1) if t == 2 else pl.ds(2 * which, 2)
        place[-1] = pl.ds(*PARTS[MAIN[t]][5])
        return remote(
            stages[t].at[(slot - 1) % 2].at[tuple(place)],
            early[2 * t + slot - 2],
            early_sems.at[0, t, slot - 2],
            early_sems.at[1, t, slot - 2],
            device_of(shifted(coords, axis, 1 if slot == 2 else 3), core),
        )

    def tile_places(j):
        return (
            (wide, grad_wide_ref, (j, slice(None), slice(None), slice(None), pl.ds(0, CHUNK))),
            (wide, grad_wide_ref, (slice(None), slice(None), j // 2, j % 2, pl.ds(CHUNK, CHUNK))),
            (shared, grad_shared_ref, (slice(None), j, slice(None), pl.ds(0, CHUNK))),
        )

    def step(k, carry):
        @pl.when(k == 1)
        def _():
            gather.near(WIDE, 2)

        @pl.when(k == 3)
        def _():
            gather.far(WIDE, 2)

        offset = jnp.where(k < 2, k, 5 - k)
        h = h_all[...].reshape(2 * TOKENS, D)
        e = e_all[...].reshape(2 * TOKENS, D)
        for t, axis in enumerate((0, 2, 1)):
            j = (coords[axis] + offset) % 4
            source, target, index = tile_places(j)[t]
            grads = mlp_tile(source[(*index, slice(None))], h, e, sums)
            copy = pltpu.make_async_copy(
                stages[t].at[k % 2], target.at[(*index, slice(None))], store_sems.at[t, k % 2]
            )

            @pl.when(k > 1)
            def _():
                copy.wait()

            @pl.when(k == 3)
            def _():
                early_copy(t, 2).wait_send()

            for place, grad in enumerate(grads):
                stages[t][k % 2, ..., 16 * place : 16 * place + 16, :] = grad
            copy.start()

            @pl.when(k == 1)
            def _():
                early_copy(t, 2).start()

            @pl.when(k == 2)
            def _():
                early_copy(t, 3).start()

        @pl.when(k == 0)
        def _():
            gather.forward(WIDE, 2)

        return carry

    lax.fori_loop(0, 4, step, 0)
    parcel[...] = half(sums[:, 1 - core])
    for copy in keep(9, 11):
        copy.start()
    for t in range(3):
        _, target, index = tile_places(0)[t]
        for which in range(2):
            pltpu.make_async_copy(
                stages[t].at[which], target.at[(*index, slice(None))], store_sems.at[t, which]
            ).wait()
        early_copy(t, 3).wait_send()
        early_copy(t, 2).wait_recv()
        early_copy(t, 3).wait_recv()
        for copy in keep(11 + 2 * t, 13 + 2 * t):
            copy.start()
    rest_store.wait()
    for copy in keep(0, KEPT):
        copy.wait()
    gather.drain()


def attention_backward(
    between, ready, x_ref, e_ref, rest_ref, cos_ref, sin_ref, slot_ref,
    middle_ref, h1p_ref, q_ref, k_ref, v_ref, mixed_ref, probs_ref, vector_ref, dh2_ref,
    input_grad_ref, grad_ref,
):
    place = gathered_place()
    pick, owner = vector_maps()
    vector = vector_ref[...]
    first_gain, second_gain = vector[:, :D], vector[:, D : 2 * D]
    cosine, sine = cos_ref[...], sin_ref[...]
    middle = middle_ref[...]
    second_scale = lax.rsqrt(jnp.mean(middle * middle, axis=-1, keepdims=True) + NORM_EPSILON)
    second_normed = middle * second_scale
    dh2 = dh2_ref[...]
    second_gain_grad = jnp.sum(dh2 * second_normed, axis=0, keepdims=True)
    grad_middle = e_ref[...].astype(jnp.float32) + norm_back(
        dh2 * second_gain, second_normed, second_scale
    )
    branch = half(grad_middle)
    wide = rest_ref[:, :, :, :, 16:32, :].reshape(1024, D)
    grad_ref[:, :, :, :, 16:32, :] = half(inner_rows(mixed_ref[...], branch)).reshape(2, 4, 4, 2, 16, D)
    grad_mixed = half(product(half(outer_cols(branch, wide)), place))
    low = low_lanes((128, 128))
    query_rows, key_rows, value_rows = [], [], []
    for b in range(2):
        here = slice(128 * b, 128 * b + 128)
        key_tiles = paired(k_ref[here, :].astype(jnp.float32))
        value_tiles = paired(v_ref[here, :].astype(jnp.float32))
        tiles = []
        sums = [[jnp.zeros((128, 128), jnp.float32) for _ in range(4)] for _ in range(2)]
        for t in range(7):
            head = grad_mixed[here, 128 * t : 128 * t + 128]
            grad_probs = outer_cols(head, value_tiles[t])
            probs = probs_ref[b, t]
            parts = []
            for p, g in zip(tiles_of(probs), tiles_of(grad_probs)):
                parts.append(half(p * (g - jnp.sum(p * g, axis=-1, keepdims=True))))
            grad_scores = jnp.concatenate(parts, axis=1)
            tiles.append(product(grad_scores, key_tiles[t]) * SCALE)
            for which, (left, right) in enumerate(
                ((grad_scores, q_ref[here, 128 * t : 128 * t + 128]), (half(probs), head))
            ):
                both = inner_rows(left, right)
                even, odd = (2 * t) // 7, (2 * t + 1) // 7
                sums[which][even] += both[0:128]
                sums[which][2 + odd] += both[128:256]
        query_rows.append(jnp.concatenate(tiles, axis=1))
        joined = []
        for which in range(2):
            even0, even1, odd0, odd1 = sums[which]
            joined.append(
                jnp.where(low, even0 + pltpu.roll(odd0, 64, 1), odd1 + pltpu.roll(even1, 64, 1))
            )
        key_rows.append(joined[0] * SCALE)
        value_rows.append(joined[1])
    between()
    grad_query = half(rotated_back(jnp.concatenate(query_rows), cosine, sine))
    grad_key = half(rotated_back(jnp.concatenate(key_rows), cosine, sine))
    grad_narrow = jnp.concatenate([grad_key, half(jnp.concatenate(value_rows))], axis=1)
    placed = h1p_ref[...]
    grad_ref[:, :, :, :, 0:16, :] = half(inner_rows(placed, grad_query)).reshape(2, 4, 4, 2, 16, D)
    ready()
    grad_ref[:, :, :, :, 32:48, 0:256] = half(inner_rows(placed, grad_narrow)).reshape(2, 4, 4, 2, 16, 256)
    bias_grad = jnp.sum(
        jnp.concatenate([grad_query, grad_narrow], axis=1).astype(jnp.float32), axis=0, keepdims=True
    )
    grad_placed = outer_cols(grad_query, rest_ref[:, :, :, :, 0:16, :].reshape(1024, D)) + outer_cols(
        grad_narrow, rest_ref[:, :, :, :, 32:48, 0:256].reshape(1024, 256)
    )
    high = half(grad_placed)
    remainder = half(grad_placed - high.astype(jnp.float32))
    grad_normed = product(high, place) + product(remainder, place)
    inputs = x_ref[...].astype(jnp.float32)
    first_scale = lax.rsqrt(jnp.mean(inputs * inputs, axis=-1, keepdims=True) + NORM_EPSILON)
    first_normed = inputs * first_scale
    first_gain_grad = jnp.sum(grad_normed * first_normed, axis=0, keepdims=True)
    input_grad_ref[...] = half(
        grad_middle + norm_back(grad_normed * first_gain, first_normed, first_scale)
    )
    vector_grad = jnp.concatenate([first_gain_grad, second_gain_grad, bias_grad], axis=1)
    spread = half(jnp.where(slot_mask(slot_ref[...]), vector_grad, 0.0))
    by_device = half(outer_cols(owner, spread))
    stored = half(inner_rows(pick, by_device))
    grad_ref[:, :, :, :, 32:48, 256:384] = stored.reshape(2, 4, 4, 2, 16, 128)
    grad_ref[:, :, :, :, 32:48, 384:] = jnp.zeros((2, 4, 4, 2, 16, D - 384), jnp.bfloat16)


LOADED = (
    "parcel", "own", "middle", "e", "x", "rest", "h1p", "q", "k", "v", "mixed", "probs", "vector",
)


def scatter_kernel(
    len_ref, cos_ref, sin_ref, slot_ref, grad_wide_ref, grad_shared_ref, *refs,
):
    coords, core = my_coords()
    z, y, x = coords
    pair, odd = x // 2, x % 2
    count = len(LOADED) + len(EARLY)
    sources, (output_ref, input_grad_ref, out_ref) = refs[:count], refs[count : count + 3]
    held = refs[count + 3 : 2 * count + 3]
    (
        wide, shared, thin, joined, mine, theirs, arrived, dh2_ref,
        load_sems, send_sems, recv_sems, twin_sems, pair_sems, held_sems,
    ) = refs[2 * count + 3 : 2 * count + 17]
    buffers = refs[2 * count + 17 :]
    (
        parcel_ref, own_ref, middle_ref, e_ref, x_ref, rest_ref, h1p_ref, q_ref, k_ref, v_ref,
        mixed_ref, probs_ref, vector_ref,
    ) = held[: len(LOADED)]
    fetches = [
        pltpu.make_async_copy(sources[n], held[n], held_sems.at[n]) for n in range(count)
    ]
    named, position = {}, 0
    early = dict(zip(EARLY, held[len(LOADED) :]))
    for key, shapes in scatter_buffer_shapes():
        named[key] = []
        for slot in range(len(shapes)):
            if (*key, slot) in early:
                named[key].append(early[(*key, slot)])
            elif shapes[slot] is None:
                named[key].append(None)
            else:
                named[key].append(buffers[position])
                position += 1
    scatter = Scatter(((wide, ()), (shared, ()), (thin, (core,))), coords, core, named, send_sems, recv_sems, EARLY)

    def load(part, by):
        spec = [FULL] * 3
        axis = PARTS[part][3][2]
        spec[axis] = (coords[axis] + by) % 4
        place = place_of(part, tuple(spec))
        source = (grad_wide_ref, grad_shared_ref)[PARTS[part][0]]
        target = (wide, shared)[PARTS[part][0]]
        return pltpu.make_async_copy(source.at[place], target.at[place], load_sems.at[part, by])

    for by in (2, 1, 3, 0):
        for part in SUMMED:
            load(part, by).start()
    for copy in fetches:
        copy.start()
    greet(coords, core)

    for part in SUMMED:
        load(part, 2).wait()
        scatter.start_far((part,), 2)
    for part in SUMMED:
        load(part, 1).wait()
        load(part, 3).wait()
    scatter.start_near(SIDE, 2)

    def between():
        scatter.forward(SUMMED, 2)

    for copy in fetches[:3]:
        copy.wait()
    parcel_copy = remote(
        parcel_ref, arrived, twin_sems.at[0, 1], twin_sems.at[1, 1], device_of(coords, 1 - core)
    )
    parcel_copy.start()
    for copy in fetches[3:]:
        copy.wait()
    parcel_copy.wait()
    output_ref[...] = half(
        (middle_ref[...] + (own_ref[0] + arrived[0].astype(F32))) * live_tokens(own_lengths(len_ref, coords, core))
    )
    dh2_ref[...] = own_ref[1] + arrived[1].astype(F32)
    def twin_copy(slot, first, rows):
        return remote(
            thin.at[1 - core, :, :, :, pl.ds(first, rows)],
            joined.at[:, :, :, pl.ds(first, rows)],
            twin_sems.at[0, slot],
            twin_sems.at[1, slot],
            device_of(coords, 1 - core),
        )

    def ready():
        twin_copy(0, 0, 32).start()

    attention_backward(
        between, ready, x_ref, e_ref, rest_ref, cos_ref, sin_ref, slot_ref,
        middle_ref, h1p_ref, q_ref, k_ref, v_ref, mixed_ref, probs_ref, vector_ref, dh2_ref,
        input_grad_ref, thin,
    )
    twin_copy(2, 32, 16).start()
    for part in SUMMED:
        load(part, 0).wait()
    for slot, first, rows, parts in ((0, 0, 32, THIN[:3]), (2, 32, 16, THIN[3:])):
        twin_copy(slot, first, rows).wait()

        def join(index):
            own = (core, *index, pl.ds(first, rows))
            thin[own] = half(thin[own].astype(F32) + joined[(*index, pl.ds(first, rows))].astype(F32))

        each_block((4, 4, 2, rows, D), join)
        scatter.start(parts, 2)
    for part in SUMMED:
        scatter.finish((part,), 2)
        scatter.start((part,), 1)
    scatter.forward(THIN, 2)
    scatter.finish(THIN, 2)
    scatter.start(THIN, 1)
    scatter.forward(SUMMED, 1)
    scatter.forward(THIN, 1)
    for part in SUMMED:
        scatter.finish((part,), 1)
        scatter.start((part,), 0)
    scatter.finish(THIN, 1)
    scatter.start(THIN, 0)
    scatter.forward(SUMMED, 0)
    scatter.forward(THIN, 0)
    scatter.finish(SUMMED, 0)
    scatter.finish(THIN, 0)
    mine[0] = shared[z, y, pair]
    mine[1] = thin[core, z, y, pair]
    partner = device_of((z, y, x + 1 - 2 * odd), core)
    pair_copy = remote(mine, theirs, pair_sems.at[0], pair_sems.at[1], partner)
    pair_copy.start()
    pair_copy.wait()
    out_ref[0] = wide[z, y, pair, odd, 0:CHUNK].astype(F32)
    out_ref[1] = wide[z, y, pair, odd, CHUNK : 2 * CHUNK].astype(F32)
    out_ref[2] = mine[0].astype(F32) + theirs[0].astype(F32)
    out_ref[3] = mine[1].astype(F32) + theirs[1].astype(F32)
    scatter.drain()


def layer(weights, tokens, cotangent, lengths):
    vmem = pl.BlockSpec(memory_space=pltpu.VMEM)
    anywhere = pl.BlockSpec(memory_space=pl.ANY)
    x = tokens.reshape(TOKENS, D)
    freqs = ROPE_BASE ** (-np.arange(HEAD // 2) * 2.0 / HEAD)
    angles = np.tile(np.arange(128)[:, None] * freqs[None, :], (2, 4))
    tables = (
        np.cos(angles).astype(np.float32),
        np.sin(angles).astype(np.float32),
        (np.arange(2944, dtype=np.int32) % 23)[None],
    )
    buffers = dict(scatter_buffer_shapes())
    kept = [
        ((TOKENS, D), F32),
        ((TOKENS, D), BF16),
        ((TOKENS, 1024), BF16),
        ((TOKENS, D), BF16),
        ((TOKENS, 128), BF16),
        ((TOKENS, 128), BF16),
        ((TOKENS, 1024), BF16),
        ((2, 7, 128, 256), F32),
        ((1, 2944), F32),
        ((2, TOKENS, D), F32),
        ((2, TOKENS, D), BF16),
    ] + [(buffers[part, stage][slot], BF16) for part, stage, slot in EARLY]
    large = [
        ((4, 4, 2, 2, 2 * CHUNK, D), BF16),
        ((4, 4, 2, CHUNK, D), BF16),
        ((2, 4, 4, 2, CHUNK, D), BF16),
    ]

    def shapes(pairs):
        return [jax.ShapeDtypeStruct(shape, dtype) for shape, dtype in pairs]

    def scratch(pairs):
        return [pltpu.VMEM(shape, dtype) for shape, dtype in pairs]

    results = pl.pallas_call(
        gather_kernel,
        out_shape=shapes(kept + large),
        in_specs=[vmem] * 14,
        out_specs=[anywhere] * (KEPT + 3),
        scratch_shapes=scratch(
            kept[:9]
            + kept[11:]
            + large
            + [
                ((2, 4, 2, 2, CHUNK, D), BF16),
                ((2, 4, 4, CHUNK, D), BF16),
                ((2, 4, 2, CHUNK, D), BF16),
                ((2, TOKENS, D), BF16),
                ((2, TOKENS, D), BF16),
                ((2, 2, TOKENS, D), F32),
                ((2, TOKENS, D), BF16),
                ((2 * CHUNK, D), BF16),
                ((2 * CHUNK, D), BF16),
                ((2 * CHUNK, D), F32),
            ]
        )
        + [
            pltpu.SemaphoreType.DMA((3,)),
            pltpu.SemaphoreType.DMA((len(PARTS), 3, 6)),
            pltpu.SemaphoreType.DMA((len(PARTS), 3, 6)),
            pltpu.SemaphoreType.DMA((2, 5)),
            pltpu.SemaphoreType.DMA((3, 2)),
            pltpu.SemaphoreType.DMA((2, 3, 2)),
            pltpu.SemaphoreType.DMA((KEPT,)),
        ],
        compiler_params=pltpu.CompilerParams(
            collective_id=0, has_side_effects=True, vmem_limit_bytes=61 * 2**20
        ),
    )(*weights, x, cotangent.reshape(TOKENS, D), lengths, *tables)
    middle, e, h1p, q, k, v, mixed, probs, vector, own, parcel = results[:11]
    early = results[11:KEPT]
    grad_wide, grad_shared, rest = results[KEPT:]
    loaded = dict(
        x=x, e=e, rest=rest, middle=middle, h1p=h1p, q=q, k=k, v=v, mixed=mixed, probs=probs,
        vector=vector, own=own, parcel=parcel,
    )
    fetched = [loaded[name] for name in LOADED] + list(early)
    output, input_grad, grads = pl.pallas_call(
        scatter_kernel,
        out_shape=shapes([((TOKENS, D), BF16), ((TOKENS, D), BF16), ((4, CHUNK, D), F32)]),
        in_specs=[vmem] * 4 + [anywhere] * (2 + len(fetched)),
        out_specs=[vmem] * 3,
        scratch_shapes=scratch(
            [(value.shape, value.dtype) for value in fetched]
            + large[:2]
            + [
                ((2, 4, 4, 2, CHUNK, D), BF16),
                ((4, 4, 2, CHUNK, D), BF16),
                ((2, CHUNK, D), BF16),
                ((2, CHUNK, D), BF16),
                ((2, TOKENS, D), BF16),
                ((TOKENS, D), F32),
            ]
        )
        + [
            pltpu.SemaphoreType.DMA((len(PARTS), 4)),
            pltpu.SemaphoreType.DMA((len(PARTS), 3, 6)),
            pltpu.SemaphoreType.DMA((len(PARTS), 3, 6)),
            pltpu.SemaphoreType.DMA((2, 3)),
            pltpu.SemaphoreType.DMA((2,)),
            pltpu.SemaphoreType.DMA((len(fetched),)),
        ]
        + [
            pltpu.VMEM(shape, BF16)
            for key, group in buffers.items()
            for slot, shape in enumerate(group)
            if shape is not None and (*key, slot) not in EARLY
        ],
        compiler_params=pltpu.CompilerParams(
            collective_id=1, has_side_effects=True, vmem_limit_bytes=62 * 2**20
        ),
    )(lengths, *tables, grad_wide, grad_shared, *fetched)
    return output, input_grad, grads


def newton_schulz(gram, values):
    gram_half = half(gram)
    first = half(NEWTON_B * gram + NEWTON_C * product(gram_half, gram_half))
    cross = product(gram_half, first)
    after = NEWTON_A * NEWTON_A * gram + 2.0 * NEWTON_A * cross + product(half(cross), first)
    after_half = half(after)
    second = half(NEWTON_B * after + NEWTON_C * product(after_half, after_half))
    values = half(NEWTON_A * values + product(half(values), first))
    return half(NEWTON_A * values.astype(F32) + product(values, second))


BLOCKS = [(i, j) for i in range(7) for j in range(i, 7)]
JOB_ROWS = (48, 48, 48, 16, 16, 16, 16)


def own_momenta(grads_ref, priors, momenta, odd):
    for parity in range(2):

        @pl.when(odd == parity)
        def _():
            for n in range(3):
                for k, (start, size) in enumerate(((0, 16), (16, 16), (32, 6))):
                    base = 16 * n + (6 * parity if k == 2 else 0)
                    momenta[n][start : start + size] = (
                        MOMENTUM * priors[n][start : start + size] + grads_ref[k, base : base + size]
                    )
            for n in range(4):
                base = 16 * min(n, 2) + 7 * parity
                lanes = slice(0, D) if n < 2 else slice(128 * n - 256, 128 * n - 128)
                momenta[3 + n][...] = (
                    MOMENTUM * priors[3 + n][...] + grads_ref[3, base : base + 7, lanes]
                )


def update_kernel(output_ref, input_grad_ref, grads_ref, tall_ref, short_ref, *refs):
    priors, masters, (first_ref, second_ref, vector_ref) = refs[:7], refs[7:14], refs[14:17]
    momenta, updated, vector_outs = refs[17:24], refs[24:31], refs[31:34]
    refs[34][...] = output_ref[...]
    refs[35][...] = input_grad_ref[...]
    odd = lax.axis_index("dp") % 2
    own_momenta(grads_ref, priors, momenta, odd)
    for n in range(7):
        size = FF if n < 3 else D
        got = tall_ref[n].astype(F32)[:38] if n < 3 else short_ref[n - 3].astype(F32)[:7]
        got = got[:, :128] if n > 4 else got
        updated[n][...] = masters[n][...] * (1.0 - MUON_RATE * MUON_DECAY) - (
            MUON_RATE * 0.2 * math.sqrt(size) * got
        )
    for parity in range(2):

        @pl.when(odd == parity)
        def _():
            start = 32 + 7 * parity
            grad = grads_ref[3, start : start + 1, 256:384][:, :23]
            first = BETA_FIRST * first_ref[...] + (1.0 - BETA_FIRST) * grad
            second = BETA_SECOND * second_ref[...] + (1.0 - BETA_SECOND) * grad * grad
            first_hat = first / (1.0 - BETA_FIRST**STEP)
            second_hat = second / (1.0 - BETA_SECOND**STEP)
            vector_outs[0][...] = first
            vector_outs[1][...] = second
            vector_outs[2][...] = vector_ref[...] * (1.0 - ADAM_RATE * ADAM_DECAY) - (
                ADAM_RATE * first_hat / (jnp.sqrt(second_hat) + ADAM_EPSILON)
            )


def muon_kernel(
    grads_ref, prior0, prior1, prior2, prior3, prior4, prior5, prior6, tall_out_ref, short_out_ref,
    momentum0, momentum1, momentum2, momentum3, momentum4, momentum5, momentum6,
    tall_wide, short_wide, tall_ref, short_ref, rows, gram_out, gram_twin, gram_half_sum, gram_in, gram_all, gram, back, tall_got, short_got,
    job_sems, twin_sems, sum_sems, all_sems, back_sems,
):
    priors = (prior0, prior1, prior2, prior3, prior4, prior5, prior6)
    momenta = (momentum0, momentum1, momentum2, momentum3, momentum4, momentum5, momentum6)
    coords, core = my_coords()
    z, y, x = coords
    job = z * 2 + y // 2
    source = z * 2 + y // 2
    member = (y % 2) * 4 + x
    tall_wide[...] = jnp.zeros_like(tall_wide)
    short_wide[...] = jnp.zeros_like(short_wide)
    own_momenta(grads_ref, priors, momenta, x % 2)
    for n in range(3):
        tall_wide[n, 0:38] = momenta[n][...]
    for n in range(4):
        short_wide[n, 0:7, 0 : D if n < 2 else 128] = momenta[3 + n][...]
    tall_ref[...] = half(tall_wide[...])
    short_ref[...] = half(short_wide[...])
    twin = device_of(coords, 1 - core)

    def group(peer):
        return device_of((z, (y // 2) * 2 + peer // 4, peer % 4), core)

    def square(k):
        return device_of((k // 2, (k % 2) * 2 + y % 2, x), core)

    barrier = pltpu.get_barrier_semaphore()
    for k in range(1, 8):
        for device in (group((member + k) % 8), square((source + k) % 8)):
            pl.semaphore_signal(barrier, inc=1, device_id=device, device_id_type=MESH)
    pl.semaphore_signal(barrier, inc=1, device_id=twin, device_id_type=MESH)
    pl.semaphore_wait(barrier, 15)

    def copy(src, dst, sems, slot, device):
        return remote(src, dst, sems.at[0, slot], sems.at[1, slot], device)

    def mine(m, tall, short):
        return tall.at[m] if m < 3 else short.at[m - 3]

    def job_copy(m):
        return remote(
            mine(m, tall_ref, short_ref),
            rows.at[source, pl.ds(0, JOB_ROWS[m])],
            job_sems.at[0, m],
            job_sems.at[1, source],
            square(m),
        )

    for m in range(7):

        @pl.when(job != m)
        def _():
            job_copy(m).start()

    for kind in range(2):
        count = (48, 16)[kind]

        @pl.when((job >= 3 * kind) & (job < 3 + 4 * kind))
        def _():
            if kind == 1:
                rows[:, 16:48] = jnp.zeros((8, 32, D), BF16)
                rows[source, 0:16] = short_ref[job - 3]
            else:
                rows[source] = tall_ref[job]
            for k in range(1, 8):
                other = (source + k) % 8
                arrival = rows.at[other, pl.ds(0, count)]
                remote(
                    arrival, arrival, job_sems.at[0, 0], job_sems.at[1, other], square(other)
                ).wait_recv()

    @pl.when(job < 7)
    def _():
        flat = rows[...].reshape(384, D)
        gram[...] = inner_rows(flat, flat)
        for index, (i, j) in enumerate(BLOCKS):
            gram_out[index // 16, index % 16] = half(
                gram[128 * i : 128 * i + 128, 128 * j : 128 * j + 128]
            )
        gram_out[1, 12:16] = jnp.zeros((4, 128, 128), BF16)
        twin_copy = copy(gram_out.at[1 - core], gram_twin, twin_sems, 0, twin)
        twin_copy.start()
        twin_copy.wait()
        gram_half_sum[...] = half(gram_out[core].astype(F32) + gram_twin[...].astype(F32))

        def sum_copy(k):
            peer = (member + k) % 8
            return copy(
                gram_half_sum.at[pl.ds(2 * peer, 2)], gram_in.at[k], sum_sems, k, group(peer)
            )

        for k in range(1, 8):
            sum_copy(k).start()
        total = gram_half_sum[pl.ds(2 * member, 2)].astype(F32)
        for k in range(1, 8):
            sum_copy(k).wait_recv()
            total = total + gram_in[k].astype(F32)
        gram_all[core, pl.ds(2 * member, 2)] = half(total)

        def all_copy(k, owner):
            ref = gram_all.at[core, pl.ds(2 * owner, 2)]
            return copy(ref, ref, all_sems, k, group((member + k) % 8))

        for k in range(1, 8):
            all_copy(k, member).start()
        for k in range(1, 8):
            all_copy(k, (member + 8 - k) % 8).wait_recv()
        last_copy = copy(gram_all.at[core], gram_all.at[core], twin_sems, 1, twin)
        last_copy.start()
        last_copy.wait()

        eye = lax.broadcasted_iota(jnp.int32, (128, 128), 0) == lax.broadcasted_iota(
            jnp.int32, (128, 128), 1
        )
        trace = 0.0
        for index, (i, j) in enumerate(BLOCKS):
            block = gram_all[index // 16, index % 16].astype(F32)
            gram[128 * i : 128 * i + 128, 128 * j : 128 * j + 128] = block
            if i == j:
                trace = trace + jnp.sum(jnp.where(eye, block, 0.0))
            else:
                gram[128 * j : 128 * j + 128, 128 * i : 128 * i + 128] = block.T
        inverse = 1.0 / (jnp.sqrt(jnp.full((1, 1), trace)) + 1e-07)
        moved = newton_schulz(
            gram[...] * (inverse * inverse), rows[...].reshape(384, D).astype(F32) * inverse
        )
        back[...] = moved.reshape(8, 48, D)
        for k in range(1, 8):
            sum_copy(k).wait_send()
            all_copy(k, member).wait_send()

    for m in range(7):

        @pl.when(job == m)
        def _():
            copies = []
            for k in range(1, 8):
                other = (source + k) % 8
                copies.append(
                    remote(
                        back.at[other, pl.ds(0, JOB_ROWS[m])],
                        mine(m, tall_got, short_got),
                        back_sems.at[0, k],
                        back_sems.at[1, m],
                        square(other),
                    )
                )
            for item in copies:
                item.start()
            if m < 3:
                tall_got[m] = back[source]
            else:
                short_got[m - 3] = back[source, 0:16]
            for item in copies:
                item.wait_send()

    for m in range(7):

        @pl.when(job != m)
        def _():
            arrival = mine(m, tall_got, short_got)
            remote(arrival, arrival, back_sems.at[0, 0], back_sems.at[1, m], square(m)).wait_recv()
            job_copy(m).wait_send()

    tall_out_ref[...] = tall_got[...]
    short_out_ref[...] = short_got[...]


def muon(results, grads, priors, masters, vectors):
    vmem = pl.BlockSpec(memory_space=pltpu.VMEM)
    tall, short = pl.pallas_call(
        muon_kernel,
        out_shape=(
            jax.ShapeDtypeStruct((3, 48, D), BF16),
            jax.ShapeDtypeStruct((4, 16, D), BF16),
        ),
        in_specs=[vmem] * 8,
        out_specs=[vmem] * 2,
        scratch_shapes=[
            *(pltpu.VMEM(value.shape, F32) for value in priors),
            pltpu.VMEM((3, 48, D), F32),
            pltpu.VMEM((4, 16, D), F32),
            pltpu.VMEM((3, 48, D), BF16),
            pltpu.VMEM((4, 16, D), BF16),
            pltpu.VMEM((8, 48, D), BF16),
            pltpu.VMEM((2, 16, 128, 128), BF16),
            pltpu.VMEM((16, 128, 128), BF16),
            pltpu.VMEM((16, 128, 128), BF16),
            pltpu.VMEM((8, 2, 128, 128), BF16),
            pltpu.VMEM((2, 16, 128, 128), BF16),
            pltpu.VMEM((D, D), F32),
            pltpu.VMEM((8, 48, D), BF16),
            pltpu.VMEM((3, 48, D), BF16),
            pltpu.VMEM((4, 16, D), BF16),
            pltpu.SemaphoreType.DMA((2, 8)),
            pltpu.SemaphoreType.DMA((2, 2)),
            pltpu.SemaphoreType.DMA((2, 8)),
            pltpu.SemaphoreType.DMA((2, 8)),
            pltpu.SemaphoreType.DMA((2, 8)),
        ],
        compiler_params=pltpu.CompilerParams(
            collective_id=3, has_side_effects=True, vmem_limit_bytes=58 * 2**20
        ),
    )(grads, *priors)
    outs = [*priors, *masters, *vectors]
    return pl.pallas_call(
        update_kernel,
        out_shape=[jax.ShapeDtypeStruct(value.shape, value.dtype) for value in [*outs, *results]],
        in_specs=[vmem] * 22,
        out_specs=[vmem] * 19,
    )(*results, grads, tall, short, *outs)


def body(
    inputs,
    cotangent,
    lengths,
    query_weight,
    key_weight,
    value_weight,
    out_weight,
    gate_weight,
    up_weight,
    down_weight,
    vectors,
    query_prior,
    key_prior,
    value_prior,
    out_prior,
    gate_prior,
    up_prior,
    down_prior,
    first_prior,
    second_prior,
):
    weights = (
        gate_weight.T, up_weight.T, down_weight, query_weight, out_weight, key_weight, value_weight,
        vectors[None],
    )
    block_output, input_grad, grads = layer(weights, inputs[:, 0], cotangent[:, 0], lengths)
    results = muon(
        (block_output, input_grad),
        grads,
        (gate_prior.T, up_prior.T, down_prior, query_prior, out_prior, key_prior, value_prior),
        (gate_weight.T, up_weight.T, down_weight, query_weight, out_weight, key_weight, value_weight),
        (first_prior[None], second_prior[None], vectors[None]),
    )

    def ordered(gate, up, down, query, out, key, value):
        return query, key, value, out, gate.T, up.T, down

    return (
        *(value.reshape(2, 1, 128, D) for value in results[17:]),
        *ordered(*results[:7]),
        *ordered(*results[7:14]),
        *(value[0] for value in results[14:17]),
    )


def solution(mesh):
    placed = (
        P(None, ("dp", "narrow"), None, None),
        P(None, ("dp", "narrow"), None, None),
        P(),
        P(("dp", "narrow"), None),
        P(("dp", "narrow"), None),
        P(("dp", "narrow"), None),
        P(("dp", "narrow"), None),
        P(None, ("dp", "narrow")),
        P(None, ("dp", "narrow")),
        P(("dp", "narrow"), None),
        P(("dp", "narrow")),
        P(("dp", "narrow"), None),
        P(("dp", "narrow"), None),
        P(("dp", "narrow"), None),
        P(("dp", "narrow"), None),
        P(None, ("dp", "narrow")),
        P(None, ("dp", "narrow")),
        P(("dp", "narrow"), None),
        P(("dp", "narrow")),
        P(("dp", "narrow")),
    )
    return jax.shard_map(
        body,
        mesh=mesh,
        in_specs=placed,
        out_specs=(
            P(None, ("dp", "narrow"), None, None),
            P(None, ("dp", "narrow"), None, None),
            P(("dp", "narrow"), None),
            P(("dp", "narrow"), None),
            P(("dp", "narrow"), None),
            P(("dp", "narrow"), None),
            P(None, ("dp", "narrow")),
            P(None, ("dp", "narrow")),
            P(("dp", "narrow"), None),
            P(("dp", "narrow"), None),
            P(("dp", "narrow"), None),
            P(("dp", "narrow"), None),
            P(("dp", "narrow"), None),
            P(None, ("dp", "narrow")),
            P(None, ("dp", "narrow")),
            P(("dp", "narrow"), None),
            P(("dp", "narrow")),
            P(("dp", "narrow")),
            P(("dp", "narrow")),
        ),
        check_vma=False,
    )
```

```python
import math

import jax
import jax.numpy as jnp
import numpy as np
from jax import lax
from jax.experimental import pallas as pl
from jax.experimental.pallas import tpu as pltpu
from jax.sharding import PartitionSpec as P

D = 896
FF = 4864
HEADS = 14
KV_HEADS = 2
HEAD = 64
STEP = 10


NORM_EPSILON = 1e-06
ROPE_BASE = 1000000.0
MOMENTUM = 0.95
NEWTON_A = 3.4445
NEWTON_B = -4.775
NEWTON_C = 2.0315
MUON_RATE = 0.4
MUON_DECAY = 0.1
ADAM_RATE = 0.5
ADAM_DECAY = 0.01
BETA_FIRST = 0.9
BETA_SECOND = 0.999
ADAM_EPSILON = 1e-08
MASKED = -1e30


def product(left, right):
    return jnp.dot(left, right, preferred_element_type=jnp.float32)


def inner_rows(left, right):
    return lax.dot_general(
        left, right, (((0,), (0,)), ((), ())), preferred_element_type=jnp.float32
    )


def outer_cols(left, right):
    return lax.dot_general(
        left, right, (((1,), (1,)), ((), ())), preferred_element_type=jnp.float32
    )


def norm_back(grad, normed, scale):
    return scale * (grad - normed * jnp.mean(grad * normed, axis=-1, keepdims=True))


def half(value):
    return value.astype(jnp.bfloat16)


MESH = pl.DeviceIdType.MESH
TOKENS = 256
FULL = (0, 4)
BF16 = jnp.bfloat16
F32 = jnp.float32
CHUNK = 48
PARTS = (
    (0, 0, CHUNK, (2, 1, 0), False, (0, D)),
    (0, CHUNK, CHUNK, (1, 0, 2), False, (0, D)),
    (1, 0, CHUNK, (0, 2, 1), True, (0, D)),
    (2, 0, 16, (2, 1, 0), True, (0, D)),
    (2, 16, 16, (1, 0, 2), True, (0, 512)),
    (2, 16, 16, (0, 2, 1), True, (512, 384)),
    (2, 32, 16, (0, 2, 1), True, (0, 384)),
    (0, 0, CHUNK, (2, 1, 0), False, (0, 768)),
    (0, CHUNK, CHUNK, (1, 0, 2), False, (0, 768)),
    (0, 0, CHUNK, (2, 0, 1), False, (768, 128)),
    (0, CHUNK, CHUNK, (0, 2, 1), False, (768, 128)),
)
WIDE = (0, 1, 2)
THIN = (3, 4, 5, 6)
MAIN, SIDE = (7, 8, 2), (9, 10)
SUMMED = MAIN + SIDE


def my_coords():
    dp = lax.axis_index("dp")
    return (dp // 16, (dp // 4) % 4, dp % 4), lax.axis_index("narrow")


def device_of(coords, core):
    return (coords[0] * 16 + coords[1] * 4 + coords[2], core)


def shifted(coords, axis, by):
    out = list(coords)
    out[axis] = (coords[axis] + by) % 4
    return tuple(out)


def facing(coords):
    return (coords[0], coords[1], 3 - coords[2])


def greet(coords, core):
    barrier = pltpu.get_barrier_semaphore()
    for axis in range(3):
        for by in (1, 2, 3):
            pl.semaphore_signal(
                barrier, inc=1, device_id=device_of(shifted(coords, axis, by), core), device_id_type=MESH
            )
    pl.semaphore_signal(barrier, inc=1, device_id=device_of(coords, 1 - core), device_id_type=MESH)
    pl.semaphore_wait(barrier, 10)


def remote(src, dst, send_sem, recv_sem, device):
    return pltpu.make_async_remote_copy(
        src_ref=src,
        dst_ref=dst,
        send_sem=send_sem,
        recv_sem=recv_sem,
        device_id=device,
        device_id_type=MESH,
    )


def place_of(part, spec):
    _, first, rows, _, shared, columns = PARTS[part]
    index = [pl.ds(*s) if isinstance(s, tuple) else s for s in spec[:2]]
    s = spec[2]
    if isinstance(s, tuple):
        index.append(pl.ds(s[0] // 2, s[1] // 2))
        index += [] if shared else [pl.ds(0, 2)]
    else:
        index.append(s // 2)
        index += [] if shared else [s % 2]
    return (*index, pl.ds(first, rows), pl.ds(*columns))


def shape_of(part, spec):
    return tuple(entry.size for entry in place_of(part, spec) if isinstance(entry, pl.Slice))


class Plan:
    def __init__(self, part, stage, coords, axis, spec, split):
        self.coords, self.axis, self.spec, self.split = coords, axis, spec, split
        self.exchange = PARTS[part][4] and axis == 2
        self.direct = not self.exchange and stage == 0

    def at(self, by):
        return shifted(self.coords, self.axis, by)

    def whole(self, by):
        spec = list(self.spec)
        spec[self.axis] = (self.coords[self.axis] + by) % 4
        return tuple(spec)

    def pieces(self, by):
        out = []
        for h in range(2):
            spec = list(self.whole(by))
            spec[self.split] = (2 * h, 2)
            out.append(tuple(spec))
        return out

    def facing(self):
        return (*self.spec[:2], 3 - self.coords[2])

    def own(self):
        return self.spec


def plan_of(part, stage, coords):
    order = PARTS[part][3]
    spec = tuple(FULL if k in order[:stage] else coords[k] for k in range(3))
    return Plan(part, stage, coords, order[stage], spec, order[stage - 1] if stage else None)


class Gather:
    def __init__(self, arrays, coords, core, send_sems, recv_sems):
        self.arrays, self.coords, self.core = arrays, coords, core
        self.send_sems, self.recv_sems = send_sems, recv_sems

    def copy(self, part, phase, slot, piece, coords):
        array, prefix = self.arrays[PARTS[part][0]]
        ref = array.at[(*prefix, *place_of(part, piece))]
        sems = (self.send_sems.at[part, phase, slot], self.recv_sems.at[part, phase, slot])
        return remote(ref, ref, *sems, device_of(coords, self.core))

    def send(self, *args):
        self.copy(*args).start()

    def neighbours(self, plan):
        return shifted(self.coords, plan.axis, 1), shifted(self.coords, plan.axis, 3)

    def start(self, parts, phase):
        for part in parts:
            plan = plan_of(part, phase, self.coords)
            if plan.exchange:
                self.send(part, phase, 0, plan.own(), facing(self.coords))
                continue
            if plan.direct:
                for by in (1, 3, 2):
                    self.send(part, phase, by, plan.own(), plan.at(by))
                continue
            right, left = self.neighbours(plan)
            first, second = plan.pieces(0)
            self.send(part, phase, 0, first, right)
            self.send(part, phase, 1, second, left)
            self.send(part, phase, 2, second, right)
            self.send(part, phase, 3, first, left)

    def forward(self, parts, phase):
        for part in parts:
            plan = plan_of(part, phase, self.coords)
            if plan.exchange or plan.direct:
                continue
            right, left = self.neighbours(plan)
            piece = plan.pieces(3)[0]
            self.copy(part, phase, 0, piece, right).wait_recv()
            self.send(part, phase, 4, piece, right)
            piece = plan.pieces(1)[1]
            self.copy(part, phase, 1, piece, left).wait_recv()
            self.send(part, phase, 5, piece, left)

    def near(self, parts, phase):
        for part in parts:
            plan = plan_of(part, phase, self.coords)
            if plan.exchange:
                self.copy(part, phase, 0, plan.facing(), facing(self.coords)).wait_recv()
                continue
            if plan.direct:
                for by in (1, 3):
                    self.copy(part, phase, by, plan.whole(4 - by), plan.at(by)).wait_recv()
                continue
            right, left = self.neighbours(plan)
            self.copy(part, phase, 2, plan.pieces(3)[1], right).wait_recv()
            self.copy(part, phase, 3, plan.pieces(1)[0], left).wait_recv()

    def far(self, parts, phase):
        for part in parts:
            plan = plan_of(part, phase, self.coords)
            if plan.exchange:
                continue
            if plan.direct:
                self.copy(part, phase, 2, plan.whole(2), plan.at(2)).wait_recv()
                continue
            right, left = self.neighbours(plan)
            self.copy(part, phase, 4, plan.pieces(2)[0], right).wait_recv()
            self.copy(part, phase, 5, plan.pieces(2)[1], left).wait_recv()

    def finish(self, parts, phase):
        self.near(parts, phase)
        self.far(parts, phase)

    def drain(self):
        for part in WIDE + THIN:
            for phase in range(3):
                plan = plan_of(part, phase, self.coords)
                if plan.exchange:
                    self.copy(part, phase, 0, plan.own(), facing(self.coords)).wait_send()
                    continue
                if plan.direct:
                    for by in (1, 3, 2):
                        self.copy(part, phase, by, plan.own(), plan.at(by)).wait_send()
                    continue
                right, _ = self.neighbours(plan)
                for slot, which in enumerate((0, 1, 1, 0, 0, 1)):
                    self.copy(part, phase, slot, plan.pieces(0)[which], right).wait_send()


def each_block(shape, body):
    lead = shape[:-2]
    count = math.prod(lead)
    if count == 1:
        body((0,) * len(lead))
        return

    def step(k, carry):
        index = []
        for n in reversed(lead):
            index.append(k % n)
            k = k // n
        body(tuple(reversed(index)))
        return carry

    lax.fori_loop(0, count, step, 0)


class Scatter:
    def __init__(self, arrays, coords, core, buffers, send_sems, recv_sems, done):
        self.arrays, self.coords, self.core, self.done = arrays, coords, core, done
        self.buffers, self.send_sems, self.recv_sems = buffers, send_sems, recv_sems

    def copy(self, part, phase, slot, piece, coords):
        array, prefix = self.arrays[PARTS[part][0]]
        ref = array.at[(*prefix, *place_of(part, piece))]
        sems = (self.send_sems.at[part, phase, slot], self.recv_sems.at[part, phase, slot])
        return remote(ref, self.buffers[part, phase][slot], *sems, device_of(coords, self.core))

    def send(self, *args):
        if args[:3] not in self.done:
            self.copy(*args).start()

    def arrive(self, *args):
        if args[:3] not in self.done:
            self.copy(*args).wait_recv()

    def add(self, part, phase, piece, *slots):
        sources = [self.buffers[part, phase][slot] for slot in slots]
        base = place_of(part, piece)
        array, prefix = self.arrays[PARTS[part][0]]

        def one(index):
            spot, position = [], 0
            for entry in base[:-2]:
                if isinstance(entry, pl.Slice):
                    spot.append(entry.start + index[position])
                    position += 1
                else:
                    spot.append(entry)
            spot = (*prefix, *spot, *base[-2:])
            value = array[spot].astype(F32)
            for source in sources:
                value = value + source[(*index, slice(None), slice(None))].astype(F32)
            array[spot] = half(value)

        each_block(shape_of(part, piece), one)

    def neighbours(self, plan):
        return shifted(self.coords, plan.axis, 1), shifted(self.coords, plan.axis, 3)

    def start_far(self, parts, phase):
        for part in parts:
            plan = plan_of(part, phase, self.coords)
            if plan.exchange or plan.direct:
                continue
            right, left = self.neighbours(plan)
            self.send(part, phase, 0, plan.pieces(2)[0], right)
            self.send(part, phase, 1, plan.pieces(2)[1], left)

    def start_near(self, parts, phase):
        for part in parts:
            plan = plan_of(part, phase, self.coords)
            if plan.exchange:
                self.send(part, phase, 0, plan.facing(), facing(self.coords))
                continue
            if plan.direct:
                for by in (1, 3, 2):
                    self.send(part, phase, by, plan.whole(by), plan.at(by))
                continue
            right, left = self.neighbours(plan)
            self.send(part, phase, 2, plan.pieces(1)[1], right)
            self.send(part, phase, 3, plan.pieces(3)[0], left)

    def start(self, parts, phase):
        self.start_far(parts, phase)
        self.start_near(parts, phase)

    def forward(self, parts, phase):
        for part in parts:
            plan = plan_of(part, phase, self.coords)
            if plan.exchange or plan.direct:
                continue
            right, left = self.neighbours(plan)
            self.arrive(part, phase, 0, plan.pieces(2)[0], right)
            self.add(part, phase, plan.pieces(1)[0], 0)
            self.send(part, phase, 4, plan.pieces(1)[0], right)
            self.arrive(part, phase, 1, plan.pieces(2)[1], left)
            self.add(part, phase, plan.pieces(3)[1], 1)
            self.send(part, phase, 5, plan.pieces(3)[1], left)

    def finish(self, parts, phase):
        for part in parts:
            plan = plan_of(part, phase, self.coords)
            if plan.exchange:
                self.arrive(part, phase, 0, plan.facing(), facing(self.coords))
                self.add(part, phase, plan.own(), 0)
                continue
            if plan.direct:
                for by in (1, 3, 2):
                    self.arrive(part, phase, by, plan.whole(by), plan.at(by))
                self.add(part, phase, plan.own(), 1, 3, 2)
                continue
            right, left = self.neighbours(plan)
            self.arrive(part, phase, 3, plan.pieces(3)[0], left)
            self.arrive(part, phase, 4, plan.pieces(1)[0], right)
            self.add(part, phase, plan.pieces(0)[0], 4, 3)
            self.arrive(part, phase, 2, plan.pieces(1)[1], right)
            self.arrive(part, phase, 5, plan.pieces(3)[1], left)
            self.add(part, phase, plan.pieces(0)[1], 2, 5)

    def drain(self):
        for part in SUMMED + THIN:
            for phase in range(3):
                plan = plan_of(part, phase, self.coords)
                if plan.exchange:
                    self.copy(part, phase, 0, plan.own(), facing(self.coords)).wait_send()
                    continue
                if plan.direct:
                    for by in (1, 3, 2):
                        self.copy(part, phase, by, plan.whole(by), plan.at(by)).wait_send()
                    continue
                right, _ = self.neighbours(plan)
                for slot, which in enumerate((0, 1, 1, 0, 0, 1)):
                    if (part, phase, slot) in self.done:
                        continue
                    self.copy(part, phase, slot, plan.pieces(0)[which], right).wait_send()


EARLY = tuple((part, 2, slot) for part in MAIN for slot in (2, 3))


def scatter_buffer_shapes():
    out = []
    for part in SUMMED + THIN:
        for phase in range(3):
            plan = plan_of(part, phase, (0, 0, 0))
            if plan.exchange:
                shapes = [shape_of(part, plan.own())]
            elif plan.direct:
                shapes = [None] + [shape_of(part, plan.own())] * 3
            else:
                first, second = (shape_of(part, piece) for piece in plan.pieces(0))
                shapes = [first, second, second, first, first, second]
            out.append(((part, phase), shapes))
    return out


SCALE = HEAD ** (-0.5)


def turn(values, sign):
    lane = lax.broadcasted_iota(jnp.int32, values.shape, 1)
    ahead = pltpu.roll(values, 96, 1)
    behind = pltpu.roll(values, 32, 1)
    return jnp.where(lane & 32 == 0, sign * ahead, -sign * behind)


def tiles_of(values):
    return [values[:, 128 * t : 128 * t + 128] for t in range(values.shape[1] // 128)]


def rotated(values, cosine, sine):
    return jnp.concatenate(
        [tile * cosine + turn(tile, -1.0) * sine for tile in tiles_of(values)], axis=1
    )


def rotated_back(values, cosine, sine):
    return jnp.concatenate(
        [tile * cosine + turn(tile * sine, 1.0) for tile in tiles_of(values)], axis=1
    )


def low_lanes(shape):
    return lax.broadcasted_iota(jnp.int32, shape, 1) < HEAD


def paired(both):
    swapped = pltpu.roll(both, 64, 1)
    low = low_lanes(both.shape)
    even = [half(jnp.where(low, v, 0.0)) for v in (both, swapped)]
    odd = [half(jnp.where(low, 0.0, v)) for v in (swapped, both)]
    kinds = [jnp.concatenate([even[a], odd[b]]) for a, b in ((0, 0), (0, 1), (1, 1))]
    return [kinds[0]] * 3 + [kinds[1]] + [kinds[2]] * 3


def gathered_place():
    row = lax.broadcasted_iota(jnp.int32, (1024, D), 0)
    feature = lax.broadcasted_iota(jnp.int32, (1024, D), 1)
    slot = row & 15
    odd = (slot >= 7).astype(jnp.int32)
    device = (((row >> 4) & 31) * 2 + odd) * 2 + (row >> 9)
    source = jnp.where(slot < 14, 7 * device + slot - 7 * odd, -1)
    return half((source == feature).astype(jnp.float32))


def vector_maps():
    device = lax.broadcasted_iota(jnp.int32, (128, 1024), 0)
    row = lax.broadcasted_iota(jnp.int32, (128, 1024), 1)
    target = (device & 1) * 512 + (device >> 2) * 16 + ((device >> 1) & 1) * 7
    pick = half((row == target).astype(jnp.float32))
    start = lax.broadcasted_iota(jnp.int32, (128, 2944), 0) * 23
    entry = lax.broadcasted_iota(jnp.int32, (128, 2944), 1)
    owner = half(((entry >= start) & (entry < start + 23)).astype(jnp.float32))
    return pick, owner


def slot_mask(slots):
    return lax.broadcasted_iota(jnp.int32, (128, 2944), 0) == slots


def own_lengths(len_ref, coords, core):
    own = (coords[0] * 16 + coords[1] * 4 + coords[2]) * 2 + core
    lane = lax.broadcasted_iota(jnp.int32, (2, 128), 1)
    length = jnp.sum(jnp.where(lane == own, len_ref[...].astype(F32), 0.0), axis=1, keepdims=True)
    return jnp.broadcast_to(length, (2, 128))


def live_tokens(lengths):
    token = lax.broadcasted_iota(jnp.int32, (128, 1), 0).astype(F32)
    return jnp.concatenate([(token < lengths[b : b + 1, 0:1]).astype(F32) for b in range(2)])


def attention_forward(
    x_ref, rest_ref, lengths, cos_ref, sin_ref, slot_ref,
    middle_ref, h1p_ref, q_ref, k_ref, v_ref, mixed_ref, probs_ref, vector_ref,
):
    place = gathered_place()
    pick, owner = vector_maps()
    stored = rest_ref[:, :, :, :, 32:48, 256:384].reshape(1024, 128)
    by_device = half(product(pick, stored))
    spread = inner_rows(by_device, owner)
    vector = jnp.sum(jnp.where(slot_mask(slot_ref[...]), spread, 0.0), axis=0, keepdims=True)
    vector_ref[...] = vector
    first_gain, second_gain = vector[:, :D], vector[:, D : 2 * D]
    query_bias, narrow_bias = vector[:, 2 * D : 3 * D], vector[:, 3 * D :]
    cosine, sine = cos_ref[...], sin_ref[...]
    inputs = x_ref[...].astype(jnp.float32)
    first_scale = lax.rsqrt(jnp.mean(inputs * inputs, axis=-1, keepdims=True) + NORM_EPSILON)
    normed = half(inputs * first_scale * first_gain)
    placed = half(outer_cols(normed, place))
    h1p_ref[...] = placed
    queries = product(placed, rest_ref[:, :, :, :, 0:16, :].reshape(1024, D)) + query_bias
    narrow = product(placed, rest_ref[:, :, :, :, 32:48, 0:256].reshape(1024, 256)) + narrow_bias
    q_ref[...] = half(rotated(queries, cosine, sine))
    keys = rotated(narrow[:, 0:128], cosine, sine)
    k_ref[...] = half(keys)
    values = narrow[:, 128:256]
    v_ref[...] = half(values)
    position = lax.broadcasted_iota(jnp.int32, (128, 256), 0)
    other = lax.broadcasted_iota(jnp.int32, (128, 256), 1) & 127
    causal = other <= position
    other = other.astype(F32)
    rows = []
    for b in range(2):
        here = slice(128 * b, 128 * b + 128)
        length = lengths[b : b + 1, :]
        allowed = causal & (other < jnp.concatenate([length, length], axis=1))
        key_tiles = paired(keys[here])
        value_tiles = paired(values[here])
        tiles = []
        for t in range(7):
            scores = outer_cols(q_ref[here, 128 * t : 128 * t + 128], key_tiles[t])
            scores = jnp.where(allowed, scores * SCALE, MASKED)
            parts = []
            for part in tiles_of(scores):
                shifted = jnp.exp(part - jnp.max(part, axis=-1, keepdims=True))
                parts.append(shifted * (1.0 / jnp.sum(shifted, axis=-1, keepdims=True)))
            probs = jnp.concatenate(parts, axis=1)
            probs_ref[b, t] = probs
            tiles.append(half(product(half(probs), value_tiles[t])))
        rows.append(jnp.concatenate(tiles, axis=1))
    mixed = half(outer_cols(jnp.concatenate(rows), place))
    mixed_ref[...] = mixed
    middle = inputs + product(mixed, rest_ref[:, :, :, :, 16:32, :].reshape(1024, D))
    middle_ref[...] = middle
    second_scale = lax.rsqrt(jnp.mean(middle * middle, axis=-1, keepdims=True) + NORM_EPSILON)
    return half(middle * second_scale * second_gain)


def mlp_tile(weights, h, e, sums):
    lead = weights.shape[:-2]
    units = 16 * math.prod(lead)
    gate_w, up_w, down_w = (
        weights[..., 16 * k : 16 * k + 16, :].reshape(units, D) for k in range(3)
    )
    gate = outer_cols(h, gate_w)
    up = outer_cols(h, up_w)
    sigma = 0.5 * jnp.tanh(0.5 * gate) + 0.5
    silu = gate * sigma
    hidden = half(silu * up)
    grad_hidden = outer_cols(e, down_w)
    sums[0] += product(hidden, down_w).reshape(2, TOKENS, D)
    grad_gate = half(grad_hidden * up * (sigma + silu * (1.0 - sigma)))
    grad_up = half(grad_hidden * silu)
    sums[1] += (product(grad_gate, gate_w) + product(grad_up, up_w)).reshape(2, TOKENS, D)
    grads = (inner_rows(grad_gate, h), inner_rows(grad_up, h), inner_rows(hidden, e))
    return [half(grad).reshape(*lead, 16, D) for grad in grads]


KEPT = 17


def gather_kernel(
    gate_ref, up_ref, down_ref, query_ref, out_ref, key_ref, value_ref, own_vector_ref,
    x_ref, cot_ref, len_ref, cos_ref, sin_ref, slot_ref, *refs,
):
    coords, core = my_coords()
    z, y, x = coords
    pair, odd = x // 2, x % 2
    lengths = own_lengths(len_ref, coords, core)
    results, (grad_wide_ref, grad_shared_ref, rest_ref) = refs[:KEPT], refs[KEPT : KEPT + 3]
    held = refs[KEPT + 3 : 2 * KEPT + 1]
    (
        wide, shared, rest, stage0, stage1, stage2, h_all, e_all, sums, parcel, tail, tail_own, tail_wide,
        local_sems, send_sems, recv_sems, twin_sems, store_sems, early_sems, kept_sems,
    ) = refs[2 * KEPT + 1 :]
    middle_ref, e_ref, h1p_ref, q_ref, k_ref, v_ref, mixed_ref, probs_ref, vector_ref = held[:9]
    early = held[9:]
    kept = [*held[:9], sums.at[:, core], parcel, *early]

    def keep(first, last):
        return [
            pltpu.make_async_copy(kept[n], results[n], kept_sems.at[n]) for n in range(first, last)
        ]

    units = (gate_ref, up_ref, down_ref)
    for n, ref in enumerate(units):
        for k in range(2):
            wide[z, y, pair, odd, CHUNK * k + 16 * n : CHUNK * k + 16 * n + 16] = half(
                ref[16 * k : 16 * k + 16]
            )
    tail_wide[...] = jnp.zeros_like(tail_wide)
    for parity in range(2):

        @pl.when(odd == parity)
        def _():
            for n, ref in enumerate(units):
                start = 16 * n + 6 * parity
                tail_wide[start : start + 6] = ref[32:38]
            for n, ref in enumerate((query_ref, out_ref)):
                start = CHUNK + 16 * n + 7 * parity
                tail_wide[start : start + 7] = ref[...]
            start = CHUNK + 32 + 7 * parity
            tail_wide[start : start + 7, 0:128] = key_ref[...]
            tail_wide[start : start + 7, 128:256] = value_ref[...]
            tail_wide[start : start + 1, 256:384] = jnp.concatenate(
                [own_vector_ref[...], jnp.zeros((1, 105), F32)], axis=1
            )

    tail_own[...] = half(tail_wide[...])
    greet(coords, core)
    twin = device_of(coords, 1 - core)

    def to_twin(src, dst, slot):
        return remote(src, dst, twin_sems.at[0, slot], twin_sems.at[1, slot], twin)

    gather = Gather(((wide, ()), (shared, ()), (rest, (core,))), coords, core, send_sems, recv_sems)
    partner = device_of((z, y, x + 1 - 2 * odd), core)
    tail_copy = remote(tail_own, tail, twin_sems.at[0, 4], twin_sems.at[1, 4], partner)
    tail_copy.start()
    gather.start((0, 1), 0)
    e_ref[...] = half(cot_ref[...].astype(F32) * live_tokens(lengths))
    e_all[core] = e_ref[...]
    e_copy = to_twin(e_ref, e_all.at[core], 0)
    e_copy.start()
    tail_copy.wait()
    both = half(tail_wide[...] + tail[...].astype(F32))
    shared[z, y, pair] = both[:CHUNK]
    rest[core, z, y, pair] = both[CHUNK:]
    gather.start(THIN, 0)
    gather.start((2,), 0)
    gather.forward(THIN, 0)
    gather.finish(THIN, 0)
    gather.start(THIN, 1)
    gather.forward(WIDE, 0)
    gather.forward(THIN, 1)
    gather.finish(THIN, 1)
    gather.start(THIN, 2)
    gather.finish(WIDE, 0)
    gather.start(WIDE, 1)
    gather.forward(THIN, 2)
    gather.finish(THIN, 2)
    rest_copy = to_twin(rest.at[core], rest.at[core], 1)
    rest_copy.start()
    gather.forward(WIDE, 1)
    gather.finish(WIDE, 1)
    gather.start(WIDE, 2)
    rest_copy.wait()
    rest_store = pltpu.make_async_copy(rest, rest_ref, local_sems.at[0])
    rest_store.start()
    h_all[core] = attention_forward(
        x_ref, rest, lengths, cos_ref, sin_ref, slot_ref,
        middle_ref, h1p_ref, q_ref, k_ref, v_ref, mixed_ref, probs_ref, vector_ref,
    )
    h_copy = to_twin(h_all.at[core], h_all.at[core], 2)
    h_copy.start()
    for copy in keep(0, 9):
        copy.start()
    sums[...] = jnp.zeros_like(sums)
    e_copy.wait()
    h_copy.wait()
    stages = (stage0, stage1, stage2)

    def early_copy(t, slot):
        axis = PARTS[t][3][2]
        which = 3 - slot
        place = [slice(None)] * (len(stages[t].shape) - 1)
        place[1 if t == 2 else 0] = pl.ds(which, 1) if t == 2 else pl.ds(2 * which, 2)
        place[-1] = pl.ds(*PARTS[MAIN[t]][5])
        return remote(
            stages[t].at[(slot - 1) % 2].at[tuple(place)],
            early[2 * t + slot - 2],
            early_sems.at[0, t, slot - 2],
            early_sems.at[1, t, slot - 2],
            device_of(shifted(coords, axis, 1 if slot == 2 else 3), core),
        )

    def tile_places(j):
        return (
            (wide, grad_wide_ref, (j, slice(None), slice(None), slice(None), pl.ds(0, CHUNK))),
            (wide, grad_wide_ref, (slice(None), slice(None), j // 2, j % 2, pl.ds(CHUNK, CHUNK))),
            (shared, grad_shared_ref, (slice(None), j, slice(None), pl.ds(0, CHUNK))),
        )

    def step(k, carry):
        @pl.when(k == 1)
        def _():
            gather.near(WIDE, 2)

        @pl.when(k == 3)
        def _():
            gather.far(WIDE, 2)

        offset = jnp.where(k < 2, k, 5 - k)
        h = h_all[...].reshape(2 * TOKENS, D)
        e = e_all[...].reshape(2 * TOKENS, D)
        for t, axis in enumerate((0, 2, 1)):
            j = (coords[axis] + offset) % 4
            source, target, index = tile_places(j)[t]
            grads = mlp_tile(source[(*index, slice(None))], h, e, sums)
            copy = pltpu.make_async_copy(
                stages[t].at[k % 2], target.at[(*index, slice(None))], store_sems.at[t, k % 2]
            )

            @pl.when(k > 1)
            def _():
                copy.wait()

            @pl.when(k == 3)
            def _():
                early_copy(t, 2).wait_send()

            for place, grad in enumerate(grads):
                stages[t][k % 2, ..., 16 * place : 16 * place + 16, :] = grad
            copy.start()

            @pl.when(k == 1)
            def _():
                early_copy(t, 2).start()

            @pl.when(k == 2)
            def _():
                early_copy(t, 3).start()

        @pl.when(k == 0)
        def _():
            gather.forward(WIDE, 2)

        return carry

    lax.fori_loop(0, 4, step, 0)
    parcel[...] = half(sums[:, 1 - core])
    for copy in keep(9, 11):
        copy.start()
    for t in range(3):
        _, target, index = tile_places(0)[t]
        for which in range(2):
            pltpu.make_async_copy(
                stages[t].at[which], target.at[(*index, slice(None))], store_sems.at[t, which]
            ).wait()
        early_copy(t, 3).wait_send()
        early_copy(t, 2).wait_recv()
        early_copy(t, 3).wait_recv()
        for copy in keep(11 + 2 * t, 13 + 2 * t):
            copy.start()
    rest_store.wait()
    for copy in keep(0, KEPT):
        copy.wait()
    gather.drain()


def attention_backward(
    between, ready, x_ref, e_ref, rest_ref, cos_ref, sin_ref, slot_ref,
    middle_ref, h1p_ref, q_ref, k_ref, v_ref, mixed_ref, probs_ref, vector_ref, dh2_ref,
    input_grad_ref, grad_ref,
):
    place = gathered_place()
    pick, owner = vector_maps()
    vector = vector_ref[...]
    first_gain, second_gain = vector[:, :D], vector[:, D : 2 * D]
    cosine, sine = cos_ref[...], sin_ref[...]
    middle = middle_ref[...]
    second_scale = lax.rsqrt(jnp.mean(middle * middle, axis=-1, keepdims=True) + NORM_EPSILON)
    second_normed = middle * second_scale
    dh2 = dh2_ref[...]
    second_gain_grad = jnp.sum(dh2 * second_normed, axis=0, keepdims=True)
    grad_middle = e_ref[...].astype(jnp.float32) + norm_back(
        dh2 * second_gain, second_normed, second_scale
    )
    branch = half(grad_middle)
    wide = rest_ref[:, :, :, :, 16:32, :].reshape(1024, D)
    grad_ref[:, :, :, :, 16:32, :] = half(inner_rows(mixed_ref[...], branch)).reshape(2, 4, 4, 2, 16, D)
    grad_mixed = half(product(half(outer_cols(branch, wide)), place))
    low = low_lanes((128, 128))
    query_rows, key_rows, value_rows = [], [], []
    for b in range(2):
        here = slice(128 * b, 128 * b + 128)
        key_tiles = paired(k_ref[here, :].astype(jnp.float32))
        value_tiles = paired(v_ref[here, :].astype(jnp.float32))
        tiles = []
        sums = [[jnp.zeros((128, 128), jnp.float32) for _ in range(4)] for _ in range(2)]
        for t in range(7):
            head = grad_mixed[here, 128 * t : 128 * t + 128]
            grad_probs = outer_cols(head, value_tiles[t])
            probs = probs_ref[b, t]
            parts = []
            for p, g in zip(tiles_of(probs), tiles_of(grad_probs)):
                parts.append(half(p * (g - jnp.sum(p * g, axis=-1, keepdims=True))))
            grad_scores = jnp.concatenate(parts, axis=1)
            tiles.append(product(grad_scores, key_tiles[t]) * SCALE)
            for which, (left, right) in enumerate(
                ((grad_scores, q_ref[here, 128 * t : 128 * t + 128]), (half(probs), head))
            ):
                both = inner_rows(left, right)
                even, odd = (2 * t) // 7, (2 * t + 1) // 7
                sums[which][even] += both[0:128]
                sums[which][2 + odd] += both[128:256]
        query_rows.append(jnp.concatenate(tiles, axis=1))
        joined = []
        for which in range(2):
            even0, even1, odd0, odd1 = sums[which]
            joined.append(
                jnp.where(low, even0 + pltpu.roll(odd0, 64, 1), odd1 + pltpu.roll(even1, 64, 1))
            )
        key_rows.append(joined[0] * SCALE)
        value_rows.append(joined[1])
    between()
    grad_query = half(rotated_back(jnp.concatenate(query_rows), cosine, sine))
    grad_key = half(rotated_back(jnp.concatenate(key_rows), cosine, sine))
    grad_narrow = jnp.concatenate([grad_key, half(jnp.concatenate(value_rows))], axis=1)
    placed = h1p_ref[...]
    grad_ref[:, :, :, :, 0:16, :] = half(inner_rows(placed, grad_query)).reshape(2, 4, 4, 2, 16, D)
    ready()
    grad_ref[:, :, :, :, 32:48, 0:256] = half(inner_rows(placed, grad_narrow)).reshape(2, 4, 4, 2, 16, 256)
    bias_grad = jnp.sum(
        jnp.concatenate([grad_query, grad_narrow], axis=1).astype(jnp.float32), axis=0, keepdims=True
    )
    grad_placed = outer_cols(grad_query, rest_ref[:, :, :, :, 0:16, :].reshape(1024, D)) + outer_cols(
        grad_narrow, rest_ref[:, :, :, :, 32:48, 0:256].reshape(1024, 256)
    )
    high = half(grad_placed)
    remainder = half(grad_placed - high.astype(jnp.float32))
    grad_normed = product(high, place) + product(remainder, place)
    inputs = x_ref[...].astype(jnp.float32)
    first_scale = lax.rsqrt(jnp.mean(inputs * inputs, axis=-1, keepdims=True) + NORM_EPSILON)
    first_normed = inputs * first_scale
    first_gain_grad = jnp.sum(grad_normed * first_normed, axis=0, keepdims=True)
    input_grad_ref[...] = half(
        grad_middle + norm_back(grad_normed * first_gain, first_normed, first_scale)
    )
    vector_grad = jnp.concatenate([first_gain_grad, second_gain_grad, bias_grad], axis=1)
    spread = half(jnp.where(slot_mask(slot_ref[...]), vector_grad, 0.0))
    by_device = half(outer_cols(owner, spread))
    stored = half(inner_rows(pick, by_device))
    grad_ref[:, :, :, :, 32:48, 256:384] = stored.reshape(2, 4, 4, 2, 16, 128)
    grad_ref[:, :, :, :, 32:48, 384:] = jnp.zeros((2, 4, 4, 2, 16, D - 384), jnp.bfloat16)


LOADED = (
    "parcel", "own", "middle", "e", "x", "rest", "h1p", "q", "k", "v", "mixed", "probs", "vector",
)


def scatter_kernel(
    len_ref, cos_ref, sin_ref, slot_ref, grad_wide_ref, grad_shared_ref, *refs,
):
    coords, core = my_coords()
    z, y, x = coords
    pair, odd = x // 2, x % 2
    count = len(LOADED) + len(EARLY)
    sources, (output_ref, input_grad_ref, out_ref) = refs[:count], refs[count : count + 3]
    held = refs[count + 3 : 2 * count + 3]
    (
        wide, shared, thin, joined, mine, theirs, arrived, dh2_ref,
        load_sems, send_sems, recv_sems, twin_sems, pair_sems, held_sems,
    ) = refs[2 * count + 3 : 2 * count + 17]
    buffers = refs[2 * count + 17 :]
    (
        parcel_ref, own_ref, middle_ref, e_ref, x_ref, rest_ref, h1p_ref, q_ref, k_ref, v_ref,
        mixed_ref, probs_ref, vector_ref,
    ) = held[: len(LOADED)]
    fetches = [
        pltpu.make_async_copy(sources[n], held[n], held_sems.at[n]) for n in range(count)
    ]
    named, position = {}, 0
    early = dict(zip(EARLY, held[len(LOADED) :]))
    for key, shapes in scatter_buffer_shapes():
        named[key] = []
        for slot in range(len(shapes)):
            if (*key, slot) in early:
                named[key].append(early[(*key, slot)])
            elif shapes[slot] is None:
                named[key].append(None)
            else:
                named[key].append(buffers[position])
                position += 1
    scatter = Scatter(((wide, ()), (shared, ()), (thin, (core,))), coords, core, named, send_sems, recv_sems, EARLY)

    def load(part, by):
        spec = [FULL] * 3
        axis = PARTS[part][3][2]
        spec[axis] = (coords[axis] + by) % 4
        place = place_of(part, tuple(spec))
        source = (grad_wide_ref, grad_shared_ref)[PARTS[part][0]]
        target = (wide, shared)[PARTS[part][0]]
        return pltpu.make_async_copy(source.at[place], target.at[place], load_sems.at[part, by])

    for by in (2, 1, 3, 0):
        for part in SUMMED:
            load(part, by).start()
    for copy in fetches:
        copy.start()
    greet(coords, core)

    for part in SUMMED:
        load(part, 2).wait()
        scatter.start_far((part,), 2)
    for part in SUMMED:
        load(part, 1).wait()
        load(part, 3).wait()
    scatter.start_near(SIDE, 2)

    def between():
        scatter.forward(SUMMED, 2)

    for copy in fetches[:3]:
        copy.wait()
    parcel_copy = remote(
        parcel_ref, arrived, twin_sems.at[0, 1], twin_sems.at[1, 1], device_of(coords, 1 - core)
    )
    parcel_copy.start()
    for copy in fetches[3:]:
        copy.wait()
    parcel_copy.wait()
    output_ref[...] = half(
        (middle_ref[...] + (own_ref[0] + arrived[0].astype(F32))) * live_tokens(own_lengths(len_ref, coords, core))
    )
    dh2_ref[...] = own_ref[1] + arrived[1].astype(F32)
    def twin_copy(slot, first, rows):
        return remote(
            thin.at[1 - core, :, :, :, pl.ds(first, rows)],
            joined.at[:, :, :, pl.ds(first, rows)],
            twin_sems.at[0, slot],
            twin_sems.at[1, slot],
            device_of(coords, 1 - core),
        )

    def ready():
        twin_copy(0, 0, 32).start()

    attention_backward(
        between, ready, x_ref, e_ref, rest_ref, cos_ref, sin_ref, slot_ref,
        middle_ref, h1p_ref, q_ref, k_ref, v_ref, mixed_ref, probs_ref, vector_ref, dh2_ref,
        input_grad_ref, thin,
    )
    twin_copy(2, 32, 16).start()
    for part in SUMMED:
        load(part, 0).wait()
    for slot, first, rows, parts in ((0, 0, 32, THIN[:3]), (2, 32, 16, THIN[3:])):
        twin_copy(slot, first, rows).wait()

        def join(index):
            own = (core, *index, pl.ds(first, rows))
            thin[own] = half(thin[own].astype(F32) + joined[(*index, pl.ds(first, rows))].astype(F32))

        each_block((4, 4, 2, rows, D), join)
        scatter.start(parts, 2)
    for part in SUMMED:
        scatter.finish((part,), 2)
        scatter.start((part,), 1)
    scatter.forward(THIN, 2)
    scatter.forward(SUMMED, 1)
    scatter.finish(THIN, 2)
    scatter.start(THIN, 1)
    scatter.forward(THIN, 1)
    for part in SUMMED:
        scatter.finish((part,), 1)
        scatter.start((part,), 0)
    scatter.finish(THIN, 1)
    scatter.start(THIN, 0)
    scatter.forward(SUMMED, 0)
    scatter.forward(THIN, 0)
    scatter.finish(SUMMED, 0)
    scatter.finish(THIN, 0)
    mine[0] = shared[z, y, pair]
    mine[1] = thin[core, z, y, pair]
    partner = device_of((z, y, x + 1 - 2 * odd), core)
    pair_copy = remote(mine, theirs, pair_sems.at[0], pair_sems.at[1], partner)
    pair_copy.start()
    pair_copy.wait()
    out_ref[0] = wide[z, y, pair, odd, 0:CHUNK].astype(F32)
    out_ref[1] = wide[z, y, pair, odd, CHUNK : 2 * CHUNK].astype(F32)
    out_ref[2] = mine[0].astype(F32) + theirs[0].astype(F32)
    out_ref[3] = mine[1].astype(F32) + theirs[1].astype(F32)
    scatter.drain()


def layer(weights, tokens, cotangent, lengths):
    vmem = pl.BlockSpec(memory_space=pltpu.VMEM)
    anywhere = pl.BlockSpec(memory_space=pl.ANY)
    x = tokens.reshape(TOKENS, D)
    freqs = ROPE_BASE ** (-np.arange(HEAD // 2) * 2.0 / HEAD)
    angles = np.tile(np.arange(128)[:, None] * freqs[None, :], (2, 4))
    tables = (
        np.cos(angles).astype(np.float32),
        np.sin(angles).astype(np.float32),
        (np.arange(2944, dtype=np.int32) % 23)[None],
    )
    buffers = dict(scatter_buffer_shapes())
    kept = [
        ((TOKENS, D), F32),
        ((TOKENS, D), BF16),
        ((TOKENS, 1024), BF16),
        ((TOKENS, D), BF16),
        ((TOKENS, 128), BF16),
        ((TOKENS, 128), BF16),
        ((TOKENS, 1024), BF16),
        ((2, 7, 128, 256), F32),
        ((1, 2944), F32),
        ((2, TOKENS, D), F32),
        ((2, TOKENS, D), BF16),
    ] + [(buffers[part, stage][slot], BF16) for part, stage, slot in EARLY]
    large = [
        ((4, 4, 2, 2, 2 * CHUNK, D), BF16),
        ((4, 4, 2, CHUNK, D), BF16),
        ((2, 4, 4, 2, CHUNK, D), BF16),
    ]

    def shapes(pairs):
        return [jax.ShapeDtypeStruct(shape, dtype) for shape, dtype in pairs]

    def scratch(pairs):
        return [pltpu.VMEM(shape, dtype) for shape, dtype in pairs]

    results = pl.pallas_call(
        gather_kernel,
        out_shape=shapes(kept + large),
        in_specs=[vmem] * 14,
        out_specs=[anywhere] * (KEPT + 3),
        scratch_shapes=scratch(
            kept[:9]
            + kept[11:]
            + large
            + [
                ((2, 4, 2, 2, CHUNK, D), BF16),
                ((2, 4, 4, CHUNK, D), BF16),
                ((2, 4, 2, CHUNK, D), BF16),
                ((2, TOKENS, D), BF16),
                ((2, TOKENS, D), BF16),
                ((2, 2, TOKENS, D), F32),
                ((2, TOKENS, D), BF16),
                ((2 * CHUNK, D), BF16),
                ((2 * CHUNK, D), BF16),
                ((2 * CHUNK, D), F32),
            ]
        )
        + [
            pltpu.SemaphoreType.DMA((3,)),
            pltpu.SemaphoreType.DMA((len(PARTS), 3, 6)),
            pltpu.SemaphoreType.DMA((len(PARTS), 3, 6)),
            pltpu.SemaphoreType.DMA((2, 5)),
            pltpu.SemaphoreType.DMA((3, 2)),
            pltpu.SemaphoreType.DMA((2, 3, 2)),
            pltpu.SemaphoreType.DMA((KEPT,)),
        ],
        compiler_params=pltpu.CompilerParams(
            collective_id=0, has_side_effects=True, vmem_limit_bytes=61 * 2**20
        ),
    )(*weights, x, cotangent.reshape(TOKENS, D), lengths, *tables)
    middle, e, h1p, q, k, v, mixed, probs, vector, own, parcel = results[:11]
    early = results[11:KEPT]
    grad_wide, grad_shared, rest = results[KEPT:]
    loaded = dict(
        x=x, e=e, rest=rest, middle=middle, h1p=h1p, q=q, k=k, v=v, mixed=mixed, probs=probs,
        vector=vector, own=own, parcel=parcel,
    )
    fetched = [loaded[name] for name in LOADED] + list(early)
    output, input_grad, grads = pl.pallas_call(
        scatter_kernel,
        out_shape=shapes([((TOKENS, D), BF16), ((TOKENS, D), BF16), ((4, CHUNK, D), F32)]),
        in_specs=[vmem] * 4 + [anywhere] * (2 + len(fetched)),
        out_specs=[vmem] * 3,
        scratch_shapes=scratch(
            [(value.shape, value.dtype) for value in fetched]
            + large[:2]
            + [
                ((2, 4, 4, 2, CHUNK, D), BF16),
                ((4, 4, 2, CHUNK, D), BF16),
                ((2, CHUNK, D), BF16),
                ((2, CHUNK, D), BF16),
                ((2, TOKENS, D), BF16),
                ((TOKENS, D), F32),
            ]
        )
        + [
            pltpu.SemaphoreType.DMA((len(PARTS), 4)),
            pltpu.SemaphoreType.DMA((len(PARTS), 3, 6)),
            pltpu.SemaphoreType.DMA((len(PARTS), 3, 6)),
            pltpu.SemaphoreType.DMA((2, 3)),
            pltpu.SemaphoreType.DMA((2,)),
            pltpu.SemaphoreType.DMA((len(fetched),)),
        ]
        + [
            pltpu.VMEM(shape, BF16)
            for key, group in buffers.items()
            for slot, shape in enumerate(group)
            if shape is not None and (*key, slot) not in EARLY
        ],
        compiler_params=pltpu.CompilerParams(
            collective_id=1, has_side_effects=True, vmem_limit_bytes=62 * 2**20
        ),
    )(lengths, *tables, grad_wide, grad_shared, *fetched)
    return output, input_grad, grads


def newton_schulz(gram, values):
    gram_half = half(gram)
    first = half(NEWTON_B * gram + NEWTON_C * product(gram_half, gram_half))
    cross = product(gram_half, first)
    after = NEWTON_A * NEWTON_A * gram + 2.0 * NEWTON_A * cross + product(half(cross), first)
    after_half = half(after)
    second = half(NEWTON_B * after + NEWTON_C * product(after_half, after_half))
    values = half(NEWTON_A * values + product(half(values), first))
    return half(NEWTON_A * values.astype(F32) + product(values, second))


BLOCKS = [(i, j) for i in range(7) for j in range(i, 7)]
JOB_ROWS = (48, 48, 48, 16, 16, 16, 16)


def own_momenta(grads_ref, priors, momenta, odd):
    for parity in range(2):

        @pl.when(odd == parity)
        def _():
            for n in range(3):
                for k, (start, size) in enumerate(((0, 16), (16, 16), (32, 6))):
                    base = 16 * n + (6 * parity if k == 2 else 0)
                    momenta[n][start : start + size] = (
                        MOMENTUM * priors[n][start : start + size] + grads_ref[k, base : base + size]
                    )
            for n in range(4):
                base = 16 * min(n, 2) + 7 * parity
                lanes = slice(0, D) if n < 2 else slice(128 * n - 256, 128 * n - 128)
                momenta[3 + n][...] = (
                    MOMENTUM * priors[3 + n][...] + grads_ref[3, base : base + 7, lanes]
                )


def update_kernel(output_ref, input_grad_ref, grads_ref, tall_ref, short_ref, *refs):
    priors, masters, (first_ref, second_ref, vector_ref) = refs[:7], refs[7:14], refs[14:17]
    momenta, updated, vector_outs = refs[17:24], refs[24:31], refs[31:34]
    refs[34][...] = output_ref[...]
    refs[35][...] = input_grad_ref[...]
    odd = lax.axis_index("dp") % 2
    own_momenta(grads_ref, priors, momenta, odd)
    for n in range(7):
        size = FF if n < 3 else D
        got = tall_ref[n].astype(F32)[:38] if n < 3 else short_ref[n - 3].astype(F32)[:7]
        got = got[:, :128] if n > 4 else got
        updated[n][...] = masters[n][...] * (1.0 - MUON_RATE * MUON_DECAY) - (
            MUON_RATE * 0.2 * math.sqrt(size) * got
        )
    for parity in range(2):

        @pl.when(odd == parity)
        def _():
            start = 32 + 7 * parity
            grad = grads_ref[3, start : start + 1, 256:384][:, :23]
            first = BETA_FIRST * first_ref[...] + (1.0 - BETA_FIRST) * grad
            second = BETA_SECOND * second_ref[...] + (1.0 - BETA_SECOND) * grad * grad
            first_hat = first / (1.0 - BETA_FIRST**STEP)
            second_hat = second / (1.0 - BETA_SECOND**STEP)
            vector_outs[0][...] = first
            vector_outs[1][...] = second
            vector_outs[2][...] = vector_ref[...] * (1.0 - ADAM_RATE * ADAM_DECAY) - (
                ADAM_RATE * first_hat / (jnp.sqrt(second_hat) + ADAM_EPSILON)
            )


def muon_kernel(
    grads_ref, prior0, prior1, prior2, prior3, prior4, prior5, prior6, tall_out_ref, short_out_ref,
    momentum0, momentum1, momentum2, momentum3, momentum4, momentum5, momentum6,
    tall_wide, short_wide, tall_ref, short_ref, rows, gram_out, gram_twin, gram_half_sum, gram_in, gram_all, gram, back, tall_got, short_got,
    job_sems, twin_sems, sum_sems, all_sems, back_sems,
):
    priors = (prior0, prior1, prior2, prior3, prior4, prior5, prior6)
    momenta = (momentum0, momentum1, momentum2, momentum3, momentum4, momentum5, momentum6)
    coords, core = my_coords()
    z, y, x = coords
    job = z * 2 + y // 2
    source = z * 2 + y // 2
    member = (y % 2) * 4 + x
    tall_wide[...] = jnp.zeros_like(tall_wide)
    short_wide[...] = jnp.zeros_like(short_wide)
    own_momenta(grads_ref, priors, momenta, x % 2)
    for n in range(3):
        tall_wide[n, 0:38] = momenta[n][...]
    for n in range(4):
        short_wide[n, 0:7, 0 : D if n < 2 else 128] = momenta[3 + n][...]
    tall_ref[...] = half(tall_wide[...])
    short_ref[...] = half(short_wide[...])
    twin = device_of(coords, 1 - core)

    def group(peer):
        return device_of((z, (y // 2) * 2 + peer // 4, peer % 4), core)

    def square(k):
        return device_of((k // 2, (k % 2) * 2 + y % 2, x), core)

    barrier = pltpu.get_barrier_semaphore()
    for k in range(1, 8):
        for device in (group((member + k) % 8), square((source + k) % 8)):
            pl.semaphore_signal(barrier, inc=1, device_id=device, device_id_type=MESH)
    pl.semaphore_signal(barrier, inc=1, device_id=twin, device_id_type=MESH)
    pl.semaphore_wait(barrier, 15)

    def copy(src, dst, sems, slot, device):
        return remote(src, dst, sems.at[0, slot], sems.at[1, slot], device)

    def mine(m, tall, short):
        return tall.at[m] if m < 3 else short.at[m - 3]

    def job_copy(m):
        return remote(
            mine(m, tall_ref, short_ref),
            rows.at[source, pl.ds(0, JOB_ROWS[m])],
            job_sems.at[0, m],
            job_sems.at[1, source],
            square(m),
        )

    for m in range(7):

        @pl.when(job != m)
        def _():
            job_copy(m).start()

    for kind in range(2):
        count = (48, 16)[kind]

        @pl.when((job >= 3 * kind) & (job < 3 + 4 * kind))
        def _():
            if kind == 1:
                rows[:, 16:48] = jnp.zeros((8, 32, D), BF16)
                rows[source, 0:16] = short_ref[job - 3]
            else:
                rows[source] = tall_ref[job]
            for k in range(1, 8):
                other = (source + k) % 8
                arrival = rows.at[other, pl.ds(0, count)]
                remote(
                    arrival, arrival, job_sems.at[0, 0], job_sems.at[1, other], square(other)
                ).wait_recv()

    @pl.when(job < 7)
    def _():
        flat = rows[...].reshape(384, D)
        gram[...] = inner_rows(flat, flat)
        for index, (i, j) in enumerate(BLOCKS):
            gram_out[index // 16, index % 16] = half(
                gram[128 * i : 128 * i + 128, 128 * j : 128 * j + 128]
            )
        gram_out[1, 12:16] = jnp.zeros((4, 128, 128), BF16)
        twin_copy = copy(gram_out.at[1 - core], gram_twin, twin_sems, 0, twin)
        twin_copy.start()
        twin_copy.wait()
        gram_half_sum[...] = half(gram_out[core].astype(F32) + gram_twin[...].astype(F32))

        def sum_copy(k):
            peer = (member + k) % 8
            return copy(
                gram_half_sum.at[pl.ds(2 * peer, 2)], gram_in.at[k], sum_sems, k, group(peer)
            )

        for k in range(1, 8):
            sum_copy(k).start()
        total = gram_half_sum[pl.ds(2 * member, 2)].astype(F32)
        for k in range(1, 8):
            sum_copy(k).wait_recv()
            total = total + gram_in[k].astype(F32)
        gram_all[core, pl.ds(2 * member, 2)] = half(total)

        def all_copy(k, owner):
            ref = gram_all.at[core, pl.ds(2 * owner, 2)]
            return copy(ref, ref, all_sems, k, group((member + k) % 8))

        for k in range(1, 8):
            all_copy(k, member).start()
        for k in range(1, 8):
            all_copy(k, (member + 8 - k) % 8).wait_recv()
        last_copy = copy(gram_all.at[core], gram_all.at[core], twin_sems, 1, twin)
        last_copy.start()
        last_copy.wait()

        eye = lax.broadcasted_iota(jnp.int32, (128, 128), 0) == lax.broadcasted_iota(
            jnp.int32, (128, 128), 1
        )
        trace = 0.0
        for index, (i, j) in enumerate(BLOCKS):
            block = gram_all[index // 16, index % 16].astype(F32)
            gram[128 * i : 128 * i + 128, 128 * j : 128 * j + 128] = block
            if i == j:
                trace = trace + jnp.sum(jnp.where(eye, block, 0.0))
            else:
                gram[128 * j : 128 * j + 128, 128 * i : 128 * i + 128] = block.T
        inverse = 1.0 / (jnp.sqrt(jnp.full((1, 1), trace)) + 1e-07)
        moved = newton_schulz(
            gram[...] * (inverse * inverse), rows[...].reshape(384, D).astype(F32) * inverse
        )
        back[...] = moved.reshape(8, 48, D)
        for k in range(1, 8):
            sum_copy(k).wait_send()
            all_copy(k, member).wait_send()

    for m in range(7):

        @pl.when(job == m)
        def _():
            copies = []
            for k in range(1, 8):
                other = (source + k) % 8
                copies.append(
                    remote(
                        back.at[other, pl.ds(0, JOB_ROWS[m])],
                        mine(m, tall_got, short_got),
                        back_sems.at[0, k],
                        back_sems.at[1, m],
                        square(other),
                    )
                )
            for item in copies:
                item.start()
            if m < 3:
                tall_got[m] = back[source]
            else:
                short_got[m - 3] = back[source, 0:16]
            for item in copies:
                item.wait_send()

    for m in range(7):

        @pl.when(job != m)
        def _():
            arrival = mine(m, tall_got, short_got)
            remote(arrival, arrival, back_sems.at[0, 0], back_sems.at[1, m], square(m)).wait_recv()
            job_copy(m).wait_send()

    tall_out_ref[...] = tall_got[...]
    short_out_ref[...] = short_got[...]


def muon(results, grads, priors, masters, vectors):
    vmem = pl.BlockSpec(memory_space=pltpu.VMEM)
    tall, short = pl.pallas_call(
        muon_kernel,
        out_shape=(
            jax.ShapeDtypeStruct((3, 48, D), BF16),
            jax.ShapeDtypeStruct((4, 16, D), BF16),
        ),
        in_specs=[vmem] * 8,
        out_specs=[vmem] * 2,
        scratch_shapes=[
            *(pltpu.VMEM(value.shape, F32) for value in priors),
            pltpu.VMEM((3, 48, D), F32),
            pltpu.VMEM((4, 16, D), F32),
            pltpu.VMEM((3, 48, D), BF16),
            pltpu.VMEM((4, 16, D), BF16),
            pltpu.VMEM((8, 48, D), BF16),
            pltpu.VMEM((2, 16, 128, 128), BF16),
            pltpu.VMEM((16, 128, 128), BF16),
            pltpu.VMEM((16, 128, 128), BF16),
            pltpu.VMEM((8, 2, 128, 128), BF16),
            pltpu.VMEM((2, 16, 128, 128), BF16),
            pltpu.VMEM((D, D), F32),
            pltpu.VMEM((8, 48, D), BF16),
            pltpu.VMEM((3, 48, D), BF16),
            pltpu.VMEM((4, 16, D), BF16),
            pltpu.SemaphoreType.DMA((2, 8)),
            pltpu.SemaphoreType.DMA((2, 2)),
            pltpu.SemaphoreType.DMA((2, 8)),
            pltpu.SemaphoreType.DMA((2, 8)),
            pltpu.SemaphoreType.DMA((2, 8)),
        ],
        compiler_params=pltpu.CompilerParams(
            collective_id=3, has_side_effects=True, vmem_limit_bytes=58 * 2**20
        ),
    )(grads, *priors)
    outs = [*priors, *masters, *vectors]
    return pl.pallas_call(
        update_kernel,
        out_shape=[jax.ShapeDtypeStruct(value.shape, value.dtype) for value in [*outs, *results]],
        in_specs=[vmem] * 22,
        out_specs=[vmem] * 19,
    )(*results, grads, tall, short, *outs)


def body(
    inputs,
    cotangent,
    lengths,
    query_weight,
    key_weight,
    value_weight,
    out_weight,
    gate_weight,
    up_weight,
    down_weight,
    vectors,
    query_prior,
    key_prior,
    value_prior,
    out_prior,
    gate_prior,
    up_prior,
    down_prior,
    first_prior,
    second_prior,
):
    weights = (
        gate_weight.T, up_weight.T, down_weight, query_weight, out_weight, key_weight, value_weight,
        vectors[None],
    )
    block_output, input_grad, grads = layer(weights, inputs[:, 0], cotangent[:, 0], lengths)
    results = muon(
        (block_output, input_grad),
        grads,
        (gate_prior.T, up_prior.T, down_prior, query_prior, out_prior, key_prior, value_prior),
        (gate_weight.T, up_weight.T, down_weight, query_weight, out_weight, key_weight, value_weight),
        (first_prior[None], second_prior[None], vectors[None]),
    )

    def ordered(gate, up, down, query, out, key, value):
        return query, key, value, out, gate.T, up.T, down

    return (
        *(value.reshape(2, 1, 128, D) for value in results[17:]),
        *ordered(*results[:7]),
        *ordered(*results[7:14]),
        *(value[0] for value in results[14:17]),
    )


def solution(mesh):
    placed = (
        P(None, ("dp", "narrow"), None, None),
        P(None, ("dp", "narrow"), None, None),
        P(),
        P(("dp", "narrow"), None),
        P(("dp", "narrow"), None),
        P(("dp", "narrow"), None),
        P(("dp", "narrow"), None),
        P(None, ("dp", "narrow")),
        P(None, ("dp", "narrow")),
        P(("dp", "narrow"), None),
        P(("dp", "narrow")),
        P(("dp", "narrow"), None),
        P(("dp", "narrow"), None),
        P(("dp", "narrow"), None),
        P(("dp", "narrow"), None),
        P(None, ("dp", "narrow")),
        P(None, ("dp", "narrow")),
        P(("dp", "narrow"), None),
        P(("dp", "narrow")),
        P(("dp", "narrow")),
    )
    return jax.shard_map(
        body,
        mesh=mesh,
        in_specs=placed,
        out_specs=(
            P(None, ("dp", "narrow"), None, None),
            P(None, ("dp", "narrow"), None, None),
            P(("dp", "narrow"), None),
            P(("dp", "narrow"), None),
            P(("dp", "narrow"), None),
            P(("dp", "narrow"), None),
            P(None, ("dp", "narrow")),
            P(None, ("dp", "narrow")),
            P(("dp", "narrow"), None),
            P(("dp", "narrow"), None),
            P(("dp", "narrow"), None),
            P(("dp", "narrow"), None),
            P(("dp", "narrow"), None),
            P(None, ("dp", "narrow")),
            P(None, ("dp", "narrow")),
            P(("dp", "narrow"), None),
            P(("dp", "narrow")),
            P(("dp", "narrow")),
            P(("dp", "narrow")),
        ),
        check_vma=False,
    )
```
